128 devices in a mesh: expert: 32 (over z, x, y_hi), tensor: 4 (over y_lo, core).
Axes of the slice: x: 4, y: 4 (y_hi: 2, y_lo: 2; y = y_hi * 2 + y_lo), z: 4, core: 2. Of those that a mesh axis runs over, the one named last changes fastest.
Arguments:
- layer_input: bfloat16 [16384, 768], P('expert'), may hold values from -6 to 6
- attn_gain: float32 [768], replicated, may hold values from 0.1 to 1.9
- query_weight: bfloat16 [768, 768], P(None, 'tensor'), may hold values from -0.21875 to 0.21875
- key_weight: bfloat16 [768, 768], P(None, 'tensor'), may hold values from -0.21875 to 0.21875
- value_weight: bfloat16 [768, 768], P(None, 'tensor'), may hold values from -0.21875 to 0.21875
- output_weight: bfloat16 [768, 768], P('tensor'), may hold values from -1.75 to 1.75
- position_bias: float32 [32, 12], P(None, 'tensor'), may hold values from -4 to 4
- moe_gain: float32 [768], replicated, may hold values from 0.1 to 1.9
- router_weight: bfloat16 [768, 64], replicated, may hold values from -0.107910156 to 0.107910156
- expert_in: bfloat16 [64, 768, 3072], P('expert', None, 'tensor'), may hold values from -0.21875 to 0.21875
- expert_out: bfloat16 [64, 3072, 768], P('expert', 'tensor'), may hold values from -12.75 to 12.75
- route_expert: int32 [16384], P('expert'), may hold values from 0 to 63, as said below
- route_slot: int32 [16384], P('expert'), may hold values from 0 to 9
- route_drop: int32 [16384], P('expert'), may hold values from 0 to 1
- out_grad: bfloat16 [16384, 768], P('expert'), may hold values from -6 to 6
Outputs:
- layer_output: bfloat16 [16384, 768], P('expert')
- input_grad: float32 [16384, 768], P('expert')
- attn_gain_grad: float32 [768], replicated
- query_grad: float32 [768, 768], P(None, 'tensor')
- key_grad: float32 [768, 768], P(None, 'tensor')
- value_grad: float32 [768, 768], P(None, 'tensor')
- output_grad: float32 [768, 768], P('tensor')
- bias_grad: float32 [32, 12], P(None, 'tensor')
- moe_gain_grad: float32 [768], replicated
- router_grad: float32 [768, 64], replicated
- expert_in_grad: float32 [64, 768, 3072], P('expert', None, 'tensor')
- expert_out_grad: float32 [64, 3072, 768], P('expert', 'tensor')
The draws below stay inside these ranges and needn't reach their ends.
Inputs may be any that keep to these rules, and one draw needn't show every extreme that they name: On each index of expert, the kept tokens (route_drop 0) hold distinct pairs of route_expert and route_slot, and 64 tokens are dropped; some expert is given all 10 slots by every index of expert, and the dropped tokens name that expert and slot 0.
All inputs are finite; a program needn't handle non-finite values.
Results may differ from the reference program's by a relative error of at most 0.029.
Values may be sent and summed in bfloat16 or wider, within the bound.
No kernel may reach another device: no remote copies, remote signals or barrier semaphores. Data moves between devices by JAX's collectives and lax.ppermute only.
A program may use at most 128 MiB of HBM per device.

```python
import jax
import jax.numpy as jnp
import numpy as np
from jax import lax

D = 768
HEADS = 12
HEAD_DIM = 64
FF = 3072
BUCKETS = 32
SEQ_LEN = 512
TOK_DEV = 512
TOKENS = 16384
EXPERTS = 64
CAP = 10
N_EXPERT = 32


def route_table(key):
    groups = TOKENS // TOK_DEV
    slot_count = EXPERTS * CAP
    kept_count = TOK_DEV - TOK_DEV // 8
    common = jax.random.randint(jax.random.fold_in(key, 1), (), 0, EXPERTS).astype(jnp.int32)

    def one_group(index):
        subkey = jax.random.fold_in(key, index + 2)
        first, second, third = jax.random.split(subkey, 3)
        own_expert = jax.random.randint(first, (), 0, EXPERTS).astype(jnp.int32)
        order = jax.random.permutation(second, slot_count).astype(jnp.int32)
        slot_expert = jnp.arange(slot_count, dtype=jnp.int32) // CAP
        priority = order + slot_count * ((slot_expert == common).astype(jnp.int32) + (slot_expert == own_expert).astype(jnp.int32))
        ignored, chosen = lax.top_k(priority, kept_count)
        chosen = chosen.astype(jnp.int32)
        shuffle = jax.random.permutation(third, TOK_DEV).astype(jnp.int32)
        rest = TOK_DEV - kept_count
        expert_values = jnp.concatenate([chosen // CAP, jnp.full((rest,), 1, jnp.int32) * common])
        slot_values = jnp.concatenate([chosen % CAP, jnp.zeros((rest,), jnp.int32)])
        drop_values = jnp.concatenate([jnp.zeros((kept_count,), jnp.int32), jnp.ones((rest,), jnp.int32)])
        expert_column = jnp.zeros((TOK_DEV,), jnp.int32).at[shuffle].set(expert_values)
        slot_column = jnp.zeros((TOK_DEV,), jnp.int32).at[shuffle].set(slot_values)
        drop_column = jnp.zeros((TOK_DEV,), jnp.int32).at[shuffle].set(drop_values)
        return (expert_column, slot_column, drop_column)
    expert_all, slot_all, drop_all = jax.vmap(one_group)(jnp.arange(groups, dtype=jnp.int32))
    return (expert_all.reshape(TOKENS), slot_all.reshape(TOKENS), drop_all.reshape(TOKENS))


def draw_route_expert(key, part):
    tables = route_table(key)
    return tables[0]


def draw_route_slot(key, part):
    tables = route_table(key)
    return tables[1]


def draw_route_drop(key, part):
    tables = route_table(key)
    return tables[2]


def steps_of(stream_key, extent, cuts, low, high):
    gain, own = 1.0, jax.random.fold_in(stream_key, 6)
    for dim, blocks in cuts:
        heights = jnp.exp(jax.random.uniform(jax.random.fold_in(own, dim), (blocks,), jnp.float32, low / len(cuts), high / len(cuts)))
        gain = gain * jnp.repeat(heights, extent[dim] // blocks).reshape([-1 if axis == dim else 1 for axis in range(len(extent))])
    return gain


def bell_draw(rng, extent, scale, limit, cuts=(), held_as=jnp.bfloat16):
    drawn = scale * jax.random.normal(rng, extent, jnp.float32)
    if cuts:
        drawn = drawn * steps_of(rng, extent, cuts, -0.22, 0.18)
    return jnp.clip(drawn, -limit, limit).astype(held_as)


def setup_inputs(seed: int = 0) -> dict:
    streams_of = jax.random.split(jax.random.key(seed), 16)
    return {
        "layer_input": bell_draw(streams_of[0], (TOKENS, D), 1.0, 6.0, ((0, 32),)),
        "attn_gain": jnp.clip(1.0 + 0.18 * jax.random.normal(streams_of[1], (D,), jnp.float32), 0.1, 1.9),
        "query_weight": bell_draw(streams_of[2], (D, D), D ** -0.5, 0.21875, ((1, 4),)),
        "key_weight": bell_draw(streams_of[3], (D, D), D ** -0.5, 0.21875, ((1, 4),)),
        "value_weight": bell_draw(streams_of[4], (D, D), D ** -0.5, 0.21875, ((1, 4),)),
        "output_weight": bell_draw(streams_of[5], (D, D), (D // 64) ** -0.5, 1.75, ((0, 4),)),
        "position_bias": bell_draw(streams_of[6], (BUCKETS, HEADS), 1.0, 4.0, ((1, 4),), jnp.float32),
        "moe_gain": jnp.clip(1.0 + 0.18 * jax.random.normal(streams_of[7], (D,), jnp.float32), 0.1, 1.9),
        "router_weight": bell_draw(streams_of[8], (D, EXPERTS), 0.018, 0.107910156),
        "expert_in": bell_draw(streams_of[9], (EXPERTS, D, FF), D ** -0.5, 0.21875, ((0, 32), (2, 4))),
        "expert_out": bell_draw(streams_of[10], (EXPERTS, FF, D), (EXPERTS / 32), 12.75, ((0, 32), (1, 4))),
        "route_expert": draw_route_expert(jax.random.fold_in(streams_of[15], 71), 0),
        "route_slot": draw_route_slot(jax.random.fold_in(streams_of[15], 71), 0),
        "route_drop": draw_route_drop(jax.random.fold_in(streams_of[15], 71), 0),
        "out_grad": bell_draw(streams_of[14], (TOKENS, D), 1.0, 6.0, ((0, 32),)),
    }


EPSILON = 1e-06
HIGHEST_PRECISION = lax.Precision.HIGHEST

@jax.custom_vjp
def low(v):
    return lax.optimization_barrier(v.astype(jnp.bfloat16)).astype(jnp.float32)

@jax.custom_vjp
def low_back(v):
    return v

def low_keep(v):
    return (low(v), None)

def low_pass(kept, grad):
    return (grad,)

def back_keep(v):
    return (v, None)

def back_low(kept, grad):
    return (low(grad),)
low.defvjp(low_keep, low_pass)
low_back.defvjp(back_keep, back_low)

def bucket_table(length, buckets):
    offsets = np.arange(length)[None, :] - np.arange(length)[:, None]
    half_count = buckets // 2
    exact_count = half_count // 2
    upper_side = (offsets > 0).astype(np.int64) * half_count
    distance = np.abs(offsets)
    ratio = np.log(np.maximum(distance, 1) / exact_count) / np.log(128.0 / exact_count)
    far_bucket = np.minimum(exact_count + (ratio * (half_count - exact_count)).astype(np.int64), half_count - 1)
    return (upper_side + np.where(distance < exact_count, distance, far_bucket)).astype(np.int32)

def rms_norm(values, gain_vector):
    return values * lax.rsqrt(lax.optimization_barrier(jnp.mean(values * values, axis=-1, keepdims=True)) + EPSILON) * gain_vector

def attend(queries, keys, values, bias):
    scores = jnp.einsum('qhc,khc->hqk', queries, keys, precision=HIGHEST_PRECISION) * HEAD_DIM ** (-0.5) + bias
    scores = low_back(scores)
    probs = low(jax.nn.softmax(scores, axis=-1))
    return jnp.einsum('hqk,khc->qhc', probs, values, precision=HIGHEST_PRECISION)

def layer(hidden, attn_gain, query_weight, key_weight, value_weight, output_weight, position_bias, moe_gain, router_weight, expert_in, expert_out, route_expert, route_slot, route_drop):
    seq_count = TOKENS // SEQ_LEN
    normed = low(rms_norm(hidden, attn_gain))

    def project(weight):
        projected = low(low_back(jnp.dot(normed, weight, precision=HIGHEST_PRECISION)))
        return projected.reshape(seq_count, SEQ_LEN, HEADS, HEAD_DIM)
    queries = project(query_weight)
    keys = project(key_weight)
    values = project(value_weight)
    bucket_index = jnp.asarray(bucket_table(SEQ_LEN, BUCKETS))
    bias = jnp.transpose(position_bias[bucket_index], (2, 0, 1))
    attend_one = jax.checkpoint(lambda pieces: attend(pieces[0], pieces[1], pieces[2], bias))
    context = lax.map(attend_one, (queries, keys, values))
    context = low(low_back(context.reshape(TOKENS, D)))
    attended = low_back(jnp.dot(context, output_weight, precision=HIGHEST_PRECISION))
    middle = hidden + attended
    mixed = low(rms_norm(middle, moe_gain))
    logits = low_back(jnp.dot(mixed, router_weight, precision=HIGHEST_PRECISION))
    router_probs = jax.nn.softmax(logits, axis=-1)
    kept_mask = (1 - route_drop).astype(jnp.float32)
    gate_value = jnp.take_along_axis(router_probs, route_expert[:, None], axis=1)[:, 0] * kept_mask
    source_index = jnp.arange(TOKENS, dtype=jnp.int32) // TOK_DEV
    slot_row = (source_index * CAP + route_slot).astype(jnp.int32)
    slots = jnp.zeros((EXPERTS, N_EXPERT * CAP, D), jnp.float32).at[route_expert, slot_row].add(mixed * kept_mask[:, None])
    pre_act = low_back(jnp.einsum('erd,edf->erf', slots, expert_in, precision=HIGHEST_PRECISION))
    activated = low(jax.nn.gelu(pre_act))
    expert_output = low(low_back(jnp.einsum('erf,efd->erd', activated, expert_out, precision=HIGHEST_PRECISION)))
    expert_rows = expert_output[route_expert, slot_row]
    return middle + gate_value[:, None] * expert_rows

def reference(layer_input, attn_gain, query_weight, key_weight, value_weight, output_weight, position_bias, moe_gain, router_weight, expert_in, expert_out, route_expert, route_slot, route_drop, out_grad):
    floats = (layer_input.astype(jnp.float32), attn_gain, query_weight.astype(jnp.float32), key_weight.astype(jnp.float32), value_weight.astype(jnp.float32), output_weight.astype(jnp.float32), position_bias, moe_gain, router_weight.astype(jnp.float32), expert_in.astype(jnp.float32), expert_out.astype(jnp.float32))

    def forward(*params):
        return layer(*params, route_expert, route_slot, route_drop)
    result, pullback = jax.vjp(forward, *floats)
    grads = pullback(out_grad.astype(jnp.float32))
    return (result.astype(jnp.bfloat16), grads[0], grads[1], grads[2], grads[3], grads[4], grads[5], grads[6], grads[7], grads[8], grads[9], grads[10])
```

```python
import jax
import jax.numpy as jnp
import numpy as np
from jax import lax
from jax.experimental import pallas as pl
from jax.experimental.pallas import tpu as pltpu
from jax.sharding import Mesh
from jax.sharding import PartitionSpec as P

BUCKETS = 32
EPS = 1e-06
SEQ = 512
D = 768
HEAD = 64
HEADS_HERE = 3
WIDTH = HEADS_HERE * HEAD
EXPERTS = 64
CAP = 10
GROUPS = 32
CHUNK = 40
ROWS = GROUPS * CHUNK
HALF = D // 2
GRADS = 896
F32 = jnp.float32
BF16 = jnp.bfloat16
GELU_C = float(np.sqrt(2.0 / np.pi))


def bucket_of(offsets):
    half_count = BUCKETS // 2
    exact_count = half_count // 2
    upper_side = (offsets > 0).astype(np.int64) * half_count
    distance = np.abs(offsets)
    ratio = np.log(np.maximum(distance, 1) / exact_count) / np.log(128.0 / exact_count)
    far_bucket = np.minimum(
        exact_count + (ratio * (half_count - exact_count)).astype(np.int64), half_count - 1
    )
    return upper_side + np.where(distance < exact_count, distance, far_bucket)


def line_ids():
    ids = np.full((8, 256), -1, np.int32)
    for row, block in enumerate((-1, 0, 1)):
        ids[row] = bucket_of(128 * block + 128 - np.arange(256))
    ids[:3, 0] = -1
    return ids


def regroup_matrix():
    sel = np.zeros((320, 320), np.float32)
    for g in range(8):
        for half in range(2):
            for e in range(2):
                for c in range(CAP):
                    sel[half * 160 + e * 80 + g * 10 + c, g * 40 + half * 20 + e * 10 + c] = 1
    return sel


def spread_matrix(width, start, total):
    out = np.zeros((width, total), np.float32)
    out[np.arange(width), start + np.arange(width)] = 1
    return out


def dot(a, b):
    return jnp.dot(a, b, preferred_element_type=F32)


def dot_nt(a, b):
    return lax.dot_general(a, b, (((1,), (1,)), ((), ())), preferred_element_type=F32)


def dot_tn(a, b):
    return lax.dot_general(a, b, (((0,), (0,)), ((), ())), preferred_element_type=F32)


def head_mask(head, rows):
    lanes = lax.broadcasted_iota(jnp.int32, (rows, WIDTH), 1)
    return (lanes >= head * HEAD) & (lanes < (head + 1) * HEAD)


def only_head(matrix, head):
    return jnp.where(head_mask(head, matrix.shape[0]), matrix, jnp.zeros_like(matrix))


def call(body, out_shape, args, scratch=(), scalars=0, limit=40, flops=0, moved=0):
    specs = [pl.BlockSpec(memory_space=pltpu.SMEM)] * scalars
    specs += [pl.BlockSpec(memory_space=pltpu.VMEM)] * (len(args) - scalars)
    return pl.pallas_call(
        body,
        out_shape=out_shape,
        in_specs=specs,
        out_specs=jax.tree.map(lambda _: pl.BlockSpec(memory_space=pltpu.VMEM), out_shape),
        scratch_shapes=scratch,
        compiler_params=pltpu.CompilerParams(vmem_limit_bytes=limit << 20),
        cost_estimate=pl.CostEstimate(flops=flops, bytes_accessed=moved, transcendentals=0),
    )(*args)


def shape(dims, dtype):
    return jax.ShapeDtypeStruct(dims, dtype)


def bias_tile(tiles_ref, far_low, far_high, head, block):
    if block < -1:
        return far_low
    if block > 1:
        return far_high
    return tiles_ref[head * 3 + block + 1]


def scores_t(keys, query_scaled, tiles_ref, table_ref, head, part):
    raw = dot_nt(keys, query_scaled)
    far_low = table_ref[BUCKETS // 2 - 1, head]
    far_high = table_ref[BUCKETS - 1, head]
    rows = []
    for key_block in range(4):
        cols = []
        for i in range(2):
            piece = raw[key_block * 128 : key_block * 128 + 128, i * 128 : i * 128 + 128]
            block = key_block - (part * 2 + i)
            cols.append(piece + bias_tile(tiles_ref, far_low, far_high, head, block))
        rows.append(jnp.concatenate(cols, axis=1))
    return jnp.concatenate(rows, axis=0)


def attention_forward(
    table_ref, x_ref, gain_ref, wq_ref, wk_ref, wv_ref, ids_ref,
    normed_ref, q_ref, k_ref, v_ref, ctx_ref, lse_ref, tiles_ref,
):
    for i in range(4):
        rows = pl.ds(i * 128, 128)
        x = x_ref[rows, :].astype(F32)
        scale = lax.rsqrt(jnp.mean(x * x, axis=-1, keepdims=True) + EPS)
        normed_ref[rows, :] = (x * scale * gain_ref[...]).astype(BF16)
    for head in range(HEADS_HERE):
        for block in range(3):
            ids = ids_ref[block : block + 1, :]
            line = jnp.zeros((1, 256), F32)
            for b in range(BUCKETS):
                line = jnp.where(ids == b, table_ref[b, head], line)
            wide = pltpu.roll(
                jnp.broadcast_to(line, (128, 256)), 0, 1, stride=1, stride_axis=0
            )
            tiles_ref[head * 3 + block] = wide[:, 128:]
    normed = normed_ref[...]
    queries = dot(normed, wq_ref[...]).astype(BF16)
    keys = dot(normed, wk_ref[...]).astype(BF16)
    values = dot(normed, wv_ref[...]).astype(BF16)
    q_ref[...] = queries
    k_ref[...] = keys
    v_ref[...] = values
    lse_ref[...] = jnp.zeros((8, SEQ), F32)
    scaled = queries * jnp.asarray(HEAD**-0.5, BF16)
    for part in range(2):
        rows = slice(part * 256, part * 256 + 256)
        context = jnp.zeros((256, WIDTH), F32)
        for head in range(HEADS_HERE):
            scores = scores_t(
                keys, only_head(scaled[rows], head), tiles_ref, table_ref, head, part
            )
            top = jnp.max(scores, axis=0, keepdims=True)
            grown = jnp.exp(scores - top)
            total = jnp.sum(grown, axis=0, keepdims=True)
            probs = (grown * (1.0 / total)).astype(BF16)
            lse_ref[head : head + 1, rows] = top + jnp.log(total)
            context = context + dot_tn(probs, only_head(values, head))
        ctx_ref[rows, :] = context.astype(BF16)


def route_columns(route_ref):
    return jnp.transpose(route_ref[...].astype(F32))


def row_of(expert, slot, drop):
    row = (expert >> 1) * CHUNK + (expert & 1) * CAP + slot
    return jnp.where(drop > 0, -1000, row)


def middle_kernel(
    place_ref, x_ref, ctx0, ctx1, ctx2, ctx3, wo0, wo1, wo2, wo3, gain_ref, router_ref,
    route_ref, grad_ref, middle_ref, mixed_ref, probs_ref, send_ref, ctx_s, wo_s, rows_s,
):
    me = place_ref[0]
    core = place_ref[1]
    for step, (c, w) in enumerate(((ctx0, wo0), (ctx1, wo1), (ctx2, wo2), (ctx3, wo3))):
        ctx_s[me ^ step] = c[...]
        wo_s[me ^ step] = w[...]
    columns = route_columns(route_ref)
    for i in range(2):
        rows = slice(i * 256, i * 256 + 256)
        attended = dot(ctx_s[0, rows, :], wo_s[0])
        for t in range(1, 4):
            attended = attended + dot(ctx_s[t, rows, :], wo_s[t])
        middle = x_ref[rows, :].astype(F32) + attended
        scale = lax.rsqrt(jnp.mean(middle * middle, axis=-1, keepdims=True) + EPS)
        mixed = (middle * scale * gain_ref[...]).astype(BF16)
        middle_ref[rows, :] = middle
        mixed_ref[rows, :] = mixed
        logits = dot(mixed, router_ref[...])
        grown = jnp.exp(logits - jnp.max(logits, axis=-1, keepdims=True))
        probs = grown / jnp.sum(grown, axis=-1, keepdims=True)
        probs_ref[rows, :] = probs
        expert = columns[rows, 0:1].astype(jnp.int32)
        lanes = lax.broadcasted_iota(jnp.int32, (256, EXPERTS), 1)
        chosen = jnp.sum(jnp.where(lanes == expert, probs, 0.0), axis=-1, keepdims=True)
        gate = chosen * (1.0 - columns[rows, 2:3])
        grads = (grad_ref[rows, :].astype(F32) * gate).astype(BF16)
        rows_s[rows, :] = jnp.where(core == 0, mixed, grads)
    target = row_of(route_ref[0:1, :], route_ref[1:2, :], route_ref[2:3, :])
    for i in range(4):
        index = lax.broadcasted_iota(jnp.int32, (320, SEQ), 0) + 320 * i
        low = (index == target).astype(F32).astype(BF16)
        high = (index == target + 20).astype(F32).astype(BF16)
        out = dot(low, rows_s[:, :HALF]) + dot(high, rows_s[:, HALF:])
        send_ref[pl.ds(i * 320, 320), :] = out.astype(BF16)


def expert_kernel(
    place_ref, own_ref, other_ref, in_ref, out_ref, sel_ref, back_ref,
    mine_ref, theirs_ref, x_ref, s_ref, act_ref, pre_ref, o_s, i_s,
):
    core = place_ref[1]
    for b in range(4):
        rows = pl.ds(b * 320, 320)
        own = own_ref[rows, :]
        other = other_ref[rows, :]
        for dest, block in (
            (x_ref, jnp.where(core == 0, own, other)),
            (s_ref, jnp.where(core == 0, other, own)),
        ):
            sorted_rows = dot(sel_ref[...], block).astype(BF16)
            for half in range(2):
                for e in range(2):
                    dest[e, pl.ds(b * 80, 80), pl.ds(half * HALF, HALF)] = sorted_rows[
                        half * 160 + e * 80 : half * 160 + e * 80 + 80
                    ]
    for e in range(2):
        x = x_ref[e]
        s = s_ref[e]
        out = jnp.zeros((320, D), F32)
        back = jnp.zeros((320, D), F32)
        for f in range(3):
            cols = slice(f * 256, f * 256 + 256)
            w_in = in_ref[e, :, cols]
            w_out = out_ref[e, cols, :]
            pre = dot(x, w_in)
            bent = jnp.tanh(GELU_C * (pre + 0.044715 * (pre * pre * pre)))
            cdf = 0.5 * (1.0 + bent)
            act = (pre * cdf).astype(BF16)
            slope = cdf + (0.5 * GELU_C) * pre * (1.0 - bent * bent) * (
                1.0 + (3 * 0.044715) * (pre * pre)
            )
            act_ref[e, :, cols] = act
            out = out + dot(act, w_out)
            act_grad = dot_nt(s, w_out)
            pre_grad = (act_grad * slope).astype(BF16)
            pre_ref[e, :, cols] = pre_grad
            back = back + dot_nt(pre_grad, w_in)
        o_s[e] = out.astype(BF16)
        i_s[e] = back.astype(BF16)
    for b in range(4):
        rows = pl.ds(b * 80, 80)
        pieces = []
        for src in (o_s, i_s):
            stacked = jnp.concatenate(
                [
                    src[e, rows, pl.ds(half * HALF, HALF)]
                    for half in range(2)
                    for e in range(2)
                ],
                axis=0,
            )
            pieces.append(dot(back_ref[...], stacked).astype(BF16))
        mine_ref[pl.ds(b * 320, 320), :] = jnp.where(core == 0, pieces[0], pieces[1])
        theirs_ref[pl.ds(b * 320, 320), :] = jnp.where(core == 0, pieces[1], pieces[0])


def expert_grads_kernel(x_ref, s_ref, act_ref, pre_ref, in_grad_ref, out_grad_ref):
    out_grad_ref[0] = dot_tn(act_ref[0], s_ref[0])
    in_grad_ref[0] = dot_tn(x_ref[0], pre_ref[0])


def expert_grads(x, s, act, pre):
    whole = pl.BlockSpec((1, 320, D), lambda e, f: (e, 0, 0))
    part = pl.BlockSpec((1, 320, 256), lambda e, f: (e, 0, f))
    return pl.pallas_call(
        expert_grads_kernel,
        grid=(2, 3),
        out_shape=(shape((2, D, D), F32), shape((2, D, D), F32)),
        in_specs=[whole, whole, part, part],
        out_specs=(
            pl.BlockSpec((1, D, 256), lambda e, f: (e, 0, f)),
            pl.BlockSpec((1, 256, D), lambda e, f: (e, f, 0)),
        ),
        compiler_params=pltpu.CompilerParams(vmem_limit_bytes=24 << 20),
        cost_estimate=pl.CostEstimate(
            flops=8 * 320 * D * D, bytes_accessed=14_000_000, transcendentals=0
        ),
    )(x, s, act, pre)


def tokens_kernel(route_ref, recv_ref, out_ref):
    columns = route_columns(route_ref).astype(jnp.int32)
    target = row_of(columns[:, 0:1], columns[:, 1:2], columns[:, 2:3])
    slots = (
        recv_ref[pl.ds(0, ROWS), :].astype(F32) + recv_ref[pl.ds(ROWS, ROWS), :].astype(F32)
    ).astype(BF16)
    for i in range(2):
        rows = slice(i * 256, i * 256 + 256)
        index = lax.broadcasted_iota(jnp.int32, (256, ROWS), 1)
        low = (index == target[rows]).astype(F32).astype(BF16)
        high = (index == target[rows] + 20).astype(F32).astype(BF16)
        out_ref[rows, pl.ds(0, HALF)] = dot(low, slots).astype(BF16)
        out_ref[rows, pl.ds(HALF, HALF)] = dot(high, slots).astype(BF16)


def backward_kernel(
    place_ref, table_ref, x_ref, middle_ref, mixed_ref, probs_ref, route_ref, grad_ref,
    own_ref, other_ref, router_ref, gain_ref, wo_ref, ctx_ref, q_ref, k_ref, v_ref, normed_ref,
    lse_ref, tiles_ref, wq_ref, wk_ref, wv_ref, ids_ref, place_q, place_r,
    output_ref, middle_grad_ref, grads_ref, small_ref, mine_ref, theirs_ref,
    low_s, logit_s, normed_s,
):
    core = place_ref[1]
    columns = route_columns(route_ref)
    gain = gain_ref[...]
    gain_grad = jnp.zeros((1, D), F32)
    for i in range(4):
        rows = slice(i * 128, i * 128 + 128)
        own = own_ref[rows, :]
        other = other_ref[rows, :]
        expert_rows = jnp.where(core == 0, own, other).astype(F32)
        mixed_grad = jnp.where(core == 0, other, own).astype(F32)
        probs = probs_ref[rows, :]
        kept = 1.0 - columns[rows, 2:3]
        lanes = lax.broadcasted_iota(jnp.int32, (128, EXPERTS), 1)
        hot = (lanes == columns[rows, 0:1].astype(jnp.int32)).astype(F32)
        chosen = jnp.sum(probs * hot, axis=-1, keepdims=True)
        middle = middle_ref[rows, :]
        upstream = grad_ref[rows, :].astype(F32)
        output_ref[rows, :] = (middle + (chosen * kept) * expert_rows).astype(BF16)
        gate_grad = jnp.sum(upstream * expert_rows, axis=-1, keepdims=True) * kept
        logit_grad = (probs * (hot - chosen) * gate_grad).astype(BF16)
        logit_s[rows, :] = logit_grad
        mixed_grad = mixed_grad + dot_nt(logit_grad, router_ref[...])
        scale = lax.rsqrt(jnp.mean(middle * middle, axis=-1, keepdims=True) + EPS)
        weighted = mixed_grad * gain
        inner = jnp.mean(weighted * middle, axis=-1, keepdims=True)
        gain_grad = gain_grad + jnp.sum(mixed_grad * middle * scale, axis=0, keepdims=True)
        middle_grad = upstream + scale * weighted - middle * (scale * scale * scale * inner)
        middle_grad_ref[rows, :] = middle_grad
        low_s[rows, :] = middle_grad.astype(BF16)
    middle_low = low_s[...]
    output_grad = dot_tn(middle_low, ctx_ref[...])
    pad = jnp.zeros((D, 256 - WIDTH), F32)
    grads_ref[:, 640:] = jnp.concatenate([output_grad, pad], axis=1).astype(BF16)
    ctx_grad = dot_nt(middle_low, wo_ref[...]).astype(BF16)

    keys = k_ref[...]
    values = v_ref[...]
    key_scaled = keys * jnp.asarray(HEAD**-0.5, BF16)
    query_scaled = q_ref[...] * jnp.asarray(HEAD**-0.5, BF16)
    key_grad = jnp.zeros((SEQ, WIDTH), F32)
    value_grad = jnp.zeros((SEQ, WIDTH), F32)
    query_grads = [jnp.zeros((256, WIDTH), F32), jnp.zeros((256, WIDTH), F32)]
    small_ref[...] = jnp.zeros((8, D), F32)
    small_ref[0:1, :] = gain_grad
    turn = (
        lax.broadcasted_iota(jnp.int32, (128, 128), 0)
        + lax.broadcasted_iota(jnp.int32, (128, 128), 1)
        == 127
    ).astype(F32)
    for head in range(HEADS_HERE):
        near = [jnp.zeros((128, 128), F32) for _ in range(3)]
        far_low = jnp.zeros((128, 128), F32)
        far_high = jnp.zeros((128, 128), F32)
        key_head = only_head(key_scaled, head)
        for part in range(2):
            rows = slice(part * 256, part * 256 + 256)
            query_head = only_head(query_scaled[rows], head)
            ctx_head = only_head(ctx_grad[rows], head)
            scores = scores_t(keys, query_head, tiles_ref, table_ref, head, part)
            probs = jnp.exp(scores - lse_ref[head : head + 1, rows])
            value_grad = value_grad + dot(probs.astype(BF16), ctx_head)
            prob_grad = dot_nt(values, ctx_head)
            inner = jnp.sum(probs * prob_grad, axis=0, keepdims=True)
            score_grad = (probs * (prob_grad - inner)).astype(BF16)
            key_grad = key_grad + dot(score_grad, query_head)
            query_grads[part] = query_grads[part] + dot_tn(score_grad, key_head)
            for key_block in range(4):
                for i in range(2):
                    piece = score_grad[
                        key_block * 128 : key_block * 128 + 128, i * 128 : i * 128 + 128
                    ].astype(F32)
                    block = key_block - (part * 2 + i)
                    if block < -1:
                        far_low = far_low + piece
                    elif block > 1:
                        far_high = far_high + piece
                    else:
                        near[block + 1] = near[block + 1] + piece
        buckets = lax.broadcasted_iota(jnp.int32, (BUCKETS, 256), 0)
        by_bucket = jnp.zeros((BUCKETS, 256), F32)
        for block in range(3):
            turned = jnp.dot(
                turn, near[block], precision=lax.Precision.HIGHEST, preferred_element_type=F32
            )
            wide = jnp.concatenate([turned, jnp.zeros((128, 128), F32)], axis=1)
            wide = pltpu.roll(wide, 1, 1, stride=1, stride_axis=0)
            line = jnp.sum(wide, axis=0, keepdims=True)
            by_bucket = by_bucket + jnp.where(
                buckets == ids_ref[block : block + 1, :], line, 0.0
            )
        side = lax.broadcasted_iota(jnp.int32, (BUCKETS, 128), 0)
        low_line = jnp.sum(far_low, axis=0, keepdims=True)
        high_line = jnp.sum(far_high, axis=0, keepdims=True)
        ends = jnp.where(side == BUCKETS // 2 - 1, low_line, 0.0) + jnp.where(
            side == BUCKETS - 1, high_line, 0.0
        )
        by_bucket = by_bucket[:, :128] + by_bucket[:, 128:] + ends
        total = jnp.sum(by_bucket, axis=1, keepdims=True)
        total = jnp.concatenate([total, jnp.zeros((128 - BUCKETS, 1), F32)], axis=0)
        total = jnp.transpose(jnp.broadcast_to(total, (128, 128)))
        small_ref[1 + head : 2 + head, 0:128] = total[0:1, :]
    query_low = jnp.concatenate(query_grads, axis=0).astype(BF16)
    key_low = key_grad.astype(BF16)
    value_low = value_grad.astype(BF16)
    spread = (
        dot(query_low, place_q[0]) + dot(key_low, place_q[1]) + dot(value_low, place_q[2])
    ).astype(BF16)
    logit_spread = dot(logit_s[...], place_r[...]).astype(BF16)
    joined = dot_tn(normed_ref[...], spread) + dot_tn(mixed_ref[...], logit_spread)
    grads_ref[:, :640] = joined.astype(BF16)
    normed_part = (
        dot_nt(query_low, wq_ref[...])
        + dot_nt(key_low, wk_ref[...])
        + dot_nt(value_low, wv_ref[...])
    )
    normed_s[...] = normed_part.astype(BF16)
    mine_ref[...] = normed_s[pl.ds(pl.multiple_of(core * 256, 256), 256), :]
    theirs_ref[...] = normed_s[pl.ds(pl.multiple_of((1 - core) * 256, 256), 256), :]


def input_kernel(
    place_ref, own_ref, other_ref, x_ref, gain_ref, middle_grad_ref, small_in, input_ref, small_ref
):
    core = place_ref[1]
    gain = gain_ref[...]
    gain_grad = jnp.zeros((1, D), F32)
    for i in range(4):
        rows = slice(i * 128, i * 128 + 128)
        local = slice((i % 2) * 128, (i % 2) * 128 + 128)
        own = own_ref[local, :]
        other = other_ref[local, :]
        normed_grad = jnp.where(core == i // 2, own, other).astype(F32)
        hidden = x_ref[rows, :].astype(F32)
        scale = lax.rsqrt(jnp.mean(hidden * hidden, axis=-1, keepdims=True) + EPS)
        weighted = normed_grad * gain
        inner = jnp.mean(weighted * hidden, axis=-1, keepdims=True)
        gain_grad = gain_grad + jnp.sum(normed_grad * hidden * scale, axis=0, keepdims=True)
        input_ref[rows, :] = (
            middle_grad_ref[rows, :]
            + scale * weighted
            - hidden * (scale * scale * scale * inner)
        )
    small_ref[...] = small_in[...]
    small_ref[4:5, :] = gain_grad


def finish_kernel(
    recv_ref, split_ref, small_ref, q_ref, k_ref, v_ref, o_ref, router_ref, whole_s
):
    small = jnp.zeros((8, GRADS), F32)
    for j in range(GROUPS):
        block = recv_ref[pl.ds(j * 32, 32), :].astype(F32)
        whole_s[pl.ds(j * 24, 24), :] = block[:24]
        small = small + block[24:]
    small_ref[...] = small[:, :D]
    joined = whole_s[:, :640].astype(BF16)
    q_ref[...] = whole_s[:, :WIDTH]
    k_ref[...] = dot(joined, split_ref[0])
    v_ref[...] = dot(joined, split_ref[1])
    router_ref[...] = dot(joined, split_ref[2])[:, :EXPERTS]
    o_ref[...] = jnp.transpose(whole_s[:, 640:])[:WIDTH, :]


def shards(
    layer_input, attn_gain, query_weight, key_weight, value_weight, output_weight, position_bias,
    moe_gain, router_weight, expert_in, expert_out, route_expert, route_slot, route_drop, out_grad,
):
    experts_axis = ("z", "x", "h")
    pair_axis = ("l", "z", "x", "h")
    core = lax.axis_index("c")
    place = jnp.stack([lax.axis_index("l") * 2 + core, core]).astype(jnp.int32)

    def swap(array, axis):
        return lax.ppermute(array, axis, [(0, 1), (1, 0)])

    ids = jnp.asarray(line_ids())
    gain_one = attn_gain.reshape(1, D)
    gain_two = moe_gain.reshape(1, D)
    zeros = jnp.zeros_like(route_drop)
    route = jnp.stack([route_expert, route_slot, route_drop] + [zeros] * 5)
    wo_link = swap(output_weight, "l")
    wo_core = swap(output_weight, "c")
    wo_far = swap(wo_link, "c")

    tall = shape((SEQ, WIDTH), BF16)
    normed, queries, keys, values, context, lse, tiles = call(
        attention_forward,
        (shape((SEQ, D), BF16), tall, tall, tall, tall, shape((8, SEQ), F32),
         shape((9, 128, 128), F32)),
        (position_bias, layer_input, gain_one, query_weight, key_weight, value_weight, ids),
        scalars=1, limit=32, flops=900_000_000, moved=5_000_000,
    )
    ctx_link = swap(context, "l")
    ctx_core = swap(context, "c")
    ctx_far = swap(ctx_link, "c")
    middle, mixed, probs, send = call(
        middle_kernel,
        (shape((SEQ, D), F32), shape((SEQ, D), BF16), shape((SEQ, EXPERTS), F32),
         shape((ROWS, HALF), BF16)),
        (place, layer_input, context, ctx_core, ctx_link, ctx_far,
         output_weight, wo_core, wo_link, wo_far, gain_two, router_weight, route, out_grad),
        scratch=(pltpu.VMEM((4, SEQ, WIDTH), BF16), pltpu.VMEM((4, WIDTH, D), BF16),
                 pltpu.VMEM((SEQ, D), BF16)),
        scalars=1, limit=32, flops=1_700_000_000, moved=8_000_000,
    )
    received = lax.all_to_all(send, experts_axis, 0, 0, tiled=True)
    received_other = swap(received, "c")
    select = regroup_matrix()
    low = shape((2, 320, D), BF16)
    mine, theirs, slots, slot_grads, act, pre_grad = call(
        expert_kernel,
        (shape((ROWS, HALF), BF16), shape((ROWS, HALF), BF16), low, low, low, low),
        (place, received, received_other, expert_in, expert_out,
         jnp.asarray(select, BF16), jnp.asarray(select.T, BF16)),
        scratch=(pltpu.VMEM((2, 320, D), BF16), pltpu.VMEM((2, 320, D), BF16)),
        scalars=1, limit=48, flops=5_000_000_000, moved=14_000_000,
    )
    partial = (mine.astype(F32) + swap(theirs, "c").astype(F32)).astype(BF16)
    back = lax.all_to_all(
        jnp.concatenate([partial, partial], axis=0), pair_axis, 0, 0, tiled=True
    )
    expert_in_grad, expert_out_grad = expert_grads(slots, slot_grads, act, pre_grad)
    rows_own = call(
        tokens_kernel, shape((SEQ, D), BF16), (route, back),
        limit=32, flops=2_000_000_000, moved=3_000_000,
    )
    rows_other = swap(rows_own, "c")
    place_q = jnp.asarray(
        np.stack([spread_matrix(WIDTH, WIDTH * i, 640) for i in range(3)]), BF16
    )
    place_r = jnp.asarray(spread_matrix(EXPERTS, 3 * WIDTH, 640), BF16)
    layer_output, middle_grad, grads, small, norm_mine, norm_theirs = call(
        backward_kernel,
        (shape((SEQ, D), BF16), shape((SEQ, D), F32), shape((D, GRADS), BF16),
         shape((8, D), F32), shape((256, D), BF16), shape((256, D), BF16)),
        (place, position_bias, layer_input, middle, mixed, probs, route, out_grad,
         rows_own, rows_other, router_weight, gain_two, output_weight, context, queries, keys,
         values, normed, lse, tiles, query_weight, key_weight, value_weight, ids,
         place_q, place_r),
        scratch=(pltpu.VMEM((SEQ, D), BF16), pltpu.VMEM((SEQ, EXPERTS), BF16),
                 pltpu.VMEM((SEQ, D), BF16)),
        scalars=2, limit=48, flops=4_000_000_000, moved=12_000_000,
    )
    scattered = lax.all_to_all(grads, experts_axis, 0, 0, tiled=True)
    halved = (norm_mine.astype(F32) + swap(norm_theirs, "c").astype(F32)).astype(BF16)
    halved = (halved.astype(F32) + swap(halved, "l").astype(F32)).astype(BF16)
    halved_other = swap(halved, "c")
    input_grad, small = call(
        input_kernel,
        (shape((SEQ, D), F32), shape((8, D), F32)),
        (place, halved, halved_other, layer_input, gain_one, middle_grad, small),
        scalars=1, limit=32, flops=10_000_000, moved=5_000_000,
    )
    summed = jnp.sum(scattered.reshape(GROUPS, 24, GRADS).astype(F32), axis=0)
    spread = jnp.concatenate([summed, jnp.pad(small, ((0, 0), (0, GRADS - D)))], axis=0)
    spread = jnp.broadcast_to(spread.astype(BF16)[None], (GROUPS, 32, GRADS))
    gathered = lax.all_to_all(
        spread.reshape(GROUPS * 32, GRADS), experts_axis, 0, 0, tiled=True
    )
    split = np.zeros((3, 640, WIDTH), np.float32)
    split[0] = spread_matrix(WIDTH, WIDTH, 640).T
    split[1] = spread_matrix(WIDTH, 2 * WIDTH, 640).T
    split[2, :, :EXPERTS] = spread_matrix(EXPERTS, 3 * WIDTH, 640).T
    out = shape((D, WIDTH), F32)
    small, query_grad, key_grad, value_grad, output_grad, router_grad = call(
        finish_kernel,
        (shape((8, D), F32), out, out, out, shape((WIDTH, D), F32), shape((D, EXPERTS), F32)),
        (gathered, jnp.asarray(split, BF16)),
        scratch=(pltpu.VMEM((D, GRADS), F32),),
        limit=32, flops=600_000_000, moved=6_000_000,
    )
    return (
        layer_output,
        input_grad,
        small[4],
        query_grad,
        key_grad,
        value_grad,
        output_grad,
        jnp.transpose(small[1:4, :BUCKETS]),
        small[0],
        router_grad,
        expert_in_grad,
        expert_out_grad,
    )


def solution(mesh):
    fine = Mesh(mesh.devices.reshape(4, 4, 2, 2, 2), ("z", "x", "h", "l", "c"))
    ex = ("z", "x", "h")
    te = ("l", "c")
    in_specs = (
        P(ex, None), P(), P(None, te), P(None, te), P(None, te), P(te, None), P(None, te), P(),
        P(), P(ex, None, te), P(ex, te, None), P(ex), P(ex), P(ex), P(ex, None),
    )
    out_specs = (
        P(ex, None), P(ex, None), P(), P(None, te), P(None, te), P(None, te), P(te, None),
        P(None, te), P(), P(), P(ex, None, te), P(ex, te, None),
    )
    return jax.shard_map(shards, mesh=fine, in_specs=in_specs, out_specs=out_specs, check_vma=False)
```

```python
import jax
import jax.numpy as jnp
import numpy as np
from jax import lax
from jax.experimental import pallas as pl
from jax.experimental.pallas import tpu as pltpu
from jax.sharding import Mesh
from jax.sharding import PartitionSpec as P

BUCKETS = 32
EPS = 1e-06
SEQ = 512
D = 768
HEAD = 64
HEADS_HERE = 3
WIDTH = HEADS_HERE * HEAD
EXPERTS = 64
CAP = 10
GROUPS = 32
CHUNK = 40
ROWS = GROUPS * CHUNK
HALF = D // 2
GRADS = 896
F32 = jnp.float32
BF16 = jnp.bfloat16
GELU_C = float(np.sqrt(2.0 / np.pi))


def bucket_of(offsets):
    half_count = BUCKETS // 2
    exact_count = half_count // 2
    upper_side = (offsets > 0).astype(np.int64) * half_count
    distance = np.abs(offsets)
    ratio = np.log(np.maximum(distance, 1) / exact_count) / np.log(128.0 / exact_count)
    far_bucket = np.minimum(
        exact_count + (ratio * (half_count - exact_count)).astype(np.int64), half_count - 1
    )
    return upper_side + np.where(distance < exact_count, distance, far_bucket)


def line_ids():
    ids = np.full((8, 256), -1, np.int32)
    for row, block in enumerate((-1, 0, 1)):
        ids[row] = bucket_of(128 * block + 128 - np.arange(256))
    ids[:3, 0] = -1
    return ids


def regroup_matrix():
    sel = np.zeros((320, 320), np.float32)
    for g in range(8):
        for half in range(2):
            for e in range(2):
                for c in range(CAP):
                    sel[half * 160 + e * 80 + g * 10 + c, g * 40 + half * 20 + e * 10 + c] = 1
    return sel


def dot(a, b):
    return jnp.dot(a, b, preferred_element_type=F32)


def dot_nt(a, b):
    return lax.dot_general(a, b, (((1,), (1,)), ((), ())), preferred_element_type=F32)


def dot_tn(a, b):
    return lax.dot_general(a, b, (((0,), (0,)), ((), ())), preferred_element_type=F32)


def head_mask(head, rows):
    lanes = lax.broadcasted_iota(jnp.int32, (rows, WIDTH), 1)
    return (lanes >= head * HEAD) & (lanes < (head + 1) * HEAD)


def only_head(matrix, head):
    return jnp.where(head_mask(head, matrix.shape[0]), matrix, jnp.zeros_like(matrix))


def call(body, out_shape, args, scratch=(), scalars=0, limit=40, flops=0, moved=0):
    specs = [pl.BlockSpec(memory_space=pltpu.SMEM)] * scalars
    specs += [pl.BlockSpec(memory_space=pltpu.VMEM)] * (len(args) - scalars)
    return pl.pallas_call(
        body,
        out_shape=out_shape,
        in_specs=specs,
        out_specs=jax.tree.map(lambda _: pl.BlockSpec(memory_space=pltpu.VMEM), out_shape),
        scratch_shapes=scratch,
        compiler_params=pltpu.CompilerParams(vmem_limit_bytes=limit << 20),
        cost_estimate=pl.CostEstimate(flops=flops, bytes_accessed=moved, transcendentals=0),
    )(*args)


def shape(dims, dtype):
    return jax.ShapeDtypeStruct(dims, dtype)


def bias_tile(tiles_ref, far_low, far_high, head, block):
    if block < -1:
        return far_low
    if block > 1:
        return far_high
    return tiles_ref[head * 3 + block + 1]


def scores_t(keys, query_scaled, tiles_ref, table_ref, head, part):
    raw = dot_nt(keys, query_scaled)
    far_low = table_ref[head, BUCKETS // 2 - 1]
    far_high = table_ref[head, BUCKETS - 1]
    rows = []
    for key_block in range(4):
        cols = []
        for i in range(2):
            piece = raw[key_block * 128 : key_block * 128 + 128, i * 128 : i * 128 + 128]
            block = key_block - (part * 2 + i)
            cols.append(piece + bias_tile(tiles_ref, far_low, far_high, head, block))
        rows.append(jnp.concatenate(cols, axis=1))
    return jnp.concatenate(rows, axis=0)


def attention_forward(
    table_ref, x_ref, gain_ref, wq_ref, wk_ref, wv_ref, ids_ref,
    normed_ref, q_ref, k_ref, v_ref, ctx_ref, lse_ref, tiles_ref,
):
    for i in range(4):
        rows = pl.ds(i * 128, 128)
        x = x_ref[rows, :].astype(F32)
        scale = lax.rsqrt(jnp.mean(x * x, axis=-1, keepdims=True) + EPS)
        normed_ref[rows, :] = (x * scale * gain_ref[...]).astype(BF16)
    for head in range(HEADS_HERE):
        for block in range(3):
            ids = ids_ref[block : block + 1, :]
            line = jnp.zeros((1, 256), F32)
            for b in range(BUCKETS):
                line = jnp.where(ids == b, table_ref[head, b], line)
            wide = pltpu.roll(
                jnp.broadcast_to(line, (128, 256)), 0, 1, stride=1, stride_axis=0
            )
            tiles_ref[head * 3 + block] = wide[:, 128:]
    normed = normed_ref[...]
    queries = dot_nt(normed, wq_ref[...]).astype(BF16)
    keys = dot_nt(normed, wk_ref[...]).astype(BF16)
    values = dot_nt(normed, wv_ref[...]).astype(BF16)
    q_ref[...] = queries
    k_ref[...] = keys
    v_ref[...] = values
    lse_ref[...] = jnp.zeros((8, SEQ), F32)
    scaled = queries * jnp.asarray(HEAD**-0.5, BF16)
    for part in range(2):
        rows = slice(part * 256, part * 256 + 256)
        context = jnp.zeros((256, WIDTH), F32)
        for head in range(HEADS_HERE):
            scores = scores_t(
                keys, only_head(scaled[rows], head), tiles_ref, table_ref, head, part
            )
            top = jnp.max(scores, axis=0, keepdims=True)
            grown = jnp.exp(scores - top)
            total = jnp.sum(grown, axis=0, keepdims=True)
            probs = (grown * (1.0 / total)).astype(BF16)
            lse_ref[head : head + 1, rows] = top + jnp.log(total)
            context = context + dot_tn(probs, only_head(values, head))
        ctx_ref[rows, :] = context.astype(BF16)


def route_columns(route_ref):
    return jnp.transpose(route_ref[...].astype(F32))


def row_of(expert, slot, drop):
    row = (expert >> 1) * CHUNK + (expert & 1) * CAP + slot
    return jnp.where(drop > 0, -1000, row)


def place_kernel(route_ref, low_ref, high_ref, low_t_ref, high_t_ref):
    target = row_of(route_ref[0:1, :], route_ref[1:2, :], route_ref[2:3, :])
    for i in range(4):
        rows = pl.ds(i * 320, 320)
        index = lax.broadcasted_iota(jnp.int32, (320, SEQ), 0) + 320 * i
        low_ref[rows, :] = (index == target).astype(F32).astype(BF16)
        high_ref[rows, :] = (index == target + 20).astype(F32).astype(BF16)
    columns = route_columns(route_ref).astype(jnp.int32)
    target = row_of(columns[:, 0:1], columns[:, 1:2], columns[:, 2:3])
    for i in range(4):
        rows = slice(i * 128, i * 128 + 128)
        index = lax.broadcasted_iota(jnp.int32, (128, ROWS), 1)
        low_t_ref[rows, :] = (index == target[rows]).astype(F32).astype(BF16)
        high_t_ref[rows, :] = (index == target[rows] + 20).astype(F32).astype(BF16)


def middle_kernel(
    place_ref, x_ref, ctx0, ctx1, ctx2, ctx3, wo0, wo1, wo2, wo3, gain_ref, router_ref,
    route_ref, low_ref, high_ref, grad_ref, middle_ref, mixed_ref, probs_ref, send_ref,
    ctx_s, wo_s, rows_s,
):
    me = place_ref[0]
    core = place_ref[1]
    for step, (c, w) in enumerate(((ctx0, wo0), (ctx1, wo1), (ctx2, wo2), (ctx3, wo3))):
        ctx_s[me ^ step] = c[...]
        wo_s[me ^ step] = w[...]
    columns = route_columns(route_ref)
    for i in range(2):
        rows = slice(i * 256, i * 256 + 256)
        attended = dot(ctx_s[0, rows, :], wo_s[0])
        for t in range(1, 4):
            attended = attended + dot(ctx_s[t, rows, :], wo_s[t])
        middle = x_ref[rows, :].astype(F32) + attended
        scale = lax.rsqrt(jnp.mean(middle * middle, axis=-1, keepdims=True) + EPS)
        mixed = (middle * scale * gain_ref[...]).astype(BF16)
        middle_ref[rows, :] = middle
        mixed_ref[rows, :] = mixed
        lanes = lax.broadcasted_iota(jnp.int32, (256, 128), 1)
        logits = jnp.where(lanes < EXPERTS, dot_nt(mixed, router_ref[...]), -jnp.inf)
        grown = jnp.exp(logits - jnp.max(logits, axis=-1, keepdims=True))
        probs = grown / jnp.sum(grown, axis=-1, keepdims=True)
        probs_ref[rows, :] = probs
        expert = columns[rows, 0:1].astype(jnp.int32)
        chosen = jnp.sum(jnp.where(lanes == expert, probs, 0.0), axis=-1, keepdims=True)
        gate = chosen * (1.0 - columns[rows, 2:3])
        grads = (grad_ref[rows, :].astype(F32) * gate).astype(BF16)
        rows_s[rows, :] = jnp.where(core == 0, mixed, grads)
    for i in range(4):
        rows = pl.ds(i * 320, 320)
        out = dot(low_ref[rows, :], rows_s[:, :HALF]) + dot(high_ref[rows, :], rows_s[:, HALF:])
        send_ref[rows, :] = out.astype(BF16)


def expert_kernel(
    place_ref, own_ref, other_ref, in_ref, out_ref, sel_ref, back_ref,
    mine_ref, theirs_ref, x_ref, s_ref, act_ref, pre_ref, o_s, i_s,
):
    core = place_ref[1]
    for b in range(4):
        rows = pl.ds(b * 320, 320)
        own = own_ref[rows, :]
        other = other_ref[rows, :]
        for dest, block in (
            (x_ref, jnp.where(core == 0, own, other)),
            (s_ref, jnp.where(core == 0, other, own)),
        ):
            sorted_rows = dot(sel_ref[...], block).astype(BF16)
            for half in range(2):
                for e in range(2):
                    dest[e, pl.ds(b * 80, 80), pl.ds(half * HALF, HALF)] = sorted_rows[
                        half * 160 + e * 80 : half * 160 + e * 80 + 80
                    ]
    for e in range(2):
        x = x_ref[e]
        s = s_ref[e]
        out = jnp.zeros((320, D), F32)
        back = jnp.zeros((320, D), F32)
        for f in range(3):
            cols = slice(f * 256, f * 256 + 256)
            w_in = in_ref[e, :, cols]
            w_out = out_ref[e, cols, :]
            pre = dot(x, w_in)
            bent = jnp.tanh(GELU_C * (pre + 0.044715 * (pre * pre * pre)))
            cdf = 0.5 * (1.0 + bent)
            act = (pre * cdf).astype(BF16)
            slope = cdf + (0.5 * GELU_C) * pre * (1.0 - bent * bent) * (
                1.0 + (3 * 0.044715) * (pre * pre)
            )
            act_ref[e, :, cols] = act
            out = out + dot(act, w_out)
            act_grad = dot_nt(s, w_out)
            pre_grad = (act_grad * slope).astype(BF16)
            pre_ref[e, :, cols] = pre_grad
            back = back + dot_nt(pre_grad, w_in)
        o_s[e] = out.astype(BF16)
        i_s[e] = back.astype(BF16)
    for b in range(4):
        rows = pl.ds(b * 80, 80)
        pieces = []
        for src in (o_s, i_s):
            stacked = jnp.concatenate(
                [
                    src[e, rows, pl.ds(half * HALF, HALF)]
                    for half in range(2)
                    for e in range(2)
                ],
                axis=0,
            )
            pieces.append(dot(back_ref[...], stacked).astype(BF16))
        mine_ref[pl.ds(b * 320, 320), :] = jnp.where(core == 0, pieces[0], pieces[1])
        theirs_ref[pl.ds(b * 320, 320), :] = jnp.where(core == 0, pieces[1], pieces[0])


def expert_grads_kernel(x_ref, s_ref, act_ref, pre_ref, in_grad_ref, out_grad_ref):
    out_grad_ref[0] = dot_tn(act_ref[0], s_ref[0])
    in_grad_ref[0] = dot_tn(x_ref[0], pre_ref[0])


def expert_grads(x, s, act, pre):
    whole = pl.BlockSpec((1, 320, D), lambda e, f: (e, 0, 0))
    part = pl.BlockSpec((1, 320, 256), lambda e, f: (e, 0, f))
    return pl.pallas_call(
        expert_grads_kernel,
        grid=(2, 3),
        out_shape=(shape((2, D, D), F32), shape((2, D, D), F32)),
        in_specs=[whole, whole, part, part],
        out_specs=(
            pl.BlockSpec((1, D, 256), lambda e, f: (e, 0, f)),
            pl.BlockSpec((1, 256, D), lambda e, f: (e, f, 0)),
        ),
        compiler_params=pltpu.CompilerParams(vmem_limit_bytes=24 << 20),
        cost_estimate=pl.CostEstimate(
            flops=8 * 320 * D * D, bytes_accessed=14_000_000, transcendentals=0
        ),
    )(x, s, act, pre)


def tokens_kernel(low_ref, high_ref, recv_ref, out_ref):
    slots = (
        recv_ref[pl.ds(0, ROWS), :].astype(F32) + recv_ref[pl.ds(ROWS, ROWS), :].astype(F32)
    ).astype(BF16)
    out_ref[:, pl.ds(0, HALF)] = dot(low_ref[...], slots).astype(BF16)
    out_ref[:, pl.ds(HALF, HALF)] = dot(high_ref[...], slots).astype(BF16)


def backward_kernel(
    place_ref, table_ref, x_ref, middle_ref, mixed_ref, probs_ref, route_ref, grad_ref,
    own_ref, other_ref, router_ref, gain_ref, wo_ref, ctx_ref, q_ref, k_ref, v_ref, normed_ref,
    lse_ref, tiles_ref, wq_ref, wk_ref, wv_ref, ids_ref, stretch_ref,
    output_ref, middle_grad_ref, grads_ref, mine_ref, theirs_ref,
    low_s, logit_s, normed_s,
):
    core = place_ref[1]
    columns = route_columns(route_ref)
    gain = gain_ref[...]
    gain_grad = jnp.zeros((1, D), F32)
    for i in range(4):
        rows = slice(i * 128, i * 128 + 128)
        own = own_ref[rows, :]
        other = other_ref[rows, :]
        expert_rows = jnp.where(core == 0, own, other).astype(F32)
        mixed_grad = jnp.where(core == 0, other, own).astype(F32)
        probs = probs_ref[rows, :]
        kept = 1.0 - columns[rows, 2:3]
        lanes = lax.broadcasted_iota(jnp.int32, (128, 128), 1)
        hot = (lanes == columns[rows, 0:1].astype(jnp.int32)).astype(F32)
        chosen = jnp.sum(probs * hot, axis=-1, keepdims=True)
        middle = middle_ref[rows, :]
        upstream = grad_ref[rows, :].astype(F32)
        output_ref[rows, :] = (middle + (chosen * kept) * expert_rows).astype(BF16)
        gate_grad = jnp.sum(upstream * expert_rows, axis=-1, keepdims=True) * kept
        logit_grad = (probs * (hot - chosen) * gate_grad).astype(BF16)
        logit_s[rows, :] = logit_grad
        mixed_grad = mixed_grad + dot(logit_grad, router_ref[...])
        scale = lax.rsqrt(jnp.mean(middle * middle, axis=-1, keepdims=True) + EPS)
        weighted = mixed_grad * gain
        inner = jnp.mean(weighted * middle, axis=-1, keepdims=True)
        gain_grad = gain_grad + jnp.sum(mixed_grad * middle * scale, axis=0, keepdims=True)
        middle_grad = upstream + scale * weighted - middle * (scale * scale * scale * inner)
        middle_grad_ref[rows, :] = middle_grad
        low_s[rows, :] = middle_grad.astype(BF16)
    middle_low = low_s[...]
    grads_ref[pl.ds(3 * WIDTH, WIDTH), :D] = dot_tn(ctx_ref[...], middle_low).astype(BF16)
    ctx_grad = dot_nt(middle_low, wo_ref[...]).astype(BF16)

    keys = k_ref[...]
    values = v_ref[...]
    key_scaled = keys * jnp.asarray(HEAD**-0.5, BF16)
    query_scaled = q_ref[...] * jnp.asarray(HEAD**-0.5, BF16)
    key_grad = jnp.zeros((SEQ, WIDTH), F32)
    value_grad = jnp.zeros((SEQ, WIDTH), F32)
    query_grads = [jnp.zeros((256, WIDTH), F32), jnp.zeros((256, WIDTH), F32)]
    bias_grad = jnp.zeros((BUCKETS, 128), F32)
    bias_lanes = lax.broadcasted_iota(jnp.int32, (BUCKETS, 128), 1)
    turn = (
        lax.broadcasted_iota(jnp.int32, (128, 128), 0)
        + lax.broadcasted_iota(jnp.int32, (128, 128), 1)
        == 127
    ).astype(F32)
    for head in range(HEADS_HERE):
        near = [jnp.zeros((128, 128), F32) for _ in range(3)]
        far_low = jnp.zeros((128, 128), F32)
        far_high = jnp.zeros((128, 128), F32)
        key_head = only_head(key_scaled, head)
        for part in range(2):
            rows = slice(part * 256, part * 256 + 256)
            query_head = only_head(query_scaled[rows], head)
            ctx_head = only_head(ctx_grad[rows], head)
            scores = scores_t(keys, query_head, tiles_ref, table_ref, head, part)
            probs = jnp.exp(scores - lse_ref[head : head + 1, rows])
            value_grad = value_grad + dot(probs.astype(BF16), ctx_head)
            prob_grad = dot_nt(values, ctx_head)
            inner = jnp.sum(probs * prob_grad, axis=0, keepdims=True)
            score_grad = (probs * (prob_grad - inner)).astype(BF16)
            key_grad = key_grad + dot(score_grad, query_head)
            query_grads[part] = query_grads[part] + dot_tn(score_grad, key_head)
            for key_block in range(4):
                for i in range(2):
                    piece = score_grad[
                        key_block * 128 : key_block * 128 + 128, i * 128 : i * 128 + 128
                    ].astype(F32)
                    block = key_block - (part * 2 + i)
                    if block < -1:
                        far_low = far_low + piece
                    elif block > 1:
                        far_high = far_high + piece
                    else:
                        near[block + 1] = near[block + 1] + piece
        buckets = lax.broadcasted_iota(jnp.int32, (BUCKETS, 256), 0)
        by_bucket = jnp.zeros((BUCKETS, 256), F32)
        for block in range(3):
            turned = jnp.dot(
                turn, near[block], precision=lax.Precision.HIGHEST, preferred_element_type=F32
            )
            wide = jnp.concatenate([turned, jnp.zeros((128, 128), F32)], axis=1)
            wide = pltpu.roll(wide, 1, 1, stride=1, stride_axis=0)
            line = jnp.sum(wide, axis=0, keepdims=True)
            by_bucket = by_bucket + jnp.where(
                buckets == ids_ref[block : block + 1, :], line, 0.0
            )
        side = lax.broadcasted_iota(jnp.int32, (BUCKETS, 128), 0)
        low_line = jnp.sum(far_low, axis=0, keepdims=True)
        high_line = jnp.sum(far_high, axis=0, keepdims=True)
        ends = jnp.where(side == BUCKETS // 2 - 1, low_line, 0.0) + jnp.where(
            side == BUCKETS - 1, high_line, 0.0
        )
        by_bucket = by_bucket[:, :128] + by_bucket[:, 128:] + ends
        total = jnp.sum(by_bucket, axis=1, keepdims=True)
        bias_grad = bias_grad + jnp.where(bias_lanes == EXPERTS + 1 + head, total, 0.0)
    query_low = jnp.concatenate(query_grads, axis=0).astype(BF16)
    key_low = key_grad.astype(BF16)
    value_low = value_grad.astype(BF16)
    normed = normed_ref[...]
    for i, low in enumerate((query_low, key_low, value_low)):
        grads_ref[pl.ds(i * WIDTH, WIDTH), :D] = dot_tn(low, normed).astype(BF16)
    rest = dot_tn(mixed_ref[...], logit_s[...]) + dot(stretch_ref[...], bias_grad.astype(BF16))
    column = jnp.transpose(jnp.broadcast_to(gain_grad, (128, D)))
    lanes = lax.broadcasted_iota(jnp.int32, (D, 128), 1)
    grads_ref[:, D:] = jnp.where(lanes == EXPERTS, column, rest).astype(BF16)
    normed_part = (
        dot(query_low, wq_ref[...])
        + dot(key_low, wk_ref[...])
        + dot(value_low, wv_ref[...])
    )
    normed_s[...] = normed_part.astype(BF16)
    mine_ref[...] = normed_s[pl.ds(pl.multiple_of(core * 256, 256), 256), :]
    theirs_ref[...] = normed_s[pl.ds(pl.multiple_of((1 - core) * 256, 256), 256), :]


def halves(core, own_ref, other_ref, i):
    local = slice((i % 2) * 128, (i % 2) * 128 + 128)
    return jnp.where(core == i // 2, own_ref[local, :], other_ref[local, :]).astype(F32)


def reduce_kernel(place_ref, parts_ref, own_ref, other_ref, x_ref, send_ref):
    core = place_ref[1]
    gain_grad = jnp.zeros((1, D), F32)
    for i in range(4):
        hidden = x_ref[pl.ds(i * 128, 128), :].astype(F32)
        scale = lax.rsqrt(jnp.mean(hidden * hidden, axis=-1, keepdims=True) + EPS)
        normed_grad = halves(core, own_ref, other_ref, i)
        gain_grad = gain_grad + jnp.sum(normed_grad * hidden * scale, axis=0, keepdims=True)
    total = jnp.zeros((24, GRADS), F32)
    for j in range(GROUPS // 2):
        pair = parts_ref[pl.ds(j * 48, 48), :].astype(F32)
        total = total + pair[:24] + pair[24:]
    lines = [
        pltpu.roll(gain_grad[:, r // 4 * 128 : r // 4 * 128 + 128], (96 - r % 4 * 32) % 128, 1)
        for r in range(24)
    ]
    lanes = lax.broadcasted_iota(jnp.int32, (24, 128), 1)
    last = jnp.where(lanes < 96, total[:, D:], jnp.concatenate(lines, axis=0))
    chunk = jnp.concatenate([total[:, :D], last], axis=1)
    pair = jnp.concatenate([chunk, chunk], axis=0).astype(BF16)
    for j in range(GROUPS // 2):
        send_ref[pl.ds(j * 48, 48), :] = pair


def input_kernel(place_ref, own_ref, other_ref, x_ref, gain_ref, middle_grad_ref, input_ref):
    core = place_ref[1]
    gain = gain_ref[...]
    for i in range(4):
        rows = slice(i * 128, i * 128 + 128)
        hidden = x_ref[rows, :].astype(F32)
        scale = lax.rsqrt(jnp.mean(hidden * hidden, axis=-1, keepdims=True) + EPS)
        weighted = halves(core, own_ref, other_ref, i) * gain
        inner = jnp.mean(weighted * hidden, axis=-1, keepdims=True)
        input_ref[rows, :] = (
            middle_grad_ref[rows, :]
            + scale * weighted
            - hidden * (scale * scale * scale * inner)
        )


def finish_kernel(
    recv_ref, stretch_ref, gain_one_ref, gain_two_ref, bias_ref,
    q_ref, k_ref, v_ref, o_ref, router_ref,
):
    for i, out in enumerate((q_ref, k_ref, v_ref, o_ref)):
        out[...] = recv_ref[pl.ds(i * WIDTH, WIDTH), :D].astype(F32)
    last = recv_ref[:, D:].astype(F32)
    summed = jnp.zeros((24, 128), F32)
    for j in range(GROUPS):
        summed = summed + last[j * 24 : j * 24 + 24]
    lanes = lax.broadcasted_iota(jnp.int32, (1, 128), 1)
    for block in range(6):
        line = jnp.zeros((1, 128), F32)
        for i in range(4):
            r = block * 4 + i
            piece = pltpu.roll(summed[r : r + 1], (32 + 32 * i) % 128, 1)
            line = jnp.where((lanes >= 32 * i) & (lanes < 32 * i + 32), piece, line)
        gain_one_ref[:, pl.ds(block * 128, 128)] = line
    turned = jnp.transpose(last)
    router_ref[...] = turned[:EXPERTS]
    tail = turned[EXPERTS : EXPERTS + 8]
    gain_two_ref[...] = tail[0:1]
    bias_ref[...] = dot(tail.astype(BF16), stretch_ref[...])


def shards(
    layer_input, attn_gain, query_weight, key_weight, value_weight, output_weight, position_bias,
    moe_gain, router_weight, expert_in, expert_out, route_expert, route_slot, route_drop, out_grad,
):
    experts_axis = ("z", "x", "h")
    pair_axis = ("l", "z", "x", "h")
    core = lax.axis_index("c")
    place = jnp.stack([lax.axis_index("l") * 2 + core, core]).astype(jnp.int32)

    def swap(array, axis):
        return lax.ppermute(array, axis, [(0, 1), (1, 0)])

    ids = jnp.asarray(line_ids())
    gain_one = attn_gain.reshape(1, D)
    gain_two = moe_gain.reshape(1, D)
    zeros = jnp.zeros_like(route_drop)
    route = jnp.stack([route_expert, route_slot, route_drop] + [zeros] * 5)
    table = jnp.transpose(position_bias)
    wq, wk, wv = (jnp.transpose(w) for w in (query_weight, key_weight, value_weight))
    router = jnp.pad(jnp.transpose(router_weight), ((0, 128 - EXPERTS), (0, 0)))
    wo_link = swap(output_weight, "l")
    wo_core = swap(output_weight, "c")
    wo_far = swap(wo_link, "c")

    tall = shape((SEQ, WIDTH), BF16)
    normed, queries, keys, values, context, lse, tiles = call(
        attention_forward,
        (shape((SEQ, D), BF16), tall, tall, tall, tall, shape((8, SEQ), F32),
         shape((9, 128, 128), F32)),
        (table, layer_input, gain_one, wq, wk, wv, ids),
        scalars=1, limit=16, flops=900_000_000, moved=5_000_000,
    )
    ctx_link = swap(context, "l")
    ctx_core = swap(context, "c")
    ctx_far = swap(ctx_link, "c")
    flat, flat_t = shape((ROWS, SEQ), BF16), shape((SEQ, ROWS), BF16)
    low_place, high_place, low_back, high_back = call(
        place_kernel, (flat, flat, flat_t, flat_t), (route,),
        limit=12, flops=10_000_000, moved=5_500_000,
    )
    middle, mixed, probs, send = call(
        middle_kernel,
        (shape((SEQ, D), F32), shape((SEQ, D), BF16), shape((SEQ, 128), F32),
         shape((ROWS, HALF), BF16)),
        (place, layer_input, context, ctx_core, ctx_link, ctx_far,
         output_weight, wo_core, wo_link, wo_far, gain_two, router, route, low_place, high_place,
         out_grad),
        scratch=(pltpu.VMEM((4, SEQ, WIDTH), BF16), pltpu.VMEM((4, WIDTH, D), BF16),
                 pltpu.VMEM((SEQ, D), BF16)),
        scalars=1, limit=16, flops=1_700_000_000, moved=8_000_000,
    )
    received = lax.all_to_all(send, experts_axis, 0, 0, tiled=True)
    received_other = swap(received, "c")
    select = regroup_matrix()
    low = shape((2, 320, D), BF16)
    mine, theirs, slots, slot_grads, act, pre_grad = call(
        expert_kernel,
        (shape((ROWS, HALF), BF16), shape((ROWS, HALF), BF16), low, low, low, low),
        (place, received, received_other, expert_in, expert_out,
         jnp.asarray(select, BF16), jnp.asarray(select.T, BF16)),
        scratch=(pltpu.VMEM((2, 320, D), BF16), pltpu.VMEM((2, 320, D), BF16)),
        scalars=1, limit=24, flops=5_000_000_000, moved=14_000_000,
    )
    partial = (mine.astype(F32) + swap(theirs, "c").astype(F32)).astype(BF16)
    back = lax.all_to_all(
        jnp.concatenate([partial, partial], axis=0), pair_axis, 0, 0, tiled=True
    )
    expert_in_grad, expert_out_grad = expert_grads(slots, slot_grads, act, pre_grad)
    rows_own = call(
        tokens_kernel, shape((SEQ, D), BF16), (low_back, high_back, back),
        limit=12, flops=2_000_000_000, moved=3_000_000,
    )
    rows_other = swap(rows_own, "c")
    stretch = np.zeros((D, 128), np.float32)
    stretch[24 * np.arange(BUCKETS), np.arange(BUCKETS)] = 1
    layer_output, middle_grad, grads, norm_mine, norm_theirs = call(
        backward_kernel,
        (shape((SEQ, D), BF16), shape((SEQ, D), F32), shape((D, GRADS), BF16),
         shape((256, D), BF16), shape((256, D), BF16)),
        (place, table, layer_input, middle, mixed, probs, route, out_grad,
         rows_own, rows_other, router, gain_two, output_weight, context, queries, keys,
         values, normed, lse, tiles, wq, wk, wv, ids, jnp.asarray(stretch[:, :BUCKETS], BF16)),
        scratch=(pltpu.VMEM((SEQ, D), BF16), pltpu.VMEM((SEQ, 128), BF16),
                 pltpu.VMEM((SEQ, D), BF16)),
        scalars=2, limit=24, flops=4_000_000_000, moved=12_000_000,
    )
    scattered = lax.all_to_all(grads, experts_axis, 0, 0, tiled=True)
    halved = (norm_mine.astype(F32) + swap(norm_theirs, "c").astype(F32)).astype(BF16)
    halved = (halved.astype(F32) + swap(halved, "l").astype(F32)).astype(BF16)
    halved_other = swap(halved, "c")
    spread = call(
        reduce_kernel, shape((D, GRADS), BF16),
        (place, scattered, halved, halved_other, layer_input),
        scalars=1, limit=12, flops=10_000_000, moved=5_000_000,
    )
    gathered = lax.all_to_all(spread, experts_axis, 0, 0, tiled=True)
    input_grad = call(
        input_kernel, shape((SEQ, D), F32),
        (place, halved, halved_other, layer_input, gain_one, middle_grad),
        scalars=1, limit=12, flops=10_000_000, moved=5_000_000,
    )
    out = shape((WIDTH, D), F32)
    line = shape((1, D), F32)
    gain_one_grad, gain_two_grad, bias_grad, query_grad, key_grad, value_grad, output_grad, \
        router_grad = call(
            finish_kernel,
            (line, line, shape((8, 128), F32), out, out, out, out, shape((EXPERTS, D), F32)),
            (gathered, jnp.asarray(stretch, BF16)),
            limit=12, flops=10_000_000, moved=6_000_000,
        )
    return (
        layer_output,
        input_grad,
        gain_one_grad.reshape(D),
        jnp.transpose(query_grad),
        jnp.transpose(key_grad),
        jnp.transpose(value_grad),
        output_grad,
        jnp.transpose(bias_grad[1 : 1 + HEADS_HERE, :BUCKETS]),
        gain_two_grad.reshape(D),
        jnp.transpose(router_grad),
        expert_in_grad,
        expert_out_grad,
    )


def solution(mesh):
    fine = Mesh(mesh.devices.reshape(4, 4, 2, 2, 2), ("z", "x", "h", "l", "c"))
    ex = ("z", "x", "h")
    te = ("l", "c")
    in_specs = (
        P(ex, None), P(), P(None, te), P(None, te), P(None, te), P(te, None), P(None, te), P(),
        P(), P(ex, None, te), P(ex, te, None), P(ex), P(ex), P(ex), P(ex, None),
    )
    out_specs = (
        P(ex, None), P(ex, None), P(), P(None, te), P(None, te), P(None, te), P(te, None),
        P(None, te), P(), P(), P(ex, None, te), P(ex, te, None),
    )
    return jax.shard_map(shards, mesh=fine, in_specs=in_specs, out_specs=out_specs, check_vma=False)
```

```python
import jax
import jax.numpy as jnp
import numpy as np
from jax import lax
from jax.experimental import pallas as pl
from jax.experimental.pallas import tpu as pltpu
from jax.sharding import Mesh
from jax.sharding import PartitionSpec as P

BUCKETS = 32
EPS = 1e-06
SEQ = 512
D = 768
HEAD = 64
HEADS_HERE = 3
WIDTH = HEADS_HERE * HEAD
EXPERTS = 64
CAP = 10
GROUPS = 32
CHUNK = 40
ROWS = GROUPS * CHUNK
HALF = D // 2
GRADS = 896
F32 = jnp.float32
BF16 = jnp.bfloat16
GELU_C = float(np.sqrt(2.0 / np.pi))


def bucket_of(offsets):
    half_count = BUCKETS // 2
    exact_count = half_count // 2
    upper_side = (offsets > 0).astype(np.int64) * half_count
    distance = np.abs(offsets)
    ratio = np.log(np.maximum(distance, 1) / exact_count) / np.log(128.0 / exact_count)
    far_bucket = np.minimum(
        exact_count + (ratio * (half_count - exact_count)).astype(np.int64), half_count - 1
    )
    return upper_side + np.where(distance < exact_count, distance, far_bucket)


FAR_STARTS = [
    int(np.argmax(bucket_of(-np.arange(256)) >= b)) for b in range(9, BUCKETS // 2)
]


def line_buckets(block, rows):
    offset = 128 * block + 128 - lax.broadcasted_iota(jnp.int32, (rows, 256), 1)
    distance = jnp.abs(offset)
    far = jnp.full((rows, 256), 8, jnp.int32)
    for start in FAR_STARTS:
        far = far + (distance >= start).astype(jnp.int32)
    bucket = jnp.where(distance < 8, distance, far)
    return jnp.where(offset > 0, bucket + BUCKETS // 2, bucket)


def regroup_matrix():
    sel = np.zeros((320, 320), np.float32)
    for g in range(8):
        for half in range(2):
            for e in range(2):
                for c in range(CAP):
                    sel[half * 160 + e * 80 + g * 10 + c, g * 40 + half * 20 + e * 10 + c] = 1
    return sel


def dot(a, b):
    return jnp.dot(a, b, preferred_element_type=F32)


def dot_nt(a, b):
    return lax.dot_general(a, b, (((1,), (1,)), ((), ())), preferred_element_type=F32)


def dot_tn(a, b):
    return lax.dot_general(a, b, (((0,), (0,)), ((), ())), preferred_element_type=F32)


def head_mask(head, rows):
    lanes = lax.broadcasted_iota(jnp.int32, (rows, WIDTH), 1)
    return (lanes >= head * HEAD) & (lanes < (head + 1) * HEAD)


def only_head(matrix, head):
    return jnp.where(head_mask(head, matrix.shape[0]), matrix, jnp.zeros_like(matrix))


def call(
    body, out_shape, args, scratch=(), scalars=0, far=(), far_out=(), limit=40, flops=0, moved=0
):
    spaces = [pltpu.SMEM] * scalars + [pltpu.VMEM] * (len(args) - scalars)
    for i in far:
        spaces[i] = pltpu.HBM
    outs = out_shape if isinstance(out_shape, tuple) else (out_shape,)
    out_spaces = [pltpu.HBM if i in far_out else pltpu.VMEM for i in range(len(outs))]
    result = pl.pallas_call(
        body,
        out_shape=outs,
        in_specs=[pl.BlockSpec(memory_space=space) for space in spaces],
        out_specs=tuple(pl.BlockSpec(memory_space=space) for space in out_spaces),
        scratch_shapes=scratch,
        compiler_params=pltpu.CompilerParams(vmem_limit_bytes=limit << 20),
        cost_estimate=pl.CostEstimate(flops=flops, bytes_accessed=moved, transcendentals=0),
    )(*args)
    return result if isinstance(out_shape, tuple) else result[0]


def shape(dims, dtype):
    return jax.ShapeDtypeStruct(dims, dtype)


def bias_tile(tiles_ref, far_low, far_high, head, block):
    if block < -1:
        return far_low
    if block > 1:
        return far_high
    return tiles_ref[head * 3 + block + 1]


def scores_t(keys, query_scaled, tiles_ref, table, head, part):
    raw = dot_nt(keys, query_scaled)
    far_low = table[head : head + 1, BUCKETS // 2 - 1 : BUCKETS // 2]
    far_high = table[head : head + 1, BUCKETS - 1 : BUCKETS]
    rows = []
    for key_block in range(4):
        cols = []
        for i in range(2):
            piece = raw[key_block * 128 : key_block * 128 + 128, i * 128 : i * 128 + 128]
            block = key_block - (part * 2 + i)
            cols.append(piece + bias_tile(tiles_ref, far_low, far_high, head, block))
        rows.append(jnp.concatenate(cols, axis=1))
    return jnp.concatenate(rows, axis=0)


def attention_forward(
    table_hbm, x_hbm, gain_hbm, wq_hbm, wk_hbm, wv_hbm,
    normed_hbm, q_hbm, k_hbm, v_hbm, tiles_hbm, ctx_ref, lse_ref,
    table_ref, x_ref, gain_ref, wq_ref, wk_ref, wv_ref, normed_ref, q_ref, k_ref, v_ref,
    tiles_ref, sems,
):
    loads = [
        pltpu.make_async_copy(src, dst, sems.at[i])
        for i, (src, dst) in enumerate(
            (
                (table_hbm, table_ref), (x_hbm, x_ref), (wq_hbm, wq_ref), (wk_hbm, wk_ref),
                (wv_hbm, wv_ref), (gain_hbm, gain_ref),
            )
        )
    ]
    for load in loads:
        load.start()
    stores = []

    def store(src, dst):
        copy = pltpu.make_async_copy(src, dst, sems.at[6 + len(stores)])
        copy.start()
        stores.append(copy)

    loads[0].wait()
    table = table_ref[...]
    lines = []
    for block in (-1, 0, 1):
        buckets = lax.broadcasted_iota(jnp.int32, (BUCKETS, 256), 0)
        hot = (buckets == line_buckets(block, BUCKETS)).astype(F32)
        lines.append(
            jnp.dot(table, hot, precision=lax.Precision.HIGHEST, preferred_element_type=F32)
        )
    for head in range(HEADS_HERE):
        for block in range(3):
            wide = pltpu.roll(
                jnp.broadcast_to(lines[block][head : head + 1], (128, 256)),
                0, 1, stride=1, stride_axis=0,
            )
            tiles_ref[head * 3 + block] = wide[:, 128:]
    store(tiles_ref, tiles_hbm)
    loads[1].wait()
    loads[5].wait()
    gain = gain_ref[...].reshape(1, D)
    for i in range(4):
        rows = pl.ds(i * 128, 128)
        x = x_ref[rows, :].astype(F32)
        scale = lax.rsqrt(jnp.mean(x * x, axis=-1, keepdims=True) + EPS)
        normed_ref[rows, :] = (x * scale * gain).astype(BF16)
    store(normed_ref, normed_hbm)
    normed = normed_ref[...]
    for load, weight, out, out_hbm in (
        (loads[2], wq_ref, q_ref, q_hbm),
        (loads[3], wk_ref, k_ref, k_hbm),
        (loads[4], wv_ref, v_ref, v_hbm),
    ):
        load.wait()
        out[...] = dot_nt(normed, weight[...]).astype(BF16)
        store(out, out_hbm)
    queries, keys, values = q_ref[...], k_ref[...], v_ref[...]
    lse_ref[...] = jnp.zeros((8, SEQ), F32)
    scaled = queries * jnp.asarray(HEAD**-0.5, BF16)
    for part in range(2):
        rows = slice(part * 256, part * 256 + 256)
        context = jnp.zeros((256, WIDTH), F32)
        for head in range(HEADS_HERE):
            scores = scores_t(keys, only_head(scaled[rows], head), tiles_ref, table, head, part)
            top = jnp.max(scores, axis=0, keepdims=True)
            grown = jnp.exp(scores - top)
            total = jnp.sum(grown, axis=0, keepdims=True)
            probs = (grown * (1.0 / total)).astype(BF16)
            lse_ref[head : head + 1, rows] = top + jnp.log(total)
            context = context + dot_tn(probs, only_head(values, head))
        ctx_ref[rows, :] = context.astype(BF16)
    for copy in stores:
        copy.wait()


def route_columns(route_ref):
    return jnp.transpose(route_ref[...].astype(F32))


def row_of(expert, slot, drop):
    row = (expert >> 1) * CHUNK + (expert & 1) * CAP + slot
    return jnp.where(drop > 0, -1000, row)


def place_kernel(route_ref, low_ref, high_ref, low_t_ref, high_t_ref):
    target = row_of(route_ref[0:1, :], route_ref[1:2, :], route_ref[2:3, :])
    for i in range(4):
        rows = pl.ds(i * 320, 320)
        index = lax.broadcasted_iota(jnp.int32, (320, SEQ), 0) + 320 * i
        low_ref[rows, :] = (index == target).astype(F32).astype(BF16)
        high_ref[rows, :] = (index == target + 20).astype(F32).astype(BF16)
    columns = route_columns(route_ref).astype(jnp.int32)
    target = row_of(columns[:, 0:1], columns[:, 1:2], columns[:, 2:3])
    for i in range(4):
        rows = slice(i * 128, i * 128 + 128)
        index = lax.broadcasted_iota(jnp.int32, (128, ROWS), 1)
        low_t_ref[rows, :] = (index == target[rows]).astype(F32).astype(BF16)
        high_t_ref[rows, :] = (index == target[rows] + 20).astype(F32).astype(BF16)


def middle_kernel(
    place_ref, x_ref, ctx0, ctx1, ctx2, ctx3, wo0, wo1, wo2, wo3, gain_ref, router_ref,
    route_ref, low_ref, high_ref, grad_ref, middle_ref, mixed_ref, probs_ref, send_ref,
    ctx_s, wo_s, rows_s,
):
    me = place_ref[0]
    core = place_ref[1]
    for step, (c, w) in enumerate(((ctx0, wo0), (ctx1, wo1), (ctx2, wo2), (ctx3, wo3))):
        ctx_s[me ^ step] = c[...]
        wo_s[me ^ step] = w[...]
    columns = route_columns(route_ref)
    for i in range(2):
        rows = slice(i * 256, i * 256 + 256)
        attended = dot(ctx_s[0, rows, :], wo_s[0])
        for t in range(1, 4):
            attended = attended + dot(ctx_s[t, rows, :], wo_s[t])
        middle = x_ref[rows, :].astype(F32) + attended
        scale = lax.rsqrt(jnp.mean(middle * middle, axis=-1, keepdims=True) + EPS)
        mixed = (middle * scale * gain_ref[...]).astype(BF16)
        middle_ref[rows, :] = middle
        mixed_ref[rows, :] = mixed
        lanes = lax.broadcasted_iota(jnp.int32, (256, 128), 1)
        logits = jnp.where(lanes < EXPERTS, dot_nt(mixed, router_ref[...]), -jnp.inf)
        grown = jnp.exp(logits - jnp.max(logits, axis=-1, keepdims=True))
        probs = grown / jnp.sum(grown, axis=-1, keepdims=True)
        probs_ref[rows, :] = probs
        expert = columns[rows, 0:1].astype(jnp.int32)
        chosen = jnp.sum(jnp.where(lanes == expert, probs, 0.0), axis=-1, keepdims=True)
        gate = chosen * (1.0 - columns[rows, 2:3])
        grads = (grad_ref[rows, :].astype(F32) * gate).astype(BF16)
        rows_s[rows, :] = jnp.where(core == 0, mixed, grads)
    for i in range(4):
        rows = pl.ds(i * 320, 320)
        out = dot(low_ref[rows, :], rows_s[:, :HALF]) + dot(high_ref[rows, :], rows_s[:, HALF:])
        send_ref[rows, :] = out.astype(BF16)


def expert_kernel(
    place_ref, own_ref, other_ref, in_ref, out_ref, sel_ref, back_ref,
    mine_ref, theirs_ref, x_ref, s_ref, act_ref, pre_ref, o_s, i_s,
):
    core = place_ref[1]
    for b in range(4):
        rows = pl.ds(b * 320, 320)
        own = own_ref[rows, :]
        other = other_ref[rows, :]
        for dest, block in (
            (x_ref, jnp.where(core == 0, own, other)),
            (s_ref, jnp.where(core == 0, other, own)),
        ):
            sorted_rows = dot(sel_ref[...], block).astype(BF16)
            for half in range(2):
                for e in range(2):
                    dest[e, pl.ds(b * 80, 80), pl.ds(half * HALF, HALF)] = sorted_rows[
                        half * 160 + e * 80 : half * 160 + e * 80 + 80
                    ]
    for e in range(2):
        x = x_ref[e]
        s = s_ref[e]
        out = jnp.zeros((320, D), F32)
        back = jnp.zeros((320, D), F32)
        for f in range(3):
            cols = slice(f * 256, f * 256 + 256)
            w_in = in_ref[e, :, cols]
            w_out = out_ref[e, cols, :]
            pre = dot(x, w_in)
            bent = jnp.tanh(GELU_C * (pre + 0.044715 * (pre * pre * pre)))
            cdf = 0.5 * (1.0 + bent)
            act = (pre * cdf).astype(BF16)
            slope = cdf + (0.5 * GELU_C) * pre * (1.0 - bent * bent) * (
                1.0 + (3 * 0.044715) * (pre * pre)
            )
            act_ref[e, :, cols] = act
            out = out + dot(act, w_out)
            act_grad = dot_nt(s, w_out)
            pre_grad = (act_grad * slope).astype(BF16)
            pre_ref[e, :, cols] = pre_grad
            back = back + dot_nt(pre_grad, w_in)
        o_s[e] = out.astype(BF16)
        i_s[e] = back.astype(BF16)
    for b in range(4):
        rows = pl.ds(b * 80, 80)
        pieces = []
        for src in (o_s, i_s):
            stacked = jnp.concatenate(
                [
                    src[e, rows, pl.ds(half * HALF, HALF)]
                    for half in range(2)
                    for e in range(2)
                ],
                axis=0,
            )
            pieces.append(dot(back_ref[...], stacked).astype(BF16))
        mine_ref[pl.ds(b * 320, 320), :] = jnp.where(core == 0, pieces[0], pieces[1])
        theirs_ref[pl.ds(b * 320, 320), :] = jnp.where(core == 0, pieces[1], pieces[0])


def expert_grads_kernel(x_ref, s_ref, act_ref, pre_ref, in_grad_ref, out_grad_ref):
    out_grad_ref[0] = dot_tn(act_ref[0], s_ref[0])
    in_grad_ref[0] = dot_tn(x_ref[0], pre_ref[0])


def expert_grads(x, s, act, pre):
    whole = pl.BlockSpec((1, 320, D), lambda e, f: (e, 0, 0))
    part = pl.BlockSpec((1, 320, 256), lambda e, f: (e, 0, f))
    return pl.pallas_call(
        expert_grads_kernel,
        grid=(2, 3),
        out_shape=(shape((2, D, D), F32), shape((2, D, D), F32)),
        in_specs=[whole, whole, part, part],
        out_specs=(
            pl.BlockSpec((1, D, 256), lambda e, f: (e, 0, f)),
            pl.BlockSpec((1, 256, D), lambda e, f: (e, f, 0)),
        ),
        compiler_params=pltpu.CompilerParams(vmem_limit_bytes=24 << 20),
        cost_estimate=pl.CostEstimate(
            flops=8 * 320 * D * D, bytes_accessed=14_000_000, transcendentals=0
        ),
    )(x, s, act, pre)


def tokens_kernel(low_ref, high_ref, recv_ref, out_ref):
    slots = (
        recv_ref[pl.ds(0, ROWS), :].astype(F32) + recv_ref[pl.ds(ROWS, ROWS), :].astype(F32)
    ).astype(BF16)
    out_ref[:, pl.ds(0, HALF)] = dot(low_ref[...], slots).astype(BF16)
    out_ref[:, pl.ds(HALF, HALF)] = dot(high_ref[...], slots).astype(BF16)


def backward_kernel(
    place_ref, table_ref, x_ref, middle_ref, mixed_ref, probs_ref, route_ref, grad_ref,
    own_ref, other_ref, router_ref, gain_ref, wo_ref, ctx_ref, q_ref, k_ref, v_ref, normed_ref,
    lse_ref, tiles_ref, wq_ref, wk_ref, wv_ref, stretch_ref,
    output_ref, middle_grad_ref, grads_ref, mine_ref, theirs_ref,
    low_s, logit_s, normed_s,
):
    core = place_ref[1]
    columns = route_columns(route_ref)
    gain = gain_ref[...]
    gain_grad = jnp.zeros((1, D), F32)
    for i in range(4):
        rows = slice(i * 128, i * 128 + 128)
        own = own_ref[rows, :]
        other = other_ref[rows, :]
        expert_rows = jnp.where(core == 0, own, other).astype(F32)
        mixed_grad = jnp.where(core == 0, other, own).astype(F32)
        probs = probs_ref[rows, :]
        kept = 1.0 - columns[rows, 2:3]
        lanes = lax.broadcasted_iota(jnp.int32, (128, 128), 1)
        hot = (lanes == columns[rows, 0:1].astype(jnp.int32)).astype(F32)
        chosen = jnp.sum(probs * hot, axis=-1, keepdims=True)
        middle = middle_ref[rows, :]
        upstream = grad_ref[rows, :].astype(F32)
        output_ref[rows, :] = (middle + (chosen * kept) * expert_rows).astype(BF16)
        gate_grad = jnp.sum(upstream * expert_rows, axis=-1, keepdims=True) * kept
        logit_grad = (probs * (hot - chosen) * gate_grad).astype(BF16)
        logit_s[rows, :] = logit_grad
        mixed_grad = mixed_grad + dot(logit_grad, router_ref[...])
        scale = lax.rsqrt(jnp.mean(middle * middle, axis=-1, keepdims=True) + EPS)
        weighted = mixed_grad * gain
        inner = jnp.mean(weighted * middle, axis=-1, keepdims=True)
        gain_grad = gain_grad + jnp.sum(mixed_grad * middle * scale, axis=0, keepdims=True)
        middle_grad = upstream + scale * weighted - middle * (scale * scale * scale * inner)
        middle_grad_ref[rows, :] = middle_grad
        low_s[rows, :] = middle_grad.astype(BF16)
    middle_low = low_s[...]
    grads_ref[pl.ds(3 * WIDTH, WIDTH), :D] = dot_tn(ctx_ref[...], middle_low).astype(BF16)
    ctx_grad = dot_nt(middle_low, wo_ref[...]).astype(BF16)

    keys = k_ref[...]
    values = v_ref[...]
    key_scaled = keys * jnp.asarray(HEAD**-0.5, BF16)
    query_scaled = q_ref[...] * jnp.asarray(HEAD**-0.5, BF16)
    key_grad = jnp.zeros((SEQ, WIDTH), F32)
    value_grad = jnp.zeros((SEQ, WIDTH), F32)
    query_grads = [jnp.zeros((256, WIDTH), F32), jnp.zeros((256, WIDTH), F32)]
    bias_grad = jnp.zeros((BUCKETS, 128), F32)
    bias_lanes = lax.broadcasted_iota(jnp.int32, (BUCKETS, 128), 1)
    turn = (
        lax.broadcasted_iota(jnp.int32, (128, 128), 0)
        + lax.broadcasted_iota(jnp.int32, (128, 128), 1)
        == 127
    ).astype(F32)
    for head in range(HEADS_HERE):
        near = [jnp.zeros((128, 128), F32) for _ in range(3)]
        far_low = jnp.zeros((128, 128), F32)
        far_high = jnp.zeros((128, 128), F32)
        key_head = only_head(key_scaled, head)
        for part in range(2):
            rows = slice(part * 256, part * 256 + 256)
            query_head = only_head(query_scaled[rows], head)
            ctx_head = only_head(ctx_grad[rows], head)
            scores = scores_t(keys, query_head, tiles_ref, table_ref[...], head, part)
            probs = jnp.exp(scores - lse_ref[head : head + 1, rows])
            value_grad = value_grad + dot(probs.astype(BF16), ctx_head)
            prob_grad = dot_nt(values, ctx_head)
            inner = jnp.sum(probs * prob_grad, axis=0, keepdims=True)
            score_grad = (probs * (prob_grad - inner)).astype(BF16)
            key_grad = key_grad + dot(score_grad, query_head)
            query_grads[part] = query_grads[part] + dot_tn(score_grad, key_head)
            for key_block in range(4):
                for i in range(2):
                    piece = score_grad[
                        key_block * 128 : key_block * 128 + 128, i * 128 : i * 128 + 128
                    ].astype(F32)
                    block = key_block - (part * 2 + i)
                    if block < -1:
                        far_low = far_low + piece
                    elif block > 1:
                        far_high = far_high + piece
                    else:
                        near[block + 1] = near[block + 1] + piece
        buckets = lax.broadcasted_iota(jnp.int32, (BUCKETS, 256), 0)
        by_bucket = jnp.zeros((BUCKETS, 256), F32)
        for block in range(3):
            turned = jnp.dot(
                turn, near[block], precision=lax.Precision.HIGHEST, preferred_element_type=F32
            )
            wide = jnp.concatenate([turned, jnp.zeros((128, 128), F32)], axis=1)
            wide = pltpu.roll(wide, 1, 1, stride=1, stride_axis=0)
            line = jnp.sum(wide, axis=0, keepdims=True)
            by_bucket = by_bucket + jnp.where(
                buckets == line_buckets(block - 1, BUCKETS), line, 0.0
            )
        side = lax.broadcasted_iota(jnp.int32, (BUCKETS, 128), 0)
        low_line = jnp.sum(far_low, axis=0, keepdims=True)
        high_line = jnp.sum(far_high, axis=0, keepdims=True)
        ends = jnp.where(side == BUCKETS // 2 - 1, low_line, 0.0) + jnp.where(
            side == BUCKETS - 1, high_line, 0.0
        )
        by_bucket = by_bucket[:, :128] + by_bucket[:, 128:] + ends
        total = jnp.sum(by_bucket, axis=1, keepdims=True)
        bias_grad = bias_grad + jnp.where(bias_lanes == EXPERTS + 1 + head, total, 0.0)
    query_low = jnp.concatenate(query_grads, axis=0).astype(BF16)
    key_low = key_grad.astype(BF16)
    value_low = value_grad.astype(BF16)
    normed = normed_ref[...]
    for i, low in enumerate((query_low, key_low, value_low)):
        grads_ref[pl.ds(i * WIDTH, WIDTH), :D] = dot_tn(low, normed).astype(BF16)
    rest = dot_tn(mixed_ref[...], logit_s[...]) + dot(stretch_ref[...], bias_grad.astype(BF16))
    column = jnp.transpose(jnp.broadcast_to(gain_grad, (128, D)))
    lanes = lax.broadcasted_iota(jnp.int32, (D, 128), 1)
    grads_ref[:, D:] = jnp.where(lanes == EXPERTS, column, rest).astype(BF16)
    normed_part = (
        dot(query_low, wq_ref[...])
        + dot(key_low, wk_ref[...])
        + dot(value_low, wv_ref[...])
    )
    normed_s[...] = normed_part.astype(BF16)
    mine_ref[...] = normed_s[pl.ds(pl.multiple_of(core * 256, 256), 256), :]
    theirs_ref[...] = normed_s[pl.ds(pl.multiple_of((1 - core) * 256, 256), 256), :]


def halves(core, own_ref, other_ref, i):
    local = slice((i % 2) * 128, (i % 2) * 128 + 128)
    return jnp.where(core == i // 2, own_ref[local, :], other_ref[local, :]).astype(F32)


def reduce_kernel(place_ref, parts_ref, own_ref, other_ref, x_ref, send_ref):
    core = place_ref[1]
    gain_grad = jnp.zeros((1, D), F32)
    for i in range(4):
        hidden = x_ref[pl.ds(i * 128, 128), :].astype(F32)
        scale = lax.rsqrt(jnp.mean(hidden * hidden, axis=-1, keepdims=True) + EPS)
        normed_grad = halves(core, own_ref, other_ref, i)
        gain_grad = gain_grad + jnp.sum(normed_grad * hidden * scale, axis=0, keepdims=True)
    total = jnp.zeros((24, GRADS), F32)
    for j in range(GROUPS // 2):
        pair = parts_ref[pl.ds(j * 48, 48), :].astype(F32)
        total = total + pair[:24] + pair[24:]
    lines = [
        pltpu.roll(gain_grad[:, r // 4 * 128 : r // 4 * 128 + 128], (96 - r % 4 * 32) % 128, 1)
        for r in range(24)
    ]
    lanes = lax.broadcasted_iota(jnp.int32, (24, 128), 1)
    last = jnp.where(lanes < 96, total[:, D:], jnp.concatenate(lines, axis=0))
    chunk = jnp.concatenate([total[:, :D], last], axis=1)
    pair = jnp.concatenate([chunk, chunk], axis=0).astype(BF16)
    for j in range(GROUPS // 2):
        send_ref[pl.ds(j * 48, 48), :] = pair


def input_kernel(place_ref, own_ref, other_ref, x_ref, gain_ref, middle_grad_ref, input_ref):
    core = place_ref[1]
    gain = gain_ref[...]
    for i in range(4):
        rows = slice(i * 128, i * 128 + 128)
        hidden = x_ref[rows, :].astype(F32)
        scale = lax.rsqrt(jnp.mean(hidden * hidden, axis=-1, keepdims=True) + EPS)
        weighted = halves(core, own_ref, other_ref, i) * gain
        inner = jnp.mean(weighted * hidden, axis=-1, keepdims=True)
        input_ref[rows, :] = (
            middle_grad_ref[rows, :]
            + scale * weighted
            - hidden * (scale * scale * scale * inner)
        )


def finish_kernel(
    recv_ref, stretch_ref, gain_one_ref, gain_two_ref, bias_ref,
    q_ref, k_ref, v_ref, o_ref, router_ref,
):
    for i, out in enumerate((q_ref, k_ref, v_ref, o_ref)):
        out[...] = recv_ref[pl.ds(i * WIDTH, WIDTH), :D].astype(F32)
    last = recv_ref[:, D:].astype(F32)
    summed = jnp.zeros((24, 128), F32)
    for j in range(GROUPS):
        summed = summed + last[j * 24 : j * 24 + 24]
    lanes = lax.broadcasted_iota(jnp.int32, (1, 128), 1)
    for block in range(6):
        line = jnp.zeros((1, 128), F32)
        for i in range(4):
            r = block * 4 + i
            piece = pltpu.roll(summed[r : r + 1], (32 + 32 * i) % 128, 1)
            line = jnp.where((lanes >= 32 * i) & (lanes < 32 * i + 32), piece, line)
        gain_one_ref[pl.ds(block * 128, 128)] = line[0]
    turned = jnp.transpose(last)
    router_ref[...] = turned[:EXPERTS]
    tail = turned[EXPERTS : EXPERTS + 8]
    gain_two_ref[...] = tail[0]
    bias_ref[...] = dot(tail.astype(BF16), stretch_ref[...])[1 : 1 + HEADS_HERE]


def shards(
    layer_input, attn_gain, query_weight, key_weight, value_weight, output_weight, position_bias,
    moe_gain, router_weight, expert_in, expert_out, route_expert, route_slot, route_drop, out_grad,
):
    experts_axis = ("z", "x", "h")
    pair_axis = ("l", "z", "x", "h")
    core = lax.axis_index("c")
    place = jnp.stack([lax.axis_index("l") * 2 + core, core]).astype(jnp.int32)

    def swap(array, axis):
        return lax.ppermute(array, axis, [(0, 1), (1, 0)])

    gain_one = attn_gain.reshape(1, D)
    gain_two = moe_gain.reshape(1, D)
    zeros = jnp.zeros_like(route_drop)
    route = jnp.stack([route_expert, route_slot, route_drop] + [zeros] * 5)
    table = jnp.transpose(position_bias)
    wq, wk, wv = (jnp.transpose(w) for w in (query_weight, key_weight, value_weight))
    router = jnp.pad(jnp.transpose(router_weight), ((0, 128 - EXPERTS), (0, 0)))
    wo_link = swap(output_weight, "l")
    wo_core = swap(output_weight, "c")
    wo_far = swap(wo_link, "c")

    tall = shape((SEQ, WIDTH), BF16)
    wide = shape((SEQ, D), BF16)
    tile_shape = (3 * HEADS_HERE, 128, 128)
    weight_vmem = pltpu.VMEM((WIDTH, D), BF16)
    tall_vmem = pltpu.VMEM((SEQ, WIDTH), BF16)
    normed, queries, keys, values, tiles, context, lse = call(
        attention_forward,
        (wide, tall, tall, tall, shape(tile_shape, F32), tall, shape((8, SEQ), F32)),
        (table, layer_input, attn_gain, wq, wk, wv),
        far=(0, 1, 2, 3, 4, 5), far_out=(0, 1, 2, 3, 4),
        scratch=(pltpu.VMEM((HEADS_HERE, BUCKETS), F32), pltpu.VMEM((SEQ, D), BF16),
                 pltpu.VMEM((D,), F32), weight_vmem, weight_vmem, weight_vmem, pltpu.VMEM((SEQ, D), BF16),
                 tall_vmem, tall_vmem, tall_vmem, pltpu.VMEM(tile_shape, F32),
                 pltpu.SemaphoreType.DMA((11,))),
        limit=60, flops=900_000_000, moved=5_000_000,
    )
    flat, flat_t = shape((ROWS, SEQ), BF16), shape((SEQ, ROWS), BF16)
    low_place, high_place, low_back, high_back = call(
        place_kernel, (flat, flat, flat_t, flat_t), (route,),
        limit=12, flops=10_000_000, moved=5_500_000,
    )
    ctx_link = swap(context, "l")
    ctx_core = swap(context, "c")
    ctx_link_late, low_place = lax.optimization_barrier((ctx_link, low_place))
    ctx_far = swap(ctx_link_late, "c")
    middle, mixed, probs, send = call(
        middle_kernel,
        (shape((SEQ, D), F32), shape((SEQ, D), BF16), shape((SEQ, 128), F32),
         shape((ROWS, HALF), BF16)),
        (place, layer_input, context, ctx_core, ctx_link, ctx_far,
         output_weight, wo_core, wo_link, wo_far, gain_two, router, route, low_place, high_place,
         out_grad),
        scratch=(pltpu.VMEM((4, SEQ, WIDTH), BF16), pltpu.VMEM((4, WIDTH, D), BF16),
                 pltpu.VMEM((SEQ, D), BF16)),
        scalars=1, limit=16, flops=1_700_000_000, moved=8_000_000,
    )
    received = lax.all_to_all(send, experts_axis, 0, 0, tiled=True)
    received_other = swap(received, "c")
    select = regroup_matrix()
    low = shape((2, 320, D), BF16)
    mine, theirs, slots, slot_grads, act, pre_grad = call(
        expert_kernel,
        (shape((ROWS, HALF), BF16), shape((ROWS, HALF), BF16), low, low, low, low),
        (place, received, received_other, expert_in, expert_out,
         jnp.asarray(select, BF16), jnp.asarray(select.T, BF16)),
        scratch=(pltpu.VMEM((2, 320, D), BF16), pltpu.VMEM((2, 320, D), BF16)),
        scalars=1, limit=24, flops=5_000_000_000, moved=14_000_000,
    )
    partial = (mine.astype(F32) + swap(theirs, "c").astype(F32)).astype(BF16)
    back = lax.all_to_all(
        jnp.concatenate([partial, partial], axis=0), pair_axis, 0, 0, tiled=True
    )
    expert_in_grad, expert_out_grad = expert_grads(slots, slot_grads, act, pre_grad)
    rows_own = call(
        tokens_kernel, shape((SEQ, D), BF16), (low_back, high_back, back),
        limit=12, flops=2_000_000_000, moved=3_000_000,
    )
    rows_other = swap(rows_own, "c")
    stretch = np.zeros((D, BUCKETS), np.float32)
    stretch[24 * np.arange(BUCKETS), np.arange(BUCKETS)] = 1
    layer_output, middle_grad, grads, norm_mine, norm_theirs = call(
        backward_kernel,
        (shape((SEQ, D), BF16), shape((SEQ, D), F32), shape((D, GRADS), BF16),
         shape((256, D), BF16), shape((256, D), BF16)),
        (place, table, layer_input, middle, mixed, probs, route, out_grad,
         rows_own, rows_other, router, gain_two, output_weight, context, queries, keys,
         values, normed, lse, tiles, wq, wk, wv, jnp.asarray(stretch, BF16)),
        scratch=(pltpu.VMEM((SEQ, D), BF16), pltpu.VMEM((SEQ, 128), BF16),
                 pltpu.VMEM((SEQ, D), BF16)),
        scalars=1, limit=24, flops=4_000_000_000, moved=12_000_000,
    )
    scattered = lax.all_to_all(grads, experts_axis, 0, 0, tiled=True)
    halved = (norm_mine.astype(F32) + swap(norm_theirs, "c").astype(F32)).astype(BF16)
    halved = (halved.astype(F32) + swap(halved, "l").astype(F32)).astype(BF16)
    halved_other = swap(halved, "c")
    spread = call(
        reduce_kernel, shape((D, GRADS), BF16),
        (place, scattered, halved, halved_other, layer_input),
        scalars=1, limit=12, flops=10_000_000, moved=5_000_000,
    )
    gathered = lax.all_to_all(spread, experts_axis, 0, 0, tiled=True)
    input_grad = call(
        input_kernel, shape((SEQ, D), F32),
        (place, halved, halved_other, layer_input, gain_one, middle_grad),
        scalars=1, limit=12, flops=10_000_000, moved=5_000_000,
    )
    out = shape((WIDTH, D), F32)
    line = shape((D,), F32)
    gain_one_grad, gain_two_grad, bias_grad, query_grad, key_grad, value_grad, output_grad, \
        router_grad = call(
            finish_kernel,
            (line, line, shape((HEADS_HERE, BUCKETS), F32), out, out, out, out,
             shape((EXPERTS, D), F32)),
            (gathered, jnp.asarray(stretch, BF16)),
            limit=12, flops=10_000_000, moved=6_000_000,
        )
    return (
        layer_output,
        input_grad,
        gain_one_grad,
        jnp.transpose(query_grad),
        jnp.transpose(key_grad),
        jnp.transpose(value_grad),
        output_grad,
        jnp.transpose(bias_grad),
        gain_two_grad,
        jnp.transpose(router_grad),
        expert_in_grad,
        expert_out_grad,
    )


def solution(mesh):
    fine = Mesh(mesh.devices.reshape(4, 4, 2, 2, 2), ("z", "x", "h", "l", "c"))
    ex = ("z", "x", "h")
    te = ("l", "c")
    in_specs = (
        P(ex, None), P(), P(None, te), P(None, te), P(None, te), P(te, None), P(None, te), P(),
        P(), P(ex, None, te), P(ex, te, None), P(ex), P(ex), P(ex), P(ex, None),
    )
    out_specs = (
        P(ex, None), P(ex, None), P(), P(None, te), P(None, te), P(None, te), P(te, None),
        P(None, te), P(), P(), P(ex, None, te), P(ex, te, None),
    )
    return jax.shard_map(shards, mesh=fine, in_specs=in_specs, out_specs=out_specs, check_vma=False)
```

```python
import jax
import jax.numpy as jnp
import numpy as np
from jax import lax
from jax.experimental import pallas as pl
from jax.experimental.pallas import tpu as pltpu
from jax.sharding import Mesh
from jax.sharding import PartitionSpec as P

BUCKETS = 32
EPS = 1e-06
SEQ = 512
D = 768
HEAD = 64
HEADS_HERE = 3
WIDTH = HEADS_HERE * HEAD
EXPERTS = 64
CAP = 10
GROUPS = 32
CHUNK = 40
ROWS = GROUPS * CHUNK
HALF = D // 2
GRADS = 896
F32 = jnp.float32
BF16 = jnp.bfloat16
GELU_C = float(np.sqrt(2.0 / np.pi))


def bucket_of(offsets):
    half_count = BUCKETS // 2
    exact_count = half_count // 2
    upper_side = (offsets > 0).astype(np.int64) * half_count
    distance = np.abs(offsets)
    ratio = np.log(np.maximum(distance, 1) / exact_count) / np.log(128.0 / exact_count)
    far_bucket = np.minimum(
        exact_count + (ratio * (half_count - exact_count)).astype(np.int64), half_count - 1
    )
    return upper_side + np.where(distance < exact_count, distance, far_bucket)


FAR_STARTS = [
    int(np.argmax(bucket_of(-np.arange(256)) >= b)) for b in range(9, BUCKETS // 2)
]


def line_buckets(block, rows):
    offset = 128 * block + 128 - lax.broadcasted_iota(jnp.int32, (rows, 256), 1)
    distance = jnp.abs(offset)
    far = jnp.full((rows, 256), 8, jnp.int32)
    for start in FAR_STARTS:
        far = far + (distance >= start).astype(jnp.int32)
    bucket = jnp.where(distance < 8, distance, far)
    return jnp.where(offset > 0, bucket + BUCKETS // 2, bucket)


def regroup_matrix():
    sel = np.zeros((320, 320), np.float32)
    for g in range(8):
        for half in range(2):
            for e in range(2):
                for c in range(CAP):
                    sel[half * 160 + e * 80 + g * 10 + c, g * 40 + half * 20 + e * 10 + c] = 1
    return sel


def dot(a, b):
    return jnp.dot(a, b, preferred_element_type=F32)


def dot_nt(a, b):
    return lax.dot_general(a, b, (((1,), (1,)), ((), ())), preferred_element_type=F32)


def dot_tn(a, b):
    return lax.dot_general(a, b, (((0,), (0,)), ((), ())), preferred_element_type=F32)


def head_mask(head, rows):
    lanes = lax.broadcasted_iota(jnp.int32, (rows, WIDTH), 1)
    return (lanes >= head * HEAD) & (lanes < (head + 1) * HEAD)


def only_head(matrix, head):
    return jnp.where(head_mask(head, matrix.shape[0]), matrix, jnp.zeros_like(matrix))


def call(
    body, out_shape, args, scratch=(), scalars=0, far=(), far_out=(), limit=40, flops=0, moved=0
):
    spaces = [pltpu.SMEM] * scalars + [pltpu.VMEM] * (len(args) - scalars)
    for i in far:
        spaces[i] = pltpu.HBM
    outs = out_shape if isinstance(out_shape, tuple) else (out_shape,)
    out_spaces = [pltpu.HBM if i in far_out else pltpu.VMEM for i in range(len(outs))]
    result = pl.pallas_call(
        body,
        out_shape=outs,
        in_specs=[pl.BlockSpec(memory_space=space) for space in spaces],
        out_specs=tuple(pl.BlockSpec(memory_space=space) for space in out_spaces),
        scratch_shapes=scratch,
        compiler_params=pltpu.CompilerParams(vmem_limit_bytes=limit << 20),
        cost_estimate=pl.CostEstimate(flops=flops, bytes_accessed=moved, transcendentals=0),
    )(*args)
    return result if isinstance(out_shape, tuple) else result[0]


def shape(dims, dtype):
    return jax.ShapeDtypeStruct(dims, dtype)


def bias_tile(tiles_ref, far_low, far_high, head, block):
    if block < -1:
        return far_low
    if block > 1:
        return far_high
    return tiles_ref[head * 3 + block + 1]


def scores_t(keys, query_scaled, tiles_ref, table, head, part):
    raw = dot_nt(keys, query_scaled)
    far_low = table[head : head + 1, BUCKETS // 2 - 1 : BUCKETS // 2]
    far_high = table[head : head + 1, BUCKETS - 1 : BUCKETS]
    rows = []
    for key_block in range(4):
        cols = []
        for i in range(2):
            piece = raw[key_block * 128 : key_block * 128 + 128, i * 128 : i * 128 + 128]
            block = key_block - (part * 2 + i)
            cols.append(piece + bias_tile(tiles_ref, far_low, far_high, head, block))
        rows.append(jnp.concatenate(cols, axis=1))
    return jnp.concatenate(rows, axis=0)


def attention_forward(
    table_hbm, x_hbm, gain_hbm, wq_hbm, wk_hbm, wv_hbm,
    normed_hbm, q_hbm, k_hbm, v_hbm, probs_hbm, ctx_ref,
    table_ref, x_ref, gain_ref, wq_ref, wk_ref, wv_ref, normed_ref, q_ref, k_ref, v_ref,
    tiles_ref, probs_ref, sems,
):
    loads = [
        pltpu.make_async_copy(src, dst, sems.at[i])
        for i, (src, dst) in enumerate(
            (
                (table_hbm, table_ref), (x_hbm, x_ref), (wq_hbm, wq_ref), (wk_hbm, wk_ref),
                (wv_hbm, wv_ref), (gain_hbm, gain_ref),
            )
        )
    ]
    for load in loads:
        load.start()
    stores = []

    def store(src, dst):
        copy = pltpu.make_async_copy(src, dst, sems.at[6 + len(stores)])
        copy.start()
        stores.append(copy)

    loads[0].wait()
    table = table_ref[...]
    lines = []
    for block in (-1, 0, 1):
        buckets = lax.broadcasted_iota(jnp.int32, (BUCKETS, 256), 0)
        hot = (buckets == line_buckets(block, 1)).astype(F32)
        lines.append(
            jnp.dot(table, hot, precision=lax.Precision.HIGHEST, preferred_element_type=F32)
        )
    for head in range(HEADS_HERE):
        for block in range(3):
            wide = pltpu.roll(
                jnp.broadcast_to(lines[block][head : head + 1], (128, 256)),
                0, 1, stride=1, stride_axis=0,
            )
            tiles_ref[head * 3 + block] = wide[:, 128:]
    loads[1].wait()
    loads[5].wait()
    gain = gain_ref[...].reshape(1, D)
    for i in range(4):
        rows = pl.ds(i * 128, 128)
        x = x_ref[rows, :].astype(F32)
        scale = lax.rsqrt(jnp.mean(x * x, axis=-1, keepdims=True) + EPS)
        normed_ref[rows, :] = (x * scale * gain).astype(BF16)
    store(normed_ref, normed_hbm)
    normed = normed_ref[...]
    for load, weight, out, out_hbm in (
        (loads[2], wq_ref, q_ref, q_hbm),
        (loads[3], wk_ref, k_ref, k_hbm),
        (loads[4], wv_ref, v_ref, v_hbm),
    ):
        load.wait()
        out[...] = dot_nt(normed, weight[...]).astype(BF16)
        store(out, out_hbm)
    queries, keys, values = q_ref[...], k_ref[...], v_ref[...]
    scaled = queries * jnp.asarray(HEAD**-0.5, BF16)
    for part in range(2):
        rows = slice(part * 256, part * 256 + 256)
        context = jnp.zeros((256, WIDTH), F32)
        for head in range(HEADS_HERE):
            scores = scores_t(keys, only_head(scaled[rows], head), tiles_ref, table, head, part)
            top = jnp.max(scores, axis=0, keepdims=True)
            grown = jnp.exp(scores - top)
            total = jnp.sum(grown, axis=0, keepdims=True)
            probs = (grown * (1.0 / total)).astype(BF16)
            probs_ref[head, part] = probs
            store(probs_ref.at[head, part], probs_hbm.at[head, part])
            context = context + dot_tn(probs, only_head(values, head))
        ctx_ref[rows, :] = context.astype(BF16)
    for copy in stores:
        copy.wait()


def route_columns(route_ref):
    return jnp.transpose(route_ref[...].astype(F32))


def row_of(expert, slot, drop):
    row = (expert >> 1) * CHUNK + (expert & 1) * CAP + slot
    return jnp.where(drop > 0, -1000, row)


def place_kernel(route_ref, low_ref, high_ref, low_t_ref, high_t_ref):
    target = row_of(route_ref[0:1, :], route_ref[1:2, :], route_ref[2:3, :])
    for i in range(4):
        rows = pl.ds(i * 320, 320)
        index = lax.broadcasted_iota(jnp.int32, (320, SEQ), 0) + 320 * i
        low_ref[rows, :] = (index == target).astype(F32).astype(BF16)
        high_ref[rows, :] = (index == target + 20).astype(F32).astype(BF16)
    columns = route_columns(route_ref).astype(jnp.int32)
    target = row_of(columns[:, 0:1], columns[:, 1:2], columns[:, 2:3])
    for i in range(4):
        rows = slice(i * 128, i * 128 + 128)
        index = lax.broadcasted_iota(jnp.int32, (128, ROWS), 1)
        low_t_ref[rows, :] = (index == target[rows]).astype(F32).astype(BF16)
        high_t_ref[rows, :] = (index == target[rows] + 20).astype(F32).astype(BF16)


def middle_kernel(
    place_ref, x_hbm, ctx0, ctx1, ctx2, ctx3, wo0, wo1, wo2, wo3, gain_hbm, router_hbm,
    route_hbm, low_hbm, high_hbm, grad_hbm, middle_hbm, mixed_hbm, probs_hbm, send_ref,
    ctx_s, wo_s, x_ref, gain_ref, router_ref, route_ref, low_ref, high_ref, grad_ref,
    middle_ref, mixed_ref, probs_ref, rows_s, sems, out_sems,
):
    me = place_ref[0]
    core = place_ref[1]
    pairs = []
    for step, (c, w) in enumerate(((ctx0, wo0), (ctx1, wo1), (ctx2, wo2), (ctx3, wo3))):
        pairs += [(c, ctx_s.at[me ^ step]), (w, wo_s.at[me ^ step])]
    pairs += [
        (x_hbm, x_ref), (gain_hbm, gain_ref), (route_hbm, route_ref), (router_hbm, router_ref),
        (grad_hbm, grad_ref), (low_hbm, low_ref), (high_hbm, high_ref),
    ]
    loads = [pltpu.make_async_copy(a, b, sems.at[i]) for i, (a, b) in enumerate(pairs)]
    for load in loads:
        load.start()
    for load in loads[:13]:
        load.wait()
    stores = []
    columns = route_columns(route_ref)
    gain = gain_ref[...].reshape(1, D)
    for i in range(4):
        rows = slice(i * 128, i * 128 + 128)
        attended = dot(ctx_s[0, rows, :], wo_s[0])
        for t in range(1, 4):
            attended = attended + dot(ctx_s[t, rows, :], wo_s[t])
        middle = x_ref[rows, :].astype(F32) + attended
        scale = lax.rsqrt(jnp.mean(middle * middle, axis=-1, keepdims=True) + EPS)
        mixed = (middle * scale * gain).astype(BF16)
        middle_ref[rows, :] = middle
        mixed_ref[rows, :] = mixed
        lanes = lax.broadcasted_iota(jnp.int32, (128, 128), 1)
        logits = jnp.where(lanes < EXPERTS, dot_nt(mixed, router_ref[...]), -jnp.inf)
        grown = jnp.exp(logits - jnp.max(logits, axis=-1, keepdims=True))
        probs = grown / jnp.sum(grown, axis=-1, keepdims=True)
        probs_ref[rows, :] = probs
        expert = columns[rows, 0:1].astype(jnp.int32)
        chosen = jnp.sum(jnp.where(lanes == expert, probs, 0.0), axis=-1, keepdims=True)
        gate = chosen * (1.0 - columns[rows, 2:3])
        grads = (grad_ref[rows, :].astype(F32) * gate).astype(BF16)
        rows_s[rows, :] = jnp.where(core == 0, mixed, grads)
        for src, dst in ((middle_ref, middle_hbm), (mixed_ref, mixed_hbm), (probs_ref, probs_hbm)):
            part = pl.ds(i * 128, 128)
            copy = pltpu.make_async_copy(src.at[part], dst.at[part], out_sems.at[len(stores)])
            copy.start()
            stores.append(copy)
    for load in loads[13:]:
        load.wait()
    for i in range(4):
        rows = pl.ds(i * 320, 320)
        out = dot(low_ref[rows, :], rows_s[:, :HALF]) + dot(high_ref[rows, :], rows_s[:, HALF:])
        send_ref[rows, :] = out.astype(BF16)
    for copy in stores:
        copy.wait()


def expert_kernel(
    place_ref, own_ref, other_ref, in_ref, out_ref, sel_ref, back_ref,
    mine_ref, theirs_ref, x_ref, s_ref, act_ref, pre_ref, o_s, i_s,
):
    core = place_ref[1]
    for b in range(4):
        rows = pl.ds(b * 320, 320)
        own = own_ref[rows, :]
        other = other_ref[rows, :]
        for dest, block in (
            (x_ref, jnp.where(core == 0, own, other)),
            (s_ref, jnp.where(core == 0, other, own)),
        ):
            sorted_rows = dot(sel_ref[...], block).astype(BF16)
            for half in range(2):
                for e in range(2):
                    dest[e, pl.ds(b * 80, 80), pl.ds(half * HALF, HALF)] = sorted_rows[
                        half * 160 + e * 80 : half * 160 + e * 80 + 80
                    ]
    for e in range(2):
        x = x_ref[e]
        s = s_ref[e]
        out = jnp.zeros((320, D), F32)
        back = jnp.zeros((320, D), F32)
        for f in range(3):
            cols = slice(f * 256, f * 256 + 256)
            w_in = in_ref[e, :, cols]
            w_out = out_ref[e, cols, :]
            pre = dot(x, w_in)
            bent = jnp.tanh(GELU_C * (pre + 0.044715 * (pre * pre * pre)))
            cdf = 0.5 * (1.0 + bent)
            act = (pre * cdf).astype(BF16)
            slope = cdf + (0.5 * GELU_C) * pre * (1.0 - bent * bent) * (
                1.0 + (3 * 0.044715) * (pre * pre)
            )
            act_ref[e, :, cols] = act
            out = out + dot(act, w_out)
            act_grad = dot_nt(s, w_out)
            pre_grad = (act_grad * slope).astype(BF16)
            pre_ref[e, :, cols] = pre_grad
            back = back + dot_nt(pre_grad, w_in)
        o_s[e] = out.astype(BF16)
        i_s[e] = back.astype(BF16)
    for b in range(4):
        rows = pl.ds(b * 80, 80)
        pieces = []
        for src in (o_s, i_s):
            stacked = jnp.concatenate(
                [
                    src[e, rows, pl.ds(half * HALF, HALF)]
                    for half in range(2)
                    for e in range(2)
                ],
                axis=0,
            )
            pieces.append(dot(back_ref[...], stacked).astype(BF16))
        mine_ref[pl.ds(b * 320, 320), :] = jnp.where(core == 0, pieces[0], pieces[1])
        theirs_ref[pl.ds(b * 320, 320), :] = jnp.where(core == 0, pieces[1], pieces[0])


def expert_grads_kernel(x_ref, s_ref, act_ref, pre_ref, in_grad_ref, out_grad_ref):
    out_grad_ref[0] = dot_tn(act_ref[0], s_ref[0])
    in_grad_ref[0] = dot_tn(x_ref[0], pre_ref[0])


def expert_grads(x, s, act, pre):
    whole = pl.BlockSpec((1, 320, D), lambda e, f: (e, 0, 0))
    part = pl.BlockSpec((1, 320, 256), lambda e, f: (e, 0, f))
    return pl.pallas_call(
        expert_grads_kernel,
        grid=(2, 3),
        out_shape=(shape((2, D, D), F32), shape((2, D, D), F32)),
        in_specs=[whole, whole, part, part],
        out_specs=(
            pl.BlockSpec((1, D, 256), lambda e, f: (e, 0, f)),
            pl.BlockSpec((1, 256, D), lambda e, f: (e, f, 0)),
        ),
        compiler_params=pltpu.CompilerParams(vmem_limit_bytes=24 << 20),
        cost_estimate=pl.CostEstimate(
            flops=8 * 320 * D * D, bytes_accessed=14_000_000, transcendentals=0
        ),
    )(x, s, act, pre)


def tokens_kernel(low_ref, high_ref, recv_ref, out_ref):
    slots = (
        recv_ref[pl.ds(0, ROWS), :].astype(F32) + recv_ref[pl.ds(ROWS, ROWS), :].astype(F32)
    ).astype(BF16)
    out_ref[:, pl.ds(0, HALF)] = dot(low_ref[...], slots).astype(BF16)
    out_ref[:, pl.ds(HALF, HALF)] = dot(high_ref[...], slots).astype(BF16)


def backward_kernel(
    place_ref, x_ref, middle_ref, mixed_ref, probs_ref, route_ref, grad_ref,
    own_ref, other_ref, router_ref, gain_ref, wo_ref, ctx_ref, q_ref, k_ref, v_ref, normed_ref,
    weights_ref, wq_ref, wk_ref, wv_ref, stretch_ref,
    output_hbm, middle_grad_hbm, grads_ref, mine_ref, theirs_ref, gain_one_ref,
    low_s, logit_s, normed_s, output_ref, middle_grad_ref, sems,
):
    core = place_ref[1]
    stores = []
    columns = route_columns(route_ref)
    gain = gain_ref[...]
    gain_grad = jnp.zeros((1, D), F32)
    for i in range(4):
        rows = slice(i * 128, i * 128 + 128)
        own = own_ref[rows, :]
        other = other_ref[rows, :]
        expert_rows = jnp.where(core == 0, own, other).astype(F32)
        mixed_grad = jnp.where(core == 0, other, own).astype(F32)
        probs = probs_ref[rows, :]
        kept = 1.0 - columns[rows, 2:3]
        lanes = lax.broadcasted_iota(jnp.int32, (128, 128), 1)
        hot = (lanes == columns[rows, 0:1].astype(jnp.int32)).astype(F32)
        chosen = jnp.sum(probs * hot, axis=-1, keepdims=True)
        middle = middle_ref[rows, :]
        upstream = grad_ref[rows, :].astype(F32)
        output_ref[rows, :] = (middle + (chosen * kept) * expert_rows).astype(BF16)
        gate_grad = jnp.sum(upstream * expert_rows, axis=-1, keepdims=True) * kept
        logit_grad = (probs * (hot - chosen) * gate_grad).astype(BF16)
        logit_s[rows, :] = logit_grad
        mixed_grad = mixed_grad + dot(logit_grad, router_ref[...])
        scale = lax.rsqrt(jnp.mean(middle * middle, axis=-1, keepdims=True) + EPS)
        weighted = mixed_grad * gain
        inner = jnp.mean(weighted * middle, axis=-1, keepdims=True)
        gain_grad = gain_grad + jnp.sum(mixed_grad * middle * scale, axis=0, keepdims=True)
        middle_grad = upstream + scale * weighted - middle * (scale * scale * scale * inner)
        middle_grad_ref[rows, :] = middle_grad
        low_s[rows, :] = middle_grad.astype(BF16)
        for src, dst in ((output_ref, output_hbm), (middle_grad_ref, middle_grad_hbm)):
            part = pl.ds(i * 128, 128)
            copy = pltpu.make_async_copy(src.at[part], dst.at[part], sems.at[len(stores)])
            copy.start()
            stores.append(copy)
    middle_low = low_s[...]
    grads_ref[pl.ds(3 * WIDTH, WIDTH), :D] = dot_tn(ctx_ref[...], middle_low).astype(BF16)
    ctx_grad = dot_nt(middle_low, wo_ref[...]).astype(BF16)

    values = v_ref[...]
    key_scaled = k_ref[...] * jnp.asarray(HEAD**-0.5, BF16)
    query_scaled = q_ref[...] * jnp.asarray(HEAD**-0.5, BF16)
    key_grad = jnp.zeros((SEQ, WIDTH), F32)
    value_grad = jnp.zeros((SEQ, WIDTH), F32)
    query_grads = [jnp.zeros((256, WIDTH), F32), jnp.zeros((256, WIDTH), F32)]
    buckets = lax.broadcasted_iota(jnp.int32, (BUCKETS, 256), 0)
    line_ids = [line_buckets(block, 1) for block in (-1, 0, 1)]
    bias_grad = jnp.zeros((BUCKETS, 128), F32)
    bias_lanes = lax.broadcasted_iota(jnp.int32, (BUCKETS, 128), 1)
    turn = (
        lax.broadcasted_iota(jnp.int32, (128, 128), 0)
        + lax.broadcasted_iota(jnp.int32, (128, 128), 1)
        == 127
    ).astype(F32)
    for head in range(HEADS_HERE):
        near = [jnp.zeros((128, 128), F32) for _ in range(3)]
        far_low = jnp.zeros((128, 128), F32)
        far_high = jnp.zeros((128, 128), F32)
        key_head = only_head(key_scaled, head)
        for part in range(2):
            rows = slice(part * 256, part * 256 + 256)
            query_head = only_head(query_scaled[rows], head)
            ctx_head = only_head(ctx_grad[rows], head)
            probs_low = weights_ref[head, part]
            probs = probs_low.astype(F32)
            value_grad = value_grad + dot(probs_low, ctx_head)
            prob_grad = dot_nt(values, ctx_head)
            inner = jnp.sum(probs * prob_grad, axis=0, keepdims=True)
            score_grad = (probs * (prob_grad - inner)).astype(BF16)
            key_grad = key_grad + dot(score_grad, query_head)
            query_grads[part] = query_grads[part] + dot_tn(score_grad, key_head)
            for key_block in range(4):
                for i in range(2):
                    piece = score_grad[
                        key_block * 128 : key_block * 128 + 128, i * 128 : i * 128 + 128
                    ].astype(F32)
                    block = key_block - (part * 2 + i)
                    if block < -1:
                        far_low = far_low + piece
                    elif block > 1:
                        far_high = far_high + piece
                    else:
                        near[block + 1] = near[block + 1] + piece
        by_bucket = jnp.zeros((BUCKETS, 256), F32)
        for block in range(3):
            turned = jnp.dot(
                turn, near[block], precision=lax.Precision.HIGHEST, preferred_element_type=F32
            )
            wide = jnp.concatenate([turned, jnp.zeros((128, 128), F32)], axis=1)
            wide = pltpu.roll(wide, 1, 1, stride=1, stride_axis=0)
            line = jnp.sum(wide, axis=0, keepdims=True)
            by_bucket = by_bucket + jnp.where(
                buckets == line_ids[block], line, 0.0
            )
        side = lax.broadcasted_iota(jnp.int32, (BUCKETS, 128), 0)
        low_line = jnp.sum(far_low, axis=0, keepdims=True)
        high_line = jnp.sum(far_high, axis=0, keepdims=True)
        ends = jnp.where(side == BUCKETS // 2 - 1, low_line, 0.0) + jnp.where(
            side == BUCKETS - 1, high_line, 0.0
        )
        by_bucket = by_bucket[:, :128] + by_bucket[:, 128:] + ends
        total = jnp.sum(by_bucket, axis=1, keepdims=True)
        bias_grad = bias_grad + jnp.where(bias_lanes == EXPERTS + 1 + head, total, 0.0)
    query_low = jnp.concatenate(query_grads, axis=0).astype(BF16)
    key_low = key_grad.astype(BF16)
    value_low = value_grad.astype(BF16)
    normed = normed_ref[...]
    for i, low in enumerate((query_low, key_low, value_low)):
        grads_ref[pl.ds(i * WIDTH, WIDTH), :D] = dot_tn(low, normed).astype(BF16)
    rest = dot_tn(mixed_ref[...], logit_s[...]) + dot(stretch_ref[...], bias_grad.astype(BF16))
    column = jnp.transpose(jnp.broadcast_to(gain_grad, (128, D)))
    lanes = lax.broadcasted_iota(jnp.int32, (D, 128), 1)
    grads_ref[:, D:] = jnp.where(lanes == EXPERTS, column, rest).astype(BF16)
    normed_part = (
        dot(query_low, wq_ref[...])
        + dot(key_low, wk_ref[...])
        + dot(value_low, wv_ref[...])
    )
    normed_s[...] = normed_part.astype(BF16)
    hidden = x_ref[...].astype(F32)
    scale = lax.rsqrt(jnp.mean(hidden * hidden, axis=-1, keepdims=True) + EPS)
    gain_one = jnp.sum(normed_part * hidden * scale, axis=0, keepdims=True)
    gain_one_ref[...] = jnp.broadcast_to(gain_one, (8, D))
    mine_ref[...] = normed_s[pl.ds(pl.multiple_of(core * 256, 256), 256), :]
    theirs_ref[...] = normed_s[pl.ds(pl.multiple_of((1 - core) * 256, 256), 256), :]
    for copy in stores:
        copy.wait()


def halves(core, own_ref, other_ref, i):
    local = slice((i % 2) * 128, (i % 2) * 128 + 128)
    return jnp.where(core == i // 2, own_ref[local, :], other_ref[local, :]).astype(F32)


def reduce_kernel(parts_ref, pair_ref, link_ref, send_ref):
    gain_grad = (pair_ref[0:1] + pair_ref[8:9]) + (link_ref[0:1] + link_ref[8:9])
    total = jnp.zeros((24, GRADS), F32)
    for j in range(GROUPS // 2):
        pair = parts_ref[pl.ds(j * 48, 48), :].astype(F32)
        total = total + pair[:24] + pair[24:]
    lines = [
        pltpu.roll(gain_grad[:, r // 4 * 128 : r // 4 * 128 + 128], (96 - r % 4 * 32) % 128, 1)
        for r in range(24)
    ]
    lanes = lax.broadcasted_iota(jnp.int32, (24, 128), 1)
    last = jnp.where(lanes < 96, total[:, D:], jnp.concatenate(lines, axis=0))
    chunk = jnp.concatenate([total[:, :D], last], axis=1)
    pair = jnp.concatenate([chunk, chunk], axis=0).astype(BF16)
    for j in range(GROUPS // 2):
        send_ref[pl.ds(j * 48, 48), :] = pair


def input_kernel(place_ref, own_ref, other_ref, x_ref, gain_ref, middle_grad_ref, input_ref):
    core = place_ref[1]
    gain = gain_ref[...]
    for i in range(4):
        rows = slice(i * 128, i * 128 + 128)
        hidden = x_ref[rows, :].astype(F32)
        scale = lax.rsqrt(jnp.mean(hidden * hidden, axis=-1, keepdims=True) + EPS)
        weighted = halves(core, own_ref, other_ref, i) * gain
        inner = jnp.mean(weighted * hidden, axis=-1, keepdims=True)
        input_ref[rows, :] = (
            middle_grad_ref[rows, :]
            + scale * weighted
            - hidden * (scale * scale * scale * inner)
        )


def finish_kernel(
    recv_ref, stretch_ref, gain_one_ref, gain_two_ref, bias_ref,
    q_ref, k_ref, v_ref, o_ref, router_ref,
):
    for i, out in enumerate((q_ref, k_ref, v_ref, o_ref)):
        out[...] = recv_ref[pl.ds(i * WIDTH, WIDTH), :D].astype(F32)
    last = recv_ref[:, D:].astype(F32)
    summed = jnp.zeros((24, 128), F32)
    for j in range(GROUPS):
        summed = summed + last[j * 24 : j * 24 + 24]
    lanes = lax.broadcasted_iota(jnp.int32, (1, 128), 1)
    for block in range(6):
        line = jnp.zeros((1, 128), F32)
        for i in range(4):
            r = block * 4 + i
            piece = pltpu.roll(summed[r : r + 1], (32 + 32 * i) % 128, 1)
            line = jnp.where((lanes >= 32 * i) & (lanes < 32 * i + 32), piece, line)
        gain_one_ref[pl.ds(block * 128, 128)] = line[0]
    turned = jnp.transpose(last)
    router_ref[...] = turned[:EXPERTS]
    tail = turned[EXPERTS : EXPERTS + 8]
    gain_two_ref[...] = tail[0]
    bias_ref[...] = dot(tail.astype(BF16), stretch_ref[...])[1 : 1 + HEADS_HERE]


def shards(
    layer_input, attn_gain, query_weight, key_weight, value_weight, output_weight, position_bias,
    moe_gain, router_weight, expert_in, expert_out, route_expert, route_slot, route_drop, out_grad,
):
    experts_axis = ("z", "x", "h")
    pair_axis = ("l", "z", "x", "h")
    core = lax.axis_index("c")
    place = jnp.stack([lax.axis_index("l") * 2 + core, core]).astype(jnp.int32)

    def swap(array, axis):
        return lax.ppermute(array, axis, [(0, 1), (1, 0)])

    gain_one = attn_gain.reshape(1, D)
    gain_two = moe_gain.reshape(1, D)
    zeros = jnp.zeros_like(route_drop)
    route = jnp.stack([route_expert, route_slot, route_drop] + [zeros] * 5)
    table = jnp.transpose(position_bias)
    wq, wk, wv = (jnp.transpose(w) for w in (query_weight, key_weight, value_weight))
    router = jnp.pad(jnp.transpose(router_weight), ((0, 128 - EXPERTS), (0, 0)))
    wo_link = swap(output_weight, "l")
    wo_core = swap(output_weight, "c")
    wo_far = swap(wo_link, "c")

    tall = shape((SEQ, WIDTH), BF16)
    wide = shape((SEQ, D), BF16)
    tile_shape = (3 * HEADS_HERE, 128, 128)
    weight_vmem = pltpu.VMEM((WIDTH, D), BF16)
    tall_vmem = pltpu.VMEM((SEQ, WIDTH), BF16)
    probs_shape = (HEADS_HERE, 2, SEQ, 256)
    normed, queries, keys, values, weights, context = call(
        attention_forward,
        (wide, tall, tall, tall, shape(probs_shape, BF16), tall),
        (table, layer_input, attn_gain, wq, wk, wv),
        far=(0, 1, 2, 3, 4, 5), far_out=(0, 1, 2, 3, 4),
        scratch=(pltpu.VMEM((HEADS_HERE, BUCKETS), F32), pltpu.VMEM((SEQ, D), BF16),
                 pltpu.VMEM((D,), F32), weight_vmem, weight_vmem, weight_vmem, pltpu.VMEM((SEQ, D), BF16),
                 tall_vmem, tall_vmem, tall_vmem, pltpu.VMEM(tile_shape, F32),
                 pltpu.VMEM(probs_shape, BF16), pltpu.SemaphoreType.DMA((16,))),
        limit=60, flops=900_000_000, moved=5_000_000,
    )
    flat, flat_t = shape((ROWS, SEQ), BF16), shape((SEQ, ROWS), BF16)
    low_place, high_place, low_back, high_back = call(
        place_kernel, (flat, flat, flat_t, flat_t), (route,),
        limit=12, flops=10_000_000, moved=5_500_000,
    )
    ctx_link = swap(context, "l")
    ctx_core = swap(context, "c")
    ctx_link_late, low_place = lax.optimization_barrier((ctx_link, low_place))
    ctx_far = swap(ctx_link_late, "c")
    middle, mixed, probs, send = call(
        middle_kernel,
        (shape((SEQ, D), F32), wide, shape((SEQ, 128), F32), shape((ROWS, HALF), BF16)),
        (place, layer_input, context, ctx_core, ctx_link, ctx_far,
         output_weight, wo_core, wo_link, wo_far, moe_gain, router, route, low_place, high_place,
         out_grad),
        scratch=(pltpu.VMEM((4, SEQ, WIDTH), BF16), pltpu.VMEM((4, WIDTH, D), BF16),
                 pltpu.VMEM((SEQ, D), BF16), pltpu.VMEM((D,), F32), pltpu.VMEM((128, D), BF16),
                 pltpu.VMEM((8, SEQ), jnp.int32), pltpu.VMEM((ROWS, SEQ), BF16),
                 pltpu.VMEM((ROWS, SEQ), BF16), pltpu.VMEM((SEQ, D), BF16),
                 pltpu.VMEM((SEQ, D), F32), pltpu.VMEM((SEQ, D), BF16),
                 pltpu.VMEM((SEQ, 128), F32), pltpu.VMEM((SEQ, D), BF16),
                 pltpu.SemaphoreType.DMA((15,)), pltpu.SemaphoreType.DMA((12,))),
        scalars=1, far=tuple(range(1, 16)), far_out=(0, 1, 2),
        limit=60, flops=1_700_000_000, moved=8_000_000,
    )
    received = lax.all_to_all(send, experts_axis, 0, 0, tiled=True)
    received_other = swap(received, "c")
    select = regroup_matrix()
    low = shape((2, 320, D), BF16)
    mine, theirs, slots, slot_grads, act, pre_grad = call(
        expert_kernel,
        (shape((ROWS, HALF), BF16), shape((ROWS, HALF), BF16), low, low, low, low),
        (place, received, received_other, expert_in, expert_out,
         jnp.asarray(select, BF16), jnp.asarray(select.T, BF16)),
        scratch=(pltpu.VMEM((2, 320, D), BF16), pltpu.VMEM((2, 320, D), BF16)),
        scalars=1, limit=24, flops=5_000_000_000, moved=14_000_000,
    )
    partial = (mine.astype(F32) + swap(theirs, "c").astype(F32)).astype(BF16)
    back = lax.all_to_all(
        jnp.concatenate([partial, partial], axis=0), pair_axis, 0, 0, tiled=True
    )
    expert_in_grad, expert_out_grad = expert_grads(slots, slot_grads, act, pre_grad)
    rows_own = call(
        tokens_kernel, shape((SEQ, D), BF16), (low_back, high_back, back),
        limit=12, flops=2_000_000_000, moved=3_000_000,
    )
    rows_other = swap(rows_own, "c")
    stretch = np.zeros((D, BUCKETS), np.float32)
    stretch[24 * np.arange(BUCKETS), np.arange(BUCKETS)] = 1
    half = shape((256, D), BF16)
    layer_output, middle_grad, grads, norm_mine, norm_theirs, gain_part = call(
        backward_kernel,
        (wide, shape((SEQ, D), F32), shape((D, GRADS), BF16), half, half, shape((8, D), F32)),
        (place, layer_input, middle, mixed, probs, route, out_grad,
         rows_own, rows_other, router, gain_two, output_weight, context, queries, keys,
         values, normed, weights, wq, wk, wv, jnp.asarray(stretch, BF16)),
        scratch=(pltpu.VMEM((SEQ, D), BF16), pltpu.VMEM((SEQ, 128), BF16),
                 pltpu.VMEM((SEQ, D), BF16), pltpu.VMEM((SEQ, D), BF16),
                 pltpu.VMEM((SEQ, D), F32), pltpu.SemaphoreType.DMA((8,))),
        far_out=(0, 1),
        scalars=1, limit=24, flops=4_000_000_000, moved=12_000_000,
    )
    gain_pair = jnp.concatenate([gain_part, swap(gain_part, "c")], axis=0)
    halved = (norm_mine.astype(F32) + swap(norm_theirs, "c").astype(F32)).astype(BF16)
    scattered = lax.all_to_all(grads, experts_axis, 0, 0, tiled=True)
    gain_link = swap(gain_pair, "l")
    halved = (halved.astype(F32) + swap(halved, "l").astype(F32)).astype(BF16)
    halved_other = swap(halved, "c")
    spread = call(
        reduce_kernel, shape((D, GRADS), BF16),
        (scattered, gain_pair, gain_link),
        limit=12, flops=10_000_000, moved=3_000_000,
    )
    gathered = lax.all_to_all(spread, experts_axis, 0, 0, tiled=True)
    input_grad = call(
        input_kernel, shape((SEQ, D), F32),
        (place, halved, halved_other, layer_input, gain_one, middle_grad),
        scalars=1, limit=12, flops=10_000_000, moved=5_000_000,
    )
    out = shape((WIDTH, D), F32)
    line = shape((D,), F32)
    gain_one_grad, gain_two_grad, bias_grad, query_grad, key_grad, value_grad, output_grad, \
        router_grad = call(
            finish_kernel,
            (line, line, shape((HEADS_HERE, BUCKETS), F32), out, out, out, out,
             shape((EXPERTS, D), F32)),
            (gathered, jnp.asarray(stretch, BF16)),
            limit=12, flops=10_000_000, moved=6_000_000,
        )
    return (
        layer_output,
        input_grad,
        gain_one_grad,
        jnp.transpose(query_grad),
        jnp.transpose(key_grad),
        jnp.transpose(value_grad),
        output_grad,
        jnp.transpose(bias_grad),
        gain_two_grad,
        jnp.transpose(router_grad),
        expert_in_grad,
        expert_out_grad,
    )


def solution(mesh):
    fine = Mesh(mesh.devices.reshape(4, 4, 2, 2, 2), ("z", "x", "h", "l", "c"))
    ex = ("z", "x", "h")
    te = ("l", "c")
    in_specs = (
        P(ex, None), P(), P(None, te), P(None, te), P(None, te), P(te, None), P(None, te), P(),
        P(), P(ex, None, te), P(ex, te, None), P(ex), P(ex), P(ex), P(ex, None),
    )
    out_specs = (
        P(ex, None), P(ex, None), P(), P(None, te), P(None, te), P(None, te), P(te, None),
        P(None, te), P(), P(), P(ex, None, te), P(ex, te, None),
    )
    return jax.shard_map(shards, mesh=fine, in_specs=in_specs, out_specs=out_specs, check_vma=False)
```

```python
import jax
import jax.numpy as jnp
import numpy as np
from jax import lax
from jax.experimental import pallas as pl
from jax.experimental.pallas import tpu as pltpu
from jax.sharding import Mesh
from jax.sharding import PartitionSpec as P

BUCKETS = 32
EPS = 1e-06
SEQ = 512
D = 768
HEAD = 64
HEADS_HERE = 3
WIDTH = HEADS_HERE * HEAD
EXPERTS = 64
CAP = 10
GROUPS = 32
CHUNK = 40
ROWS = GROUPS * CHUNK
HALF = D // 2
GRADS = 896
F32 = jnp.float32
BF16 = jnp.bfloat16
GELU_C = float(np.sqrt(2.0 / np.pi))


def bucket_of(offsets):
    half_count = BUCKETS // 2
    exact_count = half_count // 2
    upper_side = (offsets > 0).astype(np.int64) * half_count
    distance = np.abs(offsets)
    ratio = np.log(np.maximum(distance, 1) / exact_count) / np.log(128.0 / exact_count)
    far_bucket = np.minimum(
        exact_count + (ratio * (half_count - exact_count)).astype(np.int64), half_count - 1
    )
    return upper_side + np.where(distance < exact_count, distance, far_bucket)


FAR_STARTS = [
    int(np.argmax(bucket_of(-np.arange(256)) >= b)) for b in range(9, BUCKETS // 2)
]


def line_buckets(block, rows):
    offset = 128 * block + 128 - lax.broadcasted_iota(jnp.int32, (rows, 256), 1)
    distance = jnp.abs(offset)
    far = jnp.full((rows, 256), 8, jnp.int32)
    for start in FAR_STARTS:
        far = far + (distance >= start).astype(jnp.int32)
    bucket = jnp.where(distance < 8, distance, far)
    return jnp.where(offset > 0, bucket + BUCKETS // 2, bucket)


def regroup_matrix():
    sel = np.zeros((320, 320), np.float32)
    for g in range(8):
        for half in range(2):
            for e in range(2):
                for c in range(CAP):
                    sel[half * 160 + e * 80 + g * 10 + c, g * 40 + half * 20 + e * 10 + c] = 1
    return sel


def dot(a, b):
    return jnp.dot(a, b, preferred_element_type=F32)


def dot_nt(a, b):
    return lax.dot_general(a, b, (((1,), (1,)), ((), ())), preferred_element_type=F32)


def dot_tn(a, b):
    return lax.dot_general(a, b, (((0,), (0,)), ((), ())), preferred_element_type=F32)


def head_mask(head, rows):
    lanes = lax.broadcasted_iota(jnp.int32, (rows, WIDTH), 1)
    return (lanes >= head * HEAD) & (lanes < (head + 1) * HEAD)


def only_head(matrix, head):
    return jnp.where(head_mask(head, matrix.shape[0]), matrix, jnp.zeros_like(matrix))


def call(
    body, out_shape, args, scratch=(), scalars=0, far=(), far_out=(), alias=None, limit=40, flops=0, moved=0
):
    spaces = [pltpu.SMEM] * scalars + [pltpu.VMEM] * (len(args) - scalars)
    for i in far:
        spaces[i] = pltpu.HBM
    outs = out_shape if isinstance(out_shape, tuple) else (out_shape,)
    out_spaces = [pltpu.HBM if i in far_out else pltpu.VMEM for i in range(len(outs))]
    result = pl.pallas_call(
        body,
        out_shape=outs,
        in_specs=[pl.BlockSpec(memory_space=space) for space in spaces],
        out_specs=tuple(pl.BlockSpec(memory_space=space) for space in out_spaces),
        scratch_shapes=scratch,
        input_output_aliases=alias or {},
        compiler_params=pltpu.CompilerParams(vmem_limit_bytes=limit << 20),
        cost_estimate=pl.CostEstimate(flops=flops, bytes_accessed=moved, transcendentals=0),
    )(*args)
    return result if isinstance(out_shape, tuple) else result[0]


def shape(dims, dtype):
    return jax.ShapeDtypeStruct(dims, dtype)


def bias_tile(tiles_ref, far_low, far_high, head, block):
    if block < -1:
        return far_low
    if block > 1:
        return far_high
    return tiles_ref[head * 3 + block + 1]


def scores_t(keys, query_scaled, tiles_ref, table, head, part):
    raw = dot_nt(keys, query_scaled)
    far_low = table[head : head + 1, BUCKETS // 2 - 1 : BUCKETS // 2]
    far_high = table[head : head + 1, BUCKETS - 1 : BUCKETS]
    rows = []
    for key_block in range(4):
        cols = []
        for i in range(2):
            piece = raw[key_block * 128 : key_block * 128 + 128, i * 128 : i * 128 + 128]
            block = key_block - (part * 2 + i)
            cols.append(piece + bias_tile(tiles_ref, far_low, far_high, head, block))
        rows.append(jnp.concatenate(cols, axis=1))
    return jnp.concatenate(rows, axis=0)


def attention_forward(
    table_hbm, x_hbm, gain_hbm, wq_hbm, wk_hbm, wv_hbm,
    normed_hbm, q_hbm, k_hbm, v_hbm, tiles_hbm, ctx_ref, lse_ref,
    table_ref, x_ref, gain_ref, wq_ref, wk_ref, wv_ref, normed_ref, q_ref, k_ref, v_ref,
    tiles_ref, sems,
):
    loads = [
        pltpu.make_async_copy(src, dst, sems.at[i])
        for i, (src, dst) in enumerate(
            (
                (table_hbm, table_ref), (x_hbm, x_ref), (wq_hbm, wq_ref), (wk_hbm, wk_ref),
                (wv_hbm, wv_ref), (gain_hbm, gain_ref),
            )
        )
    ]
    for load in loads:
        load.start()
    stores = []

    def store(src, dst):
        copy = pltpu.make_async_copy(src, dst, sems.at[6 + len(stores)])
        copy.start()
        stores.append(copy)

    loads[0].wait()
    table = table_ref[...]
    lines = []
    for block in (-1, 0, 1):
        buckets = lax.broadcasted_iota(jnp.int32, (BUCKETS, 256), 0)
        hot = (buckets == line_buckets(block, 1)).astype(F32)
        lines.append(
            jnp.dot(table, hot, precision=lax.Precision.HIGHEST, preferred_element_type=F32)
        )
    for head in range(HEADS_HERE):
        for block in range(3):
            wide = pltpu.roll(
                jnp.broadcast_to(lines[block][head : head + 1], (128, 256)),
                0, 1, stride=1, stride_axis=0,
            )
            tiles_ref[head * 3 + block] = wide[:, 128:]
    store(tiles_ref, tiles_hbm)
    loads[1].wait()
    loads[5].wait()
    gain = gain_ref[...].reshape(1, D)
    for i in range(4):
        rows = pl.ds(i * 128, 128)
        x = x_ref[rows, :].astype(F32)
        scale = lax.rsqrt(jnp.mean(x * x, axis=-1, keepdims=True) + EPS)
        normed_ref[rows, :] = (x * scale * gain).astype(BF16)
    store(normed_ref, normed_hbm)
    normed = normed_ref[...]
    for load, weight, out, out_hbm in (
        (loads[2], wq_ref, q_ref, q_hbm),
        (loads[3], wk_ref, k_ref, k_hbm),
        (loads[4], wv_ref, v_ref, v_hbm),
    ):
        load.wait()
        out[...] = dot_nt(normed, weight[...]).astype(BF16)
        store(out, out_hbm)
    queries, keys, values = q_ref[...], k_ref[...], v_ref[...]
    lse_ref[...] = jnp.zeros((8, SEQ), F32)
    scaled = queries * jnp.asarray(HEAD**-0.5, BF16)
    for part in range(2):
        rows = slice(part * 256, part * 256 + 256)
        context = jnp.zeros((256, WIDTH), F32)
        for head in range(HEADS_HERE):
            scores = scores_t(keys, only_head(scaled[rows], head), tiles_ref, table, head, part)
            top = jnp.max(scores, axis=0, keepdims=True)
            grown = jnp.exp(scores - top)
            total = jnp.sum(grown, axis=0, keepdims=True)
            probs = (grown * (1.0 / total)).astype(BF16)
            lse_ref[head : head + 1, rows] = top + jnp.log(total)
            context = context + dot_tn(probs, only_head(values, head))
        ctx_ref[rows, :] = context.astype(BF16)
    for copy in stores:
        copy.wait()


def route_columns(route_ref):
    return jnp.transpose(route_ref[...].astype(F32))


def row_of(expert, slot, drop):
    row = (expert >> 1) * CHUNK + (expert & 1) * CAP + slot
    return jnp.where(drop > 0, -1000, row)


def place_kernel(route_ref, low_ref, high_ref, low_t_ref, high_t_ref):
    target = row_of(route_ref[0:1, :], route_ref[1:2, :], route_ref[2:3, :])
    for i in range(4):
        rows = pl.ds(i * 320, 320)
        index = lax.broadcasted_iota(jnp.int32, (320, SEQ), 0) + 320 * i
        low_ref[rows, :] = (index == target).astype(F32).astype(BF16)
        high_ref[rows, :] = (index == target + 20).astype(F32).astype(BF16)
    columns = route_columns(route_ref).astype(jnp.int32)
    target = row_of(columns[:, 0:1], columns[:, 1:2], columns[:, 2:3])
    for i in range(4):
        rows = slice(i * 128, i * 128 + 128)
        index = lax.broadcasted_iota(jnp.int32, (128, ROWS), 1)
        low_t_ref[rows, :] = (index == target[rows]).astype(F32).astype(BF16)
        high_t_ref[rows, :] = (index == target[rows] + 20).astype(F32).astype(BF16)


def middle_kernel(
    place_ref, x_ref, ctx0, ctx1, ctx2, ctx3, wo0, wo1, wo2, wo3, gain_ref, router_ref,
    route_ref, low_ref, high_ref, grad_ref, middle_ref, mixed_ref, probs_ref, send_ref,
    ctx_s, wo_s, rows_s,
):
    me = place_ref[0]
    core = place_ref[1]
    for step, (c, w) in enumerate(((ctx0, wo0), (ctx1, wo1), (ctx2, wo2), (ctx3, wo3))):
        ctx_s[me ^ step] = c[...]
        wo_s[me ^ step] = w[...]
    columns = route_columns(route_ref)
    for i in range(2):
        rows = slice(i * 256, i * 256 + 256)
        attended = dot(ctx_s[0, rows, :], wo_s[0])
        for t in range(1, 4):
            attended = attended + dot(ctx_s[t, rows, :], wo_s[t])
        middle = x_ref[rows, :].astype(F32) + attended
        scale = lax.rsqrt(jnp.mean(middle * middle, axis=-1, keepdims=True) + EPS)
        mixed = (middle * scale * gain_ref[...]).astype(BF16)
        middle_ref[rows, :] = middle
        mixed_ref[rows, :] = mixed
        lanes = lax.broadcasted_iota(jnp.int32, (256, 128), 1)
        logits = jnp.where(lanes < EXPERTS, dot_nt(mixed, router_ref[...]), -jnp.inf)
        grown = jnp.exp(logits - jnp.max(logits, axis=-1, keepdims=True))
        probs = grown / jnp.sum(grown, axis=-1, keepdims=True)
        probs_ref[rows, :] = probs
        expert = columns[rows, 0:1].astype(jnp.int32)
        chosen = jnp.sum(jnp.where(lanes == expert, probs, 0.0), axis=-1, keepdims=True)
        gate = chosen * (1.0 - columns[rows, 2:3])
        grads = (grad_ref[rows, :].astype(F32) * gate).astype(BF16)
        rows_s[rows, :] = jnp.where(core == 0, mixed, grads)
    for i in range(4):
        rows = pl.ds(i * 320, 320)
        out = dot(low_ref[rows, :], rows_s[:, :HALF]) + dot(high_ref[rows, :], rows_s[:, HALF:])
        send_ref[rows, :] = out.astype(BF16)


def first_expert_kernel(
    place_ref, own_ref, other_ref, in_ref, out_ref, sel_ref, back_ref,
    theirs_ref, x_ref, s_ref, act_ref, pre_ref, part_s,
):
    core = place_ref[1]
    for b in range(4):
        rows = pl.ds(b * 320, 320)
        own = own_ref[rows, :]
        other = other_ref[rows, :]
        for dest, block in (
            (x_ref, jnp.where(core == 0, own, other)),
            (s_ref, jnp.where(core == 0, other, own)),
        ):
            sorted_rows = dot(sel_ref[...], block).astype(BF16)
            for half in range(2):
                for e in range(2):
                    dest[e, pl.ds(b * 80, 80), pl.ds(half * HALF, HALF)] = sorted_rows[
                        half * 160 + e * 80 : half * 160 + e * 80 + 80
                    ]
    for e in range(2):
        x = x_ref[e]
        s = s_ref[e]
        for f in range(3):
            cols = slice(f * 256, f * 256 + 256)
            pre = dot(x, in_ref[e, :, cols])
            bent = jnp.tanh(GELU_C * (pre + 0.044715 * (pre * pre * pre)))
            cdf = 0.5 * (1.0 + bent)
            act_ref[e, :, cols] = (pre * cdf).astype(BF16)
            slope = cdf + (0.5 * GELU_C) * pre * (1.0 - bent * bent) * (
                1.0 + (3 * 0.044715) * (pre * pre)
            )
            act_grad = dot_nt(s, out_ref[e, cols, :])
            pre_ref[e, :, cols] = (act_grad * slope).astype(BF16)
    expert_sums(core == 1, act_ref, pre_ref, in_ref, out_ref, back_ref, theirs_ref, part_s)


def expert_sums(forward, act_ref, pre_ref, in_ref, out_ref, back_ref, sum_ref, part_s):
    @pl.when(forward)
    def _():
        for e in range(2):
            part_s[e] = dot(act_ref[e], out_ref[e]).astype(BF16)

    @pl.when(jnp.logical_not(forward))
    def _():
        for e in range(2):
            part_s[e] = dot_nt(pre_ref[e], in_ref[e]).astype(BF16)

    for b in range(4):
        rows = pl.ds(b * 80, 80)
        stacked = jnp.concatenate(
            [part_s[e, rows, pl.ds(half * HALF, HALF)] for half in range(2) for e in range(2)],
            axis=0,
        )
        sum_ref[pl.ds(b * 320, 320), :] = dot(back_ref[...], stacked).astype(BF16)


def second_expert_kernel(
    place_ref, act_ref, pre_ref, in_ref, out_ref, back_ref, mine_ref, part_s
):
    expert_sums(
        place_ref[1] == 0, act_ref, pre_ref, in_ref, out_ref, back_ref, mine_ref, part_s
    )


def expert_grads_kernel(x_ref, s_ref, act_ref, pre_ref, in_grad_ref, out_grad_ref):
    out_grad_ref[0] = dot_tn(act_ref[0], s_ref[0])
    in_grad_ref[0] = dot_tn(x_ref[0], pre_ref[0])


def expert_grads(x, s, act, pre):
    whole = pl.BlockSpec((1, 320, D), lambda e, f: (e, 0, 0))
    part = pl.BlockSpec((1, 320, 256), lambda e, f: (e, 0, f))
    return pl.pallas_call(
        expert_grads_kernel,
        grid=(2, 3),
        out_shape=(shape((2, D, D), F32), shape((2, D, D), F32)),
        in_specs=[whole, whole, part, part],
        out_specs=(
            pl.BlockSpec((1, D, 256), lambda e, f: (e, 0, f)),
            pl.BlockSpec((1, 256, D), lambda e, f: (e, f, 0)),
        ),
        compiler_params=pltpu.CompilerParams(vmem_limit_bytes=24 << 20),
        cost_estimate=pl.CostEstimate(
            flops=8 * 320 * D * D, bytes_accessed=14_000_000, transcendentals=0
        ),
    )(x, s, act, pre)


def tokens_kernel(low_ref, high_ref, recv_ref, out_ref):
    slots = (
        recv_ref[pl.ds(0, ROWS), :].astype(F32) + recv_ref[pl.ds(ROWS, ROWS), :].astype(F32)
    ).astype(BF16)
    out_ref[:, pl.ds(0, HALF)] = dot(low_ref[...], slots).astype(BF16)
    out_ref[:, pl.ds(HALF, HALF)] = dot(high_ref[...], slots).astype(BF16)


def backward_kernel(
    place_ref, table_ref, x_ref, middle_ref, mixed_ref, probs_ref, route_ref, grad_ref,
    own_ref, other_ref, router_ref, gain_ref, wo_ref, ctx_ref, q_ref, k_ref, v_ref, normed_ref,
    lse_ref, tiles_ref, wq_ref, wk_ref, wv_ref, stretch_ref,
    output_ref, middle_grad_ref, grads_ref, mine_ref, theirs_ref, gain_one_ref,
    low_s, logit_s, normed_s,
):
    core = place_ref[1]
    columns = route_columns(route_ref)
    gain = gain_ref[...]
    gain_grad = jnp.zeros((1, D), F32)
    for i in range(4):
        rows = slice(i * 128, i * 128 + 128)
        own = own_ref[rows, :]
        other = other_ref[rows, :]
        expert_rows = jnp.where(core == 0, own, other).astype(F32)
        mixed_grad = jnp.where(core == 0, other, own).astype(F32)
        probs = probs_ref[rows, :]
        kept = 1.0 - columns[rows, 2:3]
        lanes = lax.broadcasted_iota(jnp.int32, (128, 128), 1)
        hot = (lanes == columns[rows, 0:1].astype(jnp.int32)).astype(F32)
        chosen = jnp.sum(probs * hot, axis=-1, keepdims=True)
        middle = middle_ref[rows, :]
        upstream = grad_ref[rows, :].astype(F32)
        output_ref[rows, :] = (middle + (chosen * kept) * expert_rows).astype(BF16)
        gate_grad = jnp.sum(upstream * expert_rows, axis=-1, keepdims=True) * kept
        logit_grad = (probs * (hot - chosen) * gate_grad).astype(BF16)
        logit_s[rows, :] = logit_grad
        mixed_grad = mixed_grad + dot(logit_grad, router_ref[...])
        scale = lax.rsqrt(jnp.mean(middle * middle, axis=-1, keepdims=True) + EPS)
        weighted = mixed_grad * gain
        inner = jnp.mean(weighted * middle, axis=-1, keepdims=True)
        gain_grad = gain_grad + jnp.sum(mixed_grad * middle * scale, axis=0, keepdims=True)
        middle_grad = upstream + scale * weighted - middle * (scale * scale * scale * inner)
        middle_grad_ref[rows, :] = middle_grad
        low_s[rows, :] = middle_grad.astype(BF16)
    middle_low = low_s[...]
    grads_ref[pl.ds(3 * WIDTH, WIDTH), :D] = dot_tn(ctx_ref[...], middle_low).astype(BF16)
    ctx_grad = dot_nt(middle_low, wo_ref[...]).astype(BF16)

    keys = k_ref[...]
    values = v_ref[...]
    key_scaled = keys * jnp.asarray(HEAD**-0.5, BF16)
    query_scaled = q_ref[...] * jnp.asarray(HEAD**-0.5, BF16)
    key_grad = jnp.zeros((SEQ, WIDTH), F32)
    value_grad = jnp.zeros((SEQ, WIDTH), F32)
    query_grads = [jnp.zeros((256, WIDTH), F32), jnp.zeros((256, WIDTH), F32)]
    buckets = lax.broadcasted_iota(jnp.int32, (BUCKETS, 256), 0)
    line_ids = [line_buckets(block, 1) for block in (-1, 0, 1)]
    bias_grad = jnp.zeros((BUCKETS, 128), F32)
    bias_lanes = lax.broadcasted_iota(jnp.int32, (BUCKETS, 128), 1)
    turn = (
        lax.broadcasted_iota(jnp.int32, (128, 128), 0)
        + lax.broadcasted_iota(jnp.int32, (128, 128), 1)
        == 127
    ).astype(F32)
    for head in range(HEADS_HERE):
        near = [jnp.zeros((128, 128), F32) for _ in range(3)]
        far_low = jnp.zeros((128, 128), F32)
        far_high = jnp.zeros((128, 128), F32)
        key_head = only_head(key_scaled, head)
        for part in range(2):
            rows = slice(part * 256, part * 256 + 256)
            query_head = only_head(query_scaled[rows], head)
            ctx_head = only_head(ctx_grad[rows], head)
            scores = scores_t(keys, query_head, tiles_ref, table_ref[...], head, part)
            probs = jnp.exp(scores - lse_ref[head : head + 1, rows])
            value_grad = value_grad + dot(probs.astype(BF16), ctx_head)
            prob_grad = dot_nt(values, ctx_head)
            inner = jnp.sum(probs * prob_grad, axis=0, keepdims=True)
            score_grad = (probs * (prob_grad - inner)).astype(BF16)
            key_grad = key_grad + dot(score_grad, query_head)
            query_grads[part] = query_grads[part] + dot_tn(score_grad, key_head)
            for key_block in range(4):
                for i in range(2):
                    piece = score_grad[
                        key_block * 128 : key_block * 128 + 128, i * 128 : i * 128 + 128
                    ].astype(F32)
                    block = key_block - (part * 2 + i)
                    if block < -1:
                        far_low = far_low + piece
                    elif block > 1:
                        far_high = far_high + piece
                    else:
                        near[block + 1] = near[block + 1] + piece
        by_bucket = jnp.zeros((BUCKETS, 256), F32)
        for block in range(3):
            turned = jnp.dot(
                turn, near[block], precision=lax.Precision.HIGHEST, preferred_element_type=F32
            )
            wide = jnp.concatenate([turned, jnp.zeros((128, 128), F32)], axis=1)
            wide = pltpu.roll(wide, 1, 1, stride=1, stride_axis=0)
            line = jnp.sum(wide, axis=0, keepdims=True)
            by_bucket = by_bucket + jnp.where(
                buckets == line_ids[block], line, 0.0
            )
        side = lax.broadcasted_iota(jnp.int32, (BUCKETS, 128), 0)
        low_line = jnp.sum(far_low, axis=0, keepdims=True)
        high_line = jnp.sum(far_high, axis=0, keepdims=True)
        ends = jnp.where(side == BUCKETS // 2 - 1, low_line, 0.0) + jnp.where(
            side == BUCKETS - 1, high_line, 0.0
        )
        by_bucket = by_bucket[:, :128] + by_bucket[:, 128:] + ends
        total = jnp.sum(by_bucket, axis=1, keepdims=True)
        bias_grad = bias_grad + jnp.where(bias_lanes == EXPERTS + 1 + head, total, 0.0)
    query_low = jnp.concatenate(query_grads, axis=0).astype(BF16)
    key_low = key_grad.astype(BF16)
    value_low = value_grad.astype(BF16)
    normed = normed_ref[...]
    for i, low in enumerate((query_low, key_low, value_low)):
        grads_ref[pl.ds(i * WIDTH, WIDTH), :D] = dot_tn(low, normed).astype(BF16)
    rest = dot_tn(mixed_ref[...], logit_s[...]) + dot(stretch_ref[...], bias_grad.astype(BF16))
    column = jnp.transpose(jnp.broadcast_to(gain_grad, (128, D)))
    lanes = lax.broadcasted_iota(jnp.int32, (D, 128), 1)
    grads_ref[:, D:] = jnp.where(lanes == EXPERTS, column, rest).astype(BF16)
    gain_one = jnp.zeros((1, D), F32)
    for i in range(4):
        rows = slice(i * 128, i * 128 + 128)
        normed_part = (
            dot(query_low[rows], wq_ref[...])
            + dot(key_low[rows], wk_ref[...])
            + dot(value_low[rows], wv_ref[...])
        )
        normed_s[rows, :] = normed_part.astype(BF16)
        hidden = x_ref[rows, :].astype(F32)
        scale = lax.rsqrt(jnp.mean(hidden * hidden, axis=-1, keepdims=True) + EPS)
        gain_one = gain_one + jnp.sum(normed_part * hidden * scale, axis=0, keepdims=True)
    gain_one_ref[...] = jnp.broadcast_to(gain_one, (8, D))
    mine_ref[...] = normed_s[pl.ds(pl.multiple_of(core * 256, 256), 256), :]
    theirs_ref[...] = normed_s[pl.ds(pl.multiple_of((1 - core) * 256, 256), 256), :]


def halves(core, own_ref, other_ref, i):
    local = slice((i % 2) * 128, (i % 2) * 128 + 128)
    return jnp.where(core == i // 2, own_ref[local, :], other_ref[local, :]).astype(F32)


def reduce_kernel(parts_ref, pair_ref, link_ref, send_ref):
    gain_grad = (pair_ref[0:1] + pair_ref[8:9]) + (link_ref[0:1] + link_ref[8:9])
    total = jnp.zeros((24, GRADS), F32)
    for j in range(GROUPS // 2):
        pair = parts_ref[pl.ds(j * 48, 48), :].astype(F32)
        total = total + pair[:24] + pair[24:]
    lines = [
        pltpu.roll(gain_grad[:, r // 4 * 128 : r // 4 * 128 + 128], (96 - r % 4 * 32) % 128, 1)
        for r in range(24)
    ]
    lanes = lax.broadcasted_iota(jnp.int32, (24, 128), 1)
    last = jnp.where(lanes < 96, total[:, D:], jnp.concatenate(lines, axis=0))
    chunk = jnp.concatenate([total[:, :D], last], axis=1)
    pair = jnp.concatenate([chunk, chunk], axis=0).astype(BF16)
    for j in range(GROUPS // 2):
        send_ref[pl.ds(j * 48, 48), :] = pair


def input_kernel(place_ref, own_ref, other_ref, x_ref, gain_ref, middle_grad_ref, input_ref):
    core = place_ref[1]
    gain = gain_ref[...]
    for i in range(4):
        rows = slice(i * 128, i * 128 + 128)
        hidden = x_ref[rows, :].astype(F32)
        scale = lax.rsqrt(jnp.mean(hidden * hidden, axis=-1, keepdims=True) + EPS)
        weighted = halves(core, own_ref, other_ref, i) * gain
        inner = jnp.mean(weighted * hidden, axis=-1, keepdims=True)
        input_ref[rows, :] = (
            middle_grad_ref[rows, :]
            + scale * weighted
            - hidden * (scale * scale * scale * inner)
        )


def finish_kernel(
    recv_ref, stretch_ref, gain_one_ref, gain_two_ref, bias_ref,
    q_ref, k_ref, v_ref, o_ref, router_ref,
):
    for i, out in enumerate((q_ref, k_ref, v_ref, o_ref)):
        out[...] = recv_ref[pl.ds(i * WIDTH, WIDTH), :D].astype(F32)
    last = recv_ref[:, D:].astype(F32)
    summed = jnp.zeros((24, 128), F32)
    for j in range(GROUPS):
        summed = summed + last[j * 24 : j * 24 + 24]
    lanes = lax.broadcasted_iota(jnp.int32, (1, 128), 1)
    for block in range(6):
        line = jnp.zeros((1, 128), F32)
        for i in range(4):
            r = block * 4 + i
            piece = pltpu.roll(summed[r : r + 1], (32 + 32 * i) % 128, 1)
            line = jnp.where((lanes >= 32 * i) & (lanes < 32 * i + 32), piece, line)
        gain_one_ref[pl.ds(block * 128, 128)] = line[0]
    turned = jnp.transpose(last)
    router_ref[...] = turned[:EXPERTS]
    tail = turned[EXPERTS : EXPERTS + 8]
    gain_two_ref[...] = tail[0]
    bias_ref[...] = dot(tail.astype(BF16), stretch_ref[...])[1 : 1 + HEADS_HERE]


def shards(
    layer_input, attn_gain, query_weight, key_weight, value_weight, output_weight, position_bias,
    moe_gain, router_weight, expert_in, expert_out, route_expert, route_slot, route_drop, out_grad,
):
    experts_axis = ("z", "x", "h")
    pair_axis = ("l", "z", "x", "h")
    core = lax.axis_index("c")
    place = jnp.stack([lax.axis_index("l") * 2 + core, core]).astype(jnp.int32)

    def swap(array, axis):
        return lax.ppermute(array, axis, [(0, 1), (1, 0)])

    gain_one = attn_gain.reshape(1, D)
    gain_two = moe_gain.reshape(1, D)
    zeros = jnp.zeros_like(route_drop)
    route = jnp.stack([route_expert, route_slot, route_drop] + [zeros] * 5)
    table = jnp.transpose(position_bias)
    wq, wk, wv = (jnp.transpose(w) for w in (query_weight, key_weight, value_weight))
    router = jnp.pad(jnp.transpose(router_weight), ((0, 128 - EXPERTS), (0, 0)))
    wo_link = swap(output_weight, "l")
    wo_core = swap(output_weight, "c")
    wo_far = swap(wo_link, "c")

    tall = shape((SEQ, WIDTH), BF16)
    wide = shape((SEQ, D), BF16)
    tile_shape = (3 * HEADS_HERE, 128, 128)
    weight_vmem = pltpu.VMEM((WIDTH, D), BF16)
    tall_vmem = pltpu.VMEM((SEQ, WIDTH), BF16)
    normed, queries, keys, values, tiles, context, lse = call(
        attention_forward,
        (wide, tall, tall, tall, shape(tile_shape, F32), tall, shape((8, SEQ), F32)),
        (table, layer_input, attn_gain, wq, wk, wv),
        far=(0, 1, 2, 3, 4, 5), far_out=(0, 1, 2, 3, 4),
        scratch=(pltpu.VMEM((HEADS_HERE, BUCKETS), F32), pltpu.VMEM((SEQ, D), BF16),
                 pltpu.VMEM((D,), F32), weight_vmem, weight_vmem, weight_vmem, pltpu.VMEM((SEQ, D), BF16),
                 tall_vmem, tall_vmem, tall_vmem, pltpu.VMEM(tile_shape, F32),
                 pltpu.SemaphoreType.DMA((11,))),
        limit=60, flops=900_000_000, moved=5_000_000,
    )
    flat, flat_t = shape((ROWS, SEQ), BF16), shape((SEQ, ROWS), BF16)
    low_place, high_place, low_back, high_back = call(
        place_kernel, (flat, flat, flat_t, flat_t), (route,),
        limit=12, flops=10_000_000, moved=5_500_000,
    )
    ctx_link = swap(context, "l")
    ctx_core = swap(context, "c")
    ctx_link_late, low_place = lax.optimization_barrier((ctx_link, low_place))
    ctx_far = swap(ctx_link_late, "c")
    middle, mixed, probs, send = call(
        middle_kernel,
        (shape((SEQ, D), F32), shape((SEQ, D), BF16), shape((SEQ, 128), F32),
         shape((ROWS, HALF), BF16)),
        (place, layer_input, context, ctx_core, ctx_link, ctx_far,
         output_weight, wo_core, wo_link, wo_far, gain_two, router, route, low_place, high_place,
         out_grad),
        scratch=(pltpu.VMEM((4, SEQ, WIDTH), BF16), pltpu.VMEM((4, WIDTH, D), BF16),
                 pltpu.VMEM((SEQ, D), BF16)),
        scalars=1, limit=16, flops=1_700_000_000, moved=8_000_000,
    )
    received = lax.all_to_all(send, experts_axis, 0, 0, tiled=True)
    received_other = swap(received, "c")
    select = regroup_matrix()
    low = shape((2, 320, D), BF16)
    sums = shape((ROWS, HALF), BF16)
    back_select = jnp.asarray(select.T, BF16)
    theirs, slots, slot_grads, act, pre_grad = call(
        first_expert_kernel,
        (sums, low, low, low, low),
        (place, received, received_other, expert_in, expert_out,
         jnp.asarray(select, BF16), back_select),
        scratch=(pltpu.VMEM((2, 320, D), BF16),),
        scalars=1, limit=24, flops=4_000_000_000, moved=14_000_000,
    )
    mine = call(
        second_expert_kernel, sums,
        (place, act, pre_grad, expert_in, expert_out, back_select),
        scratch=(pltpu.VMEM((2, 320, D), BF16),),
        scalars=1, limit=12, flops=1_000_000_000, moved=4_000_000,
    )
    partial = (mine.astype(F32) + swap(theirs, "c").astype(F32)).astype(BF16)
    back = lax.all_to_all(
        jnp.concatenate([partial, partial], axis=0), pair_axis, 0, 0, tiled=True
    )
    rows_own = call(
        tokens_kernel, shape((SEQ, D), BF16), (low_back, high_back, back),
        limit=12, flops=2_000_000_000, moved=3_000_000,
    )
    rows_other = swap(rows_own, "c")
    stretch = np.zeros((D, BUCKETS), np.float32)
    stretch[24 * np.arange(BUCKETS), np.arange(BUCKETS)] = 1
    layer_output, middle_grad, grads, norm_mine, norm_theirs, gain_part = call(
        backward_kernel,
        (shape((SEQ, D), BF16), shape((SEQ, D), F32), shape((D, GRADS), BF16),
         shape((256, D), BF16), shape((256, D), BF16), shape((8, D), F32)),
        (place, table, layer_input, middle, mixed, probs, route, out_grad,
         rows_own, rows_other, router, gain_two, output_weight, context, queries, keys,
         values, normed, lse, tiles, wq, wk, wv, jnp.asarray(stretch, BF16)),
        scratch=(pltpu.VMEM((SEQ, D), BF16), pltpu.VMEM((SEQ, 128), BF16),
                 pltpu.VMEM((SEQ, D), BF16)),
        scalars=1, limit=24, flops=4_000_000_000, moved=12_000_000,
    )
    gain_pair = jnp.concatenate([gain_part, swap(gain_part, "c")], axis=0)
    halved = (norm_mine.astype(F32) + swap(norm_theirs, "c").astype(F32)).astype(BF16)
    scattered = lax.all_to_all(grads, experts_axis, 0, 0, tiled=True)
    gain_link, halved_link = lax.optimization_barrier(
        (swap(gain_pair, "l"), swap(halved, "l"))
    )
    halved = (halved.astype(F32) + halved_link.astype(F32)).astype(BF16)
    halved_other = swap(halved, "c")
    spread = call(
        reduce_kernel, shape((D, GRADS), BF16),
        (scattered, gain_pair, gain_link),
        limit=12, flops=10_000_000, moved=3_000_000,
    )
    spread, slots, slot_grads, act, pre_grad = lax.optimization_barrier(
        (spread, slots, slot_grads, act, pre_grad)
    )
    expert_in_grad, expert_out_grad = expert_grads(slots, slot_grads, act, pre_grad)
    gathered = lax.all_to_all(spread, experts_axis, 0, 0, tiled=True)
    input_grad = call(
        input_kernel, shape((SEQ, D), F32),
        (place, halved, halved_other, layer_input, gain_one, middle_grad),
        alias={5: 0}, scalars=1, limit=12, flops=10_000_000, moved=5_000_000,
    )
    out = shape((WIDTH, D), F32)
    line = shape((D,), F32)
    gain_one_grad, gain_two_grad, bias_grad, query_grad, key_grad, value_grad, output_grad, \
        router_grad = call(
            finish_kernel,
            (line, line, shape((HEADS_HERE, BUCKETS), F32), out, out, out, out,
             shape((EXPERTS, D), F32)),
            (gathered, jnp.asarray(stretch, BF16)),
            limit=12, flops=10_000_000, moved=6_000_000,
        )
    return (
        layer_output,
        input_grad,
        gain_one_grad,
        jnp.transpose(query_grad),
        jnp.transpose(key_grad),
        jnp.transpose(value_grad),
        output_grad,
        jnp.transpose(bias_grad),
        gain_two_grad,
        jnp.transpose(router_grad),
        expert_in_grad,
        expert_out_grad,
    )


def solution(mesh):
    fine = Mesh(mesh.devices.reshape(4, 4, 2, 2, 2), ("z", "x", "h", "l", "c"))
    ex = ("z", "x", "h")
    te = ("l", "c")
    in_specs = (
        P(ex, None), P(), P(None, te), P(None, te), P(None, te), P(te, None), P(None, te), P(),
        P(), P(ex, None, te), P(ex, te, None), P(ex), P(ex), P(ex), P(ex, None),
    )
    out_specs = (
        P(ex, None), P(ex, None), P(), P(None, te), P(None, te), P(None, te), P(te, None),
        P(None, te), P(), P(), P(ex, None, te), P(ex, te, None),
    )
    return jax.shard_map(shards, mesh=fine, in_specs=in_specs, out_specs=out_specs, check_vma=False)
```

```python
import jax
import jax.numpy as jnp
import numpy as np
from jax import lax
from jax.experimental import pallas as pl
from jax.experimental.pallas import tpu as pltpu
from jax.sharding import Mesh
from jax.sharding import PartitionSpec as P

BUCKETS = 32
EPS = 1e-06
SEQ = 512
D = 768
HEAD = 64
HEADS_HERE = 3
WIDTH = HEADS_HERE * HEAD
EXPERTS = 64
CAP = 10
GROUPS = 32
CHUNK = 40
ROWS = GROUPS * CHUNK
HALF = D // 2
GRADS = 896
F32 = jnp.float32
BF16 = jnp.bfloat16
GELU_C = float(np.sqrt(2.0 / np.pi))


def bucket_of(offsets):
    half_count = BUCKETS // 2
    exact_count = half_count // 2
    upper_side = (offsets > 0).astype(np.int64) * half_count
    distance = np.abs(offsets)
    ratio = np.log(np.maximum(distance, 1) / exact_count) / np.log(128.0 / exact_count)
    far_bucket = np.minimum(
        exact_count + (ratio * (half_count - exact_count)).astype(np.int64), half_count - 1
    )
    return upper_side + np.where(distance < exact_count, distance, far_bucket)


FAR_STARTS = [
    int(np.argmax(bucket_of(-np.arange(256)) >= b)) for b in range(9, BUCKETS // 2)
]


def line_buckets(block, rows):
    offset = 128 * block + 128 - lax.broadcasted_iota(jnp.int32, (rows, 256), 1)
    distance = jnp.abs(offset)
    far = jnp.full((rows, 256), 8, jnp.int32)
    for start in FAR_STARTS:
        far = far + (distance >= start).astype(jnp.int32)
    bucket = jnp.where(distance < 8, distance, far)
    return jnp.where(offset > 0, bucket + BUCKETS // 2, bucket)


def regroup_matrix():
    sel = np.zeros((320, 320), np.float32)
    for g in range(8):
        for half in range(2):
            for e in range(2):
                for c in range(CAP):
                    sel[half * 160 + e * 80 + g * 10 + c, g * 40 + half * 20 + e * 10 + c] = 1
    return sel


def dot(a, b):
    return jnp.dot(a, b, preferred_element_type=F32)


def dot_nt(a, b):
    return lax.dot_general(a, b, (((1,), (1,)), ((), ())), preferred_element_type=F32)


def dot_tn(a, b):
    return lax.dot_general(a, b, (((0,), (0,)), ((), ())), preferred_element_type=F32)


def head_mask(head, rows):
    lanes = lax.broadcasted_iota(jnp.int32, (rows, WIDTH), 1)
    return (lanes >= head * HEAD) & (lanes < (head + 1) * HEAD)


def only_head(matrix, head):
    return jnp.where(head_mask(head, matrix.shape[0]), matrix, jnp.zeros_like(matrix))


def call(
    body, out_shape, args, scratch=(), scalars=0, far=(), far_out=(), alias=None, limit=40, flops=0, moved=0
):
    spaces = [pltpu.SMEM] * scalars + [pltpu.VMEM] * (len(args) - scalars)
    for i in far:
        spaces[i] = pltpu.HBM
    outs = out_shape if isinstance(out_shape, tuple) else (out_shape,)
    out_spaces = [pltpu.HBM if i in far_out else pltpu.VMEM for i in range(len(outs))]
    result = pl.pallas_call(
        body,
        out_shape=outs,
        in_specs=[pl.BlockSpec(memory_space=space) for space in spaces],
        out_specs=tuple(pl.BlockSpec(memory_space=space) for space in out_spaces),
        scratch_shapes=scratch,
        input_output_aliases=alias or {},
        compiler_params=pltpu.CompilerParams(vmem_limit_bytes=limit << 20),
        cost_estimate=pl.CostEstimate(flops=flops, bytes_accessed=moved, transcendentals=0),
    )(*args)
    return result if isinstance(out_shape, tuple) else result[0]


def shape(dims, dtype):
    return jax.ShapeDtypeStruct(dims, dtype)


def bias_tile(tiles_ref, far_low, far_high, head, block):
    if block < -1:
        return far_low
    if block > 1:
        return far_high
    return tiles_ref[head * 3 + block + 1]


def scores_t(keys, query_scaled, tiles_ref, table, head, part):
    raw = dot_nt(keys, query_scaled)
    far_low = table[head : head + 1, BUCKETS // 2 - 1 : BUCKETS // 2]
    far_high = table[head : head + 1, BUCKETS - 1 : BUCKETS]
    rows = []
    for key_block in range(4):
        cols = []
        for i in range(2):
            piece = raw[key_block * 128 : key_block * 128 + 128, i * 128 : i * 128 + 128]
            block = key_block - (part * 2 + i)
            cols.append(piece + bias_tile(tiles_ref, far_low, far_high, head, block))
        rows.append(jnp.concatenate(cols, axis=1))
    return jnp.concatenate(rows, axis=0)


def attention_forward(
    table_hbm, x_hbm, gain_hbm, wq_hbm, wk_hbm, wv_hbm,
    normed_hbm, q_hbm, k_hbm, v_hbm, tiles_hbm, ctx_ref, lse_ref,
    table_ref, x_ref, gain_ref, wq_ref, wk_ref, wv_ref, normed_ref, q_ref, k_ref, v_ref,
    tiles_ref, sems,
):
    loads = [
        pltpu.make_async_copy(src, dst, sems.at[i])
        for i, (src, dst) in enumerate(
            (
                (table_hbm, table_ref), (x_hbm, x_ref), (wq_hbm, wq_ref), (wk_hbm, wk_ref),
                (wv_hbm, wv_ref), (gain_hbm, gain_ref),
            )
        )
    ]
    for load in loads:
        load.start()
    stores = []

    def store(src, dst):
        copy = pltpu.make_async_copy(src, dst, sems.at[6 + len(stores)])
        copy.start()
        stores.append(copy)

    loads[0].wait()
    table = table_ref[...]
    lines = []
    for block in (-1, 0, 1):
        buckets = lax.broadcasted_iota(jnp.int32, (BUCKETS, 256), 0)
        hot = (buckets == line_buckets(block, 1)).astype(F32)
        lines.append(
            jnp.dot(table, hot, precision=lax.Precision.HIGHEST, preferred_element_type=F32)
        )
    for head in range(HEADS_HERE):
        for block in range(3):
            wide = pltpu.roll(
                jnp.broadcast_to(lines[block][head : head + 1], (128, 256)),
                0, 1, stride=1, stride_axis=0,
            )
            tiles_ref[head * 3 + block] = wide[:, 128:]
    store(tiles_ref, tiles_hbm)
    loads[1].wait()
    loads[5].wait()
    gain = gain_ref[...].reshape(1, D)
    for i in range(4):
        rows = pl.ds(i * 128, 128)
        x = x_ref[rows, :].astype(F32)
        scale = lax.rsqrt(jnp.mean(x * x, axis=-1, keepdims=True) + EPS)
        normed_ref[rows, :] = (x * scale * gain).astype(BF16)
    store(normed_ref, normed_hbm)
    normed = normed_ref[...]
    for load, weight, out, out_hbm in (
        (loads[2], wq_ref, q_ref, q_hbm),
        (loads[3], wk_ref, k_ref, k_hbm),
        (loads[4], wv_ref, v_ref, v_hbm),
    ):
        load.wait()
        out[...] = dot_nt(normed, weight[...]).astype(BF16)
        store(out, out_hbm)
    queries, keys, values = q_ref[...], k_ref[...], v_ref[...]
    lse_ref[...] = jnp.zeros((8, SEQ), F32)
    scaled = queries * jnp.asarray(HEAD**-0.5, BF16)
    for part in range(2):
        rows = slice(part * 256, part * 256 + 256)
        context = jnp.zeros((256, WIDTH), F32)
        for head in range(HEADS_HERE):
            scores = scores_t(keys, only_head(scaled[rows], head), tiles_ref, table, head, part)
            top = jnp.max(scores, axis=0, keepdims=True)
            grown = jnp.exp(scores - top)
            total = jnp.sum(grown, axis=0, keepdims=True)
            probs = (grown * (1.0 / total)).astype(BF16)
            lse_ref[head : head + 1, rows] = top + jnp.log(total)
            context = context + dot_tn(probs, only_head(values, head))
        ctx_ref[rows, :] = context.astype(BF16)
    for copy in stores:
        copy.wait()


def route_columns(route_ref):
    return jnp.transpose(route_ref[...].astype(F32))


def row_of(expert, slot, drop):
    row = (expert >> 1) * CHUNK + (expert & 1) * CAP + slot
    return jnp.where(drop > 0, -1000, row)


def near_kernel(
    place_ref, route_ref, ctx0, ctx1, wo0, wo1, grad_ref, low_ref, high_ref, base_ref, raw_ref
):
    target = row_of(route_ref[0:1, :], route_ref[1:2, :], route_ref[2:3, :])
    for i in range(4):
        rows = pl.ds(i * 320, 320)
        index = lax.broadcasted_iota(jnp.int32, (320, SEQ), 0) + 320 * i
        low = (index == target).astype(F32).astype(BF16)
        high = (index == target + 20).astype(F32).astype(BF16)
        low_ref[rows, :] = low
        high_ref[rows, :] = high
        raw = dot(low, grad_ref[:, :HALF]) + dot(high, grad_ref[:, HALF:])
        raw_ref[rows, :] = raw.astype(BF16)
    pair_of_heads(place_ref[1], ctx0, ctx1, wo0, wo1, base_ref)


def pair_of_heads(core, ctx0, ctx1, wo0, wo1, sum_ref):
    @pl.when(core == 0)
    def _():
        sum_ref[...] = dot(ctx0[...], wo0[...]) + dot(ctx1[...], wo1[...])

    @pl.when(core == 1)
    def _():
        sum_ref[...] = dot(ctx1[...], wo1[...]) + dot(ctx0[...], wo0[...])


def back_place_kernel(route_ref, low_ref, high_ref):
    columns = route_columns(route_ref).astype(jnp.int32)
    target = row_of(columns[:, 0:1], columns[:, 1:2], columns[:, 2:3])
    for i in range(4):
        rows = slice(i * 128, i * 128 + 128)
        index = lax.broadcasted_iota(jnp.int32, (128, ROWS), 1)
        low_ref[rows, :] = (index == target[rows]).astype(F32).astype(BF16)
        high_ref[rows, :] = (index == target[rows] + 20).astype(F32).astype(BF16)


def middle_kernel(
    place_ref, x_ref, base_ref, ctx2, ctx3, wo2, wo3, gain_ref, router_ref, route_ref,
    low_ref, high_ref, raw_ref, middle_ref, mixed_ref, probs_ref, send_ref, far_s, gate_s,
):
    core = place_ref[1]
    columns = route_columns(route_ref)
    pair_of_heads(core, ctx2, ctx3, wo2, wo3, far_s)
    for i in range(4):
        rows = slice(i * 128, i * 128 + 128)
        middle = x_ref[rows, :].astype(F32) + (base_ref[rows, :] + far_s[rows, :])
        scale = lax.rsqrt(jnp.mean(middle * middle, axis=-1, keepdims=True) + EPS)
        mixed = (middle * scale * gain_ref[...]).astype(BF16)
        middle_ref[rows, :] = middle
        mixed_ref[rows, :] = mixed
        lanes = lax.broadcasted_iota(jnp.int32, (128, 128), 1)
        logits = jnp.where(lanes < EXPERTS, dot_nt(mixed, router_ref[...]), -jnp.inf)
        grown = jnp.exp(logits - jnp.max(logits, axis=-1, keepdims=True))
        probs = grown / jnp.sum(grown, axis=-1, keepdims=True)
        probs_ref[rows, :] = probs
        expert = columns[rows, 0:1].astype(jnp.int32)
        chosen = jnp.sum(jnp.where(lanes == expert, probs, 0.0), axis=-1, keepdims=True)
        gate = chosen * (1.0 - columns[rows, 2:3])
        first = gate.astype(BF16).astype(F32)
        second = (gate - first).astype(BF16).astype(F32)
        third = gate - first - second
        pieces = jnp.where(lanes == 0, first, jnp.where(lanes == 1, second, third))
        gate_s[rows, :] = jnp.where(lanes < 3, pieces, 0.0).astype(BF16)

    @pl.when(core == 0)
    def _():
        for i in range(4):
            rows = pl.ds(i * 320, 320)
            out = dot(low_ref[rows, :], mixed_ref[:, :HALF])
            out = out + dot(high_ref[rows, :], mixed_ref[:, HALF:])
            send_ref[rows, :] = out.astype(BF16)

    @pl.when(core == 1)
    def _():
        for i in range(4):
            rows = pl.ds(i * 320, 320)
            gate = dot(low_ref[rows, :], gate_s[...]) + dot(high_ref[rows, :], gate_s[...])
            gate = jnp.sum(gate, axis=-1, keepdims=True)
            send_ref[rows, :] = (raw_ref[rows, :].astype(F32) * gate).astype(BF16)


def first_expert_kernel(
    place_ref, own_ref, other_ref, in_ref, out_ref, sel_ref, back_ref,
    theirs_ref, x_ref, s_ref, act_ref, pre_ref, part_s,
):
    core = place_ref[1]
    for b in range(4):
        rows = pl.ds(b * 320, 320)
        own = own_ref[rows, :]
        other = other_ref[rows, :]
        for dest, block in (
            (x_ref, jnp.where(core == 0, own, other)),
            (s_ref, jnp.where(core == 0, other, own)),
        ):
            sorted_rows = dot(sel_ref[...], block).astype(BF16)
            for half in range(2):
                for e in range(2):
                    dest[e, pl.ds(b * 80, 80), pl.ds(half * HALF, HALF)] = sorted_rows[
                        half * 160 + e * 80 : half * 160 + e * 80 + 80
                    ]
    for e in range(2):
        x = x_ref[e]
        s = s_ref[e]
        for f in range(3):
            cols = slice(f * 256, f * 256 + 256)
            pre = dot(x, in_ref[e, :, cols])
            bent = jnp.tanh(GELU_C * (pre + 0.044715 * (pre * pre * pre)))
            cdf = 0.5 * (1.0 + bent)
            act_ref[e, :, cols] = (pre * cdf).astype(BF16)
            slope = cdf + (0.5 * GELU_C) * pre * (1.0 - bent * bent) * (
                1.0 + (3 * 0.044715) * (pre * pre)
            )
            act_grad = dot_nt(s, out_ref[e, cols, :])
            pre_ref[e, :, cols] = (act_grad * slope).astype(BF16)
    expert_sums(core == 1, act_ref, pre_ref, in_ref, out_ref, back_ref, theirs_ref, part_s)


def expert_sums(forward, act_ref, pre_ref, in_ref, out_ref, back_ref, sum_ref, part_s):
    @pl.when(forward)
    def _():
        for e in range(2):
            part_s[e] = dot(act_ref[e], out_ref[e]).astype(BF16)

    @pl.when(jnp.logical_not(forward))
    def _():
        for e in range(2):
            part_s[e] = dot_nt(pre_ref[e], in_ref[e]).astype(BF16)

    for b in range(4):
        rows = pl.ds(b * 80, 80)
        stacked = jnp.concatenate(
            [part_s[e, rows, pl.ds(half * HALF, HALF)] for half in range(2) for e in range(2)],
            axis=0,
        )
        sum_ref[pl.ds(b * 320, 320), :] = dot(back_ref[...], stacked).astype(BF16)


def second_expert_kernel(
    place_ref, act_ref, pre_ref, in_ref, out_ref, back_ref, mine_ref, part_s
):
    expert_sums(
        place_ref[1] == 0, act_ref, pre_ref, in_ref, out_ref, back_ref, mine_ref, part_s
    )


def expert_grads_kernel(x_ref, s_ref, act_ref, pre_ref, in_grad_ref, out_grad_ref):
    out_grad_ref[0] = dot_tn(act_ref[0], s_ref[0])
    in_grad_ref[0] = dot_tn(x_ref[0], pre_ref[0])


def expert_grads(x, s, act, pre):
    whole = pl.BlockSpec((1, 320, D), lambda e, f: (e, 0, 0))
    part = pl.BlockSpec((1, 320, 256), lambda e, f: (e, 0, f))
    return pl.pallas_call(
        expert_grads_kernel,
        grid=(2, 3),
        out_shape=(shape((2, D, D), F32), shape((2, D, D), F32)),
        in_specs=[whole, whole, part, part],
        out_specs=(
            pl.BlockSpec((1, D, 256), lambda e, f: (e, 0, f)),
            pl.BlockSpec((1, 256, D), lambda e, f: (e, f, 0)),
        ),
        compiler_params=pltpu.CompilerParams(vmem_limit_bytes=24 << 20),
        cost_estimate=pl.CostEstimate(
            flops=8 * 320 * D * D, bytes_accessed=14_000_000, transcendentals=0
        ),
    )(x, s, act, pre)


def tokens_kernel(low_ref, high_ref, recv_ref, out_ref):
    slots = (
        recv_ref[pl.ds(0, ROWS), :].astype(F32) + recv_ref[pl.ds(ROWS, ROWS), :].astype(F32)
    ).astype(BF16)
    out_ref[:, pl.ds(0, HALF)] = dot(low_ref[...], slots).astype(BF16)
    out_ref[:, pl.ds(HALF, HALF)] = dot(high_ref[...], slots).astype(BF16)


def backward_kernel(
    place_ref, table_ref, middle_ref, mixed_ref, probs_ref, route_ref, grad_ref,
    own_ref, other_ref, router_ref, gain_ref, wo_ref, ctx_ref, q_ref, k_ref, v_ref, normed_ref,
    lse_ref, tiles_ref, stretch_ref,
    output_ref, middle_grad_ref, grads_ref, query_out, key_out, value_out, low_s, logit_s,
):
    core = place_ref[1]
    columns = route_columns(route_ref)
    gain = gain_ref[...]
    gain_grad = jnp.zeros((1, D), F32)
    for i in range(4):
        rows = slice(i * 128, i * 128 + 128)
        own = own_ref[rows, :]
        other = other_ref[rows, :]
        expert_rows = jnp.where(core == 0, own, other).astype(F32)
        mixed_grad = jnp.where(core == 0, other, own).astype(F32)
        probs = probs_ref[rows, :]
        kept = 1.0 - columns[rows, 2:3]
        lanes = lax.broadcasted_iota(jnp.int32, (128, 128), 1)
        hot = (lanes == columns[rows, 0:1].astype(jnp.int32)).astype(F32)
        chosen = jnp.sum(probs * hot, axis=-1, keepdims=True)
        middle = middle_ref[rows, :]
        upstream = grad_ref[rows, :].astype(F32)
        output_ref[rows, :] = (middle + (chosen * kept) * expert_rows).astype(BF16)
        gate_grad = jnp.sum(upstream * expert_rows, axis=-1, keepdims=True) * kept
        logit_grad = (probs * (hot - chosen) * gate_grad).astype(BF16)
        logit_s[rows, :] = logit_grad
        mixed_grad = mixed_grad + dot(logit_grad, router_ref[...])
        scale = lax.rsqrt(jnp.mean(middle * middle, axis=-1, keepdims=True) + EPS)
        weighted = mixed_grad * gain
        inner = jnp.mean(weighted * middle, axis=-1, keepdims=True)
        gain_grad = gain_grad + jnp.sum(mixed_grad * middle * scale, axis=0, keepdims=True)
        middle_grad = upstream + scale * weighted - middle * (scale * scale * scale * inner)
        middle_grad_ref[rows, :] = middle_grad
        low_s[rows, :] = middle_grad.astype(BF16)
    middle_low = low_s[...]
    grads_ref[pl.ds(3 * WIDTH, WIDTH), :D] = dot_tn(ctx_ref[...], middle_low).astype(BF16)
    ctx_grad = dot_nt(middle_low, wo_ref[...]).astype(BF16)

    keys = k_ref[...]
    values = v_ref[...]
    key_scaled = keys * jnp.asarray(HEAD**-0.5, BF16)
    query_scaled = q_ref[...] * jnp.asarray(HEAD**-0.5, BF16)
    key_grad = jnp.zeros((SEQ, WIDTH), F32)
    value_grad = jnp.zeros((SEQ, WIDTH), F32)
    query_grads = [jnp.zeros((256, WIDTH), F32), jnp.zeros((256, WIDTH), F32)]
    buckets = lax.broadcasted_iota(jnp.int32, (BUCKETS, 256), 0)
    line_ids = [line_buckets(block, 1) for block in (-1, 0, 1)]
    bias_grad = jnp.zeros((BUCKETS, 128), F32)
    bias_lanes = lax.broadcasted_iota(jnp.int32, (BUCKETS, 128), 1)
    turn = (
        lax.broadcasted_iota(jnp.int32, (128, 128), 0)
        + lax.broadcasted_iota(jnp.int32, (128, 128), 1)
        == 127
    ).astype(F32)
    for head in range(HEADS_HERE):
        near = [jnp.zeros((128, 128), F32) for _ in range(3)]
        far_low = jnp.zeros((128, 128), F32)
        far_high = jnp.zeros((128, 128), F32)
        key_head = only_head(key_scaled, head)
        for part in range(2):
            rows = slice(part * 256, part * 256 + 256)
            query_head = only_head(query_scaled[rows], head)
            ctx_head = only_head(ctx_grad[rows], head)
            scores = scores_t(keys, query_head, tiles_ref, table_ref[...], head, part)
            probs = jnp.exp(scores - lse_ref[head : head + 1, rows])
            value_grad = value_grad + dot(probs.astype(BF16), ctx_head)
            prob_grad = dot_nt(values, ctx_head)
            inner = jnp.sum(probs * prob_grad, axis=0, keepdims=True)
            score_grad = (probs * (prob_grad - inner)).astype(BF16)
            key_grad = key_grad + dot(score_grad, query_head)
            query_grads[part] = query_grads[part] + dot_tn(score_grad, key_head)
            for key_block in range(4):
                for i in range(2):
                    piece = score_grad[
                        key_block * 128 : key_block * 128 + 128, i * 128 : i * 128 + 128
                    ].astype(F32)
                    block = key_block - (part * 2 + i)
                    if block < -1:
                        far_low = far_low + piece
                    elif block > 1:
                        far_high = far_high + piece
                    else:
                        near[block + 1] = near[block + 1] + piece
        by_bucket = jnp.zeros((BUCKETS, 256), F32)
        for block in range(3):
            turned = jnp.dot(
                turn, near[block], precision=lax.Precision.HIGHEST, preferred_element_type=F32
            )
            wide = jnp.concatenate([turned, jnp.zeros((128, 128), F32)], axis=1)
            wide = pltpu.roll(wide, 1, 1, stride=1, stride_axis=0)
            line = jnp.sum(wide, axis=0, keepdims=True)
            by_bucket = by_bucket + jnp.where(
                buckets == line_ids[block], line, 0.0
            )
        side = lax.broadcasted_iota(jnp.int32, (BUCKETS, 128), 0)
        low_line = jnp.sum(far_low, axis=0, keepdims=True)
        high_line = jnp.sum(far_high, axis=0, keepdims=True)
        ends = jnp.where(side == BUCKETS // 2 - 1, low_line, 0.0) + jnp.where(
            side == BUCKETS - 1, high_line, 0.0
        )
        by_bucket = by_bucket[:, :128] + by_bucket[:, 128:] + ends
        total = jnp.sum(by_bucket, axis=1, keepdims=True)
        bias_grad = bias_grad + jnp.where(bias_lanes == EXPERTS + 1 + head, total, 0.0)
    query_low = jnp.concatenate(query_grads, axis=0).astype(BF16)
    key_low = key_grad.astype(BF16)
    value_low = value_grad.astype(BF16)
    normed = normed_ref[...]
    for i, low in enumerate((query_low, key_low, value_low)):
        grads_ref[pl.ds(i * WIDTH, WIDTH), :D] = dot_tn(low, normed).astype(BF16)
    rest = dot_tn(mixed_ref[...], logit_s[...]) + dot(stretch_ref[...], bias_grad.astype(BF16))
    column = jnp.transpose(jnp.broadcast_to(gain_grad, (128, D)))
    lanes = lax.broadcasted_iota(jnp.int32, (D, 128), 1)
    grads_ref[:, D:] = jnp.where(lanes == EXPERTS, column, rest).astype(BF16)
    query_out[...] = query_low
    key_out[...] = key_low
    value_out[...] = value_low


def normed_kernel(
    place_ref, x_ref, q_ref, k_ref, v_ref, wq_ref, wk_ref, wv_ref,
    mine_ref, theirs_ref, gain_one_ref, normed_s,
):
    core = place_ref[1]
    gain_one = jnp.zeros((1, D), F32)
    for i in range(4):
        rows = slice(i * 128, i * 128 + 128)
        normed_part = (
            dot(q_ref[rows, :], wq_ref[...])
            + dot(k_ref[rows, :], wk_ref[...])
            + dot(v_ref[rows, :], wv_ref[...])
        )
        normed_s[rows, :] = normed_part.astype(BF16)
        hidden = x_ref[rows, :].astype(F32)
        scale = lax.rsqrt(jnp.mean(hidden * hidden, axis=-1, keepdims=True) + EPS)
        gain_one = gain_one + jnp.sum(normed_part * hidden * scale, axis=0, keepdims=True)
    gain_one_ref[...] = jnp.broadcast_to(gain_one, (8, D))
    mine_ref[...] = normed_s[pl.ds(pl.multiple_of(core * 256, 256), 256), :]
    theirs_ref[...] = normed_s[pl.ds(pl.multiple_of((1 - core) * 256, 256), 256), :]


def halves(core, own_ref, other_ref, i):
    local = slice((i % 2) * 128, (i % 2) * 128 + 128)
    return jnp.where(core == i // 2, own_ref[local, :], other_ref[local, :]).astype(F32)


def reduce_kernel(parts_ref, pair_ref, link_ref, send_ref):
    gain_grad = (pair_ref[0:1] + pair_ref[8:9]) + (link_ref[0:1] + link_ref[8:9])
    total = jnp.zeros((24, GRADS), F32)
    for j in range(GROUPS // 2):
        pair = parts_ref[pl.ds(j * 48, 48), :].astype(F32)
        total = total + pair[:24] + pair[24:]
    lines = [
        pltpu.roll(gain_grad[:, r // 4 * 128 : r // 4 * 128 + 128], (96 - r % 4 * 32) % 128, 1)
        for r in range(24)
    ]
    lanes = lax.broadcasted_iota(jnp.int32, (24, 128), 1)
    last = jnp.where(lanes < 96, total[:, D:], jnp.concatenate(lines, axis=0))
    chunk = jnp.concatenate([total[:, :D], last], axis=1)
    pair = jnp.concatenate([chunk, chunk], axis=0).astype(BF16)
    for j in range(GROUPS // 2):
        send_ref[pl.ds(j * 48, 48), :] = pair


def input_kernel(place_ref, own_ref, other_ref, x_ref, gain_ref, middle_grad_ref, input_ref):
    core = place_ref[1]
    gain = gain_ref[...]
    for i in range(4):
        rows = slice(i * 128, i * 128 + 128)
        hidden = x_ref[rows, :].astype(F32)
        scale = lax.rsqrt(jnp.mean(hidden * hidden, axis=-1, keepdims=True) + EPS)
        weighted = halves(core, own_ref, other_ref, i) * gain
        inner = jnp.mean(weighted * hidden, axis=-1, keepdims=True)
        input_ref[rows, :] = (
            middle_grad_ref[rows, :]
            + scale * weighted
            - hidden * (scale * scale * scale * inner)
        )


def finish_kernel(
    recv_ref, stretch_ref, gain_one_ref, gain_two_ref, bias_ref,
    q_ref, k_ref, v_ref, o_ref, router_ref,
):
    for i, out in enumerate((q_ref, k_ref, v_ref, o_ref)):
        out[...] = recv_ref[pl.ds(i * WIDTH, WIDTH), :D].astype(F32)
    last = recv_ref[:, D:].astype(F32)
    summed = jnp.zeros((24, 128), F32)
    for j in range(GROUPS):
        summed = summed + last[j * 24 : j * 24 + 24]
    lanes = lax.broadcasted_iota(jnp.int32, (1, 128), 1)
    for block in range(6):
        line = jnp.zeros((1, 128), F32)
        for i in range(4):
            r = block * 4 + i
            piece = pltpu.roll(summed[r : r + 1], (32 + 32 * i) % 128, 1)
            line = jnp.where((lanes >= 32 * i) & (lanes < 32 * i + 32), piece, line)
        gain_one_ref[pl.ds(block * 128, 128)] = line[0]
    turned = jnp.transpose(last)
    router_ref[...] = turned[:EXPERTS]
    tail = turned[EXPERTS : EXPERTS + 8]
    gain_two_ref[...] = tail[0]
    bias_ref[...] = dot(tail.astype(BF16), stretch_ref[...])[1 : 1 + HEADS_HERE]


def shards(
    layer_input, attn_gain, query_weight, key_weight, value_weight, output_weight, position_bias,
    moe_gain, router_weight, expert_in, expert_out, route_expert, route_slot, route_drop, out_grad,
):
    experts_axis = ("z", "x", "h")
    pair_axis = ("l", "z", "x", "h")
    core = lax.axis_index("c")
    place = jnp.stack([lax.axis_index("l") * 2 + core, core]).astype(jnp.int32)

    def swap(array, axis):
        return lax.ppermute(array, axis, [(0, 1), (1, 0)])

    gain_one = attn_gain.reshape(1, D)
    gain_two = moe_gain.reshape(1, D)
    zeros = jnp.zeros_like(route_drop)
    route = jnp.stack([route_expert, route_slot, route_drop] + [zeros] * 5)
    table = jnp.transpose(position_bias)
    wq, wk, wv = (jnp.transpose(w) for w in (query_weight, key_weight, value_weight))
    router = jnp.pad(jnp.transpose(router_weight), ((0, 128 - EXPERTS), (0, 0)))
    wo_link = swap(output_weight, "l")
    wo_core = swap(output_weight, "c")
    wo_far = swap(wo_link, "c")

    tall = shape((SEQ, WIDTH), BF16)
    wide = shape((SEQ, D), BF16)
    tile_shape = (3 * HEADS_HERE, 128, 128)
    weight_vmem = pltpu.VMEM((WIDTH, D), BF16)
    tall_vmem = pltpu.VMEM((SEQ, WIDTH), BF16)
    normed, queries, keys, values, tiles, context, lse = call(
        attention_forward,
        (wide, tall, tall, tall, shape(tile_shape, F32), tall, shape((8, SEQ), F32)),
        (table, layer_input, attn_gain, wq, wk, wv),
        far=(0, 1, 2, 3, 4, 5), far_out=(0, 1, 2, 3, 4),
        scratch=(pltpu.VMEM((HEADS_HERE, BUCKETS), F32), pltpu.VMEM((SEQ, D), BF16),
                 pltpu.VMEM((D,), F32), weight_vmem, weight_vmem, weight_vmem, pltpu.VMEM((SEQ, D), BF16),
                 tall_vmem, tall_vmem, tall_vmem, pltpu.VMEM(tile_shape, F32),
                 pltpu.SemaphoreType.DMA((11,))),
        limit=60, flops=900_000_000, moved=5_000_000,
    )
    flat, flat_t = shape((ROWS, SEQ), BF16), shape((SEQ, ROWS), BF16)
    sums = shape((ROWS, HALF), BF16)
    ctx_link = swap(context, "l")
    ctx_core = swap(context, "c")
    low_place, high_place, base, raw = call(
        near_kernel, (flat, flat, shape((SEQ, D), F32), sums),
        (place, route, context, ctx_core, output_weight, wo_core, out_grad),
        scalars=1, limit=16, flops=1_500_000_000, moved=7_000_000,
    )
    ctx_link_late, low_place = lax.optimization_barrier((ctx_link, low_place))
    ctx_far = swap(ctx_link_late, "c")
    middle, mixed, probs, send = call(
        middle_kernel,
        (shape((SEQ, D), F32), wide, shape((SEQ, 128), F32), sums),
        (place, layer_input, base, ctx_link, ctx_far, wo_link, wo_far, gain_two, router, route,
         low_place, high_place, raw),
        scratch=(pltpu.VMEM((SEQ, D), F32), pltpu.VMEM((SEQ, 128), BF16)),
        scalars=1, limit=16, flops=1_700_000_000, moved=8_000_000,
    )
    received = lax.all_to_all(send, experts_axis, 0, 0, tiled=True)
    received, route_late = lax.optimization_barrier((received, route))
    low_back, high_back = call(
        back_place_kernel, (flat_t, flat_t), (route_late,),
        limit=12, flops=10_000_000, moved=2_700_000,
    )
    received_other, low_back, high_back = lax.optimization_barrier(
        (swap(received, "c"), low_back, high_back)
    )
    select = regroup_matrix()
    low = shape((2, 320, D), BF16)
    back_select = jnp.asarray(select.T, BF16)
    theirs, slots, slot_grads, act, pre_grad = call(
        first_expert_kernel,
        (sums, low, low, low, low),
        (place, received, received_other, expert_in, expert_out,
         jnp.asarray(select, BF16), back_select),
        scratch=(pltpu.VMEM((2, 320, D), BF16),),
        scalars=1, limit=24, flops=4_000_000_000, moved=14_000_000,
    )
    mine = call(
        second_expert_kernel, sums,
        (place, act, pre_grad, expert_in, expert_out, back_select),
        scratch=(pltpu.VMEM((2, 320, D), BF16),),
        scalars=1, limit=12, flops=1_000_000_000, moved=4_000_000,
    )
    partial = (mine.astype(F32) + swap(theirs, "c").astype(F32)).astype(BF16)
    back = lax.all_to_all(
        jnp.concatenate([partial, partial], axis=0), pair_axis, 0, 0, tiled=True
    )
    rows_own = call(
        tokens_kernel, shape((SEQ, D), BF16), (low_back, high_back, back),
        limit=12, flops=2_000_000_000, moved=3_000_000,
    )
    rows_other = swap(rows_own, "c")
    stretch = np.zeros((D, BUCKETS), np.float32)
    stretch[24 * np.arange(BUCKETS), np.arange(BUCKETS)] = 1
    layer_output, middle_grad, grads, query_low, key_low, value_low = call(
        backward_kernel,
        (wide, shape((SEQ, D), F32), shape((D, GRADS), BF16), tall, tall, tall),
        (place, table, middle, mixed, probs, route, out_grad,
         rows_own, rows_other, router, gain_two, output_weight, context, queries, keys,
         values, normed, lse, tiles, jnp.asarray(stretch, BF16)),
        scratch=(pltpu.VMEM((SEQ, D), BF16), pltpu.VMEM((SEQ, 128), BF16)),
        scalars=1, limit=24, flops=4_000_000_000, moved=12_000_000,
    )
    half = shape((256, D), BF16)
    norm_mine, norm_theirs, gain_part = call(
        normed_kernel, (half, half, shape((8, D), F32)),
        (place, layer_input, query_low, key_low, value_low, wq, wk, wv),
        scratch=(pltpu.VMEM((SEQ, D), BF16),),
        scalars=1, limit=12, flops=500_000_000, moved=3_500_000,
    )
    gain_pair = jnp.concatenate([gain_part, swap(gain_part, "c")], axis=0)
    halved = (norm_mine.astype(F32) + swap(norm_theirs, "c").astype(F32)).astype(BF16)
    scattered = lax.all_to_all(grads, experts_axis, 0, 0, tiled=True)
    gain_link, halved_link = lax.optimization_barrier(
        (swap(gain_pair, "l"), swap(halved, "l"))
    )
    halved = (halved.astype(F32) + halved_link.astype(F32)).astype(BF16)
    halved_other = swap(halved, "c")
    spread = call(
        reduce_kernel, shape((D, GRADS), BF16),
        (scattered, gain_pair, gain_link),
        limit=12, flops=10_000_000, moved=3_000_000,
    )
    spread, slots, slot_grads, act, pre_grad = lax.optimization_barrier(
        (spread, slots, slot_grads, act, pre_grad)
    )
    expert_in_grad, expert_out_grad = expert_grads(slots, slot_grads, act, pre_grad)
    gathered = lax.all_to_all(spread, experts_axis, 0, 0, tiled=True)
    input_grad = call(
        input_kernel, shape((SEQ, D), F32),
        (place, halved, halved_other, layer_input, gain_one, middle_grad),
        alias={5: 0}, scalars=1, limit=12, flops=10_000_000, moved=5_000_000,
    )
    out = shape((WIDTH, D), F32)
    line = shape((D,), F32)
    gain_one_grad, gain_two_grad, bias_grad, query_grad, key_grad, value_grad, output_grad, \
        router_grad = call(
            finish_kernel,
            (line, line, shape((HEADS_HERE, BUCKETS), F32), out, out, out, out,
             shape((EXPERTS, D), F32)),
            (gathered, jnp.asarray(stretch, BF16)),
            limit=12, flops=10_000_000, moved=6_000_000,
        )
    return (
        layer_output,
        input_grad,
        gain_one_grad,
        jnp.transpose(query_grad),
        jnp.transpose(key_grad),
        jnp.transpose(value_grad),
        output_grad,
        jnp.transpose(bias_grad),
        gain_two_grad,
        jnp.transpose(router_grad),
        expert_in_grad,
        expert_out_grad,
    )


def solution(mesh):
    fine = Mesh(mesh.devices.reshape(4, 4, 2, 2, 2), ("z", "x", "h", "l", "c"))
    ex = ("z", "x", "h")
    te = ("l", "c")
    in_specs = (
        P(ex, None), P(), P(None, te), P(None, te), P(None, te), P(te, None), P(None, te), P(),
        P(), P(ex, None, te), P(ex, te, None), P(ex), P(ex), P(ex), P(ex, None),
    )
    out_specs = (
        P(ex, None), P(ex, None), P(), P(None, te), P(None, te), P(None, te), P(te, None),
        P(None, te), P(), P(), P(ex, None, te), P(ex, te, None),
    )
    return jax.shard_map(shards, mesh=fine, in_specs=in_specs, out_specs=out_specs, check_vma=False)
```

```python
import jax
import jax.numpy as jnp
import numpy as np
from jax import lax
from jax.experimental import pallas as pl
from jax.experimental.pallas import tpu as pltpu
from jax.sharding import Mesh
from jax.sharding import PartitionSpec as P

BUCKETS = 32
EPS = 1e-06
SEQ = 512
D = 768
HEAD = 64
HEADS_HERE = 3
WIDTH = HEADS_HERE * HEAD
EXPERTS = 64
CAP = 10
GROUPS = 32
CHUNK = 40
ROWS = GROUPS * CHUNK
HALF = D // 2
GRADS = 896
F32 = jnp.float32
BF16 = jnp.bfloat16
GELU_C = float(np.sqrt(2.0 / np.pi))


def bucket_of(offsets):
    half_count = BUCKETS // 2
    exact_count = half_count // 2
    upper_side = (offsets > 0).astype(np.int64) * half_count
    distance = np.abs(offsets)
    ratio = np.log(np.maximum(distance, 1) / exact_count) / np.log(128.0 / exact_count)
    far_bucket = np.minimum(
        exact_count + (ratio * (half_count - exact_count)).astype(np.int64), half_count - 1
    )
    return upper_side + np.where(distance < exact_count, distance, far_bucket)


FAR_STARTS = [
    int(np.argmax(bucket_of(-np.arange(256)) >= b)) for b in range(9, BUCKETS // 2)
]


def line_buckets(block, rows):
    offset = 128 * block + 128 - lax.broadcasted_iota(jnp.int32, (rows, 256), 1)
    distance = jnp.abs(offset)
    far = jnp.full((rows, 256), 8, jnp.int32)
    for start in FAR_STARTS:
        far = far + (distance >= start).astype(jnp.int32)
    bucket = jnp.where(distance < 8, distance, far)
    return jnp.where(offset > 0, bucket + BUCKETS // 2, bucket)


def regroup_matrix():
    sel = np.zeros((320, 320), np.float32)
    for g in range(8):
        for half in range(2):
            for e in range(2):
                for c in range(CAP):
                    sel[half * 160 + e * 80 + g * 10 + c, g * 40 + half * 20 + e * 10 + c] = 1
    return sel


def dot(a, b):
    return jnp.dot(a, b, preferred_element_type=F32)


def dot_nt(a, b):
    return lax.dot_general(a, b, (((1,), (1,)), ((), ())), preferred_element_type=F32)


def dot_tn(a, b):
    return lax.dot_general(a, b, (((0,), (0,)), ((), ())), preferred_element_type=F32)


def head_mask(head, rows):
    lanes = lax.broadcasted_iota(jnp.int32, (rows, WIDTH), 1)
    return (lanes >= head * HEAD) & (lanes < (head + 1) * HEAD)


def only_head(matrix, head):
    return jnp.where(head_mask(head, matrix.shape[0]), matrix, jnp.zeros_like(matrix))


def call(
    body, out_shape, args, scratch=(), scalars=0, far=(), far_out=(), alias=None, limit=40, flops=0, moved=0
):
    spaces = [pltpu.SMEM] * scalars + [pltpu.VMEM] * (len(args) - scalars)
    for i in far:
        spaces[i] = pltpu.HBM
    outs = out_shape if isinstance(out_shape, tuple) else (out_shape,)
    out_spaces = [pltpu.HBM if i in far_out else pltpu.VMEM for i in range(len(outs))]
    result = pl.pallas_call(
        body,
        out_shape=outs,
        in_specs=[pl.BlockSpec(memory_space=space) for space in spaces],
        out_specs=tuple(pl.BlockSpec(memory_space=space) for space in out_spaces),
        scratch_shapes=scratch,
        input_output_aliases=alias or {},
        compiler_params=pltpu.CompilerParams(vmem_limit_bytes=limit << 20),
        cost_estimate=pl.CostEstimate(flops=flops, bytes_accessed=moved, transcendentals=0),
    )(*args)
    return result if isinstance(out_shape, tuple) else result[0]


def shape(dims, dtype):
    return jax.ShapeDtypeStruct(dims, dtype)


def bias_tile(tiles_ref, far_low, far_high, head, block):
    if block < -1:
        return far_low
    if block > 1:
        return far_high
    return tiles_ref[head * 3 + block + 1]


def scores_t(keys, query_scaled, tiles_ref, table, head, part):
    raw = dot_nt(keys, query_scaled)
    far_low = table[head : head + 1, BUCKETS // 2 - 1 : BUCKETS // 2]
    far_high = table[head : head + 1, BUCKETS - 1 : BUCKETS]
    rows = []
    for key_block in range(4):
        cols = []
        for i in range(2):
            piece = raw[key_block * 128 : key_block * 128 + 128, i * 128 : i * 128 + 128]
            block = key_block - (part * 2 + i)
            cols.append(piece + bias_tile(tiles_ref, far_low, far_high, head, block))
        rows.append(jnp.concatenate(cols, axis=1))
    return jnp.concatenate(rows, axis=0)


def attention_forward(
    table_hbm, x_hbm, gain_hbm, wq_hbm, wk_hbm, wv_hbm,
    normed_hbm, q_hbm, k_hbm, v_hbm, tiles_hbm, ctx_ref, lse_ref,
    table_ref, x_ref, gain_ref, wq_ref, wk_ref, wv_ref, normed_ref, q_ref, k_ref, v_ref,
    tiles_ref, sems,
):
    loads = [
        pltpu.make_async_copy(src, dst, sems.at[i])
        for i, (src, dst) in enumerate(
            (
                (table_hbm, table_ref), (x_hbm, x_ref), (wq_hbm, wq_ref), (wk_hbm, wk_ref),
                (wv_hbm, wv_ref), (gain_hbm, gain_ref),
            )
        )
    ]
    for load in loads:
        load.start()
    stores = []

    def store(src, dst):
        copy = pltpu.make_async_copy(src, dst, sems.at[6 + len(stores)])
        copy.start()
        stores.append(copy)

    loads[0].wait()
    table = table_ref[...]
    lines = []
    for block in (-1, 0, 1):
        buckets = lax.broadcasted_iota(jnp.int32, (BUCKETS, 256), 0)
        hot = (buckets == line_buckets(block, 1)).astype(F32)
        lines.append(
            jnp.dot(table, hot, precision=lax.Precision.HIGHEST, preferred_element_type=F32)
        )
    for head in range(HEADS_HERE):
        for block in range(3):
            wide = pltpu.roll(
                jnp.broadcast_to(lines[block][head : head + 1], (128, 256)),
                0, 1, stride=1, stride_axis=0,
            )
            tiles_ref[head * 3 + block] = wide[:, 128:]
    store(tiles_ref, tiles_hbm)
    loads[1].wait()
    loads[5].wait()
    gain = gain_ref[...].reshape(1, D)
    for i in range(SEQ // 32):
        rows = pl.ds(i * 32, 32)
        x = x_ref[rows, :].astype(F32)
        scale = lax.rsqrt(jnp.mean(x * x, axis=-1, keepdims=True) + EPS)
        normed_ref[rows, :] = (x * scale * gain).astype(BF16)
    store(normed_ref, normed_hbm)
    normed = normed_ref[...]
    for load, weight, out, out_hbm in (
        (loads[2], wq_ref, q_ref, q_hbm),
        (loads[3], wk_ref, k_ref, k_hbm),
        (loads[4], wv_ref, v_ref, v_hbm),
    ):
        load.wait()
        out[...] = dot_nt(normed, weight[...]).astype(BF16)
        store(out, out_hbm)
    queries, keys, values = q_ref[...], k_ref[...], v_ref[...]
    lse_ref[...] = jnp.zeros((8, SEQ), F32)
    scaled = queries * jnp.asarray(HEAD**-0.5, BF16)
    for part in range(2):
        rows = slice(part * 256, part * 256 + 256)
        context = jnp.zeros((256, WIDTH), F32)
        for head in range(HEADS_HERE):
            scores = scores_t(keys, only_head(scaled[rows], head), tiles_ref, table, head, part)
            top = jnp.max(scores, axis=0, keepdims=True)
            grown = jnp.exp(scores - top)
            total = jnp.sum(grown, axis=0, keepdims=True)
            probs = (grown * (1.0 / total)).astype(BF16)
            lse_ref[head : head + 1, rows] = top + jnp.log(total)
            context = context + dot_tn(probs, only_head(values, head))
        ctx_ref[rows, :] = context.astype(BF16)
    for copy in stores:
        copy.wait()


def route_columns(route_ref):
    return jnp.transpose(route_ref[...].astype(F32))


def row_of(expert, slot, drop):
    row = (expert >> 1) * CHUNK + (expert & 1) * CAP + slot
    return jnp.where(drop > 0, -1000, row)


def near_kernel(
    place_ref, route_ref, ctx0, ctx1, wo0, wo1, grad_ref, low_ref, high_ref, base_ref, raw_ref
):
    target = row_of(route_ref[0:1, :], route_ref[1:2, :], route_ref[2:3, :])
    for i in range(4):
        rows = pl.ds(i * 320, 320)
        index = lax.broadcasted_iota(jnp.int32, (320, SEQ), 0) + 320 * i
        low = (index == target).astype(F32).astype(BF16)
        high = (index == target + 20).astype(F32).astype(BF16)
        low_ref[rows, :] = low
        high_ref[rows, :] = high
        raw = dot(low, grad_ref[:, :HALF]) + dot(high, grad_ref[:, HALF:])
        raw_ref[rows, :] = raw.astype(BF16)
    pair_of_heads(place_ref[1], ctx0, ctx1, wo0, wo1, base_ref)


def pair_of_heads(core, ctx0, ctx1, wo0, wo1, sum_ref):
    @pl.when(core == 0)
    def _():
        sum_ref[...] = dot(ctx0[...], wo0[...]) + dot(ctx1[...], wo1[...])

    @pl.when(core == 1)
    def _():
        sum_ref[...] = dot(ctx1[...], wo1[...]) + dot(ctx0[...], wo0[...])


def back_place_kernel(route_ref, low_ref, high_ref):
    columns = route_columns(route_ref).astype(jnp.int32)
    target = row_of(columns[:, 0:1], columns[:, 1:2], columns[:, 2:3])
    for i in range(4):
        rows = slice(i * 128, i * 128 + 128)
        index = lax.broadcasted_iota(jnp.int32, (128, ROWS), 1)
        low_ref[rows, :] = (index == target[rows]).astype(F32).astype(BF16)
        high_ref[rows, :] = (index == target[rows] + 20).astype(F32).astype(BF16)


def middle_kernel(
    place_ref, x_ref, base_ref, ctx2, ctx3, wo2, wo3, gain_ref, router_ref, route_ref,
    low_ref, high_ref, raw_ref, middle_ref, mixed_ref, probs_ref, send_ref, far_s, gate_s,
):
    core = place_ref[1]
    columns = route_columns(route_ref)
    pair_of_heads(core, ctx2, ctx3, wo2, wo3, far_s)
    for i in range(SEQ // 32):
        rows = slice(i * 32, i * 32 + 32)
        middle = x_ref[rows, :].astype(F32) + (base_ref[rows, :] + far_s[rows, :])
        scale = lax.rsqrt(jnp.mean(middle * middle, axis=-1, keepdims=True) + EPS)
        middle_ref[rows, :] = middle
        mixed_ref[rows, :] = (middle * scale * gain_ref[...]).astype(BF16)
    for i in range(4):
        rows = slice(i * 128, i * 128 + 128)
        lanes = lax.broadcasted_iota(jnp.int32, (128, 128), 1)
        logits = dot_nt(mixed_ref[rows, :], router_ref[...])
        logits = jnp.where(lanes < EXPERTS, logits, -jnp.inf)
        grown = jnp.exp(logits - jnp.max(logits, axis=-1, keepdims=True))
        probs = grown / jnp.sum(grown, axis=-1, keepdims=True)
        probs_ref[rows, :] = probs
        expert = columns[rows, 0:1].astype(jnp.int32)
        chosen = jnp.sum(jnp.where(lanes == expert, probs, 0.0), axis=-1, keepdims=True)
        gate = chosen * (1.0 - columns[rows, 2:3])
        first = gate.astype(BF16).astype(F32)
        second = (gate - first).astype(BF16).astype(F32)
        third = gate - first - second
        pieces = jnp.where(lanes == 0, first, jnp.where(lanes == 1, second, third))
        gate_s[rows, :] = jnp.where(lanes < 3, pieces, 0.0).astype(BF16)

    @pl.when(core == 0)
    def _():
        for i in range(4):
            rows = pl.ds(i * 320, 320)
            out = dot(low_ref[rows, :], mixed_ref[:, :HALF])
            out = out + dot(high_ref[rows, :], mixed_ref[:, HALF:])
            send_ref[rows, :] = out.astype(BF16)

    @pl.when(core == 1)
    def _():
        for i in range(4):
            rows = pl.ds(i * 320, 320)
            gate = dot(low_ref[rows, :], gate_s[...]) + dot(high_ref[rows, :], gate_s[...])
            gate = jnp.sum(gate, axis=-1, keepdims=True)
            send_ref[rows, :] = (raw_ref[rows, :].astype(F32) * gate).astype(BF16)


def first_expert_kernel(
    place_ref, own_ref, other_ref, in_ref, out_ref, sel_ref, back_ref,
    theirs_ref, x_ref, s_ref, act_ref, pre_ref, part_s,
):
    core = place_ref[1]
    for b in range(4):
        rows = pl.ds(b * 320, 320)
        own = own_ref[rows, :]
        other = other_ref[rows, :]
        for dest, block in (
            (x_ref, jnp.where(core == 0, own, other)),
            (s_ref, jnp.where(core == 0, other, own)),
        ):
            sorted_rows = dot(sel_ref[...], block).astype(BF16)
            for half in range(2):
                for e in range(2):
                    dest[e, pl.ds(b * 80, 80), pl.ds(half * HALF, HALF)] = sorted_rows[
                        half * 160 + e * 80 : half * 160 + e * 80 + 80
                    ]
    for e in range(2):
        x = x_ref[e]
        s = s_ref[e]
        for f in range(3):
            cols = slice(f * 256, f * 256 + 256)
            pre = dot(x, in_ref[e, :, cols])
            bent = jnp.tanh(GELU_C * (pre + 0.044715 * (pre * pre * pre)))
            cdf = 0.5 * (1.0 + bent)
            act_ref[e, :, cols] = (pre * cdf).astype(BF16)
            slope = cdf + (0.5 * GELU_C) * pre * (1.0 - bent * bent) * (
                1.0 + (3 * 0.044715) * (pre * pre)
            )
            act_grad = dot_nt(s, out_ref[e, cols, :])
            pre_ref[e, :, cols] = (act_grad * slope).astype(BF16)
    expert_sums(core == 1, act_ref, pre_ref, in_ref, out_ref, back_ref, theirs_ref, part_s)


def expert_sums(forward, act_ref, pre_ref, in_ref, out_ref, back_ref, sum_ref, part_s):
    @pl.when(forward)
    def _():
        for e in range(2):
            part_s[e] = dot(act_ref[e], out_ref[e]).astype(BF16)

    @pl.when(jnp.logical_not(forward))
    def _():
        for e in range(2):
            part_s[e] = dot_nt(pre_ref[e], in_ref[e]).astype(BF16)

    for b in range(4):
        rows = pl.ds(b * 80, 80)
        stacked = jnp.concatenate(
            [part_s[e, rows, pl.ds(half * HALF, HALF)] for half in range(2) for e in range(2)],
            axis=0,
        )
        sum_ref[pl.ds(b * 320, 320), :] = dot(back_ref[...], stacked).astype(BF16)


def second_expert_kernel(
    place_ref, act_ref, pre_ref, in_ref, out_ref, back_ref, mine_ref, part_s
):
    expert_sums(
        place_ref[1] == 0, act_ref, pre_ref, in_ref, out_ref, back_ref, mine_ref, part_s
    )


def expert_grads_kernel(x_ref, s_ref, act_ref, pre_ref, in_grad_ref, out_grad_ref):
    out_grad_ref[0] = dot_tn(act_ref[0], s_ref[0])
    in_grad_ref[0] = dot_tn(x_ref[0], pre_ref[0])


def expert_grads(x, s, act, pre):
    whole = pl.BlockSpec((1, 320, D), lambda e, f: (e, 0, 0))
    part = pl.BlockSpec((1, 320, 256), lambda e, f: (e, 0, f))
    return pl.pallas_call(
        expert_grads_kernel,
        grid=(2, 3),
        out_shape=(shape((2, D, D), F32), shape((2, D, D), F32)),
        in_specs=[whole, whole, part, part],
        out_specs=(
            pl.BlockSpec((1, D, 256), lambda e, f: (e, 0, f)),
            pl.BlockSpec((1, 256, D), lambda e, f: (e, f, 0)),
        ),
        compiler_params=pltpu.CompilerParams(vmem_limit_bytes=24 << 20),
        cost_estimate=pl.CostEstimate(
            flops=8 * 320 * D * D, bytes_accessed=14_000_000, transcendentals=0
        ),
    )(x, s, act, pre)


def tokens_kernel(low_ref, high_ref, recv_ref, out_ref):
    slots = (
        recv_ref[pl.ds(0, ROWS), :].astype(F32) + recv_ref[pl.ds(ROWS, ROWS), :].astype(F32)
    ).astype(BF16)
    out_ref[:, pl.ds(0, HALF)] = dot(low_ref[...], slots).astype(BF16)
    out_ref[:, pl.ds(HALF, HALF)] = dot(high_ref[...], slots).astype(BF16)


def backward_kernel(
    place_ref, x_ref, table_ref, middle_ref, mixed_ref, probs_ref, route_ref, grad_ref,
    own_ref, other_ref, router_ref, gain_ref, wo_ref, ctx_ref, q_ref, k_ref, v_ref, normed_ref,
    lse_ref, tiles_ref, wq_ref, wk_ref, wv_ref, stretch_ref,
    output_hbm, middle_grad_hbm, grads_ref, mine_ref, theirs_ref,
    low_s, logit_s, normed_s, wide_s, output_ref, middle_grad_ref, sems,
):
    core = place_ref[1]
    columns = route_columns(route_ref)
    gain = gain_ref[...]
    for i in range(SEQ // 32):
        rows = slice(i * 32, i * 32 + 32)
        expert_rows = jnp.where(core == 0, own_ref[rows, :], other_ref[rows, :]).astype(F32)
        probs = probs_ref[rows, :]
        kept = 1.0 - columns[rows, 2:3]
        lanes = lax.broadcasted_iota(jnp.int32, (32, 128), 1)
        hot = (lanes == columns[rows, 0:1].astype(jnp.int32)).astype(F32)
        chosen = jnp.sum(probs * hot, axis=-1, keepdims=True)
        upstream = grad_ref[rows, :].astype(F32)
        output_ref[rows, :] = (
            middle_ref[rows, :] + (chosen * kept) * expert_rows
        ).astype(BF16)
        gate_grad = jnp.sum(upstream * expert_rows, axis=-1, keepdims=True) * kept
        logit_s[rows, :] = (probs * (hot - chosen) * gate_grad).astype(BF16)
    output_copy = pltpu.make_async_copy(output_ref, output_hbm, sems.at[0])
    output_copy.start()
    wide_s[...] = dot(logit_s[...], router_ref[...])
    gain_grad = jnp.zeros((8, D), F32)
    for i in range(SEQ // 32):
        rows = slice(i * 32, i * 32 + 32)
        mixed_grad = jnp.where(core == 0, other_ref[rows, :], own_ref[rows, :]).astype(F32)
        mixed_grad = mixed_grad + wide_s[rows, :]
        middle = middle_ref[rows, :]
        scale = lax.rsqrt(jnp.mean(middle * middle, axis=-1, keepdims=True) + EPS)
        along = mixed_grad * middle
        inner = jnp.mean(along * gain, axis=-1, keepdims=True)
        gain_grad = gain_grad + jnp.sum((along * scale).reshape(4, 8, D), axis=0)
        middle_grad = (
            grad_ref[rows, :].astype(F32)
            + scale * (mixed_grad * gain)
            - middle * (scale * scale * scale * inner)
        )
        middle_grad_ref[rows, :] = middle_grad
        low_s[rows, :] = middle_grad.astype(BF16)
    gain_grad = jnp.sum(gain_grad, axis=0, keepdims=True)
    middle_copy = pltpu.make_async_copy(middle_grad_ref, middle_grad_hbm, sems.at[1])
    middle_copy.start()
    middle_low = low_s[...]
    grads_ref[pl.ds(3 * WIDTH, WIDTH), :D] = dot_tn(ctx_ref[...], middle_low).astype(BF16)
    ctx_grad = dot_nt(middle_low, wo_ref[...]).astype(BF16)

    keys = k_ref[...]
    values = v_ref[...]
    key_scaled = keys * jnp.asarray(HEAD**-0.5, BF16)
    query_scaled = q_ref[...] * jnp.asarray(HEAD**-0.5, BF16)
    key_grad = jnp.zeros((SEQ, WIDTH), F32)
    value_grad = jnp.zeros((SEQ, WIDTH), F32)
    query_grads = [jnp.zeros((256, WIDTH), F32), jnp.zeros((256, WIDTH), F32)]
    buckets = lax.broadcasted_iota(jnp.int32, (BUCKETS, 256), 0)
    line_ids = [line_buckets(block, 1) for block in (-1, 0, 1)]
    bias_grad = jnp.zeros((BUCKETS, 128), F32)
    bias_lanes = lax.broadcasted_iota(jnp.int32, (BUCKETS, 128), 1)
    turn = (
        lax.broadcasted_iota(jnp.int32, (128, 128), 0)
        + lax.broadcasted_iota(jnp.int32, (128, 128), 1)
        == 127
    ).astype(F32)
    for head in range(HEADS_HERE):
        near = [jnp.zeros((128, 128), F32) for _ in range(3)]
        far_low = jnp.zeros((128, 128), F32)
        far_high = jnp.zeros((128, 128), F32)
        key_head = only_head(key_scaled, head)
        for part in range(2):
            rows = slice(part * 256, part * 256 + 256)
            query_head = only_head(query_scaled[rows], head)
            ctx_head = only_head(ctx_grad[rows], head)
            scores = scores_t(keys, query_head, tiles_ref, table_ref[...], head, part)
            probs = jnp.exp(scores - lse_ref[head : head + 1, rows])
            value_grad = value_grad + dot(probs.astype(BF16), ctx_head)
            prob_grad = dot_nt(values, ctx_head)
            inner = jnp.sum(probs * prob_grad, axis=0, keepdims=True)
            score_grad = (probs * (prob_grad - inner)).astype(BF16)
            key_grad = key_grad + dot(score_grad, query_head)
            query_grads[part] = query_grads[part] + dot_tn(score_grad, key_head)
            for key_block in range(4):
                for i in range(2):
                    piece = score_grad[
                        key_block * 128 : key_block * 128 + 128, i * 128 : i * 128 + 128
                    ].astype(F32)
                    block = key_block - (part * 2 + i)
                    if block < -1:
                        far_low = far_low + piece
                    elif block > 1:
                        far_high = far_high + piece
                    else:
                        near[block + 1] = near[block + 1] + piece
        by_bucket = jnp.zeros((BUCKETS, 256), F32)
        for block in range(3):
            turned = jnp.dot(
                turn, near[block], precision=lax.Precision.HIGHEST, preferred_element_type=F32
            )
            wide = jnp.concatenate([turned, jnp.zeros((128, 128), F32)], axis=1)
            wide = pltpu.roll(wide, 1, 1, stride=1, stride_axis=0)
            line = jnp.sum(wide, axis=0, keepdims=True)
            by_bucket = by_bucket + jnp.where(
                buckets == line_ids[block], line, 0.0
            )
        side = lax.broadcasted_iota(jnp.int32, (BUCKETS, 128), 0)
        low_line = jnp.sum(far_low, axis=0, keepdims=True)
        high_line = jnp.sum(far_high, axis=0, keepdims=True)
        ends = jnp.where(side == BUCKETS // 2 - 1, low_line, 0.0) + jnp.where(
            side == BUCKETS - 1, high_line, 0.0
        )
        by_bucket = by_bucket[:, :128] + by_bucket[:, 128:] + ends
        total = jnp.sum(by_bucket, axis=1, keepdims=True)
        bias_grad = bias_grad + jnp.where(bias_lanes == EXPERTS + 1 + head, total, 0.0)
    query_low = jnp.concatenate(query_grads, axis=0).astype(BF16)
    key_low = key_grad.astype(BF16)
    value_low = value_grad.astype(BF16)
    normed = normed_ref[...]
    for i, low in enumerate((query_low, key_low, value_low)):
        grads_ref[pl.ds(i * WIDTH, WIDTH), :D] = dot_tn(low, normed).astype(BF16)
    rest = dot_tn(mixed_ref[...], logit_s[...]) + dot(stretch_ref[...], bias_grad.astype(BF16))
    column = jnp.transpose(jnp.broadcast_to(gain_grad, (128, D)))
    lanes = lax.broadcasted_iota(jnp.int32, (D, 128), 1)
    grads_ref[:, D:] = jnp.where(lanes == EXPERTS, column, rest).astype(BF16)
    wide_s[...] = (
        dot(query_low, wq_ref[...]) + dot(key_low, wk_ref[...]) + dot(value_low, wv_ref[...])
    )
    gain_one = jnp.zeros((8, D), F32)
    for i in range(SEQ // 32):
        rows = slice(i * 32, i * 32 + 32)
        normed_part = wide_s[rows, :]
        normed_s[rows, :] = normed_part.astype(BF16)
        hidden = x_ref[rows, :].astype(F32)
        scale = lax.rsqrt(jnp.mean(hidden * hidden, axis=-1, keepdims=True) + EPS)
        gain_one = gain_one + jnp.sum((normed_part * hidden * scale).reshape(4, 8, D), axis=0)
    gain_rows = jnp.broadcast_to(jnp.sum(gain_one, axis=0, keepdims=True), (16, D)).astype(BF16)
    for out, start in ((mine_ref, core * 256), (theirs_ref, (1 - core) * 256)):
        out[:256, :] = normed_s[pl.ds(pl.multiple_of(start, 256), 256), :]
        out[256:, :] = gain_rows
    output_copy.wait()
    middle_copy.wait()


def halves(core, own_ref, other_ref, i):
    local = slice((i % 2) * 128, (i % 2) * 128 + 128)
    return jnp.where(core == i // 2, own_ref[local, :], other_ref[local, :]).astype(F32)


def reduce_kernel(parts_ref, halved_ref, link_ref, send_ref):
    extra = pl.ds(256, 16)
    gain_grad = (halved_ref[extra, :].astype(F32) + link_ref[extra, :].astype(F32))[0:1]
    total = jnp.zeros((24, GRADS), F32)
    for j in range(GROUPS // 2):
        pair = parts_ref[pl.ds(j * 48, 48), :].astype(F32)
        total = total + pair[:24] + pair[24:]
    lines = [
        pltpu.roll(gain_grad[:, r // 4 * 128 : r // 4 * 128 + 128], (96 - r % 4 * 32) % 128, 1)
        for r in range(24)
    ]
    lanes = lax.broadcasted_iota(jnp.int32, (24, 128), 1)
    last = jnp.where(lanes < 96, total[:, D:], jnp.concatenate(lines, axis=0))
    chunk = jnp.concatenate([total[:, :D], last], axis=1)
    pair = jnp.concatenate([chunk, chunk], axis=0).astype(BF16)
    for j in range(GROUPS // 2):
        send_ref[pl.ds(j * 48, 48), :] = pair


def input_kernel(place_ref, own_ref, other_ref, x_ref, gain_ref, middle_grad_ref, input_ref):
    core = place_ref[1]
    gain = gain_ref[...]
    for i in range(4):
        rows = slice(i * 128, i * 128 + 128)
        hidden = x_ref[rows, :].astype(F32)
        scale = lax.rsqrt(jnp.mean(hidden * hidden, axis=-1, keepdims=True) + EPS)
        weighted = halves(core, own_ref, other_ref, i) * gain
        inner = jnp.mean(weighted * hidden, axis=-1, keepdims=True)
        input_ref[rows, :] = (
            middle_grad_ref[rows, :]
            + scale * weighted
            - hidden * (scale * scale * scale * inner)
        )


def finish_kernel(
    recv_ref, stretch_ref, gain_one_ref, gain_two_ref, bias_ref,
    q_ref, k_ref, v_ref, o_ref, router_ref,
):
    for i, out in enumerate((q_ref, k_ref, v_ref, o_ref)):
        out[...] = recv_ref[pl.ds(i * WIDTH, WIDTH), :D].astype(F32)
    last = recv_ref[:, D:].astype(F32)
    summed = jnp.zeros((24, 128), F32)
    for j in range(GROUPS):
        summed = summed + last[j * 24 : j * 24 + 24]
    lanes = lax.broadcasted_iota(jnp.int32, (1, 128), 1)
    for block in range(6):
        line = jnp.zeros((1, 128), F32)
        for i in range(4):
            r = block * 4 + i
            piece = pltpu.roll(summed[r : r + 1], (32 + 32 * i) % 128, 1)
            line = jnp.where((lanes >= 32 * i) & (lanes < 32 * i + 32), piece, line)
        gain_one_ref[pl.ds(block * 128, 128)] = line[0]
    turned = jnp.transpose(last)
    router_ref[...] = turned[:EXPERTS]
    tail = turned[EXPERTS : EXPERTS + 8]
    gain_two_ref[...] = tail[0]
    bias_ref[...] = dot(tail.astype(BF16), stretch_ref[...])[1 : 1 + HEADS_HERE]


def shards(
    layer_input, attn_gain, query_weight, key_weight, value_weight, output_weight, position_bias,
    moe_gain, router_weight, expert_in, expert_out, route_expert, route_slot, route_drop, out_grad,
):
    experts_axis = ("z", "x", "h")
    pair_axis = ("l", "z", "x", "h")
    core = lax.axis_index("c")
    place = jnp.stack([lax.axis_index("l") * 2 + core, core]).astype(jnp.int32)

    def swap(array, axis):
        return lax.ppermute(array, axis, [(0, 1), (1, 0)])

    gain_one = attn_gain.reshape(1, D)
    gain_two = moe_gain.reshape(1, D)
    zeros = jnp.zeros_like(route_drop)
    route = jnp.stack([route_expert, route_slot, route_drop] + [zeros] * 5)
    table = jnp.transpose(position_bias)
    wq, wk, wv = (jnp.transpose(w) for w in (query_weight, key_weight, value_weight))
    router = jnp.pad(jnp.transpose(router_weight), ((0, 128 - EXPERTS), (0, 0)))
    wo_link = swap(output_weight, "l")
    wo_core = swap(output_weight, "c")
    wo_far = swap(wo_link, "c")

    tall = shape((SEQ, WIDTH), BF16)
    wide = shape((SEQ, D), BF16)
    tile_shape = (3 * HEADS_HERE, 128, 128)
    weight_vmem = pltpu.VMEM((WIDTH, D), BF16)
    tall_vmem = pltpu.VMEM((SEQ, WIDTH), BF16)
    normed, queries, keys, values, tiles, context, lse = call(
        attention_forward,
        (wide, tall, tall, tall, shape(tile_shape, F32), tall, shape((8, SEQ), F32)),
        (table, layer_input, attn_gain, wq, wk, wv),
        far=(0, 1, 2, 3, 4, 5), far_out=(0, 1, 2, 3, 4),
        scratch=(pltpu.VMEM((HEADS_HERE, BUCKETS), F32), pltpu.VMEM((SEQ, D), BF16),
                 pltpu.VMEM((D,), F32), weight_vmem, weight_vmem, weight_vmem, pltpu.VMEM((SEQ, D), BF16),
                 tall_vmem, tall_vmem, tall_vmem, pltpu.VMEM(tile_shape, F32),
                 pltpu.SemaphoreType.DMA((11,))),
        limit=60, flops=900_000_000, moved=5_000_000,
    )
    flat, flat_t = shape((ROWS, SEQ), BF16), shape((SEQ, ROWS), BF16)
    sums = shape((ROWS, HALF), BF16)
    ctx_link = swap(context, "l")
    ctx_core = swap(context, "c")
    low_place, high_place, base, raw = call(
        near_kernel, (flat, flat, shape((SEQ, D), F32), sums),
        (place, route, context, ctx_core, output_weight, wo_core, out_grad),
        scalars=1, limit=16, flops=1_500_000_000, moved=7_000_000,
    )
    ctx_link_late, low_place = lax.optimization_barrier((ctx_link, low_place))
    ctx_far = swap(ctx_link_late, "c")
    middle, mixed, probs, send = call(
        middle_kernel,
        (shape((SEQ, D), F32), wide, shape((SEQ, 128), F32), sums),
        (place, layer_input, base, ctx_link, ctx_far, wo_link, wo_far, gain_two, router, route,
         low_place, high_place, raw),
        scratch=(pltpu.VMEM((SEQ, D), F32), pltpu.VMEM((SEQ, 128), BF16)),
        scalars=1, limit=16, flops=1_700_000_000, moved=8_000_000,
    )
    received = lax.all_to_all(send, experts_axis, 0, 0, tiled=True)
    received, route_late = lax.optimization_barrier((received, route))
    low_back, high_back = call(
        back_place_kernel, (flat_t, flat_t), (route_late,),
        limit=12, flops=10_000_000, moved=2_700_000,
    )
    received_other, low_back, high_back = lax.optimization_barrier(
        (swap(received, "c"), low_back, high_back)
    )
    select = regroup_matrix()
    low = shape((2, 320, D), BF16)
    back_select = jnp.asarray(select.T, BF16)
    theirs, slots, slot_grads, act, pre_grad = call(
        first_expert_kernel,
        (sums, low, low, low, low),
        (place, received, received_other, expert_in, expert_out,
         jnp.asarray(select, BF16), back_select),
        scratch=(pltpu.VMEM((2, 320, D), BF16),),
        scalars=1, limit=24, flops=4_000_000_000, moved=14_000_000,
    )
    mine = call(
        second_expert_kernel, sums,
        (place, act, pre_grad, expert_in, expert_out, back_select),
        scratch=(pltpu.VMEM((2, 320, D), BF16),),
        scalars=1, limit=12, flops=1_000_000_000, moved=4_000_000,
    )
    partial = (mine.astype(F32) + swap(theirs, "c").astype(F32)).astype(BF16)
    back = lax.all_to_all(
        jnp.concatenate([partial, partial], axis=0), pair_axis, 0, 0, tiled=True
    )
    rows_own = call(
        tokens_kernel, shape((SEQ, D), BF16), (low_back, high_back, back),
        limit=12, flops=2_000_000_000, moved=3_000_000,
    )
    rows_other = swap(rows_own, "c")
    stretch = np.zeros((D, BUCKETS), np.float32)
    stretch[24 * np.arange(BUCKETS), np.arange(BUCKETS)] = 1
    half = shape((256 + 16, D), BF16)
    layer_output, middle_grad, grads, norm_mine, norm_theirs = call(
        backward_kernel,
        (wide, shape((SEQ, D), F32), shape((D, GRADS), BF16), half, half),
        (place, layer_input, table, middle, mixed, probs, route, out_grad,
         rows_own, rows_other, router, gain_two, output_weight, context, queries, keys,
         values, normed, lse, tiles, wq, wk, wv, jnp.asarray(stretch, BF16)),
        scratch=(pltpu.VMEM((SEQ, D), BF16), pltpu.VMEM((SEQ, 128), BF16),
                 pltpu.VMEM((SEQ, D), BF16), pltpu.VMEM((SEQ, D), F32),
                 pltpu.VMEM((SEQ, D), BF16), pltpu.VMEM((SEQ, D), F32),
                 pltpu.SemaphoreType.DMA((2,))),
        far_out=(0, 1),
        scalars=1, limit=24, flops=4_000_000_000, moved=12_000_000,
    )
    halved = (norm_mine.astype(F32) + swap(norm_theirs, "c").astype(F32)).astype(BF16)
    scattered = lax.all_to_all(grads, experts_axis, 0, 0, tiled=True)
    halved_link = swap(halved, "l")
    reduced = (halved.astype(F32) + halved_link.astype(F32)).astype(BF16)
    reduced_other = swap(reduced, "c")
    spread = call(
        reduce_kernel, shape((D, GRADS), BF16),
        (scattered, halved, halved_link),
        limit=12, flops=10_000_000, moved=3_000_000,
    )
    spread, slots, slot_grads, act, pre_grad = lax.optimization_barrier(
        (spread, slots, slot_grads, act, pre_grad)
    )
    expert_in_grad, expert_out_grad = expert_grads(slots, slot_grads, act, pre_grad)
    gathered = lax.all_to_all(spread, experts_axis, 0, 0, tiled=True)
    input_grad = call(
        input_kernel, shape((SEQ, D), F32),
        (place, reduced, reduced_other, layer_input, gain_one, middle_grad),
        alias={5: 0}, scalars=1, limit=12, flops=10_000_000, moved=5_000_000,
    )
    out = shape((WIDTH, D), F32)
    line = shape((D,), F32)
    gain_one_grad, gain_two_grad, bias_grad, query_grad, key_grad, value_grad, output_grad, \
        router_grad = call(
            finish_kernel,
            (line, line, shape((HEADS_HERE, BUCKETS), F32), out, out, out, out,
             shape((EXPERTS, D), F32)),
            (gathered, jnp.asarray(stretch, BF16)),
            limit=12, flops=10_000_000, moved=6_000_000,
        )
    return (
        layer_output,
        input_grad,
        gain_one_grad,
        jnp.transpose(query_grad),
        jnp.transpose(key_grad),
        jnp.transpose(value_grad),
        output_grad,
        jnp.transpose(bias_grad),
        gain_two_grad,
        jnp.transpose(router_grad),
        expert_in_grad,
        expert_out_grad,
    )


def solution(mesh):
    fine = Mesh(mesh.devices.reshape(4, 4, 2, 2, 2), ("z", "x", "h", "l", "c"))
    ex = ("z", "x", "h")
    te = ("l", "c")
    in_specs = (
        P(ex, None), P(), P(None, te), P(None, te), P(None, te), P(te, None), P(None, te), P(),
        P(), P(ex, None, te), P(ex, te, None), P(ex), P(ex), P(ex), P(ex, None),
    )
    out_specs = (
        P(ex, None), P(ex, None), P(), P(None, te), P(None, te), P(None, te), P(te, None),
        P(None, te), P(), P(), P(ex, None, te), P(ex, te, None),
    )
    return jax.shard_map(shards, mesh=fine, in_specs=in_specs, out_specs=out_specs, check_vma=False)
```

```python
import jax
import jax.numpy as jnp
import numpy as np
from jax import lax
from jax.experimental import pallas as pl
from jax.experimental.pallas import tpu as pltpu
from jax.sharding import Mesh
from jax.sharding import PartitionSpec as P

BUCKETS = 32
EPS = 1e-06
SEQ = 512
D = 768
HEAD = 64
HEADS_HERE = 3
WIDTH = HEADS_HERE * HEAD
EXPERTS = 64
CAP = 10
GROUPS = 32
CHUNK = 40
ROWS = GROUPS * CHUNK
HALF = D // 2
GRADS = 896
F32 = jnp.float32
BF16 = jnp.bfloat16
GELU_C = float(np.sqrt(2.0 / np.pi))


def bucket_of(offsets):
    half_count = BUCKETS // 2
    exact_count = half_count // 2
    upper_side = (offsets > 0).astype(np.int64) * half_count
    distance = np.abs(offsets)
    ratio = np.log(np.maximum(distance, 1) / exact_count) / np.log(128.0 / exact_count)
    far_bucket = np.minimum(
        exact_count + (ratio * (half_count - exact_count)).astype(np.int64), half_count - 1
    )
    return upper_side + np.where(distance < exact_count, distance, far_bucket)


FAR_STARTS = [
    int(np.argmax(bucket_of(-np.arange(256)) >= b)) for b in range(9, BUCKETS // 2)
]


def line_buckets(block, rows):
    offset = 128 * block + 128 - lax.broadcasted_iota(jnp.int32, (rows, 256), 1)
    distance = jnp.abs(offset)
    far = jnp.full((rows, 256), 8, jnp.int32)
    for start in FAR_STARTS:
        far = far + (distance >= start).astype(jnp.int32)
    bucket = jnp.where(distance < 8, distance, far)
    return jnp.where(offset > 0, bucket + BUCKETS // 2, bucket)


def regroup_matrix():
    sel = np.zeros((320, 320), np.float32)
    for g in range(8):
        for half in range(2):
            for e in range(2):
                for c in range(CAP):
                    sel[half * 160 + e * 80 + g * 10 + c, g * 40 + half * 20 + e * 10 + c] = 1
    return sel


def dot(a, b):
    return jnp.dot(a, b, preferred_element_type=F32)


def dot_nt(a, b):
    return lax.dot_general(a, b, (((1,), (1,)), ((), ())), preferred_element_type=F32)


def dot_tn(a, b):
    return lax.dot_general(a, b, (((0,), (0,)), ((), ())), preferred_element_type=F32)


def head_mask(head, rows):
    lanes = lax.broadcasted_iota(jnp.int32, (rows, WIDTH), 1)
    return (lanes >= head * HEAD) & (lanes < (head + 1) * HEAD)


def only_head(matrix, head):
    return jnp.where(head_mask(head, matrix.shape[0]), matrix, jnp.zeros_like(matrix))


def call(
    body, out_shape, args, scratch=(), scalars=0, far=(), far_out=(), alias=None, limit=40, flops=0, moved=0
):
    spaces = [pltpu.SMEM] * scalars + [pltpu.VMEM] * (len(args) - scalars)
    for i in far:
        spaces[i] = pltpu.HBM
    outs = out_shape if isinstance(out_shape, tuple) else (out_shape,)
    out_spaces = [pltpu.HBM if i in far_out else pltpu.VMEM for i in range(len(outs))]
    result = pl.pallas_call(
        body,
        out_shape=outs,
        in_specs=[pl.BlockSpec(memory_space=space) for space in spaces],
        out_specs=tuple(pl.BlockSpec(memory_space=space) for space in out_spaces),
        scratch_shapes=scratch,
        input_output_aliases=alias or {},
        compiler_params=pltpu.CompilerParams(vmem_limit_bytes=limit << 20),
        cost_estimate=pl.CostEstimate(flops=flops, bytes_accessed=moved, transcendentals=0),
    )(*args)
    return result if isinstance(out_shape, tuple) else result[0]


def shape(dims, dtype):
    return jax.ShapeDtypeStruct(dims, dtype)


def bias_tile(tiles_ref, far_low, far_high, head, block):
    if block < -1:
        return far_low
    if block > 1:
        return far_high
    return tiles_ref[head * 3 + block + 1]


def scores_t(keys, query_scaled, tiles_ref, table, head, part):
    raw = dot_nt(keys, query_scaled)
    far_low = table[head : head + 1, BUCKETS // 2 - 1 : BUCKETS // 2]
    far_high = table[head : head + 1, BUCKETS - 1 : BUCKETS]
    rows = []
    for key_block in range(4):
        cols = []
        for i in range(2):
            piece = raw[key_block * 128 : key_block * 128 + 128, i * 128 : i * 128 + 128]
            block = key_block - (part * 2 + i)
            cols.append(piece + bias_tile(tiles_ref, far_low, far_high, head, block))
        rows.append(jnp.concatenate(cols, axis=1))
    return jnp.concatenate(rows, axis=0)


def attention_forward(
    table_hbm, x_hbm, gain_hbm, wq_hbm, wk_hbm, wv_hbm,
    normed_hbm, q_hbm, k_hbm, v_hbm, tiles_hbm, ctx_ref, lse_ref,
    table_ref, x_ref, gain_ref, wq_ref, wk_ref, wv_ref, normed_ref, q_ref, k_ref, v_ref,
    tiles_ref, sems,
):
    loads = [
        pltpu.make_async_copy(src, dst, sems.at[i])
        for i, (src, dst) in enumerate(
            (
                (table_hbm, table_ref), (x_hbm, x_ref), (wq_hbm, wq_ref), (wk_hbm, wk_ref),
                (wv_hbm, wv_ref), (gain_hbm, gain_ref),
            )
        )
    ]
    for load in loads:
        load.start()
    stores = []

    def store(src, dst):
        copy = pltpu.make_async_copy(src, dst, sems.at[6 + len(stores)])
        copy.start()
        stores.append(copy)

    loads[0].wait()
    table = table_ref[...]
    lines = []
    for block in (-1, 0, 1):
        buckets = lax.broadcasted_iota(jnp.int32, (BUCKETS, 256), 0)
        hot = (buckets == line_buckets(block, 1)).astype(F32)
        lines.append(
            jnp.dot(table, hot, precision=lax.Precision.HIGHEST, preferred_element_type=F32)
        )
    for head in range(HEADS_HERE):
        for block in range(3):
            wide = pltpu.roll(
                jnp.broadcast_to(lines[block][head : head + 1], (128, 256)),
                0, 1, stride=1, stride_axis=0,
            )
            tiles_ref[head * 3 + block] = wide[:, 128:]
    store(tiles_ref, tiles_hbm)
    loads[1].wait()
    loads[5].wait()
    gain = gain_ref[...].reshape(1, D)
    for i in range(SEQ // 32):
        rows = pl.ds(i * 32, 32)
        x = x_ref[rows, :].astype(F32)
        scale = lax.rsqrt(jnp.mean(x * x, axis=-1, keepdims=True) + EPS)
        normed_ref[rows, :] = (x * scale * gain).astype(BF16)
    store(normed_ref, normed_hbm)
    normed = normed_ref[...]
    for load, weight, out, out_hbm in (
        (loads[2], wq_ref, q_ref, q_hbm),
        (loads[3], wk_ref, k_ref, k_hbm),
        (loads[4], wv_ref, v_ref, v_hbm),
    ):
        load.wait()
        out[...] = dot_nt(normed, weight[...]).astype(BF16)
        store(out, out_hbm)
    queries, keys, values = q_ref[...], k_ref[...], v_ref[...]
    lse_ref[...] = jnp.zeros((8, SEQ), F32)
    scaled = queries * jnp.asarray(HEAD**-0.5, BF16)
    for part in range(2):
        rows = slice(part * 256, part * 256 + 256)
        context = jnp.zeros((256, WIDTH), F32)
        for head in range(HEADS_HERE):
            scores = scores_t(keys, only_head(scaled[rows], head), tiles_ref, table, head, part)
            top = jnp.max(scores, axis=0, keepdims=True)
            grown = jnp.exp(scores - top)
            total = jnp.sum(grown, axis=0, keepdims=True)
            probs = (grown * (1.0 / total)).astype(BF16)
            lse_ref[head : head + 1, rows] = top + jnp.log(total)
            context = context + dot_tn(probs, only_head(values, head))
        ctx_ref[rows, :] = context.astype(BF16)
    for copy in stores:
        copy.wait()


def route_columns(route_ref):
    return jnp.transpose(route_ref[...].astype(F32))


def row_of(expert, slot, drop):
    row = (expert >> 1) * CHUNK + (expert & 1) * CAP + slot
    return jnp.where(drop > 0, -1000, row)


def near_kernel(
    place_ref, route_ref, ctx0, ctx1, wo0, wo1, grad_ref, low_ref, high_ref, base_ref, raw_ref
):
    target = row_of(route_ref[0:1, :], route_ref[1:2, :], route_ref[2:3, :])
    for i in range(4):
        rows = pl.ds(i * 320, 320)
        index = lax.broadcasted_iota(jnp.int32, (320, SEQ), 0) + 320 * i
        low = (index == target).astype(F32).astype(BF16)
        high = (index == target + 20).astype(F32).astype(BF16)
        low_ref[rows, :] = low
        high_ref[rows, :] = high
        raw = dot(low, grad_ref[:, :HALF]) + dot(high, grad_ref[:, HALF:])
        raw_ref[rows, :] = raw.astype(BF16)
    pair_of_heads(place_ref[1], ctx0, ctx1, wo0, wo1, base_ref)


def pair_of_heads(core, ctx0, ctx1, wo0, wo1, sum_ref):
    @pl.when(core == 0)
    def _():
        sum_ref[...] = dot(ctx0[...], wo0[...]) + dot(ctx1[...], wo1[...])

    @pl.when(core == 1)
    def _():
        sum_ref[...] = dot(ctx1[...], wo1[...]) + dot(ctx0[...], wo0[...])


def back_place_kernel(route_ref, low_ref, high_ref):
    columns = route_columns(route_ref).astype(jnp.int32)
    target = row_of(columns[:, 0:1], columns[:, 1:2], columns[:, 2:3])
    for i in range(4):
        rows = slice(i * 128, i * 128 + 128)
        index = lax.broadcasted_iota(jnp.int32, (128, ROWS), 1)
        low_ref[rows, :] = (index == target[rows]).astype(F32).astype(BF16)
        high_ref[rows, :] = (index == target[rows] + 20).astype(F32).astype(BF16)


def middle_kernel(
    place_ref, x_ref, base_ref, ctx2, ctx3, wo2, wo3, gain_ref, router_ref, route_ref,
    low_ref, high_ref, raw_ref, middle_ref, mixed_ref, probs_ref, send_ref, far_s, gate_s,
):
    core = place_ref[1]
    columns = route_columns(route_ref)
    pair_of_heads(core, ctx2, ctx3, wo2, wo3, far_s)
    for i in range(SEQ // 32):
        rows = slice(i * 32, i * 32 + 32)
        middle = x_ref[rows, :].astype(F32) + (base_ref[rows, :] + far_s[rows, :])
        scale = lax.rsqrt(jnp.mean(middle * middle, axis=-1, keepdims=True) + EPS)
        middle_ref[rows, :] = middle
        mixed_ref[rows, :] = (middle * scale * gain_ref[...]).astype(BF16)
    for i in range(4):
        rows = slice(i * 128, i * 128 + 128)
        lanes = lax.broadcasted_iota(jnp.int32, (128, 128), 1)
        logits = dot_nt(mixed_ref[rows, :], router_ref[...])
        logits = jnp.where(lanes < EXPERTS, logits, -jnp.inf)
        grown = jnp.exp(logits - jnp.max(logits, axis=-1, keepdims=True))
        probs = grown / jnp.sum(grown, axis=-1, keepdims=True)
        probs_ref[rows, :] = probs
        expert = columns[rows, 0:1].astype(jnp.int32)
        chosen = jnp.sum(jnp.where(lanes == expert, probs, 0.0), axis=-1, keepdims=True)
        gate = chosen * (1.0 - columns[rows, 2:3])
        first = gate.astype(BF16).astype(F32)
        second = (gate - first).astype(BF16).astype(F32)
        third = gate - first - second
        pieces = jnp.where(lanes == 0, first, jnp.where(lanes == 1, second, third))
        gate_s[rows, :] = jnp.where(lanes < 3, pieces, 0.0).astype(BF16)

    @pl.when(core == 0)
    def _():
        for i in range(4):
            rows = pl.ds(i * 320, 320)
            out = dot(low_ref[rows, :], mixed_ref[:, :HALF])
            out = out + dot(high_ref[rows, :], mixed_ref[:, HALF:])
            send_ref[rows, :] = out.astype(BF16)

    @pl.when(core == 1)
    def _():
        for i in range(4):
            rows = pl.ds(i * 320, 320)
            gate = dot(low_ref[rows, :], gate_s[...]) + dot(high_ref[rows, :], gate_s[...])
            gate = jnp.sum(gate, axis=-1, keepdims=True)
            send_ref[rows, :] = (raw_ref[rows, :].astype(F32) * gate).astype(BF16)


def regroup(rows_ref, sel_ref, sorted_ref):
    for b in range(4):
        sorted_rows = dot(sel_ref[...], rows_ref[pl.ds(b * 320, 320), :]).astype(BF16)
        for half in range(2):
            for e in range(2):
                sorted_ref[e, pl.ds(b * 80, 80), pl.ds(half * HALF, HALF)] = sorted_rows[
                    half * 160 + e * 80 : half * 160 + e * 80 + 80
                ]


def first_product(forward, sorted_ref, in_ref, out_ref, product_ref):
    @pl.when(forward)
    def _():
        for e in range(2):
            product_ref[e] = dot(sorted_ref[e], in_ref[e])

    @pl.when(jnp.logical_not(forward))
    def _():
        for e in range(2):
            product_ref[e] = dot_nt(sorted_ref[e], out_ref[e])


def own_expert_kernel(place_ref, own_ref, in_ref, out_ref, sel_ref, sorted_ref, product_ref):
    regroup(own_ref, sel_ref, sorted_ref)
    first_product(place_ref[1] == 0, sorted_ref, in_ref, out_ref, product_ref)


def first_expert_kernel(
    place_ref, other_ref, own_product_ref, in_ref, out_ref, sel_ref, back_ref,
    theirs_ref, sorted_ref, act_ref, pre_ref, product_s, part_s,
):
    core = place_ref[1]
    regroup(other_ref, sel_ref, sorted_ref)
    first_product(core == 1, sorted_ref, in_ref, out_ref, product_s)
    for e in range(2):
        for f in range(10):
            rows = slice(f * 32, f * 32 + 32)
            own = own_product_ref[e, rows, :]
            other = product_s[e, rows, :]
            pre = jnp.where(core == 0, own, other)
            act_grad = jnp.where(core == 0, other, own)
            square = pre * pre
            bent = jnp.tanh(GELU_C * (pre + 0.044715 * (square * pre)))
            cdf = 0.5 * (1.0 + bent)
            act_ref[e, rows, :] = (pre * cdf).astype(BF16)
            slope = cdf + (0.5 * GELU_C) * pre * (1.0 - bent * bent) * (
                1.0 + (3 * 0.044715) * square
            )
            pre_ref[e, rows, :] = (act_grad * slope).astype(BF16)
    expert_sums(core == 1, act_ref, pre_ref, in_ref, out_ref, back_ref, theirs_ref, part_s)


def expert_sums(forward, act_ref, pre_ref, in_ref, out_ref, back_ref, sum_ref, part_s):
    @pl.when(forward)
    def _():
        for e in range(2):
            part_s[e] = dot(act_ref[e], out_ref[e]).astype(BF16)

    @pl.when(jnp.logical_not(forward))
    def _():
        for e in range(2):
            part_s[e] = dot_nt(pre_ref[e], in_ref[e]).astype(BF16)

    for b in range(4):
        rows = pl.ds(b * 80, 80)
        stacked = jnp.concatenate(
            [part_s[e, rows, pl.ds(half * HALF, HALF)] for half in range(2) for e in range(2)],
            axis=0,
        )
        sum_ref[pl.ds(b * 320, 320), :] = dot(back_ref[...], stacked).astype(BF16)


def second_expert_kernel(
    place_ref, act_ref, pre_ref, in_ref, out_ref, back_ref, mine_ref, part_s
):
    expert_sums(
        place_ref[1] == 0, act_ref, pre_ref, in_ref, out_ref, back_ref, mine_ref, part_s
    )


def expert_grads_kernel(
    place_ref, own_ref, other_ref, act_ref, pre_ref, in_grad_ref, out_grad_ref
):
    core = place_ref[1]
    own, other = own_ref[0], other_ref[0]
    out_grad_ref[0] = dot_tn(act_ref[0], jnp.where(core == 0, other, own))
    in_grad_ref[0] = dot_tn(jnp.where(core == 0, own, other), pre_ref[0])


def expert_grads(place, own, other, act, pre):
    whole = pl.BlockSpec((1, 320, D), lambda e, f: (e, 0, 0))
    part = pl.BlockSpec((1, 320, 256), lambda e, f: (e, 0, f))
    return pl.pallas_call(
        expert_grads_kernel,
        grid=(2, 3),
        out_shape=(shape((2, D, D), F32), shape((2, D, D), F32)),
        in_specs=[pl.BlockSpec(memory_space=pltpu.SMEM), whole, whole, part, part],
        out_specs=(
            pl.BlockSpec((1, D, 256), lambda e, f: (e, 0, f)),
            pl.BlockSpec((1, 256, D), lambda e, f: (e, f, 0)),
        ),
        compiler_params=pltpu.CompilerParams(vmem_limit_bytes=24 << 20),
        cost_estimate=pl.CostEstimate(
            flops=8 * 320 * D * D, bytes_accessed=14_000_000, transcendentals=0
        ),
    )(place, own, other, act, pre)


def tokens_kernel(low_ref, high_ref, recv_ref, out_ref):
    slots = (
        recv_ref[pl.ds(0, ROWS), :].astype(F32) + recv_ref[pl.ds(ROWS, ROWS), :].astype(F32)
    ).astype(BF16)
    out_ref[:, pl.ds(0, HALF)] = dot(low_ref[...], slots).astype(BF16)
    out_ref[:, pl.ds(HALF, HALF)] = dot(high_ref[...], slots).astype(BF16)


def window_kernel(
    table_ref, q_ref, k_ref, lse_ref, tiles_ref, x_ref, middle_ref, probs_ref, route_ref,
    weights_ref, stats_ref,
):
    scaled = q_ref[...] * jnp.asarray(HEAD**-0.5, BF16)
    keys = k_ref[...]
    for head in range(HEADS_HERE):
        for part in range(2):
            rows = slice(part * 256, part * 256 + 256)
            scores = scores_t(
                keys, only_head(scaled[rows], head), tiles_ref, table_ref[...], head, part
            )
            weights_ref[head, part] = jnp.exp(scores - lse_ref[head : head + 1, rows]).astype(BF16)
    columns = route_columns(route_ref)
    for i in range(SEQ // 32):
        rows = slice(i * 32, i * 32 + 32)
        lanes = lax.broadcasted_iota(jnp.int32, (32, 128), 1)
        middle = middle_ref[rows, :]
        scale_two = lax.rsqrt(jnp.mean(middle * middle, axis=-1, keepdims=True) + EPS)
        hidden = x_ref[rows, :].astype(F32)
        scale_one = lax.rsqrt(jnp.mean(hidden * hidden, axis=-1, keepdims=True) + EPS)
        hot = lanes == columns[rows, 0:1].astype(jnp.int32)
        chosen = jnp.sum(jnp.where(hot, probs_ref[rows, :], 0.0), axis=-1, keepdims=True)
        stats_ref[rows, :] = jnp.where(
            lanes == 0, scale_one, jnp.where(lanes == 1, scale_two, chosen)
        )


def backward_kernel(
    place_ref, x_ref, middle_ref, mixed_ref, probs_ref, route_ref, grad_ref,
    own_ref, other_ref, router_ref, gain_ref, wo_ref, ctx_ref, q_ref, k_ref, v_ref, normed_ref,
    weights_ref, stats_ref, wq_ref, wk_ref, wv_ref, stretch_ref,
    output_hbm, middle_grad_hbm, grads_ref, mine_ref, theirs_ref,
    low_s, logit_s, normed_s, wide_s, output_ref, middle_grad_ref, sems,
):
    core = place_ref[1]
    columns = route_columns(route_ref)
    gain = gain_ref[...]
    for i in range(SEQ // 32):
        rows = slice(i * 32, i * 32 + 32)
        expert_rows = jnp.where(core == 0, own_ref[rows, :], other_ref[rows, :]).astype(F32)
        probs = probs_ref[rows, :]
        kept = 1.0 - columns[rows, 2:3]
        lanes = lax.broadcasted_iota(jnp.int32, (32, 128), 1)
        hot = (lanes == columns[rows, 0:1].astype(jnp.int32)).astype(F32)
        chosen = stats_ref[rows, 2:3]
        upstream = grad_ref[rows, :].astype(F32)
        output_ref[rows, :] = (
            middle_ref[rows, :] + (chosen * kept) * expert_rows
        ).astype(BF16)
        gate_grad = jnp.sum(upstream * expert_rows, axis=-1, keepdims=True) * kept
        logit_s[rows, :] = (probs * (hot - chosen) * gate_grad).astype(BF16)
    output_copy = pltpu.make_async_copy(output_ref, output_hbm, sems.at[0])
    output_copy.start()
    wide_s[...] = dot(logit_s[...], router_ref[...])
    gain_grad = jnp.zeros((8, D), F32)
    for i in range(SEQ // 32):
        rows = slice(i * 32, i * 32 + 32)
        mixed_grad = jnp.where(core == 0, other_ref[rows, :], own_ref[rows, :]).astype(F32)
        mixed_grad = mixed_grad + wide_s[rows, :]
        middle = middle_ref[rows, :]
        scale = stats_ref[rows, 1:2]
        along = mixed_grad * middle
        inner = jnp.mean(along * gain, axis=-1, keepdims=True)
        gain_grad = gain_grad + jnp.sum((along * scale).reshape(4, 8, D), axis=0)
        middle_grad = (
            grad_ref[rows, :].astype(F32)
            + scale * (mixed_grad * gain)
            - middle * (scale * scale * scale * inner)
        )
        middle_grad_ref[rows, :] = middle_grad
        low_s[rows, :] = middle_grad.astype(BF16)
    gain_grad = jnp.sum(gain_grad, axis=0, keepdims=True)
    middle_copy = pltpu.make_async_copy(middle_grad_ref, middle_grad_hbm, sems.at[1])
    middle_copy.start()
    middle_low = low_s[...]
    grads_ref[pl.ds(3 * WIDTH, WIDTH), :D] = dot_tn(ctx_ref[...], middle_low).astype(BF16)
    ctx_grad = dot_nt(middle_low, wo_ref[...]).astype(BF16)

    values = v_ref[...]
    key_scaled = k_ref[...] * jnp.asarray(HEAD**-0.5, BF16)
    query_scaled = q_ref[...] * jnp.asarray(HEAD**-0.5, BF16)
    key_grad = jnp.zeros((SEQ, WIDTH), F32)
    value_grad = jnp.zeros((SEQ, WIDTH), F32)
    query_grads = [jnp.zeros((256, WIDTH), F32), jnp.zeros((256, WIDTH), F32)]
    buckets = lax.broadcasted_iota(jnp.int32, (BUCKETS, 256), 0)
    line_ids = [line_buckets(block, 1) for block in (-1, 0, 1)]
    bias_grad = jnp.zeros((BUCKETS, 128), F32)
    bias_lanes = lax.broadcasted_iota(jnp.int32, (BUCKETS, 128), 1)
    turn = (
        lax.broadcasted_iota(jnp.int32, (128, 128), 0)
        + lax.broadcasted_iota(jnp.int32, (128, 128), 1)
        == 127
    ).astype(F32)
    for head in range(HEADS_HERE):
        near = [jnp.zeros((128, 128), F32) for _ in range(3)]
        far_low = jnp.zeros((128, 128), F32)
        far_high = jnp.zeros((128, 128), F32)
        key_head = only_head(key_scaled, head)
        for part in range(2):
            rows = slice(part * 256, part * 256 + 256)
            query_head = only_head(query_scaled[rows], head)
            ctx_head = only_head(ctx_grad[rows], head)
            probs_low = weights_ref[head, part]
            probs = probs_low.astype(F32)
            value_grad = value_grad + dot(probs_low, ctx_head)
            prob_grad = dot_nt(values, ctx_head)
            inner = jnp.sum(probs * prob_grad, axis=0, keepdims=True)
            score_grad = (probs * (prob_grad - inner)).astype(BF16)
            key_grad = key_grad + dot(score_grad, query_head)
            query_grads[part] = query_grads[part] + dot_tn(score_grad, key_head)
            for key_block in range(4):
                for i in range(2):
                    piece = score_grad[
                        key_block * 128 : key_block * 128 + 128, i * 128 : i * 128 + 128
                    ].astype(F32)
                    block = key_block - (part * 2 + i)
                    if block < -1:
                        far_low = far_low + piece
                    elif block > 1:
                        far_high = far_high + piece
                    else:
                        near[block + 1] = near[block + 1] + piece
        by_bucket = jnp.zeros((BUCKETS, 256), F32)
        for block in range(3):
            turned = jnp.dot(
                turn, near[block], precision=lax.Precision.HIGHEST, preferred_element_type=F32
            )
            wide = jnp.concatenate([turned, jnp.zeros((128, 128), F32)], axis=1)
            wide = pltpu.roll(wide, 1, 1, stride=1, stride_axis=0)
            line = jnp.sum(wide, axis=0, keepdims=True)
            by_bucket = by_bucket + jnp.where(
                buckets == line_ids[block], line, 0.0
            )
        side = lax.broadcasted_iota(jnp.int32, (BUCKETS, 128), 0)
        low_line = jnp.sum(far_low, axis=0, keepdims=True)
        high_line = jnp.sum(far_high, axis=0, keepdims=True)
        ends = jnp.where(side == BUCKETS // 2 - 1, low_line, 0.0) + jnp.where(
            side == BUCKETS - 1, high_line, 0.0
        )
        by_bucket = by_bucket[:, :128] + by_bucket[:, 128:] + ends
        total = jnp.sum(by_bucket, axis=1, keepdims=True)
        bias_grad = bias_grad + jnp.where(bias_lanes == EXPERTS + 1 + head, total, 0.0)
    query_low = jnp.concatenate(query_grads, axis=0).astype(BF16)
    key_low = key_grad.astype(BF16)
    value_low = value_grad.astype(BF16)
    normed = normed_ref[...]
    for i, low in enumerate((query_low, key_low, value_low)):
        grads_ref[pl.ds(i * WIDTH, WIDTH), :D] = dot_tn(low, normed).astype(BF16)
    rest = dot_tn(mixed_ref[...], logit_s[...]) + dot(stretch_ref[...], bias_grad.astype(BF16))
    column = jnp.transpose(jnp.broadcast_to(gain_grad, (128, D)))
    lanes = lax.broadcasted_iota(jnp.int32, (D, 128), 1)
    grads_ref[:, D:] = jnp.where(lanes == EXPERTS, column, rest).astype(BF16)
    wide_s[...] = (
        dot(query_low, wq_ref[...]) + dot(key_low, wk_ref[...]) + dot(value_low, wv_ref[...])
    )
    gain_one = jnp.zeros((8, D), F32)
    for i in range(SEQ // 32):
        rows = slice(i * 32, i * 32 + 32)
        normed_part = wide_s[rows, :]
        normed_s[rows, :] = normed_part.astype(BF16)
        hidden = x_ref[rows, :].astype(F32)
        scale = stats_ref[rows, 0:1]
        gain_one = gain_one + jnp.sum((normed_part * hidden * scale).reshape(4, 8, D), axis=0)
    gain_rows = jnp.broadcast_to(jnp.sum(gain_one, axis=0, keepdims=True), (16, D)).astype(BF16)
    for out, start in ((mine_ref, core * 256), (theirs_ref, (1 - core) * 256)):
        out[:256, :] = normed_s[pl.ds(pl.multiple_of(start, 256), 256), :]
        out[256:, :] = gain_rows
    output_copy.wait()
    middle_copy.wait()


def halves(core, own_ref, other_ref, i):
    local = slice((i % 2) * 128, (i % 2) * 128 + 128)
    return jnp.where(core == i // 2, own_ref[local, :], other_ref[local, :]).astype(F32)


def reduce_kernel(parts_ref, halved_ref, link_ref, old_hbm, send_ref):
    extra = pl.ds(256, 16)
    gain_grad = (halved_ref[extra, :].astype(F32) + link_ref[extra, :].astype(F32))[0:1]
    total = jnp.zeros((24, GRADS), F32)
    for j in range(GROUPS // 2):
        pair = parts_ref[pl.ds(j * 48, 48), :].astype(F32)
        total = total + pair[:24] + pair[24:]
    lines = [
        pltpu.roll(gain_grad[:, r // 4 * 128 : r // 4 * 128 + 128], (96 - r % 4 * 32) % 128, 1)
        for r in range(24)
    ]
    lanes = lax.broadcasted_iota(jnp.int32, (24, 128), 1)
    last = jnp.where(lanes < 96, total[:, D:], jnp.concatenate(lines, axis=0))
    chunk = jnp.concatenate([total[:, :D], last], axis=1)
    pair = jnp.concatenate([chunk, chunk], axis=0).astype(BF16)
    for j in range(GROUPS // 2):
        send_ref[pl.ds(j * 48, 48), :] = pair


def input_kernel(place_ref, own_ref, other_ref, x_ref, gain_ref, middle_grad_ref, input_ref):
    core = place_ref[1]
    gain = gain_ref[...]
    for i in range(4):
        rows = slice(i * 128, i * 128 + 128)
        hidden = x_ref[rows, :].astype(F32)
        scale = lax.rsqrt(jnp.mean(hidden * hidden, axis=-1, keepdims=True) + EPS)
        weighted = halves(core, own_ref, other_ref, i) * gain
        inner = jnp.mean(weighted * hidden, axis=-1, keepdims=True)
        input_ref[rows, :] = (
            middle_grad_ref[rows, :]
            + scale * weighted
            - hidden * (scale * scale * scale * inner)
        )


def finish_kernel(
    recv_ref, stretch_ref, gain_one_ref, gain_two_ref, bias_ref,
    q_ref, k_ref, v_ref, o_ref, router_ref,
):
    for i, out in enumerate((q_ref, k_ref, v_ref, o_ref)):
        out[...] = recv_ref[pl.ds(i * WIDTH, WIDTH), :D].astype(F32)
    last = recv_ref[:, D:].astype(F32)
    summed = jnp.zeros((24, 128), F32)
    for j in range(GROUPS):
        summed = summed + last[j * 24 : j * 24 + 24]
    lanes = lax.broadcasted_iota(jnp.int32, (1, 128), 1)
    for block in range(6):
        line = jnp.zeros((1, 128), F32)
        for i in range(4):
            r = block * 4 + i
            piece = pltpu.roll(summed[r : r + 1], (32 + 32 * i) % 128, 1)
            line = jnp.where((lanes >= 32 * i) & (lanes < 32 * i + 32), piece, line)
        gain_one_ref[pl.ds(block * 128, 128)] = line[0]
    turned = jnp.transpose(last)
    router_ref[...] = turned[:EXPERTS]
    tail = turned[EXPERTS : EXPERTS + 8]
    gain_two_ref[...] = tail[0]
    bias_ref[...] = dot(tail.astype(BF16), stretch_ref[...])[1 : 1 + HEADS_HERE]


def shards(
    layer_input, attn_gain, query_weight, key_weight, value_weight, output_weight, position_bias,
    moe_gain, router_weight, expert_in, expert_out, route_expert, route_slot, route_drop, out_grad,
):
    experts_axis = ("z", "x", "h")
    pair_axis = ("l", "z", "x", "h")
    core = lax.axis_index("c")
    place = jnp.stack([lax.axis_index("l") * 2 + core, core]).astype(jnp.int32)

    def swap(array, axis):
        return lax.ppermute(array, axis, [(0, 1), (1, 0)])

    gain_one = attn_gain.reshape(1, D)
    gain_two = moe_gain.reshape(1, D)
    zeros = jnp.zeros_like(route_drop)
    route = jnp.stack([route_expert, route_slot, route_drop] + [zeros] * 5)
    table = jnp.transpose(position_bias)
    wq, wk, wv = (jnp.transpose(w) for w in (query_weight, key_weight, value_weight))
    router = jnp.pad(jnp.transpose(router_weight), ((0, 128 - EXPERTS), (0, 0)))
    wo_link = swap(output_weight, "l")
    wo_core = swap(output_weight, "c")
    wo_far = swap(wo_link, "c")

    tall = shape((SEQ, WIDTH), BF16)
    wide = shape((SEQ, D), BF16)
    tile_shape = (3 * HEADS_HERE, 128, 128)
    weight_vmem = pltpu.VMEM((WIDTH, D), BF16)
    tall_vmem = pltpu.VMEM((SEQ, WIDTH), BF16)
    normed, queries, keys, values, tiles, context, lse = call(
        attention_forward,
        (wide, tall, tall, tall, shape(tile_shape, F32), tall, shape((8, SEQ), F32)),
        (table, layer_input, attn_gain, wq, wk, wv),
        far=(0, 1, 2, 3, 4, 5), far_out=(0, 1, 2, 3, 4),
        scratch=(pltpu.VMEM((HEADS_HERE, BUCKETS), F32), pltpu.VMEM((SEQ, D), BF16),
                 pltpu.VMEM((D,), F32), weight_vmem, weight_vmem, weight_vmem, pltpu.VMEM((SEQ, D), BF16),
                 tall_vmem, tall_vmem, tall_vmem, pltpu.VMEM(tile_shape, F32),
                 pltpu.SemaphoreType.DMA((11,))),
        limit=60, flops=900_000_000, moved=5_000_000,
    )
    flat, flat_t = shape((ROWS, SEQ), BF16), shape((SEQ, ROWS), BF16)
    sums = shape((ROWS, HALF), BF16)
    ctx_link = swap(context, "l")
    ctx_core = swap(context, "c")
    low_place, high_place, base, raw = call(
        near_kernel, (flat, flat, shape((SEQ, D), F32), sums),
        (place, route, context, ctx_core, output_weight, wo_core, out_grad),
        scalars=1, limit=16, flops=1_500_000_000, moved=7_000_000,
    )
    ctx_link_late, low_place = lax.optimization_barrier((ctx_link, low_place))
    ctx_far = swap(ctx_link_late, "c")
    middle, mixed, probs, send = call(
        middle_kernel,
        (shape((SEQ, D), F32), wide, shape((SEQ, 128), F32), sums),
        (place, layer_input, base, ctx_link, ctx_far, wo_link, wo_far, gain_two, router, route,
         low_place, high_place, raw),
        scratch=(pltpu.VMEM((SEQ, D), F32), pltpu.VMEM((SEQ, 128), BF16)),
        scalars=1, limit=16, flops=1_700_000_000, moved=8_000_000,
    )
    received = lax.all_to_all(send, experts_axis, 0, 0, tiled=True)
    received, route_late = lax.optimization_barrier((received, route))
    low_back, high_back = call(
        back_place_kernel, (flat_t, flat_t), (route_late,),
        limit=12, flops=10_000_000, moved=2_700_000,
    )
    select = regroup_matrix()
    forward_select = jnp.asarray(select, BF16)
    back_select = jnp.asarray(select.T, BF16)
    low = shape((2, 320, D), BF16)
    own_sorted, own_product = call(
        own_expert_kernel, (low, shape((2, 320, D), F32)),
        (place, received, expert_in, expert_out, forward_select),
        scalars=1, limit=14, flops=1_400_000_000, moved=9_000_000,
    )
    received_other, low_back, high_back, own_product = lax.optimization_barrier(
        (swap(received, "c"), low_back, high_back, own_product)
    )
    theirs, other_sorted, act, pre_grad = call(
        first_expert_kernel, (sums, low, low, low),
        (place, received_other, own_product, expert_in, expert_out, forward_select, back_select),
        scratch=(pltpu.VMEM((2, 320, D), F32), pltpu.VMEM((2, 320, D), BF16)),
        scalars=1, limit=20, flops=2_400_000_000, moved=12_000_000,
    )
    mine = call(
        second_expert_kernel, sums,
        (place, act, pre_grad, expert_in, expert_out, back_select),
        scratch=(pltpu.VMEM((2, 320, D), BF16),),
        scalars=1, limit=12, flops=1_000_000_000, moved=4_000_000,
    )
    partial = (mine.astype(F32) + swap(theirs, "c").astype(F32)).astype(BF16)
    back = lax.all_to_all(
        jnp.concatenate([partial, partial], axis=0), pair_axis, 0, 0, tiled=True
    )
    rows_own = call(
        tokens_kernel, shape((SEQ, D), BF16), (low_back, high_back, back),
        limit=12, flops=2_000_000_000, moved=3_000_000,
    )
    rows_own, queries_late, middle_late = lax.optimization_barrier((rows_own, queries, middle))
    weights, stats = call(
        window_kernel, (shape((HEADS_HERE, 2, SEQ, 256), BF16), shape((SEQ, 128), F32)),
        (table, queries_late, keys, lse, tiles, layer_input, middle_late, probs, route),
        limit=14, flops=300_000_000, moved=6_000_000,
    )
    rows_other, stats = lax.optimization_barrier((swap(rows_own, "c"), stats))
    stretch = np.zeros((D, BUCKETS), np.float32)
    stretch[24 * np.arange(BUCKETS), np.arange(BUCKETS)] = 1
    half = shape((256 + 16, D), BF16)
    layer_output, middle_grad, grads, norm_mine, norm_theirs = call(
        backward_kernel,
        (wide, shape((SEQ, D), F32), shape((D, GRADS), BF16), half, half),
        (place, layer_input, middle, mixed, probs, route, out_grad,
         rows_own, rows_other, router, gain_two, output_weight, context, queries, keys,
         values, normed, weights, stats, wq, wk, wv, jnp.asarray(stretch, BF16)),
        scratch=(pltpu.VMEM((SEQ, D), BF16), pltpu.VMEM((SEQ, 128), BF16),
                 pltpu.VMEM((SEQ, D), BF16), pltpu.VMEM((SEQ, D), F32),
                 pltpu.VMEM((SEQ, D), BF16), pltpu.VMEM((SEQ, D), F32),
                 pltpu.SemaphoreType.DMA((2,))),
        far_out=(0, 1),
        scalars=1, limit=24, flops=4_000_000_000, moved=12_000_000,
    )
    halved = (norm_mine.astype(F32) + swap(norm_theirs, "c").astype(F32)).astype(BF16)
    scattered = lax.all_to_all(grads, experts_axis, 0, 0, tiled=True)
    halved_link = swap(halved, "l")
    reduced = (halved.astype(F32) + halved_link.astype(F32)).astype(BF16)
    reduced_other = swap(reduced, "c")
    spread = call(
        reduce_kernel, shape((D, GRADS), BF16),
        (scattered, halved, halved_link, grads),
        far=(3,), alias={3: 0}, limit=12, flops=10_000_000, moved=3_000_000,
    )
    spread, own_sorted, other_sorted, act, pre_grad = lax.optimization_barrier(
        (spread, own_sorted, other_sorted, act, pre_grad)
    )
    expert_in_grad, expert_out_grad = expert_grads(
        place, own_sorted, other_sorted, act, pre_grad
    )
    gathered = lax.all_to_all(spread, experts_axis, 0, 0, tiled=True)
    input_grad = call(
        input_kernel, shape((SEQ, D), F32),
        (place, reduced, reduced_other, layer_input, gain_one, middle_grad),
        alias={5: 0}, scalars=1, limit=12, flops=10_000_000, moved=5_000_000,
    )
    out = shape((WIDTH, D), F32)
    line = shape((D,), F32)
    gain_one_grad, gain_two_grad, bias_grad, query_grad, key_grad, value_grad, output_grad, \
        router_grad = call(
            finish_kernel,
            (line, line, shape((HEADS_HERE, BUCKETS), F32), out, out, out, out,
             shape((EXPERTS, D), F32)),
            (gathered, jnp.asarray(stretch, BF16)),
            limit=12, flops=10_000_000, moved=6_000_000,
        )
    return (
        layer_output,
        input_grad,
        gain_one_grad,
        jnp.transpose(query_grad),
        jnp.transpose(key_grad),
        jnp.transpose(value_grad),
        output_grad,
        jnp.transpose(bias_grad),
        gain_two_grad,
        jnp.transpose(router_grad),
        expert_in_grad,
        expert_out_grad,
    )


def solution(mesh):
    fine = Mesh(mesh.devices.reshape(4, 4, 2, 2, 2), ("z", "x", "h", "l", "c"))
    ex = ("z", "x", "h")
    te = ("l", "c")
    in_specs = (
        P(ex, None), P(), P(None, te), P(None, te), P(None, te), P(te, None), P(None, te), P(),
        P(), P(ex, None, te), P(ex, te, None), P(ex), P(ex), P(ex), P(ex, None),
    )
    out_specs = (
        P(ex, None), P(ex, None), P(), P(None, te), P(None, te), P(None, te), P(te, None),
        P(None, te), P(), P(), P(ex, None, te), P(ex, te, None),
    )
    return jax.shard_map(shards, mesh=fine, in_specs=in_specs, out_specs=out_specs, check_vma=False)
```

```python
import jax
import jax.numpy as jnp
import numpy as np
from jax import lax
from jax.experimental import pallas as pl
from jax.experimental.pallas import tpu as pltpu
from jax.sharding import Mesh
from jax.sharding import PartitionSpec as P

BUCKETS = 32
EPS = 1e-06
SEQ = 512
D = 768
HEAD = 64
HEADS_HERE = 3
WIDTH = HEADS_HERE * HEAD
EXPERTS = 64
CAP = 10
GROUPS = 32
CHUNK = 40
ROWS = GROUPS * CHUNK
HALF = D // 2
GRADS = 896
F32 = jnp.float32
BF16 = jnp.bfloat16
GELU_C = float(np.sqrt(2.0 / np.pi))


def bucket_of(offsets):
    half_count = BUCKETS // 2
    exact_count = half_count // 2
    upper_side = (offsets > 0).astype(np.int64) * half_count
    distance = np.abs(offsets)
    ratio = np.log(np.maximum(distance, 1) / exact_count) / np.log(128.0 / exact_count)
    far_bucket = np.minimum(
        exact_count + (ratio * (half_count - exact_count)).astype(np.int64), half_count - 1
    )
    return upper_side + np.where(distance < exact_count, distance, far_bucket)


FAR_STARTS = [
    int(np.argmax(bucket_of(-np.arange(256)) >= b)) for b in range(9, BUCKETS // 2)
]


def line_buckets(block, rows):
    offset = 128 * block + 128 - lax.broadcasted_iota(jnp.int32, (rows, 256), 1)
    distance = jnp.abs(offset)
    far = jnp.full((rows, 256), 8, jnp.int32)
    for start in FAR_STARTS:
        far = far + (distance >= start).astype(jnp.int32)
    bucket = jnp.where(distance < 8, distance, far)
    return jnp.where(offset > 0, bucket + BUCKETS // 2, bucket)


def regroup_matrix():
    sel = np.zeros((320, 320), np.float32)
    for g in range(8):
        for half in range(2):
            for e in range(2):
                for c in range(CAP):
                    sel[half * 160 + e * 80 + g * 10 + c, g * 40 + half * 20 + e * 10 + c] = 1
    return sel


def dot(a, b):
    return jnp.dot(a, b, preferred_element_type=F32)


def dot_nt(a, b):
    return lax.dot_general(a, b, (((1,), (1,)), ((), ())), preferred_element_type=F32)


def dot_tn(a, b):
    return lax.dot_general(a, b, (((0,), (0,)), ((), ())), preferred_element_type=F32)


def head_mask(head, rows):
    lanes = lax.broadcasted_iota(jnp.int32, (rows, WIDTH), 1)
    return (lanes >= head * HEAD) & (lanes < (head + 1) * HEAD)


def only_head(matrix, head):
    return jnp.where(head_mask(head, matrix.shape[0]), matrix, jnp.zeros_like(matrix))


def call(
    body, out_shape, args, scratch=(), scalars=0, far=(), far_out=(), alias=None, limit=40, flops=0, moved=0
):
    spaces = [pltpu.SMEM] * scalars + [pltpu.VMEM] * (len(args) - scalars)
    for i in far:
        spaces[i] = pltpu.HBM
    outs = out_shape if isinstance(out_shape, tuple) else (out_shape,)
    out_spaces = [pltpu.HBM if i in far_out else pltpu.VMEM for i in range(len(outs))]
    result = pl.pallas_call(
        body,
        out_shape=outs,
        in_specs=[pl.BlockSpec(memory_space=space) for space in spaces],
        out_specs=tuple(pl.BlockSpec(memory_space=space) for space in out_spaces),
        scratch_shapes=scratch,
        input_output_aliases=alias or {},
        compiler_params=pltpu.CompilerParams(vmem_limit_bytes=limit << 20),
        cost_estimate=pl.CostEstimate(flops=flops, bytes_accessed=moved, transcendentals=0),
    )(*args)
    return result if isinstance(out_shape, tuple) else result[0]


def shape(dims, dtype):
    return jax.ShapeDtypeStruct(dims, dtype)


def bias_tile(tiles_ref, far_low, far_high, head, block):
    if block < -1:
        return far_low
    if block > 1:
        return far_high
    return tiles_ref[head * 3 + block + 1]


def scores_t(keys, query_scaled, tiles_ref, table, head, part):
    raw = dot_nt(keys, query_scaled)
    far_low = table[head : head + 1, BUCKETS // 2 - 1 : BUCKETS // 2]
    far_high = table[head : head + 1, BUCKETS - 1 : BUCKETS]
    rows = []
    for key_block in range(4):
        cols = []
        for i in range(2):
            piece = raw[key_block * 128 : key_block * 128 + 128, i * 128 : i * 128 + 128]
            block = key_block - (part * 2 + i)
            cols.append(piece + bias_tile(tiles_ref, far_low, far_high, head, block))
        rows.append(jnp.concatenate(cols, axis=1))
    return jnp.concatenate(rows, axis=0)


def attention_forward(
    table_hbm, x_hbm, gain_hbm, wq_hbm, wk_hbm, wv_hbm,
    normed_hbm, q_hbm, k_hbm, v_hbm, tiles_hbm, ctx_ref, lse_ref,
    table_ref, x_ref, gain_ref, wq_ref, wk_ref, wv_ref, normed_ref, q_ref, k_ref, v_ref,
    tiles_ref, sems,
):
    loads = [
        pltpu.make_async_copy(src, dst, sems.at[i])
        for i, (src, dst) in enumerate(
            (
                (table_hbm, table_ref), (x_hbm, x_ref), (wq_hbm, wq_ref), (wk_hbm, wk_ref),
                (wv_hbm, wv_ref), (gain_hbm, gain_ref),
            )
        )
    ]
    for load in loads:
        load.start()
    stores = []

    def store(src, dst):
        copy = pltpu.make_async_copy(src, dst, sems.at[6 + len(stores)])
        copy.start()
        stores.append(copy)

    loads[0].wait()
    table = table_ref[...]
    lines = []
    for block in (-1, 0, 1):
        buckets = lax.broadcasted_iota(jnp.int32, (BUCKETS, 256), 0)
        hot = (buckets == line_buckets(block, 1)).astype(F32)
        lines.append(
            jnp.dot(table, hot, precision=lax.Precision.HIGHEST, preferred_element_type=F32)
        )
    for head in range(HEADS_HERE):
        for block in range(3):
            wide = pltpu.roll(
                jnp.broadcast_to(lines[block][head : head + 1], (128, 256)),
                0, 1, stride=1, stride_axis=0,
            )
            tiles_ref[head * 3 + block] = wide[:, 128:]
    store(tiles_ref, tiles_hbm)
    loads[1].wait()
    loads[5].wait()
    gain = gain_ref[...].reshape(1, D)
    for i in range(SEQ // 32):
        rows = pl.ds(i * 32, 32)
        x = x_ref[rows, :].astype(F32)
        scale = lax.rsqrt(jnp.mean(x * x, axis=-1, keepdims=True) + EPS)
        normed_ref[rows, :] = (x * scale * gain).astype(BF16)
    store(normed_ref, normed_hbm)
    normed = normed_ref[...]
    for load, weight, out, out_hbm in (
        (loads[2], wq_ref, q_ref, q_hbm),
        (loads[3], wk_ref, k_ref, k_hbm),
        (loads[4], wv_ref, v_ref, v_hbm),
    ):
        load.wait()
        out[...] = dot_nt(normed, weight[...]).astype(BF16)
        store(out, out_hbm)
    queries, keys, values = q_ref[...], k_ref[...], v_ref[...]
    lse_ref[...] = jnp.zeros((8, SEQ), F32)
    scaled = queries * jnp.asarray(HEAD**-0.5, BF16)
    for part in range(2):
        rows = slice(part * 256, part * 256 + 256)
        context = jnp.zeros((256, WIDTH), F32)
        for head in range(HEADS_HERE):
            scores = scores_t(keys, only_head(scaled[rows], head), tiles_ref, table, head, part)
            top = jnp.max(scores, axis=0, keepdims=True)
            grown = jnp.exp(scores - top)
            total = jnp.sum(grown, axis=0, keepdims=True)
            probs = (grown * (1.0 / total)).astype(BF16)
            lse_ref[head : head + 1, rows] = top + jnp.log(total)
            context = context + dot_tn(probs, only_head(values, head))
        ctx_ref[rows, :] = context.astype(BF16)
    for copy in stores:
        copy.wait()


def route_columns(route_ref):
    return jnp.transpose(route_ref[...].astype(F32))


def row_of(expert, slot, drop):
    row = (expert >> 1) * CHUNK + (expert & 1) * CAP + slot
    return jnp.where(drop > 0, -1000, row)


def near_kernel(
    place_ref, route_ref, ctx0, ctx1, wo0, wo1, grad_ref, low_ref, high_ref, base_ref, raw_ref
):
    target = row_of(route_ref[0:1, :], route_ref[1:2, :], route_ref[2:3, :])
    for i in range(4):
        rows = pl.ds(i * 320, 320)
        index = lax.broadcasted_iota(jnp.int32, (320, SEQ), 0) + 320 * i
        low = (index == target).astype(F32).astype(BF16)
        high = (index == target + 20).astype(F32).astype(BF16)
        low_ref[rows, :] = low
        high_ref[rows, :] = high
        raw = dot(low, grad_ref[:, :HALF]) + dot(high, grad_ref[:, HALF:])
        raw_ref[rows, :] = raw.astype(BF16)
    pair_of_heads(place_ref[1], ctx0, ctx1, wo0, wo1, base_ref)


def pair_of_heads(core, ctx0, ctx1, wo0, wo1, sum_ref):
    @pl.when(core == 0)
    def _():
        sum_ref[...] = dot(ctx0[...], wo0[...]) + dot(ctx1[...], wo1[...])

    @pl.when(core == 1)
    def _():
        sum_ref[...] = dot(ctx1[...], wo1[...]) + dot(ctx0[...], wo0[...])


def back_place_kernel(route_ref, low_ref, high_ref):
    columns = route_columns(route_ref).astype(jnp.int32)
    target = row_of(columns[:, 0:1], columns[:, 1:2], columns[:, 2:3])
    for i in range(4):
        rows = slice(i * 128, i * 128 + 128)
        index = lax.broadcasted_iota(jnp.int32, (128, ROWS), 1)
        low_ref[rows, :] = (index == target[rows]).astype(F32).astype(BF16)
        high_ref[rows, :] = (index == target[rows] + 20).astype(F32).astype(BF16)


def middle_kernel(
    place_ref, x_ref, base_ref, ctx2, ctx3, wo2, wo3, gain_ref, router_ref, route_ref,
    low_ref, high_ref, raw_ref, middle_ref, mixed_ref, probs_ref, send_ref, far_s, gate_s,
):
    core = place_ref[1]
    columns = route_columns(route_ref)
    pair_of_heads(core, ctx2, ctx3, wo2, wo3, far_s)
    for i in range(SEQ // 32):
        rows = slice(i * 32, i * 32 + 32)
        middle = x_ref[rows, :].astype(F32) + (base_ref[rows, :] + far_s[rows, :])
        scale = lax.rsqrt(jnp.mean(middle * middle, axis=-1, keepdims=True) + EPS)
        middle_ref[rows, :] = middle
        mixed_ref[rows, :] = (middle * scale * gain_ref[...]).astype(BF16)
    for i in range(4):
        rows = slice(i * 128, i * 128 + 128)
        lanes = lax.broadcasted_iota(jnp.int32, (128, 128), 1)
        logits = dot_nt(mixed_ref[rows, :], router_ref[...])
        logits = jnp.where(lanes < EXPERTS, logits, -jnp.inf)
        grown = jnp.exp(logits - jnp.max(logits, axis=-1, keepdims=True))
        probs = grown / jnp.sum(grown, axis=-1, keepdims=True)
        probs_ref[rows, :] = probs
        expert = columns[rows, 0:1].astype(jnp.int32)
        chosen = jnp.sum(jnp.where(lanes == expert, probs, 0.0), axis=-1, keepdims=True)
        gate = chosen * (1.0 - columns[rows, 2:3])
        first = gate.astype(BF16).astype(F32)
        second = (gate - first).astype(BF16).astype(F32)
        third = gate - first - second
        pieces = jnp.where(lanes == 0, first, jnp.where(lanes == 1, second, third))
        gate_s[rows, :] = jnp.where(lanes < 3, pieces, 0.0).astype(BF16)

    @pl.when(core == 0)
    def _():
        for i in range(4):
            rows = pl.ds(i * 320, 320)
            out = dot(low_ref[rows, :], mixed_ref[:, :HALF])
            out = out + dot(high_ref[rows, :], mixed_ref[:, HALF:])
            send_ref[rows, :] = out.astype(BF16)

    @pl.when(core == 1)
    def _():
        for i in range(4):
            rows = pl.ds(i * 320, 320)
            gate = dot(low_ref[rows, :], gate_s[...]) + dot(high_ref[rows, :], gate_s[...])
            gate = jnp.sum(gate, axis=-1, keepdims=True)
            send_ref[rows, :] = (raw_ref[rows, :].astype(F32) * gate).astype(BF16)


def first_expert_kernel(
    place_ref, own_ref, other_ref, in_ref, out_ref, sel_ref, back_ref,
    theirs_ref, x_ref, s_ref, act_ref, pre_ref, part_s,
):
    core = place_ref[1]
    for b in range(4):
        rows = pl.ds(b * 320, 320)
        own = own_ref[rows, :]
        other = other_ref[rows, :]
        for dest, block in (
            (x_ref, jnp.where(core == 0, own, other)),
            (s_ref, jnp.where(core == 0, other, own)),
        ):
            sorted_rows = dot(sel_ref[...], block).astype(BF16)
            for half in range(2):
                for e in range(2):
                    dest[e, pl.ds(b * 80, 80), pl.ds(half * HALF, HALF)] = sorted_rows[
                        half * 160 + e * 80 : half * 160 + e * 80 + 80
                    ]
    for e in range(2):
        x = x_ref[e]
        s = s_ref[e]
        for f in range(3):
            cols = slice(f * 256, f * 256 + 256)
            pre = dot(x, in_ref[e, :, cols])
            bent = jnp.tanh(GELU_C * (pre + 0.044715 * (pre * pre * pre)))
            cdf = 0.5 * (1.0 + bent)
            act_ref[e, :, cols] = (pre * cdf).astype(BF16)
            slope = cdf + (0.5 * GELU_C) * pre * (1.0 - bent * bent) * (
                1.0 + (3 * 0.044715) * (pre * pre)
            )
            act_grad = dot_nt(s, out_ref[e, cols, :])
            pre_ref[e, :, cols] = (act_grad * slope).astype(BF16)
    expert_sums(core == 1, act_ref, pre_ref, in_ref, out_ref, back_ref, theirs_ref, part_s)


def expert_sums(forward, act_ref, pre_ref, in_ref, out_ref, back_ref, sum_ref, part_s):
    @pl.when(forward)
    def _():
        for e in range(2):
            part_s[e] = dot(act_ref[e], out_ref[e]).astype(BF16)

    @pl.when(jnp.logical_not(forward))
    def _():
        for e in range(2):
            part_s[e] = dot_nt(pre_ref[e], in_ref[e]).astype(BF16)

    for b in range(4):
        rows = pl.ds(b * 80, 80)
        stacked = jnp.concatenate(
            [part_s[e, rows, pl.ds(half * HALF, HALF)] for half in range(2) for e in range(2)],
            axis=0,
        )
        sum_ref[pl.ds(b * 320, 320), :] = dot(back_ref[...], stacked).astype(BF16)


def second_expert_kernel(
    place_ref, act_ref, pre_ref, in_ref, out_ref, back_ref, mine_ref, part_s
):
    expert_sums(
        place_ref[1] == 0, act_ref, pre_ref, in_ref, out_ref, back_ref, mine_ref, part_s
    )


def expert_grads_kernel(x_ref, s_ref, act_ref, pre_ref, in_grad_ref, out_grad_ref):
    out_grad_ref[0] = dot_tn(act_ref[0], s_ref[0])
    in_grad_ref[0] = dot_tn(x_ref[0], pre_ref[0])


def expert_grads(x, s, act, pre):
    whole = pl.BlockSpec((1, 320, D), lambda e, f: (e, 0, 0))
    part = pl.BlockSpec((1, 320, 256), lambda e, f: (e, 0, f))
    return pl.pallas_call(
        expert_grads_kernel,
        grid=(2, 3),
        out_shape=(shape((2, D, D), F32), shape((2, D, D), F32)),
        in_specs=[whole, whole, part, part],
        out_specs=(
            pl.BlockSpec((1, D, 256), lambda e, f: (e, 0, f)),
            pl.BlockSpec((1, 256, D), lambda e, f: (e, f, 0)),
        ),
        compiler_params=pltpu.CompilerParams(vmem_limit_bytes=24 << 20),
        cost_estimate=pl.CostEstimate(
            flops=8 * 320 * D * D, bytes_accessed=14_000_000, transcendentals=0
        ),
    )(x, s, act, pre)


def tokens_kernel(low_ref, high_ref, recv_ref, out_ref):
    slots = (
        recv_ref[pl.ds(0, ROWS), :].astype(F32) + recv_ref[pl.ds(ROWS, ROWS), :].astype(F32)
    ).astype(BF16)
    out_ref[:, pl.ds(0, HALF)] = dot(low_ref[...], slots).astype(BF16)
    out_ref[:, pl.ds(HALF, HALF)] = dot(high_ref[...], slots).astype(BF16)


def window_kernel(
    table_ref, q_ref, k_ref, lse_ref, tiles_ref, x_ref, middle_ref, probs_ref, route_ref,
    weights_ref, stats_ref,
):
    scaled = q_ref[...] * jnp.asarray(HEAD**-0.5, BF16)
    keys = k_ref[...]
    for head in range(HEADS_HERE):
        for part in range(2):
            rows = slice(part * 256, part * 256 + 256)
            scores = scores_t(
                keys, only_head(scaled[rows], head), tiles_ref, table_ref[...], head, part
            )
            weights_ref[head, part] = jnp.exp(scores - lse_ref[head : head + 1, rows]).astype(BF16)
    columns = route_columns(route_ref)
    for i in range(SEQ // 32):
        rows = slice(i * 32, i * 32 + 32)
        lanes = lax.broadcasted_iota(jnp.int32, (32, 128), 1)
        middle = middle_ref[rows, :]
        scale_two = lax.rsqrt(jnp.mean(middle * middle, axis=-1, keepdims=True) + EPS)
        hidden = x_ref[rows, :].astype(F32)
        scale_one = lax.rsqrt(jnp.mean(hidden * hidden, axis=-1, keepdims=True) + EPS)
        hot = lanes == columns[rows, 0:1].astype(jnp.int32)
        chosen = jnp.sum(jnp.where(hot, probs_ref[rows, :], 0.0), axis=-1, keepdims=True)
        stats_ref[rows, :] = jnp.where(
            lanes == 0, scale_one, jnp.where(lanes == 1, scale_two, chosen)
        )


def backward_kernel(
    place_ref, x_ref, middle_ref, mixed_ref, probs_ref, route_ref, grad_ref,
    own_ref, other_ref, router_ref, gain_ref, wo_ref, ctx_ref, q_ref, k_ref, v_ref, normed_ref,
    weights_ref, stats_ref, wq_ref, wk_ref, wv_ref, stretch_ref,
    output_hbm, middle_grad_hbm, grads_hbm, mine_ref, theirs_ref, gain_one_ref,
    low_s, logit_s, normed_s, wide_s, output_ref, middle_grad_ref, grads_ref, sems,
):
    core = place_ref[1]
    columns = route_columns(route_ref)
    gain = gain_ref[...]
    for i in range(SEQ // 32):
        rows = slice(i * 32, i * 32 + 32)
        expert_rows = jnp.where(core == 0, own_ref[rows, :], other_ref[rows, :]).astype(F32)
        probs = probs_ref[rows, :]
        kept = 1.0 - columns[rows, 2:3]
        lanes = lax.broadcasted_iota(jnp.int32, (32, 128), 1)
        hot = (lanes == columns[rows, 0:1].astype(jnp.int32)).astype(F32)
        chosen = stats_ref[rows, 2:3]
        upstream = grad_ref[rows, :].astype(F32)
        output_ref[rows, :] = (
            middle_ref[rows, :] + (chosen * kept) * expert_rows
        ).astype(BF16)
        gate_grad = jnp.sum(upstream * expert_rows, axis=-1, keepdims=True) * kept
        logit_s[rows, :] = (probs * (hot - chosen) * gate_grad).astype(BF16)
    output_copy = pltpu.make_async_copy(output_ref, output_hbm, sems.at[0])
    output_copy.start()
    wide_s[...] = dot(logit_s[...], router_ref[...])
    gain_grad = jnp.zeros((8, D), F32)
    for i in range(SEQ // 32):
        rows = slice(i * 32, i * 32 + 32)
        mixed_grad = jnp.where(core == 0, other_ref[rows, :], own_ref[rows, :]).astype(F32)
        mixed_grad = mixed_grad + wide_s[rows, :]
        middle = middle_ref[rows, :]
        scale = stats_ref[rows, 1:2]
        along = mixed_grad * middle
        inner = jnp.mean(along * gain, axis=-1, keepdims=True)
        gain_grad = gain_grad + jnp.sum((along * scale).reshape(4, 8, D), axis=0)
        middle_grad = (
            grad_ref[rows, :].astype(F32)
            + scale * (mixed_grad * gain)
            - middle * (scale * scale * scale * inner)
        )
        middle_grad_ref[rows, :] = middle_grad
        low_s[rows, :] = middle_grad.astype(BF16)
    gain_grad = jnp.sum(gain_grad, axis=0, keepdims=True)
    middle_copy = pltpu.make_async_copy(middle_grad_ref, middle_grad_hbm, sems.at[1])
    middle_copy.start()
    middle_low = low_s[...]
    grads_ref[pl.ds(3 * WIDTH, WIDTH), :D] = dot_tn(ctx_ref[...], middle_low).astype(BF16)
    ctx_grad = dot_nt(middle_low, wo_ref[...]).astype(BF16)

    values = v_ref[...]
    key_scaled = k_ref[...] * jnp.asarray(HEAD**-0.5, BF16)
    query_scaled = q_ref[...] * jnp.asarray(HEAD**-0.5, BF16)
    key_grad = jnp.zeros((SEQ, WIDTH), F32)
    value_grad = jnp.zeros((SEQ, WIDTH), F32)
    query_grads = [jnp.zeros((256, WIDTH), F32), jnp.zeros((256, WIDTH), F32)]
    buckets = lax.broadcasted_iota(jnp.int32, (BUCKETS, 256), 0)
    line_ids = [line_buckets(block, 1) for block in (-1, 0, 1)]
    bias_grad = jnp.zeros((BUCKETS, 128), F32)
    bias_lanes = lax.broadcasted_iota(jnp.int32, (BUCKETS, 128), 1)
    turn = (
        lax.broadcasted_iota(jnp.int32, (128, 128), 0)
        + lax.broadcasted_iota(jnp.int32, (128, 128), 1)
        == 127
    ).astype(F32)
    for head in range(HEADS_HERE):
        near = [jnp.zeros((128, 128), F32) for _ in range(3)]
        far_low = jnp.zeros((128, 128), F32)
        far_high = jnp.zeros((128, 128), F32)
        key_head = only_head(key_scaled, head)
        for part in range(2):
            rows = slice(part * 256, part * 256 + 256)
            query_head = only_head(query_scaled[rows], head)
            ctx_head = only_head(ctx_grad[rows], head)
            probs_low = weights_ref[head, part]
            probs = probs_low.astype(F32)
            value_grad = value_grad + dot(probs_low, ctx_head)
            prob_grad = dot_nt(values, ctx_head)
            inner = jnp.sum(probs * prob_grad, axis=0, keepdims=True)
            score_grad = (probs * (prob_grad - inner)).astype(BF16)
            key_grad = key_grad + dot(score_grad, query_head)
            query_grads[part] = query_grads[part] + dot_tn(score_grad, key_head)
            for key_block in range(4):
                for i in range(2):
                    piece = score_grad[
                        key_block * 128 : key_block * 128 + 128, i * 128 : i * 128 + 128
                    ].astype(F32)
                    block = key_block - (part * 2 + i)
                    if block < -1:
                        far_low = far_low + piece
                    elif block > 1:
                        far_high = far_high + piece
                    else:
                        near[block + 1] = near[block + 1] + piece
        by_bucket = jnp.zeros((BUCKETS, 256), F32)
        for block in range(3):
            turned = jnp.dot(
                turn, near[block], precision=lax.Precision.HIGHEST, preferred_element_type=F32
            )
            wide = jnp.concatenate([turned, jnp.zeros((128, 128), F32)], axis=1)
            wide = pltpu.roll(wide, 1, 1, stride=1, stride_axis=0)
            line = jnp.sum(wide, axis=0, keepdims=True)
            by_bucket = by_bucket + jnp.where(
                buckets == line_ids[block], line, 0.0
            )
        side = lax.broadcasted_iota(jnp.int32, (BUCKETS, 128), 0)
        low_line = jnp.sum(far_low, axis=0, keepdims=True)
        high_line = jnp.sum(far_high, axis=0, keepdims=True)
        ends = jnp.where(side == BUCKETS // 2 - 1, low_line, 0.0) + jnp.where(
            side == BUCKETS - 1, high_line, 0.0
        )
        by_bucket = by_bucket[:, :128] + by_bucket[:, 128:] + ends
        total = jnp.sum(by_bucket, axis=1, keepdims=True)
        bias_grad = bias_grad + jnp.where(bias_lanes == EXPERTS + 1 + head, total, 0.0)
    query_low = jnp.concatenate(query_grads, axis=0).astype(BF16)
    key_low = key_grad.astype(BF16)
    value_low = value_grad.astype(BF16)
    rest = dot_tn(mixed_ref[...], logit_s[...]) + dot(stretch_ref[...], bias_grad.astype(BF16))
    column = jnp.transpose(jnp.broadcast_to(gain_grad, (128, D)))
    lanes = lax.broadcasted_iota(jnp.int32, (D, 128), 1)
    grads_ref[:, D:] = jnp.where(lanes == EXPERTS, column, rest).astype(BF16)
    normed = normed_ref[...]
    copies = []
    for i, low in ((3, None), (0, query_low), (1, key_low), (2, value_low)):
        part = pl.ds(i * WIDTH, WIDTH)
        if low is not None:
            grads_ref[part, :D] = dot_tn(low, normed).astype(BF16)
        copies.append(
            pltpu.make_async_copy(grads_ref.at[part], grads_hbm.at[part], sems.at[2 + i])
        )
        copies[-1].start()
    wide_s[...] = (
        dot(query_low, wq_ref[...]) + dot(key_low, wk_ref[...]) + dot(value_low, wv_ref[...])
    )
    gain_one = jnp.zeros((8, D), F32)
    for i in range(SEQ // 32):
        rows = slice(i * 32, i * 32 + 32)
        normed_part = wide_s[rows, :]
        normed_s[rows, :] = normed_part.astype(BF16)
        hidden = x_ref[rows, :].astype(F32)
        scale = stats_ref[rows, 0:1]
        gain_one = gain_one + jnp.sum((normed_part * hidden * scale).reshape(4, 8, D), axis=0)
    gain_one_ref[...] = jnp.broadcast_to(jnp.sum(gain_one, axis=0, keepdims=True), (8, D))
    for out, start in ((mine_ref, core * 256), (theirs_ref, (1 - core) * 256)):
        out[...] = normed_s[pl.ds(pl.multiple_of(start, 256), 256), :]
    for copy in copies:
        copy.wait()
    output_copy.wait()
    middle_copy.wait()


def halves(core, own_ref, other_ref, i):
    local = slice((i % 2) * 128, (i % 2) * 128 + 128)
    return jnp.where(core == i // 2, own_ref[local, :], other_ref[local, :]).astype(F32)


def reduce_kernel(parts_ref, pair_ref, link_ref, old_hbm, send_ref):
    gain_grad = (pair_ref[0:1] + pair_ref[8:9]) + (link_ref[0:1] + link_ref[8:9])
    total = jnp.zeros((24, GRADS), F32)
    for j in range(GROUPS // 2):
        pair = parts_ref[pl.ds(j * 48, 48), :].astype(F32)
        total = total + pair[:24] + pair[24:]
    lines = [
        pltpu.roll(gain_grad[:, r // 4 * 128 : r // 4 * 128 + 128], (96 - r % 4 * 32) % 128, 1)
        for r in range(24)
    ]
    lanes = lax.broadcasted_iota(jnp.int32, (24, 128), 1)
    last = jnp.where(lanes < 96, total[:, D:], jnp.concatenate(lines, axis=0))
    chunk = jnp.concatenate([total[:, :D], last], axis=1)
    pair = jnp.concatenate([chunk, chunk], axis=0).astype(BF16)
    for j in range(GROUPS // 2):
        send_ref[pl.ds(j * 48, 48), :] = pair


def input_kernel(place_ref, own_ref, other_ref, x_ref, gain_ref, middle_grad_ref, input_ref):
    core = place_ref[1]
    gain = gain_ref[...]
    for i in range(4):
        rows = slice(i * 128, i * 128 + 128)
        hidden = x_ref[rows, :].astype(F32)
        scale = lax.rsqrt(jnp.mean(hidden * hidden, axis=-1, keepdims=True) + EPS)
        weighted = halves(core, own_ref, other_ref, i) * gain
        inner = jnp.mean(weighted * hidden, axis=-1, keepdims=True)
        input_ref[rows, :] = (
            middle_grad_ref[rows, :]
            + scale * weighted
            - hidden * (scale * scale * scale * inner)
        )


def finish_kernel(
    recv_ref, stretch_ref, gain_one_ref, gain_two_ref, bias_ref,
    q_ref, k_ref, v_ref, o_ref, router_ref,
):
    for i, out in enumerate((q_ref, k_ref, v_ref, o_ref)):
        out[...] = recv_ref[pl.ds(i * WIDTH, WIDTH), :D].astype(F32)
    last = recv_ref[:, D:].astype(F32)
    summed = jnp.zeros((24, 128), F32)
    for j in range(GROUPS):
        summed = summed + last[j * 24 : j * 24 + 24]
    lanes = lax.broadcasted_iota(jnp.int32, (1, 128), 1)
    for block in range(6):
        line = jnp.zeros((1, 128), F32)
        for i in range(4):
            r = block * 4 + i
            piece = pltpu.roll(summed[r : r + 1], (32 + 32 * i) % 128, 1)
            line = jnp.where((lanes >= 32 * i) & (lanes < 32 * i + 32), piece, line)
        gain_one_ref[pl.ds(block * 128, 128)] = line[0]
    turned = jnp.transpose(last)
    router_ref[...] = turned[:EXPERTS]
    tail = turned[EXPERTS : EXPERTS + 8]
    gain_two_ref[...] = tail[0]
    bias_ref[...] = dot(tail.astype(BF16), stretch_ref[...])[1 : 1 + HEADS_HERE]


def shards(
    layer_input, attn_gain, query_weight, key_weight, value_weight, output_weight, position_bias,
    moe_gain, router_weight, expert_in, expert_out, route_expert, route_slot, route_drop, out_grad,
):
    experts_axis = ("z", "x", "h")
    pair_axis = ("l", "z", "x", "h")
    core = lax.axis_index("c")
    place = jnp.stack([lax.axis_index("l") * 2 + core, core]).astype(jnp.int32)

    def swap(array, axis):
        return lax.ppermute(array, axis, [(0, 1), (1, 0)])

    gain_one = attn_gain.reshape(1, D)
    gain_two = moe_gain.reshape(1, D)
    zeros = jnp.zeros_like(route_drop)
    route = jnp.stack([route_expert, route_slot, route_drop] + [zeros] * 5)
    table = jnp.transpose(position_bias)
    wq, wk, wv = (jnp.transpose(w) for w in (query_weight, key_weight, value_weight))
    router = jnp.pad(jnp.transpose(router_weight), ((0, 128 - EXPERTS), (0, 0)))
    wo_link = swap(output_weight, "l")
    wo_core = swap(output_weight, "c")
    wo_far = swap(wo_link, "c")

    tall = shape((SEQ, WIDTH), BF16)
    wide = shape((SEQ, D), BF16)
    tile_shape = (3 * HEADS_HERE, 128, 128)
    weight_vmem = pltpu.VMEM((WIDTH, D), BF16)
    tall_vmem = pltpu.VMEM((SEQ, WIDTH), BF16)
    normed, queries, keys, values, tiles, context, lse = call(
        attention_forward,
        (wide, tall, tall, tall, shape(tile_shape, F32), tall, shape((8, SEQ), F32)),
        (table, layer_input, attn_gain, wq, wk, wv),
        far=(0, 1, 2, 3, 4, 5), far_out=(0, 1, 2, 3, 4),
        scratch=(pltpu.VMEM((HEADS_HERE, BUCKETS), F32), pltpu.VMEM((SEQ, D), BF16),
                 pltpu.VMEM((D,), F32), weight_vmem, weight_vmem, weight_vmem, pltpu.VMEM((SEQ, D), BF16),
                 tall_vmem, tall_vmem, tall_vmem, pltpu.VMEM(tile_shape, F32),
                 pltpu.SemaphoreType.DMA((11,))),
        limit=60, flops=900_000_000, moved=5_000_000,
    )
    flat, flat_t = shape((ROWS, SEQ), BF16), shape((SEQ, ROWS), BF16)
    sums = shape((ROWS, HALF), BF16)
    ctx_link = swap(context, "l")
    ctx_core = swap(context, "c")
    low_place, high_place, base, raw = call(
        near_kernel, (flat, flat, shape((SEQ, D), F32), sums),
        (place, route, context, ctx_core, output_weight, wo_core, out_grad),
        scalars=1, limit=16, flops=1_500_000_000, moved=7_000_000,
    )
    ctx_link_late, low_place = lax.optimization_barrier((ctx_link, low_place))
    ctx_far = swap(ctx_link_late, "c")
    middle, mixed, probs, send = call(
        middle_kernel,
        (shape((SEQ, D), F32), wide, shape((SEQ, 128), F32), sums),
        (place, layer_input, base, ctx_link, ctx_far, wo_link, wo_far, gain_two, router, route,
         low_place, high_place, raw),
        scratch=(pltpu.VMEM((SEQ, D), F32), pltpu.VMEM((SEQ, 128), BF16)),
        scalars=1, limit=16, flops=1_700_000_000, moved=8_000_000,
    )
    received = lax.all_to_all(send, experts_axis, 0, 0, tiled=True)
    received, route_late = lax.optimization_barrier((received, route))
    low_back, high_back = call(
        back_place_kernel, (flat_t, flat_t), (route_late,),
        limit=12, flops=10_000_000, moved=2_700_000,
    )
    received_other, low_back, high_back = lax.optimization_barrier(
        (swap(received, "c"), low_back, high_back)
    )
    select = regroup_matrix()
    low = shape((2, 320, D), BF16)
    back_select = jnp.asarray(select.T, BF16)
    theirs, slots, slot_grads, act, pre_grad = call(
        first_expert_kernel,
        (sums, low, low, low, low),
        (place, received, received_other, expert_in, expert_out,
         jnp.asarray(select, BF16), back_select),
        scratch=(pltpu.VMEM((2, 320, D), BF16),),
        scalars=1, limit=24, flops=4_000_000_000, moved=14_000_000,
    )
    mine = call(
        second_expert_kernel, sums,
        (place, act, pre_grad, expert_in, expert_out, back_select),
        scratch=(pltpu.VMEM((2, 320, D), BF16),),
        scalars=1, limit=12, flops=1_000_000_000, moved=4_000_000,
    )
    partial = (mine.astype(F32) + swap(theirs, "c").astype(F32)).astype(BF16)
    back = lax.all_to_all(
        jnp.concatenate([partial, partial], axis=0), pair_axis, 0, 0, tiled=True
    )
    rows_own = call(
        tokens_kernel, shape((SEQ, D), BF16), (low_back, high_back, back),
        limit=12, flops=2_000_000_000, moved=3_000_000,
    )
    rows_own, queries_late, middle_late = lax.optimization_barrier((rows_own, queries, middle))
    weights, stats = call(
        window_kernel, (shape((HEADS_HERE, 2, SEQ, 256), BF16), shape((SEQ, 128), F32)),
        (table, queries_late, keys, lse, tiles, layer_input, middle_late, probs, route),
        limit=14, flops=300_000_000, moved=6_000_000,
    )
    rows_other, stats = lax.optimization_barrier((swap(rows_own, "c"), stats))
    stretch = np.zeros((D, BUCKETS), np.float32)
    stretch[24 * np.arange(BUCKETS), np.arange(BUCKETS)] = 1
    half = shape((256, D), BF16)
    layer_output, middle_grad, grads, norm_mine, norm_theirs, gain_part = call(
        backward_kernel,
        (wide, shape((SEQ, D), F32), shape((D, GRADS), BF16), half, half, shape((8, D), F32)),
        (place, layer_input, middle, mixed, probs, route, out_grad,
         rows_own, rows_other, router, gain_two, output_weight, context, queries, keys,
         values, normed, weights, stats, wq, wk, wv, jnp.asarray(stretch, BF16)),
        scratch=(pltpu.VMEM((SEQ, D), BF16), pltpu.VMEM((SEQ, 128), BF16),
                 pltpu.VMEM((SEQ, D), BF16), pltpu.VMEM((SEQ, D), F32),
                 pltpu.VMEM((SEQ, D), BF16), pltpu.VMEM((SEQ, D), F32),
                 pltpu.VMEM((D, GRADS), BF16), pltpu.SemaphoreType.DMA((6,))),
        far_out=(0, 1, 2),
        scalars=1, limit=24, flops=4_000_000_000, moved=12_000_000,
    )
    halved = (norm_mine.astype(F32) + swap(norm_theirs, "c").astype(F32)).astype(BF16)
    gain_pair = jnp.concatenate([gain_part, swap(gain_part, "c")], axis=0)
    gain_pair, halved = lax.optimization_barrier((gain_pair, halved))
    scattered = lax.all_to_all(grads, experts_axis, 0, 0, tiled=True)
    gain_link = swap(gain_pair, "l")
    halved_link = swap(halved, "l")
    spread = call(
        reduce_kernel, shape((D, GRADS), BF16),
        (scattered, gain_pair, gain_link, grads),
        far=(3,), alias={3: 0}, limit=12, flops=10_000_000, moved=3_000_000,
    )
    halved_link, slots, slot_grads, act, pre_grad = lax.optimization_barrier(
        (halved_link, slots, slot_grads, act, pre_grad)
    )
    expert_in_grad, expert_out_grad = expert_grads(slots, slot_grads, act, pre_grad)
    reduced = (halved.astype(F32) + halved_link.astype(F32)).astype(BF16)
    reduced_other = swap(reduced, "c")
    gathered = lax.all_to_all(spread, experts_axis, 0, 0, tiled=True)
    input_grad = call(
        input_kernel, shape((SEQ, D), F32),
        (place, reduced, reduced_other, layer_input, gain_one, middle_grad),
        alias={5: 0}, scalars=1, limit=12, flops=10_000_000, moved=5_000_000,
    )
    out = shape((WIDTH, D), F32)
    line = shape((D,), F32)
    gain_one_grad, gain_two_grad, bias_grad, query_grad, key_grad, value_grad, output_grad, \
        router_grad = call(
            finish_kernel,
            (line, line, shape((HEADS_HERE, BUCKETS), F32), out, out, out, out,
             shape((EXPERTS, D), F32)),
            (gathered, jnp.asarray(stretch, BF16)),
            limit=12, flops=10_000_000, moved=6_000_000,
        )
    return (
        layer_output,
        input_grad,
        gain_one_grad,
        jnp.transpose(query_grad),
        jnp.transpose(key_grad),
        jnp.transpose(value_grad),
        output_grad,
        jnp.transpose(bias_grad),
        gain_two_grad,
        jnp.transpose(router_grad),
        expert_in_grad,
        expert_out_grad,
    )


def solution(mesh):
    fine = Mesh(mesh.devices.reshape(4, 4, 2, 2, 2), ("z", "x", "h", "l", "c"))
    ex = ("z", "x", "h")
    te = ("l", "c")
    in_specs = (
        P(ex, None), P(), P(None, te), P(None, te), P(None, te), P(te, None), P(None, te), P(),
        P(), P(ex, None, te), P(ex, te, None), P(ex), P(ex), P(ex), P(ex, None),
    )
    out_specs = (
        P(ex, None), P(ex, None), P(), P(None, te), P(None, te), P(None, te), P(te, None),
        P(None, te), P(), P(), P(ex, None, te), P(ex, te, None),
    )
    return jax.shard_map(shards, mesh=fine, in_specs=in_specs, out_specs=out_specs, check_vma=False)
```

```python
import jax
import jax.numpy as jnp
import numpy as np
from jax import lax
from jax.experimental import pallas as pl
from jax.experimental.pallas import tpu as pltpu
from jax.sharding import Mesh
from jax.sharding import PartitionSpec as P

BUCKETS = 32
EPS = 1e-06
SEQ = 512
D = 768
HEAD = 64
HEADS_HERE = 3
WIDTH = HEADS_HERE * HEAD
EXPERTS = 64
CAP = 10
GROUPS = 32
CHUNK = 40
ROWS = GROUPS * CHUNK
HALF = D // 2
GRADS = 896
F32 = jnp.float32
BF16 = jnp.bfloat16
GELU_C = float(np.sqrt(2.0 / np.pi))


def bucket_of(offsets):
    half_count = BUCKETS // 2
    exact_count = half_count // 2
    upper_side = (offsets > 0).astype(np.int64) * half_count
    distance = np.abs(offsets)
    ratio = np.log(np.maximum(distance, 1) / exact_count) / np.log(128.0 / exact_count)
    far_bucket = np.minimum(
        exact_count + (ratio * (half_count - exact_count)).astype(np.int64), half_count - 1
    )
    return upper_side + np.where(distance < exact_count, distance, far_bucket)


FAR_STARTS = [
    int(np.argmax(bucket_of(-np.arange(256)) >= b)) for b in range(9, BUCKETS // 2)
]


def line_buckets(block, rows):
    offset = 128 * block + 128 - lax.broadcasted_iota(jnp.int32, (rows, 256), 1)
    distance = jnp.abs(offset)
    far = jnp.full((rows, 256), 8, jnp.int32)
    for start in FAR_STARTS:
        far = far + (distance >= start).astype(jnp.int32)
    bucket = jnp.where(distance < 8, distance, far)
    return jnp.where(offset > 0, bucket + BUCKETS // 2, bucket)


def regroup_matrix():
    sel = np.zeros((320, 320), np.float32)
    for g in range(8):
        for half in range(2):
            for e in range(2):
                for c in range(CAP):
                    sel[half * 160 + e * 80 + g * 10 + c, g * 40 + half * 20 + e * 10 + c] = 1
    return sel


def dot(a, b):
    return jnp.dot(a, b, preferred_element_type=F32)


def dot_nt(a, b):
    return lax.dot_general(a, b, (((1,), (1,)), ((), ())), preferred_element_type=F32)


def dot_tn(a, b):
    return lax.dot_general(a, b, (((0,), (0,)), ((), ())), preferred_element_type=F32)


def head_mask(head, rows):
    lanes = lax.broadcasted_iota(jnp.int32, (rows, WIDTH), 1)
    return (lanes >= head * HEAD) & (lanes < (head + 1) * HEAD)


def only_head(matrix, head):
    return jnp.where(head_mask(head, matrix.shape[0]), matrix, jnp.zeros_like(matrix))


def call(
    body, out_shape, args, scratch=(), scalars=0, far=(), far_out=(), alias=None, limit=40, flops=0, moved=0
):
    spaces = [pltpu.SMEM] * scalars + [pltpu.VMEM] * (len(args) - scalars)
    for i in far:
        spaces[i] = pltpu.HBM
    outs = out_shape if isinstance(out_shape, tuple) else (out_shape,)
    out_spaces = [pltpu.HBM if i in far_out else pltpu.VMEM for i in range(len(outs))]
    result = pl.pallas_call(
        body,
        out_shape=outs,
        in_specs=[pl.BlockSpec(memory_space=space) for space in spaces],
        out_specs=tuple(pl.BlockSpec(memory_space=space) for space in out_spaces),
        scratch_shapes=scratch,
        input_output_aliases=alias or {},
        compiler_params=pltpu.CompilerParams(vmem_limit_bytes=limit << 20),
        cost_estimate=pl.CostEstimate(flops=flops, bytes_accessed=moved, transcendentals=0),
    )(*args)
    return result if isinstance(out_shape, tuple) else result[0]


def shape(dims, dtype):
    return jax.ShapeDtypeStruct(dims, dtype)


def bias_tile(tiles_ref, far_low, far_high, head, block):
    if block < -1:
        return far_low
    if block > 1:
        return far_high
    return tiles_ref[head * 3 + block + 1]


def scores_t(keys, query_scaled, tiles_ref, table, head, part):
    raw = dot_nt(keys, query_scaled)
    far_low = table[head : head + 1, BUCKETS // 2 - 1 : BUCKETS // 2]
    far_high = table[head : head + 1, BUCKETS - 1 : BUCKETS]
    rows = []
    for key_block in range(4):
        cols = []
        for i in range(2):
            piece = raw[key_block * 128 : key_block * 128 + 128, i * 128 : i * 128 + 128]
            block = key_block - (part * 2 + i)
            cols.append(piece + bias_tile(tiles_ref, far_low, far_high, head, block))
        rows.append(jnp.concatenate(cols, axis=1))
    return jnp.concatenate(rows, axis=0)


def attention_forward(
    table_hbm, x_hbm, gain_hbm, wq_hbm, wk_hbm, wv_hbm,
    normed_hbm, q_hbm, k_hbm, v_hbm, tiles_hbm, ctx_ref, lse_ref,
    table_ref, x_ref, gain_ref, wq_ref, wk_ref, wv_ref, normed_ref, q_ref, k_ref, v_ref,
    tiles_ref, sems,
):
    loads = [
        pltpu.make_async_copy(src, dst, sems.at[i])
        for i, (src, dst) in enumerate(
            (
                (table_hbm, table_ref), (x_hbm, x_ref), (wq_hbm, wq_ref), (wk_hbm, wk_ref),
                (wv_hbm, wv_ref), (gain_hbm, gain_ref),
            )
        )
    ]
    for load in loads:
        load.start()
    stores = []

    def store(src, dst):
        copy = pltpu.make_async_copy(src, dst, sems.at[6 + len(stores)])
        copy.start()
        stores.append(copy)

    loads[0].wait()
    table = table_ref[...]
    lines = []
    for block in (-1, 0, 1):
        buckets = lax.broadcasted_iota(jnp.int32, (BUCKETS, 256), 0)
        hot = (buckets == line_buckets(block, 1)).astype(F32)
        lines.append(
            jnp.dot(table, hot, precision=lax.Precision.HIGHEST, preferred_element_type=F32)
        )
    for head in range(HEADS_HERE):
        for block in range(3):
            wide = pltpu.roll(
                jnp.broadcast_to(lines[block][head : head + 1], (128, 256)),
                0, 1, stride=1, stride_axis=0,
            )
            tiles_ref[head * 3 + block] = wide[:, 128:]
    store(tiles_ref, tiles_hbm)
    loads[1].wait()
    loads[5].wait()
    gain = gain_ref[...].reshape(1, D)
    for i in range(SEQ // 32):
        rows = pl.ds(i * 32, 32)
        x = x_ref[rows, :].astype(F32)
        scale = lax.rsqrt(jnp.mean(x * x, axis=-1, keepdims=True) + EPS)
        normed_ref[rows, :] = (x * scale * gain).astype(BF16)
    store(normed_ref, normed_hbm)
    normed = normed_ref[...]
    for load, weight, out, out_hbm in (
        (loads[2], wq_ref, q_ref, q_hbm),
        (loads[3], wk_ref, k_ref, k_hbm),
        (loads[4], wv_ref, v_ref, v_hbm),
    ):
        load.wait()
        out[...] = dot_nt(normed, weight[...]).astype(BF16)
        store(out, out_hbm)
    queries, keys = q_ref[...], k_ref[...]
    values_t = jnp.transpose(v_ref[...])
    lse_ref[...] = jnp.zeros((8, SEQ), F32)
    scaled = queries * jnp.asarray(HEAD**-0.5, BF16)
    for part in range(2):
        rows = slice(part * 256, part * 256 + 256)
        context = []
        for head in range(HEADS_HERE):
            scores = scores_t(keys, only_head(scaled[rows], head), tiles_ref, table, head, part)
            top = jnp.max(scores, axis=0, keepdims=True)
            grown = jnp.exp(scores - top)
            total = jnp.sum(grown, axis=0, keepdims=True)
            probs = (grown * (1.0 / total)).astype(BF16)
            lse_ref[head : head + 1, rows] = top + jnp.log(total)
            context.append(dot(values_t[head * HEAD : (head + 1) * HEAD], probs))
        context = jnp.concatenate(context, axis=0).astype(BF16)
        ctx_ref[rows, :] = jnp.transpose(context)
    for copy in stores:
        copy.wait()


def route_columns(route_ref):
    return jnp.transpose(route_ref[...].astype(F32))


def row_of(expert, slot, drop):
    row = (expert >> 1) * CHUNK + (expert & 1) * CAP + slot
    return jnp.where(drop > 0, -1000, row)


def near_kernel(
    place_ref, route_ref, ctx0, ctx1, wo0, wo1, grad_ref, low_ref, high_ref, base_ref, raw_ref
):
    target = row_of(route_ref[0:1, :], route_ref[1:2, :], route_ref[2:3, :])
    for i in range(4):
        rows = pl.ds(i * 320, 320)
        index = lax.broadcasted_iota(jnp.int32, (320, SEQ), 0) + 320 * i
        low = (index == target).astype(F32).astype(BF16)
        high = (index == target + 20).astype(F32).astype(BF16)
        low_ref[rows, :] = low
        high_ref[rows, :] = high
        raw = dot(low, grad_ref[:, :HALF]) + dot(high, grad_ref[:, HALF:])
        raw_ref[rows, :] = raw.astype(BF16)
    pair_of_heads(place_ref[1], ctx0, ctx1, wo0, wo1, base_ref)


def pair_of_heads(core, ctx0, ctx1, wo0, wo1, sum_ref):
    @pl.when(core == 0)
    def _():
        sum_ref[...] = dot(ctx0[...], wo0[...]) + dot(ctx1[...], wo1[...])

    @pl.when(core == 1)
    def _():
        sum_ref[...] = dot(ctx1[...], wo1[...]) + dot(ctx0[...], wo0[...])


def back_place_kernel(route_ref, low_ref, high_ref):
    columns = route_columns(route_ref).astype(jnp.int32)
    target = row_of(columns[:, 0:1], columns[:, 1:2], columns[:, 2:3])
    for i in range(4):
        rows = slice(i * 128, i * 128 + 128)
        index = lax.broadcasted_iota(jnp.int32, (128, ROWS), 1)
        low_ref[rows, :] = (index == target[rows]).astype(F32).astype(BF16)
        high_ref[rows, :] = (index == target[rows] + 20).astype(F32).astype(BF16)


def middle_kernel(
    place_ref, x_ref, base_ref, ctx2, ctx3, wo2, wo3, gain_ref, router_ref, route_ref,
    low_ref, high_ref, raw_ref, middle_ref, mixed_ref, probs_ref, send_ref, far_s, gate_s,
):
    core = place_ref[1]
    columns = route_columns(route_ref)
    pair_of_heads(core, ctx2, ctx3, wo2, wo3, far_s)
    for i in range(SEQ // 32):
        rows = slice(i * 32, i * 32 + 32)
        middle = x_ref[rows, :].astype(F32) + (base_ref[rows, :] + far_s[rows, :])
        scale = lax.rsqrt(jnp.mean(middle * middle, axis=-1, keepdims=True) + EPS)
        middle_ref[rows, :] = middle
        mixed_ref[rows, :] = (middle * scale * gain_ref[...]).astype(BF16)
    for i in range(4):
        rows = slice(i * 128, i * 128 + 128)
        lanes = lax.broadcasted_iota(jnp.int32, (128, 128), 1)
        logits = dot_nt(mixed_ref[rows, :], router_ref[...])
        logits = jnp.where(lanes < EXPERTS, logits, -jnp.inf)
        grown = jnp.exp(logits - jnp.max(logits, axis=-1, keepdims=True))
        probs = grown / jnp.sum(grown, axis=-1, keepdims=True)
        probs_ref[rows, :] = probs
        expert = columns[rows, 0:1].astype(jnp.int32)
        chosen = jnp.sum(jnp.where(lanes == expert, probs, 0.0), axis=-1, keepdims=True)
        gate = chosen * (1.0 - columns[rows, 2:3])
        first = gate.astype(BF16).astype(F32)
        second = (gate - first).astype(BF16).astype(F32)
        third = gate - first - second
        pieces = jnp.where(lanes == 0, first, jnp.where(lanes == 1, second, third))
        gate_s[rows, :] = jnp.where(lanes < 3, pieces, 0.0).astype(BF16)

    @pl.when(core == 0)
    def _():
        for i in range(4):
            rows = pl.ds(i * 320, 320)
            out = dot(low_ref[rows, :], mixed_ref[:, :HALF])
            out = out + dot(high_ref[rows, :], mixed_ref[:, HALF:])
            send_ref[rows, :] = out.astype(BF16)

    @pl.when(core == 1)
    def _():
        for i in range(4):
            rows = pl.ds(i * 320, 320)
            gate = dot(low_ref[rows, :], gate_s[...]) + dot(high_ref[rows, :], gate_s[...])
            gate = jnp.sum(gate, axis=-1, keepdims=True)
            send_ref[rows, :] = (raw_ref[rows, :].astype(F32) * gate).astype(BF16)


def first_expert_kernel(
    place_ref, own_ref, other_ref, in_ref, out_ref, sel_ref, back_ref,
    theirs_ref, x_ref, s_ref, act_ref, pre_ref, part_s,
):
    core = place_ref[1]
    for b in range(4):
        rows = pl.ds(b * 320, 320)
        own = own_ref[rows, :]
        other = other_ref[rows, :]
        for dest, block in (
            (x_ref, jnp.where(core == 0, own, other)),
            (s_ref, jnp.where(core == 0, other, own)),
        ):
            sorted_rows = dot(sel_ref[...], block).astype(BF16)
            for half in range(2):
                for e in range(2):
                    dest[e, pl.ds(b * 80, 80), pl.ds(half * HALF, HALF)] = sorted_rows[
                        half * 160 + e * 80 : half * 160 + e * 80 + 80
                    ]
    for e in range(2):
        x = x_ref[e]
        s = s_ref[e]
        for f in range(3):
            cols = slice(f * 256, f * 256 + 256)
            pre = dot(x, in_ref[e, :, cols])
            bent = jnp.tanh(GELU_C * (pre + 0.044715 * (pre * pre * pre)))
            cdf = 0.5 * (1.0 + bent)
            act_ref[e, :, cols] = (pre * cdf).astype(BF16)
            slope = cdf + (0.5 * GELU_C) * pre * (1.0 - bent * bent) * (
                1.0 + (3 * 0.044715) * (pre * pre)
            )
            act_grad = dot_nt(s, out_ref[e, cols, :])
            pre_ref[e, :, cols] = (act_grad * slope).astype(BF16)
    expert_sums(core == 1, act_ref, pre_ref, in_ref, out_ref, back_ref, theirs_ref, part_s)


def expert_sums(forward, act_ref, pre_ref, in_ref, out_ref, back_ref, sum_ref, part_s):
    @pl.when(forward)
    def _():
        for e in range(2):
            part_s[e] = dot(act_ref[e], out_ref[e]).astype(BF16)

    @pl.when(jnp.logical_not(forward))
    def _():
        for e in range(2):
            part_s[e] = dot_nt(pre_ref[e], in_ref[e]).astype(BF16)

    for b in range(4):
        rows = pl.ds(b * 80, 80)
        stacked = jnp.concatenate(
            [part_s[e, rows, pl.ds(half * HALF, HALF)] for half in range(2) for e in range(2)],
            axis=0,
        )
        sum_ref[pl.ds(b * 320, 320), :] = dot(back_ref[...], stacked).astype(BF16)


def second_expert_kernel(
    place_ref, act_ref, pre_ref, in_ref, out_ref, back_ref, mine_ref, part_s
):
    expert_sums(
        place_ref[1] == 0, act_ref, pre_ref, in_ref, out_ref, back_ref, mine_ref, part_s
    )


def expert_grads_kernel(x_ref, s_ref, act_ref, pre_ref, in_grad_ref, out_grad_ref):
    out_grad_ref[0] = dot_tn(act_ref[0], s_ref[0])
    in_grad_ref[0] = dot_tn(x_ref[0], pre_ref[0])


def expert_grads(x, s, act, pre):
    whole = pl.BlockSpec((1, 320, D), lambda e, f: (e, 0, 0))
    part = pl.BlockSpec((1, 320, 256), lambda e, f: (e, 0, f))
    return pl.pallas_call(
        expert_grads_kernel,
        grid=(2, 3),
        out_shape=(shape((2, D, D), F32), shape((2, D, D), F32)),
        in_specs=[whole, whole, part, part],
        out_specs=(
            pl.BlockSpec((1, D, 256), lambda e, f: (e, 0, f)),
            pl.BlockSpec((1, 256, D), lambda e, f: (e, f, 0)),
        ),
        compiler_params=pltpu.CompilerParams(vmem_limit_bytes=24 << 20),
        cost_estimate=pl.CostEstimate(
            flops=8 * 320 * D * D, bytes_accessed=14_000_000, transcendentals=0
        ),
    )(x, s, act, pre)


def tokens_kernel(low_ref, high_ref, recv_ref, out_ref):
    slots = (
        recv_ref[pl.ds(0, ROWS), :].astype(F32) + recv_ref[pl.ds(ROWS, ROWS), :].astype(F32)
    ).astype(BF16)
    out_ref[:, pl.ds(0, HALF)] = dot(low_ref[...], slots).astype(BF16)
    out_ref[:, pl.ds(HALF, HALF)] = dot(high_ref[...], slots).astype(BF16)


def window_kernel(
    table_ref, q_ref, k_ref, lse_ref, tiles_ref, x_ref, middle_ref, probs_ref, route_ref,
    weights_ref, stats_ref,
):
    scaled = q_ref[...] * jnp.asarray(HEAD**-0.5, BF16)
    keys = k_ref[...]
    for head in range(HEADS_HERE):
        for part in range(2):
            rows = slice(part * 256, part * 256 + 256)
            scores = scores_t(
                keys, only_head(scaled[rows], head), tiles_ref, table_ref[...], head, part
            )
            weights_ref[head, part] = jnp.exp(scores - lse_ref[head : head + 1, rows]).astype(BF16)
    columns = route_columns(route_ref)
    for i in range(SEQ // 32):
        rows = slice(i * 32, i * 32 + 32)
        lanes = lax.broadcasted_iota(jnp.int32, (32, 128), 1)
        middle = middle_ref[rows, :]
        scale_two = lax.rsqrt(jnp.mean(middle * middle, axis=-1, keepdims=True) + EPS)
        hidden = x_ref[rows, :].astype(F32)
        scale_one = lax.rsqrt(jnp.mean(hidden * hidden, axis=-1, keepdims=True) + EPS)
        hot = lanes == columns[rows, 0:1].astype(jnp.int32)
        chosen = jnp.sum(jnp.where(hot, probs_ref[rows, :], 0.0), axis=-1, keepdims=True)
        stats_ref[rows, :] = jnp.where(
            lanes == 0, scale_one, jnp.where(lanes == 1, scale_two, chosen)
        )


def backward_kernel(
    place_ref, x_ref, middle_ref, mixed_ref, probs_ref, route_ref, grad_ref,
    own_ref, other_ref, router_ref, gain_ref, wo_ref, ctx_ref, q_ref, k_ref, v_ref, normed_ref,
    weights_ref, stats_ref, wq_ref, wk_ref, wv_ref,
    output_hbm, middle_grad_hbm, grads_ref, mine_ref, theirs_ref,
    low_s, logit_s, normed_s, wide_s, output_ref, middle_grad_ref, sems,
):
    core = place_ref[1]
    columns = route_columns(route_ref)
    gain = gain_ref[...]
    for i in range(SEQ // 32):
        rows = slice(i * 32, i * 32 + 32)
        expert_rows = jnp.where(core == 0, own_ref[rows, :], other_ref[rows, :]).astype(F32)
        probs = probs_ref[rows, :]
        kept = 1.0 - columns[rows, 2:3]
        lanes = lax.broadcasted_iota(jnp.int32, (32, 128), 1)
        hot = (lanes == columns[rows, 0:1].astype(jnp.int32)).astype(F32)
        chosen = stats_ref[rows, 2:3]
        upstream = grad_ref[rows, :].astype(F32)
        output_ref[rows, :] = (
            middle_ref[rows, :] + (chosen * kept) * expert_rows
        ).astype(BF16)
        gate_grad = jnp.sum(upstream * expert_rows, axis=-1, keepdims=True) * kept
        logit_s[rows, :] = (probs * (hot - chosen) * gate_grad).astype(BF16)
    output_copy = pltpu.make_async_copy(output_ref, output_hbm, sems.at[0])
    output_copy.start()
    wide_s[...] = dot(logit_s[...], router_ref[...])
    gain_grad = jnp.zeros((8, D), F32)
    for i in range(SEQ // 32):
        rows = slice(i * 32, i * 32 + 32)
        mixed_grad = jnp.where(core == 0, other_ref[rows, :], own_ref[rows, :]).astype(F32)
        mixed_grad = mixed_grad + wide_s[rows, :]
        middle = middle_ref[rows, :]
        scale = stats_ref[rows, 1:2]
        along = mixed_grad * middle
        inner = jnp.mean(along * gain, axis=-1, keepdims=True)
        gain_grad = gain_grad + jnp.sum((along * scale).reshape(4, 8, D), axis=0)
        middle_grad = (
            grad_ref[rows, :].astype(F32)
            + scale * (mixed_grad * gain)
            - middle * (scale * scale * scale * inner)
        )
        middle_grad_ref[rows, :] = middle_grad
        low_s[rows, :] = middle_grad.astype(BF16)
    gain_grad = jnp.sum(gain_grad, axis=0, keepdims=True)
    middle_copy = pltpu.make_async_copy(middle_grad_ref, middle_grad_hbm, sems.at[1])
    middle_copy.start()
    middle_low = low_s[...]
    grads_ref[pl.ds(3 * WIDTH, WIDTH), :D] = dot_tn(ctx_ref[...], middle_low).astype(BF16)
    ctx_grad = dot_nt(middle_low, wo_ref[...]).astype(BF16)

    values = v_ref[...]
    keys_t = jnp.transpose(k_ref[...] * jnp.asarray(HEAD**-0.5, BF16))
    query_scaled = q_ref[...] * jnp.asarray(HEAD**-0.5, BF16)
    key_grad = jnp.zeros((SEQ, WIDTH), F32)
    value_grad = jnp.zeros((SEQ, WIDTH), F32)
    query_grads = []
    buckets = lax.broadcasted_iota(jnp.int32, (BUCKETS, 256), 0)
    line_ids = [line_buckets(block, 1) for block in (-1, 0, 1)]
    bias_columns = []
    turn = (
        lax.broadcasted_iota(jnp.int32, (128, 128), 0)
        + lax.broadcasted_iota(jnp.int32, (128, 128), 1)
        == 127
    ).astype(F32)
    for head in range(HEADS_HERE):
        near = [jnp.zeros((128, 128), F32) for _ in range(3)]
        far_low = jnp.zeros((128, 128), F32)
        far_high = jnp.zeros((128, 128), F32)
        key_head = keys_t[head * HEAD : (head + 1) * HEAD]
        query_parts = []
        for part in range(2):
            rows = slice(part * 256, part * 256 + 256)
            query_head = only_head(query_scaled[rows], head)
            ctx_head = only_head(ctx_grad[rows], head)
            probs_low = weights_ref[head, part]
            probs = probs_low.astype(F32)
            value_grad = value_grad + dot(probs_low, ctx_head)
            prob_grad = dot_nt(values, ctx_head)
            inner = jnp.sum(probs * prob_grad, axis=0, keepdims=True)
            score_grad = (probs * (prob_grad - inner)).astype(BF16)
            key_grad = key_grad + dot(score_grad, query_head)
            query_parts.append(dot(key_head, score_grad))
            for key_block in range(4):
                for i in range(2):
                    piece = score_grad[
                        key_block * 128 : key_block * 128 + 128, i * 128 : i * 128 + 128
                    ].astype(F32)
                    block = key_block - (part * 2 + i)
                    if block < -1:
                        far_low = far_low + piece
                    elif block > 1:
                        far_high = far_high + piece
                    else:
                        near[block + 1] = near[block + 1] + piece
        query_grads.append(jnp.concatenate(query_parts, axis=1))
        by_bucket = jnp.zeros((BUCKETS, 256), F32)
        for block in range(3):
            turned = jnp.dot(
                turn, near[block], precision=lax.Precision.HIGHEST, preferred_element_type=F32
            )
            wide = jnp.concatenate([turned, jnp.zeros((128, 128), F32)], axis=1)
            wide = pltpu.roll(wide, 1, 1, stride=1, stride_axis=0)
            line = jnp.sum(wide, axis=0, keepdims=True)
            by_bucket = by_bucket + jnp.where(
                buckets == line_ids[block], line, 0.0
            )
        side = lax.broadcasted_iota(jnp.int32, (BUCKETS, 128), 0)
        low_line = jnp.sum(far_low, axis=0, keepdims=True)
        high_line = jnp.sum(far_high, axis=0, keepdims=True)
        ends = jnp.where(side == BUCKETS // 2 - 1, low_line, 0.0) + jnp.where(
            side == BUCKETS - 1, high_line, 0.0
        )
        by_bucket = by_bucket[:, :128] + by_bucket[:, 128:] + ends
        bias_columns.append(jnp.sum(by_bucket, axis=1, keepdims=True))
    query_t = jnp.concatenate(query_grads, axis=0).astype(BF16)
    key_low = key_grad.astype(BF16)
    value_low = value_grad.astype(BF16)
    normed = normed_ref[...]
    grads_ref[pl.ds(0, WIDTH), :D] = dot(query_t, normed).astype(BF16)
    for i, low in ((1, key_low), (2, value_low)):
        grads_ref[pl.ds(i * WIDTH, WIDTH), :D] = dot_tn(low, normed).astype(BF16)
    lanes = lax.broadcasted_iota(jnp.int32, (BUCKETS, 128), 1)
    bias = sum(jnp.where(lanes == h, bias_columns[h], 0.0) for h in range(HEADS_HERE))
    bias = jnp.concatenate([bias, jnp.zeros((128 - BUCKETS, 128), F32)], axis=0)
    bias = jnp.transpose(bias)[:8]
    bias = jnp.concatenate([bias, jnp.zeros((8, D - 128), F32)], axis=1)
    rest = dot_tn(logit_s[...], mixed_ref[...])
    index = lax.broadcasted_iota(jnp.int32, (8, D), 0)
    tail = jnp.where(index == 0, gain_grad, pltpu.roll(bias, 1, 0))
    rest = jnp.concatenate([rest[:EXPERTS], tail, rest[EXPERTS + 8 :]], axis=0)
    grads_ref[:, D:] = jnp.transpose(rest).astype(BF16)
    wide_s[...] = (
        dot_tn(query_t, wq_ref[...]) + dot(key_low, wk_ref[...]) + dot(value_low, wv_ref[...])
    )
    gain_one = jnp.zeros((8, D), F32)
    for i in range(SEQ // 32):
        rows = slice(i * 32, i * 32 + 32)
        normed_part = wide_s[rows, :]
        normed_s[rows, :] = normed_part.astype(BF16)
        hidden = x_ref[rows, :].astype(F32)
        scale = stats_ref[rows, 0:1]
        gain_one = gain_one + jnp.sum((normed_part * hidden * scale).reshape(4, 8, D), axis=0)
    gain_rows = jnp.broadcast_to(jnp.sum(gain_one, axis=0, keepdims=True), (16, D)).astype(BF16)
    for out, start in ((mine_ref, core * 256), (theirs_ref, (1 - core) * 256)):
        out[:256, :] = normed_s[pl.ds(pl.multiple_of(start, 256), 256), :]
        out[256:, :] = gain_rows
    output_copy.wait()
    middle_copy.wait()


def halves(core, own_ref, other_ref, i):
    local = slice((i % 2) * 128, (i % 2) * 128 + 128)
    return jnp.where(core == i // 2, own_ref[local, :], other_ref[local, :]).astype(F32)


def reduce_kernel(parts_ref, halved_ref, link_ref, send_ref):
    extra = pl.ds(256, 16)
    gain_grad = (halved_ref[extra, :].astype(F32) + link_ref[extra, :].astype(F32))[0:1]
    total = jnp.zeros((24, GRADS), F32)
    for j in range(GROUPS // 2):
        pair = parts_ref[pl.ds(j * 48, 48), :].astype(F32)
        total = total + pair[:24] + pair[24:]
    lines = [
        pltpu.roll(gain_grad[:, r // 4 * 128 : r // 4 * 128 + 128], (96 - r % 4 * 32) % 128, 1)
        for r in range(24)
    ]
    lanes = lax.broadcasted_iota(jnp.int32, (24, 128), 1)
    last = jnp.where(lanes < 96, total[:, D:], jnp.concatenate(lines, axis=0))
    chunk = jnp.concatenate([total[:, :D], last], axis=1)
    pair = jnp.concatenate([chunk, chunk], axis=0).astype(BF16)
    for j in range(GROUPS // 2):
        send_ref[pl.ds(j * 48, 48), :] = pair


def input_kernel(place_ref, own_ref, other_ref, x_ref, gain_ref, middle_grad_ref, input_ref):
    core = place_ref[1]
    gain = gain_ref[...]
    for i in range(4):
        rows = slice(i * 128, i * 128 + 128)
        hidden = x_ref[rows, :].astype(F32)
        scale = lax.rsqrt(jnp.mean(hidden * hidden, axis=-1, keepdims=True) + EPS)
        weighted = halves(core, own_ref, other_ref, i) * gain
        inner = jnp.mean(weighted * hidden, axis=-1, keepdims=True)
        input_ref[rows, :] = (
            middle_grad_ref[rows, :]
            + scale * weighted
            - hidden * (scale * scale * scale * inner)
        )


def finish_kernel(
    recv_ref, gain_one_ref, gain_two_ref, bias_ref,
    q_ref, k_ref, v_ref, o_ref, router_ref,
):
    for i, out in enumerate((q_ref, k_ref, v_ref, o_ref)):
        out[...] = recv_ref[pl.ds(i * WIDTH, WIDTH), :D].astype(F32)
    last = recv_ref[:, D:].astype(F32)
    summed = jnp.zeros((24, 128), F32)
    for j in range(GROUPS):
        summed = summed + last[j * 24 : j * 24 + 24]
    lanes = lax.broadcasted_iota(jnp.int32, (1, 128), 1)
    for block in range(6):
        line = jnp.zeros((1, 128), F32)
        for i in range(4):
            r = block * 4 + i
            piece = pltpu.roll(summed[r : r + 1], (32 + 32 * i) % 128, 1)
            line = jnp.where((lanes >= 32 * i) & (lanes < 32 * i + 32), piece, line)
        gain_one_ref[pl.ds(block * 128, 128)] = line[0]
    turned = jnp.transpose(last)
    router_ref[...] = turned[:EXPERTS]
    tail = turned[EXPERTS : EXPERTS + 8]
    gain_two_ref[...] = tail[0]
    bias_ref[...] = tail[1 : 1 + HEADS_HERE, :BUCKETS]


def shards(
    layer_input, attn_gain, query_weight, key_weight, value_weight, output_weight, position_bias,
    moe_gain, router_weight, expert_in, expert_out, route_expert, route_slot, route_drop, out_grad,
):
    experts_axis = ("z", "x", "h")
    pair_axis = ("l", "z", "x", "h")
    core = lax.axis_index("c")
    place = jnp.stack([lax.axis_index("l") * 2 + core, core]).astype(jnp.int32)

    def swap(array, axis):
        return lax.ppermute(array, axis, [(0, 1), (1, 0)])

    gain_one = attn_gain.reshape(1, D)
    gain_two = moe_gain.reshape(1, D)
    zeros = jnp.zeros_like(route_drop)
    route = jnp.stack([route_expert, route_slot, route_drop] + [zeros] * 5)
    table = jnp.transpose(position_bias)
    wq, wk, wv = (jnp.transpose(w) for w in (query_weight, key_weight, value_weight))
    router = jnp.pad(jnp.transpose(router_weight), ((0, 128 - EXPERTS), (0, 0)))
    wo_link = swap(output_weight, "l")
    wo_core = swap(output_weight, "c")
    wo_far = swap(wo_link, "c")

    tall = shape((SEQ, WIDTH), BF16)
    wide = shape((SEQ, D), BF16)
    tile_shape = (3 * HEADS_HERE, 128, 128)
    weight_vmem = pltpu.VMEM((WIDTH, D), BF16)
    tall_vmem = pltpu.VMEM((SEQ, WIDTH), BF16)
    normed, queries, keys, values, tiles, context, lse = call(
        attention_forward,
        (wide, tall, tall, tall, shape(tile_shape, F32), tall, shape((8, SEQ), F32)),
        (table, layer_input, attn_gain, wq, wk, wv),
        far=(0, 1, 2, 3, 4, 5), far_out=(0, 1, 2, 3, 4),
        scratch=(pltpu.VMEM((HEADS_HERE, BUCKETS), F32), pltpu.VMEM((SEQ, D), BF16),
                 pltpu.VMEM((D,), F32), weight_vmem, weight_vmem, weight_vmem, pltpu.VMEM((SEQ, D), BF16),
                 tall_vmem, tall_vmem, tall_vmem, pltpu.VMEM(tile_shape, F32),
                 pltpu.SemaphoreType.DMA((11,))),
        limit=60, flops=900_000_000, moved=5_000_000,
    )
    flat, flat_t = shape((ROWS, SEQ), BF16), shape((SEQ, ROWS), BF16)
    sums = shape((ROWS, HALF), BF16)
    ctx_link = swap(context, "l")
    ctx_core = swap(context, "c")
    low_place, high_place, base, raw = call(
        near_kernel, (flat, flat, shape((SEQ, D), F32), sums),
        (place, route, context, ctx_core, output_weight, wo_core, out_grad),
        scalars=1, limit=16, flops=1_500_000_000, moved=7_000_000,
    )
    ctx_link_late, low_place = lax.optimization_barrier((ctx_link, low_place))
    ctx_far = swap(ctx_link_late, "c")
    middle, mixed, probs, send = call(
        middle_kernel,
        (shape((SEQ, D), F32), wide, shape((SEQ, 128), F32), sums),
        (place, layer_input, base, ctx_link, ctx_far, wo_link, wo_far, gain_two, router, route,
         low_place, high_place, raw),
        scratch=(pltpu.VMEM((SEQ, D), F32), pltpu.VMEM((SEQ, 128), BF16)),
        scalars=1, limit=16, flops=1_700_000_000, moved=8_000_000,
    )
    received = lax.all_to_all(send, experts_axis, 0, 0, tiled=True)
    received, route_late = lax.optimization_barrier((received, route))
    low_back, high_back = call(
        back_place_kernel, (flat_t, flat_t), (route_late,),
        limit=12, flops=10_000_000, moved=2_700_000,
    )
    received_other, low_back, high_back = lax.optimization_barrier(
        (swap(received, "c"), low_back, high_back)
    )
    select = regroup_matrix()
    low = shape((2, 320, D), BF16)
    back_select = jnp.asarray(select.T, BF16)
    theirs, slots, slot_grads, act, pre_grad = call(
        first_expert_kernel,
        (sums, low, low, low, low),
        (place, received, received_other, expert_in, expert_out,
         jnp.asarray(select, BF16), back_select),
        scratch=(pltpu.VMEM((2, 320, D), BF16),),
        scalars=1, limit=24, flops=4_000_000_000, moved=14_000_000,
    )
    mine = call(
        second_expert_kernel, sums,
        (place, act, pre_grad, expert_in, expert_out, back_select),
        scratch=(pltpu.VMEM((2, 320, D), BF16),),
        scalars=1, limit=12, flops=1_000_000_000, moved=4_000_000,
    )
    partial = (mine.astype(F32) + swap(theirs, "c").astype(F32)).astype(BF16)
    back = lax.all_to_all(
        jnp.concatenate([partial, partial], axis=0), pair_axis, 0, 0, tiled=True
    )
    rows_own = call(
        tokens_kernel, shape((SEQ, D), BF16), (low_back, high_back, back),
        limit=12, flops=2_000_000_000, moved=3_000_000,
    )
    rows_own, queries_late, middle_late = lax.optimization_barrier((rows_own, queries, middle))
    weights, stats = call(
        window_kernel, (shape((HEADS_HERE, 2, SEQ, 256), BF16), shape((SEQ, 128), F32)),
        (table, queries_late, keys, lse, tiles, layer_input, middle_late, probs, route),
        limit=14, flops=300_000_000, moved=6_000_000,
    )
    rows_other, stats = lax.optimization_barrier((swap(rows_own, "c"), stats))
    half = shape((256 + 16, D), BF16)
    layer_output, middle_grad, grads, norm_mine, norm_theirs = call(
        backward_kernel,
        (wide, shape((SEQ, D), F32), shape((D, GRADS), BF16), half, half),
        (place, layer_input, middle, mixed, probs, route, out_grad,
         rows_own, rows_other, router, gain_two, output_weight, context, queries, keys,
         values, normed, weights, stats, wq, wk, wv),
        scratch=(pltpu.VMEM((SEQ, D), BF16), pltpu.VMEM((SEQ, 128), BF16),
                 pltpu.VMEM((SEQ, D), BF16), pltpu.VMEM((SEQ, D), F32),
                 pltpu.VMEM((SEQ, D), BF16), pltpu.VMEM((SEQ, D), F32),
                 pltpu.SemaphoreType.DMA((2,))),
        far_out=(0, 1),
        scalars=1, limit=24, flops=4_000_000_000, moved=12_000_000,
    )
    halved = (norm_mine.astype(F32) + swap(norm_theirs, "c").astype(F32)).astype(BF16)
    scattered = lax.all_to_all(grads, experts_axis, 0, 0, tiled=True)
    halved_link = swap(halved, "l")
    reduced = (halved.astype(F32) + halved_link.astype(F32)).astype(BF16)
    reduced_other = swap(reduced, "c")
    spread = call(
        reduce_kernel, shape((D, GRADS), BF16),
        (scattered, halved, halved_link),
        limit=12, flops=10_000_000, moved=3_000_000,
    )
    spread, slots, slot_grads, act, pre_grad = lax.optimization_barrier(
        (spread, slots, slot_grads, act, pre_grad)
    )
    expert_in_grad, expert_out_grad = expert_grads(slots, slot_grads, act, pre_grad)
    gathered = lax.all_to_all(spread, experts_axis, 0, 0, tiled=True)
    input_grad = call(
        input_kernel, shape((SEQ, D), F32),
        (place, reduced, reduced_other, layer_input, gain_one, middle_grad),
        alias={5: 0}, scalars=1, limit=12, flops=10_000_000, moved=5_000_000,
    )
    out = shape((WIDTH, D), F32)
    line = shape((D,), F32)
    gain_one_grad, gain_two_grad, bias_grad, query_grad, key_grad, value_grad, output_grad, \
        router_grad = call(
            finish_kernel,
            (line, line, shape((HEADS_HERE, BUCKETS), F32), out, out, out, out,
             shape((EXPERTS, D), F32)),
            (gathered,),
            limit=12, flops=10_000_000, moved=6_000_000,
        )
    return (
        layer_output,
        input_grad,
        gain_one_grad,
        jnp.transpose(query_grad),
        jnp.transpose(key_grad),
        jnp.transpose(value_grad),
        output_grad,
        jnp.transpose(bias_grad),
        gain_two_grad,
        jnp.transpose(router_grad),
        expert_in_grad,
        expert_out_grad,
    )


def solution(mesh):
    fine = Mesh(mesh.devices.reshape(4, 4, 2, 2, 2), ("z", "x", "h", "l", "c"))
    ex = ("z", "x", "h")
    te = ("l", "c")
    in_specs = (
        P(ex, None), P(), P(None, te), P(None, te), P(None, te), P(te, None), P(None, te), P(),
        P(), P(ex, None, te), P(ex, te, None), P(ex), P(ex), P(ex), P(ex, None),
    )
    out_specs = (
        P(ex, None), P(ex, None), P(), P(None, te), P(None, te), P(None, te), P(te, None),
        P(None, te), P(), P(), P(ex, None, te), P(ex, te, None),
    )
    return jax.shard_map(shards, mesh=fine, in_specs=in_specs, out_specs=out_specs, check_vma=False)
```

```python
import jax
import jax.numpy as jnp
import numpy as np
from jax import lax
from jax.experimental import pallas as pl
from jax.experimental.pallas import tpu as pltpu
from jax.sharding import Mesh
from jax.sharding import PartitionSpec as P

BUCKETS = 32
EPS = 1e-06
SEQ = 512
D = 768
HEAD = 64
HEADS_HERE = 3
WIDTH = HEADS_HERE * HEAD
EXPERTS = 64
CAP = 10
GROUPS = 32
CHUNK = 40
ROWS = GROUPS * CHUNK
HALF = D // 2
GRADS = 896
F32 = jnp.float32
BF16 = jnp.bfloat16
GELU_C = float(np.sqrt(2.0 / np.pi))


def bucket_of(offsets):
    half_count = BUCKETS // 2
    exact_count = half_count // 2
    upper_side = (offsets > 0).astype(np.int64) * half_count
    distance = np.abs(offsets)
    ratio = np.log(np.maximum(distance, 1) / exact_count) / np.log(128.0 / exact_count)
    far_bucket = np.minimum(
        exact_count + (ratio * (half_count - exact_count)).astype(np.int64), half_count - 1
    )
    return upper_side + np.where(distance < exact_count, distance, far_bucket)


FAR_STARTS = [
    int(np.argmax(bucket_of(-np.arange(256)) >= b)) for b in range(9, BUCKETS // 2)
]


def line_buckets(block, rows):
    offset = 128 * block + 128 - lax.broadcasted_iota(jnp.int32, (rows, 256), 1)
    distance = jnp.abs(offset)
    far = jnp.full((rows, 256), 8, jnp.int32)
    for start in FAR_STARTS:
        far = far + (distance >= start).astype(jnp.int32)
    bucket = jnp.where(distance < 8, distance, far)
    return jnp.where(offset > 0, bucket + BUCKETS // 2, bucket)


def regroup_matrix():
    sel = np.zeros((320, 320), np.float32)
    for g in range(8):
        for half in range(2):
            for e in range(2):
                for c in range(CAP):
                    sel[half * 160 + e * 80 + g * 10 + c, g * 40 + half * 20 + e * 10 + c] = 1
    return sel


def dot(a, b):
    return jnp.dot(a, b, preferred_element_type=F32)


def dot_nt(a, b):
    return lax.dot_general(a, b, (((1,), (1,)), ((), ())), preferred_element_type=F32)


def dot_tn(a, b):
    return lax.dot_general(a, b, (((0,), (0,)), ((), ())), preferred_element_type=F32)


def head_mask(head, rows):
    lanes = lax.broadcasted_iota(jnp.int32, (rows, WIDTH), 1)
    return (lanes >= head * HEAD) & (lanes < (head + 1) * HEAD)


def only_head(matrix, head):
    return jnp.where(head_mask(head, matrix.shape[0]), matrix, jnp.zeros_like(matrix))


def call(
    body, out_shape, args, scratch=(), scalars=0, far=(), far_out=(), alias=None, limit=40, flops=0, moved=0
):
    spaces = [pltpu.SMEM] * scalars + [pltpu.VMEM] * (len(args) - scalars)
    for i in far:
        spaces[i] = pltpu.HBM
    outs = out_shape if isinstance(out_shape, tuple) else (out_shape,)
    out_spaces = [pltpu.HBM if i in far_out else pltpu.VMEM for i in range(len(outs))]
    result = pl.pallas_call(
        body,
        out_shape=outs,
        in_specs=[pl.BlockSpec(memory_space=space) for space in spaces],
        out_specs=tuple(pl.BlockSpec(memory_space=space) for space in out_spaces),
        scratch_shapes=scratch,
        input_output_aliases=alias or {},
        compiler_params=pltpu.CompilerParams(vmem_limit_bytes=limit << 20),
        cost_estimate=pl.CostEstimate(flops=flops, bytes_accessed=moved, transcendentals=0),
    )(*args)
    return result if isinstance(out_shape, tuple) else result[0]


def shape(dims, dtype):
    return jax.ShapeDtypeStruct(dims, dtype)


def bias_tile(tiles_ref, far_low, far_high, head, block):
    if block < -1:
        return far_low
    if block > 1:
        return far_high
    return tiles_ref[head * 3 + block + 1]


def scores_t(keys, query_scaled, tiles_ref, table, head, part):
    raw = dot_nt(keys, query_scaled)
    far_low = table[head : head + 1, BUCKETS // 2 - 1 : BUCKETS // 2]
    far_high = table[head : head + 1, BUCKETS - 1 : BUCKETS]
    rows = []
    for key_block in range(4):
        cols = []
        for i in range(2):
            piece = raw[key_block * 128 : key_block * 128 + 128, i * 128 : i * 128 + 128]
            block = key_block - (part * 2 + i)
            cols.append(piece + bias_tile(tiles_ref, far_low, far_high, head, block))
        rows.append(jnp.concatenate(cols, axis=1))
    return jnp.concatenate(rows, axis=0)


def attention_forward(
    table_hbm, x_hbm, gain_hbm, wq_hbm, wk_hbm, wv_hbm,
    normed_hbm, q_hbm, k_hbm, v_hbm, tiles_hbm, ctx_hbm, lse_ref,
    table_ref, x_ref, gain_ref, wq_ref, wk_ref, wv_ref, normed_ref, q_ref, k_ref, v_ref,
    ctx_ref, tiles_ref, sems,
):
    loads = [
        pltpu.make_async_copy(src, dst, sems.at[i])
        for i, (src, dst) in enumerate(
            (
                (table_hbm, table_ref), (x_hbm, x_ref), (wq_hbm, wq_ref), (wk_hbm, wk_ref),
                (wv_hbm, wv_ref), (gain_hbm, gain_ref),
            )
        )
    ]
    for load in loads:
        load.start()
    stores = []

    def store(src, dst):
        copy = pltpu.make_async_copy(src, dst, sems.at[6 + len(stores)])
        copy.start()
        stores.append(copy)

    loads[0].wait()
    table = table_ref[...]
    lines = []
    for block in (-1, 0, 1):
        buckets = lax.broadcasted_iota(jnp.int32, (BUCKETS, 256), 0)
        hot = (buckets == line_buckets(block, 1)).astype(F32)
        lines.append(
            jnp.dot(table, hot, precision=lax.Precision.HIGHEST, preferred_element_type=F32)
        )
    for head in range(HEADS_HERE):
        for block in range(3):
            wide = pltpu.roll(
                jnp.broadcast_to(lines[block][head : head + 1], (128, 256)),
                0, 1, stride=1, stride_axis=0,
            )
            tiles_ref[head * 3 + block] = wide[:, 128:]
    store(tiles_ref, tiles_hbm)
    loads[1].wait()
    loads[5].wait()
    gain = gain_ref[...].reshape(1, D)
    for i in range(SEQ // 32):
        rows = pl.ds(i * 32, 32)
        x = x_ref[rows, :].astype(F32)
        scale = lax.rsqrt(jnp.mean(x * x, axis=-1, keepdims=True) + EPS)
        normed_ref[rows, :] = (x * scale * gain).astype(BF16)
    store(normed_ref, normed_hbm)
    normed = normed_ref[...]
    for load, weight, out, out_hbm in (
        (loads[2], wq_ref, q_ref, q_hbm),
        (loads[3], wk_ref, k_ref, k_hbm),
        (loads[4], wv_ref, v_ref, v_hbm),
    ):
        load.wait()
        out[...] = dot_nt(normed, weight[...]).astype(BF16)
        store(out, out_hbm)
    queries, keys, values = q_ref[...], k_ref[...], v_ref[...]
    lse_ref[...] = jnp.zeros((8, SEQ), F32)
    scaled = queries * jnp.asarray(HEAD**-0.5, BF16)
    for part in range(2):
        rows = slice(part * 256, part * 256 + 256)
        context = jnp.zeros((256, WIDTH), F32)
        for head in range(HEADS_HERE):
            scores = scores_t(keys, only_head(scaled[rows], head), tiles_ref, table, head, part)
            top = jnp.max(scores, axis=0, keepdims=True)
            grown = jnp.exp(scores - top)
            total = jnp.sum(grown, axis=0, keepdims=True)
            probs = (grown * (1.0 / total)).astype(BF16)
            lse_ref[head : head + 1, rows] = top + jnp.log(total)
            context = context + dot_tn(probs, only_head(values, head))
        ctx_ref[rows, :] = context.astype(BF16)
        store(ctx_ref.at[pl.ds(part * 256, 256)], ctx_hbm.at[pl.ds(part * 256, 256)])
    for copy in stores:
        copy.wait()


def route_columns(route_ref):
    return jnp.transpose(route_ref[...].astype(F32))


def row_of(expert, slot, drop):
    row = (expert >> 1) * CHUNK + (expert & 1) * CAP + slot
    return jnp.where(drop > 0, -1000, row)


def near_kernel(
    place_ref, route_ref, ctx0, ctx1, wo0, wo1, grad_ref, low_ref, high_ref, base_ref, raw_ref
):
    target = row_of(route_ref[0:1, :], route_ref[1:2, :], route_ref[2:3, :])
    for i in range(4):
        rows = pl.ds(i * 320, 320)
        index = lax.broadcasted_iota(jnp.int32, (320, SEQ), 0) + 320 * i
        low = (index == target).astype(F32).astype(BF16)
        high = (index == target + 20).astype(F32).astype(BF16)
        low_ref[rows, :] = low
        high_ref[rows, :] = high
        raw = dot(low, grad_ref[:, :HALF]) + dot(high, grad_ref[:, HALF:])
        raw_ref[rows, :] = raw.astype(BF16)
    pair_of_heads(place_ref[1], ctx0, ctx1, wo0, wo1, base_ref)


def pair_of_heads(core, ctx0, ctx1, wo0, wo1, sum_ref):
    @pl.when(core == 0)
    def _():
        sum_ref[...] = dot(ctx0[...], wo0[...]) + dot(ctx1[...], wo1[...])

    @pl.when(core == 1)
    def _():
        sum_ref[...] = dot(ctx1[...], wo1[...]) + dot(ctx0[...], wo0[...])


def back_place_kernel(route_ref, low_ref, high_ref):
    columns = route_columns(route_ref).astype(jnp.int32)
    target = row_of(columns[:, 0:1], columns[:, 1:2], columns[:, 2:3])
    for i in range(4):
        rows = slice(i * 128, i * 128 + 128)
        index = lax.broadcasted_iota(jnp.int32, (128, ROWS), 1)
        low_ref[rows, :] = (index == target[rows]).astype(F32).astype(BF16)
        high_ref[rows, :] = (index == target[rows] + 20).astype(F32).astype(BF16)


def middle_kernel(
    place_ref, x_ref, base_ref, ctx2, ctx3, wo2, wo3, gain_ref, router_ref, route_ref,
    low_ref, high_ref, raw_ref, middle_ref, mixed_ref, probs_ref, send_ref, far_s, gate_s,
):
    core = place_ref[1]
    columns = route_columns(route_ref)
    pair_of_heads(core, ctx2, ctx3, wo2, wo3, far_s)
    for i in range(SEQ // 32):
        rows = slice(i * 32, i * 32 + 32)
        middle = x_ref[rows, :].astype(F32) + (base_ref[rows, :] + far_s[rows, :])
        scale = lax.rsqrt(jnp.mean(middle * middle, axis=-1, keepdims=True) + EPS)
        middle_ref[rows, :] = middle
        mixed_ref[rows, :] = (middle * scale * gain_ref[...]).astype(BF16)
    for i in range(4):
        rows = slice(i * 128, i * 128 + 128)
        lanes = lax.broadcasted_iota(jnp.int32, (128, 128), 1)
        logits = dot_nt(mixed_ref[rows, :], router_ref[...])
        logits = jnp.where(lanes < EXPERTS, logits, -jnp.inf)
        grown = jnp.exp(logits - jnp.max(logits, axis=-1, keepdims=True))
        probs = grown / jnp.sum(grown, axis=-1, keepdims=True)
        probs_ref[rows, :] = probs
        expert = columns[rows, 0:1].astype(jnp.int32)
        chosen = jnp.sum(jnp.where(lanes == expert, probs, 0.0), axis=-1, keepdims=True)
        gate = chosen * (1.0 - columns[rows, 2:3])
        first = gate.astype(BF16).astype(F32)
        second = (gate - first).astype(BF16).astype(F32)
        third = gate - first - second
        pieces = jnp.where(lanes == 0, first, jnp.where(lanes == 1, second, third))
        gate_s[rows, :] = jnp.where(lanes < 3, pieces, 0.0).astype(BF16)

    @pl.when(core == 0)
    def _():
        for i in range(4):
            rows = pl.ds(i * 320, 320)
            out = dot(low_ref[rows, :], mixed_ref[:, :HALF])
            out = out + dot(high_ref[rows, :], mixed_ref[:, HALF:])
            send_ref[rows, :] = out.astype(BF16)

    @pl.when(core == 1)
    def _():
        for i in range(4):
            rows = pl.ds(i * 320, 320)
            gate = dot(low_ref[rows, :], gate_s[...]) + dot(high_ref[rows, :], gate_s[...])
            gate = jnp.sum(gate, axis=-1, keepdims=True)
            send_ref[rows, :] = (raw_ref[rows, :].astype(F32) * gate).astype(BF16)


def first_expert_kernel(
    place_ref, own_ref, other_ref, in_ref, out_ref, sel_ref, back_ref,
    theirs_ref, x_ref, s_ref, act_ref, pre_ref, part_s,
):
    core = place_ref[1]
    for b in range(4):
        rows = pl.ds(b * 320, 320)
        own = own_ref[rows, :]
        other = other_ref[rows, :]
        for dest, block in (
            (x_ref, jnp.where(core == 0, own, other)),
            (s_ref, jnp.where(core == 0, other, own)),
        ):
            sorted_rows = dot(sel_ref[...], block).astype(BF16)
            for half in range(2):
                for e in range(2):
                    dest[e, pl.ds(b * 80, 80), pl.ds(half * HALF, HALF)] = sorted_rows[
                        half * 160 + e * 80 : half * 160 + e * 80 + 80
                    ]
    for e in range(2):
        x = x_ref[e]
        s = s_ref[e]
        for f in range(3):
            cols = slice(f * 256, f * 256 + 256)
            pre = dot(x, in_ref[e, :, cols])
            bent = jnp.tanh(GELU_C * (pre + 0.044715 * (pre * pre * pre)))
            cdf = 0.5 * (1.0 + bent)
            act_ref[e, :, cols] = (pre * cdf).astype(BF16)
            slope = cdf + (0.5 * GELU_C) * pre * (1.0 - bent * bent) * (
                1.0 + (3 * 0.044715) * (pre * pre)
            )
            act_grad = dot_nt(s, out_ref[e, cols, :])
            pre_ref[e, :, cols] = (act_grad * slope).astype(BF16)
    expert_sums(core == 1, act_ref, pre_ref, in_ref, out_ref, back_ref, theirs_ref, part_s)


def expert_sums(forward, act_ref, pre_ref, in_ref, out_ref, back_ref, sum_ref, part_s):
    @pl.when(forward)
    def _():
        for e in range(2):
            part_s[e] = dot(act_ref[e], out_ref[e]).astype(BF16)

    @pl.when(jnp.logical_not(forward))
    def _():
        for e in range(2):
            part_s[e] = dot_nt(pre_ref[e], in_ref[e]).astype(BF16)

    for b in range(4):
        rows = pl.ds(b * 80, 80)
        stacked = jnp.concatenate(
            [part_s[e, rows, pl.ds(half * HALF, HALF)] for half in range(2) for e in range(2)],
            axis=0,
        )
        sum_ref[pl.ds(b * 320, 320), :] = dot(back_ref[...], stacked).astype(BF16)


def second_expert_kernel(
    place_ref, act_ref, pre_ref, in_ref, out_ref, back_ref, mine_ref, part_s
):
    expert_sums(
        place_ref[1] == 0, act_ref, pre_ref, in_ref, out_ref, back_ref, mine_ref, part_s
    )


def expert_grads_kernel(x_ref, s_ref, act_ref, pre_ref, in_grad_ref, out_grad_ref):
    out_grad_ref[0] = dot_tn(act_ref[0], s_ref[0])
    in_grad_ref[0] = dot_tn(x_ref[0], pre_ref[0])


def expert_grads(x, s, act, pre):
    whole = pl.BlockSpec((1, 320, D), lambda e, f: (e, 0, 0))
    part = pl.BlockSpec((1, 320, 256), lambda e, f: (e, 0, f))
    return pl.pallas_call(
        expert_grads_kernel,
        grid=(2, 3),
        out_shape=(shape((2, D, D), F32), shape((2, D, D), F32)),
        in_specs=[whole, whole, part, part],
        out_specs=(
            pl.BlockSpec((1, D, 256), lambda e, f: (e, 0, f)),
            pl.BlockSpec((1, 256, D), lambda e, f: (e, f, 0)),
        ),
        compiler_params=pltpu.CompilerParams(vmem_limit_bytes=24 << 20),
        cost_estimate=pl.CostEstimate(
            flops=8 * 320 * D * D, bytes_accessed=14_000_000, transcendentals=0
        ),
    )(x, s, act, pre)


def tokens_kernel(low_ref, high_ref, recv_ref, out_ref):
    slots = (
        recv_ref[pl.ds(0, ROWS), :].astype(F32) + recv_ref[pl.ds(ROWS, ROWS), :].astype(F32)
    ).astype(BF16)
    out_ref[:, pl.ds(0, HALF)] = dot(low_ref[...], slots).astype(BF16)
    out_ref[:, pl.ds(HALF, HALF)] = dot(high_ref[...], slots).astype(BF16)


def window_kernel(
    table_ref, q_ref, k_ref, lse_ref, tiles_ref, x_ref, middle_ref, probs_ref, route_ref,
    weights_ref, stats_ref,
):
    scaled = q_ref[...] * jnp.asarray(HEAD**-0.5, BF16)
    keys = k_ref[...]
    for head in range(HEADS_HERE):
        for part in range(2):
            rows = slice(part * 256, part * 256 + 256)
            scores = scores_t(
                keys, only_head(scaled[rows], head), tiles_ref, table_ref[...], head, part
            )
            weights_ref[head, part] = jnp.exp(scores - lse_ref[head : head + 1, rows]).astype(BF16)
    columns = route_columns(route_ref)
    for i in range(SEQ // 32):
        rows = slice(i * 32, i * 32 + 32)
        lanes = lax.broadcasted_iota(jnp.int32, (32, 128), 1)
        middle = middle_ref[rows, :]
        scale_two = lax.rsqrt(jnp.mean(middle * middle, axis=-1, keepdims=True) + EPS)
        hidden = x_ref[rows, :].astype(F32)
        scale_one = lax.rsqrt(jnp.mean(hidden * hidden, axis=-1, keepdims=True) + EPS)
        hot = lanes == columns[rows, 0:1].astype(jnp.int32)
        chosen = jnp.sum(jnp.where(hot, probs_ref[rows, :], 0.0), axis=-1, keepdims=True)
        stats_ref[rows, :] = jnp.where(
            lanes == 0, scale_one, jnp.where(lanes == 1, scale_two, chosen)
        )


def backward_kernel(
    place_ref, x_ref, middle_ref, mixed_ref, probs_ref, route_ref, grad_ref,
    own_ref, other_ref, router_ref, gain_ref, wo_ref, ctx_ref, q_ref, k_ref, v_ref, normed_ref,
    weights_ref, stats_ref, wq_ref, wk_ref, wv_ref,
    output_hbm, middle_grad_hbm, grads_hbm, mine_ref, theirs_ref,
    low_s, logit_s, normed_s, wide_s, output_ref, middle_grad_ref, grads_ref, sems,
):
    core = place_ref[1]
    columns = route_columns(route_ref)
    gain = gain_ref[...]
    for i in range(SEQ // 32):
        rows = slice(i * 32, i * 32 + 32)
        expert_rows = jnp.where(core == 0, own_ref[rows, :], other_ref[rows, :]).astype(F32)
        probs = probs_ref[rows, :]
        kept = 1.0 - columns[rows, 2:3]
        lanes = lax.broadcasted_iota(jnp.int32, (32, 128), 1)
        hot = (lanes == columns[rows, 0:1].astype(jnp.int32)).astype(F32)
        chosen = stats_ref[rows, 2:3]
        upstream = grad_ref[rows, :].astype(F32)
        output_ref[rows, :] = (
            middle_ref[rows, :] + (chosen * kept) * expert_rows
        ).astype(BF16)
        gate_grad = jnp.sum(upstream * expert_rows, axis=-1, keepdims=True) * kept
        logit_s[rows, :] = (probs * (hot - chosen) * gate_grad).astype(BF16)
    output_copy = pltpu.make_async_copy(output_ref, output_hbm, sems.at[0])
    output_copy.start()
    wide_s[...] = dot(logit_s[...], router_ref[...])
    gain_grad = jnp.zeros((8, D), F32)
    for i in range(SEQ // 32):
        rows = slice(i * 32, i * 32 + 32)
        mixed_grad = jnp.where(core == 0, other_ref[rows, :], own_ref[rows, :]).astype(F32)
        mixed_grad = mixed_grad + wide_s[rows, :]
        middle = middle_ref[rows, :]
        scale = stats_ref[rows, 1:2]
        along = mixed_grad * middle
        inner = jnp.mean(along * gain, axis=-1, keepdims=True)
        gain_grad = gain_grad + jnp.sum((along * scale).reshape(4, 8, D), axis=0)
        middle_grad = (
            grad_ref[rows, :].astype(F32)
            + scale * (mixed_grad * gain)
            - middle * (scale * scale * scale * inner)
        )
        middle_grad_ref[rows, :] = middle_grad
        low_s[rows, :] = middle_grad.astype(BF16)
    gain_grad = jnp.sum(gain_grad, axis=0, keepdims=True)
    middle_copy = pltpu.make_async_copy(middle_grad_ref, middle_grad_hbm, sems.at[1])
    middle_copy.start()
    middle_low = low_s[...]
    grads_ref[pl.ds(3 * WIDTH, WIDTH), :D] = dot_tn(ctx_ref[...], middle_low).astype(BF16)
    ctx_grad = dot_nt(middle_low, wo_ref[...]).astype(BF16)

    values = v_ref[...]
    keys_t = jnp.transpose(k_ref[...] * jnp.asarray(HEAD**-0.5, BF16))
    query_scaled = q_ref[...] * jnp.asarray(HEAD**-0.5, BF16)
    key_grad = jnp.zeros((SEQ, WIDTH), F32)
    value_grad = jnp.zeros((SEQ, WIDTH), F32)
    query_grads = []
    buckets = lax.broadcasted_iota(jnp.int32, (BUCKETS, 256), 0)
    line_ids = [line_buckets(block, 1) for block in (-1, 0, 1)]
    bias_columns = []
    turn = (
        lax.broadcasted_iota(jnp.int32, (128, 128), 0)
        + lax.broadcasted_iota(jnp.int32, (128, 128), 1)
        == 127
    ).astype(F32)
    for head in range(HEADS_HERE):
        near = [jnp.zeros((128, 128), F32) for _ in range(3)]
        far_low = jnp.zeros((128, 128), F32)
        far_high = jnp.zeros((128, 128), F32)
        key_head = keys_t[head * HEAD : (head + 1) * HEAD]
        query_parts = []
        for part in range(2):
            rows = slice(part * 256, part * 256 + 256)
            query_head = only_head(query_scaled[rows], head)
            ctx_head = only_head(ctx_grad[rows], head)
            probs_low = weights_ref[head, part]
            probs = probs_low.astype(F32)
            value_grad = value_grad + dot(probs_low, ctx_head)
            prob_grad = dot_nt(values, ctx_head)
            inner = jnp.sum(probs * prob_grad, axis=0, keepdims=True)
            score_grad = (probs * (prob_grad - inner)).astype(BF16)
            key_grad = key_grad + dot(score_grad, query_head)
            query_parts.append(dot(key_head, score_grad))
            for key_block in range(4):
                for i in range(2):
                    piece = score_grad[
                        key_block * 128 : key_block * 128 + 128, i * 128 : i * 128 + 128
                    ].astype(F32)
                    block = key_block - (part * 2 + i)
                    if block < -1:
                        far_low = far_low + piece
                    elif block > 1:
                        far_high = far_high + piece
                    else:
                        near[block + 1] = near[block + 1] + piece
        query_grads.append(jnp.concatenate(query_parts, axis=1))
        by_bucket = jnp.zeros((BUCKETS, 256), F32)
        for block in range(3):
            turned = jnp.dot(
                turn, near[block], precision=lax.Precision.HIGHEST, preferred_element_type=F32
            )
            wide = jnp.concatenate([turned, jnp.zeros((128, 128), F32)], axis=1)
            wide = pltpu.roll(wide, 1, 1, stride=1, stride_axis=0)
            line = jnp.sum(wide, axis=0, keepdims=True)
            by_bucket = by_bucket + jnp.where(
                buckets == line_ids[block], line, 0.0
            )
        side = lax.broadcasted_iota(jnp.int32, (BUCKETS, 128), 0)
        low_line = jnp.sum(far_low, axis=0, keepdims=True)
        high_line = jnp.sum(far_high, axis=0, keepdims=True)
        ends = jnp.where(side == BUCKETS // 2 - 1, low_line, 0.0) + jnp.where(
            side == BUCKETS - 1, high_line, 0.0
        )
        by_bucket = by_bucket[:, :128] + by_bucket[:, 128:] + ends
        bias_columns.append(jnp.sum(by_bucket, axis=1, keepdims=True))
    query_t = jnp.concatenate(query_grads, axis=0).astype(BF16)
    key_low = key_grad.astype(BF16)
    value_low = value_grad.astype(BF16)
    lanes = lax.broadcasted_iota(jnp.int32, (BUCKETS, 128), 1)
    bias = sum(jnp.where(lanes == h, bias_columns[h], 0.0) for h in range(HEADS_HERE))
    bias = jnp.concatenate([bias, jnp.zeros((128 - BUCKETS, 128), F32)], axis=0)
    bias = jnp.transpose(bias)[:8]
    bias = jnp.concatenate([bias, jnp.zeros((8, D - 128), F32)], axis=1)
    rest = dot_tn(logit_s[...], mixed_ref[...])
    index = lax.broadcasted_iota(jnp.int32, (8, D), 0)
    tail = jnp.where(index == 0, gain_grad, pltpu.roll(bias, 1, 0))
    rest = jnp.concatenate([rest[:EXPERTS], tail, rest[EXPERTS + 8 :]], axis=0)
    grads_ref[:, D:] = jnp.transpose(rest).astype(BF16)
    normed = normed_ref[...]
    copies = []
    for i in (3, 0, 1, 2):
        part = pl.ds(i * WIDTH, WIDTH)
        if i == 0:
            grads_ref[part, :D] = dot(query_t, normed).astype(BF16)
        elif i < 3:
            grads_ref[part, :D] = dot_tn((key_low, value_low)[i - 1], normed).astype(BF16)
        copies.append(
            pltpu.make_async_copy(grads_ref.at[part], grads_hbm.at[part], sems.at[2 + i])
        )
        copies[-1].start()
    wide_s[...] = (
        dot_tn(query_t, wq_ref[...]) + dot(key_low, wk_ref[...]) + dot(value_low, wv_ref[...])
    )
    gain_one = jnp.zeros((8, D), F32)
    for i in range(SEQ // 32):
        rows = slice(i * 32, i * 32 + 32)
        normed_part = wide_s[rows, :]
        normed_s[rows, :] = normed_part.astype(BF16)
        hidden = x_ref[rows, :].astype(F32)
        scale = stats_ref[rows, 0:1]
        gain_one = gain_one + jnp.sum((normed_part * hidden * scale).reshape(4, 8, D), axis=0)
    gain_rows = jnp.broadcast_to(jnp.sum(gain_one, axis=0, keepdims=True), (16, D)).astype(BF16)
    for out, start in ((mine_ref, core * 256), (theirs_ref, (1 - core) * 256)):
        out[:256, :] = normed_s[pl.ds(pl.multiple_of(start, 256), 256), :]
        out[256:, :] = gain_rows
    for copy in copies:
        copy.wait()
    output_copy.wait()
    middle_copy.wait()


def halves(core, own_ref, other_ref, i):
    local = slice((i % 2) * 128, (i % 2) * 128 + 128)
    return jnp.where(core == i // 2, own_ref[local, :], other_ref[local, :]).astype(F32)


def reduce_kernel(parts_ref, halved_ref, link_ref, old_hbm, send_ref):
    extra = pl.ds(256, 16)
    gain_grad = (halved_ref[extra, :].astype(F32) + link_ref[extra, :].astype(F32))[0:1]
    total = jnp.zeros((24, GRADS), F32)
    for j in range(GROUPS // 2):
        pair = parts_ref[pl.ds(j * 48, 48), :].astype(F32)
        total = total + pair[:24] + pair[24:]
    lines = [
        pltpu.roll(gain_grad[:, r // 4 * 128 : r // 4 * 128 + 128], (96 - r % 4 * 32) % 128, 1)
        for r in range(24)
    ]
    lanes = lax.broadcasted_iota(jnp.int32, (24, 128), 1)
    last = jnp.where(lanes < 96, total[:, D:], jnp.concatenate(lines, axis=0))
    chunk = jnp.concatenate([total[:, :D], last], axis=1)
    pair = jnp.concatenate([chunk, chunk], axis=0).astype(BF16)
    for j in range(GROUPS // 2):
        send_ref[pl.ds(j * 48, 48), :] = pair


def input_kernel(place_ref, own_ref, other_ref, x_ref, gain_ref, middle_grad_ref, input_ref):
    core = place_ref[1]
    gain = gain_ref[...]
    for i in range(4):
        rows = slice(i * 128, i * 128 + 128)
        hidden = x_ref[rows, :].astype(F32)
        scale = lax.rsqrt(jnp.mean(hidden * hidden, axis=-1, keepdims=True) + EPS)
        weighted = halves(core, own_ref, other_ref, i) * gain
        inner = jnp.mean(weighted * hidden, axis=-1, keepdims=True)
        input_ref[rows, :] = (
            middle_grad_ref[rows, :]
            + scale * weighted
            - hidden * (scale * scale * scale * inner)
        )


def finish_kernel(
    recv_ref, gain_one_ref, gain_two_ref, bias_ref,
    q_hbm, k_hbm, v_hbm, o_hbm, router_ref, wide_s, sems,
):
    copies = []
    for i, out in enumerate((q_hbm, k_hbm, v_hbm, o_hbm)):
        wide_s[i] = recv_ref[pl.ds(i * WIDTH, WIDTH), :D].astype(F32)
        copies.append(pltpu.make_async_copy(wide_s.at[i], out, sems.at[i]))
        copies[-1].start()
    last = recv_ref[:, D:].astype(F32)
    summed = jnp.zeros((24, 128), F32)
    for j in range(GROUPS):
        summed = summed + last[j * 24 : j * 24 + 24]
    lanes = lax.broadcasted_iota(jnp.int32, (1, 128), 1)
    for block in range(6):
        line = jnp.zeros((1, 128), F32)
        for i in range(4):
            r = block * 4 + i
            piece = pltpu.roll(summed[r : r + 1], (32 + 32 * i) % 128, 1)
            line = jnp.where((lanes >= 32 * i) & (lanes < 32 * i + 32), piece, line)
        gain_one_ref[pl.ds(block * 128, 128)] = line[0]
    turned = jnp.transpose(last)
    router_ref[...] = turned[:EXPERTS]
    tail = turned[EXPERTS : EXPERTS + 8]
    gain_two_ref[...] = tail[0]
    bias_ref[...] = tail[1 : 1 + HEADS_HERE, :BUCKETS]
    for copy in copies:
        copy.wait()


def shards(
    layer_input, attn_gain, query_weight, key_weight, value_weight, output_weight, position_bias,
    moe_gain, router_weight, expert_in, expert_out, route_expert, route_slot, route_drop, out_grad,
):
    experts_axis = ("z", "x", "h")
    pair_axis = ("l", "z", "x", "h")
    core = lax.axis_index("c")
    place = jnp.stack([lax.axis_index("l") * 2 + core, core]).astype(jnp.int32)

    def swap(array, axis):
        return lax.ppermute(array, axis, [(0, 1), (1, 0)])

    gain_one = attn_gain.reshape(1, D)
    gain_two = moe_gain.reshape(1, D)
    zeros = jnp.zeros_like(route_drop)
    route = jnp.stack([route_expert, route_slot, route_drop] + [zeros] * 5)
    table = jnp.transpose(position_bias)
    wq, wk, wv = (jnp.transpose(w) for w in (query_weight, key_weight, value_weight))
    router = jnp.pad(jnp.transpose(router_weight), ((0, 128 - EXPERTS), (0, 0)))
    wo_link = swap(output_weight, "l")
    wo_core = swap(output_weight, "c")
    wo_far = swap(wo_link, "c")

    tall = shape((SEQ, WIDTH), BF16)
    wide = shape((SEQ, D), BF16)
    tile_shape = (3 * HEADS_HERE, 128, 128)
    weight_vmem = pltpu.VMEM((WIDTH, D), BF16)
    tall_vmem = pltpu.VMEM((SEQ, WIDTH), BF16)
    normed, queries, keys, values, tiles, context, lse = call(
        attention_forward,
        (wide, tall, tall, tall, shape(tile_shape, F32), tall, shape((8, SEQ), F32)),
        (table, layer_input, attn_gain, wq, wk, wv),
        far=(0, 1, 2, 3, 4, 5), far_out=(0, 1, 2, 3, 4, 5),
        scratch=(pltpu.VMEM((HEADS_HERE, BUCKETS), F32), pltpu.VMEM((SEQ, D), BF16),
                 pltpu.VMEM((D,), F32), weight_vmem, weight_vmem, weight_vmem, pltpu.VMEM((SEQ, D), BF16),
                 tall_vmem, tall_vmem, tall_vmem, tall_vmem, pltpu.VMEM(tile_shape, F32),
                 pltpu.SemaphoreType.DMA((13,))),
        limit=60, flops=900_000_000, moved=5_000_000,
    )
    flat, flat_t = shape((ROWS, SEQ), BF16), shape((SEQ, ROWS), BF16)
    sums = shape((ROWS, HALF), BF16)
    ctx_link = swap(context, "l")
    ctx_core = swap(context, "c")
    low_place, high_place, base, raw = call(
        near_kernel, (flat, flat, shape((SEQ, D), F32), sums),
        (place, route, context, ctx_core, output_weight, wo_core, out_grad),
        scalars=1, limit=16, flops=1_500_000_000, moved=7_000_000,
    )
    ctx_link_late, low_place = lax.optimization_barrier((ctx_link, low_place))
    ctx_far = swap(ctx_link_late, "c")
    middle, mixed, probs, send = call(
        middle_kernel,
        (shape((SEQ, D), F32), wide, shape((SEQ, 128), F32), sums),
        (place, layer_input, base, ctx_link, ctx_far, wo_link, wo_far, gain_two, router, route,
         low_place, high_place, raw),
        scratch=(pltpu.VMEM((SEQ, D), F32), pltpu.VMEM((SEQ, 128), BF16)),
        scalars=1, limit=16, flops=1_700_000_000, moved=8_000_000,
    )
    received = lax.all_to_all(send, experts_axis, 0, 0, tiled=True)
    received, route_late = lax.optimization_barrier((received, route))
    low_back, high_back = call(
        back_place_kernel, (flat_t, flat_t), (route_late,),
        limit=12, flops=10_000_000, moved=2_700_000,
    )
    received_other, low_back, high_back = lax.optimization_barrier(
        (swap(received, "c"), low_back, high_back)
    )
    select = regroup_matrix()
    low = shape((2, 320, D), BF16)
    back_select = jnp.asarray(select.T, BF16)
    theirs, slots, slot_grads, act, pre_grad = call(
        first_expert_kernel,
        (sums, low, low, low, low),
        (place, received, received_other, expert_in, expert_out,
         jnp.asarray(select, BF16), back_select),
        scratch=(pltpu.VMEM((2, 320, D), BF16),),
        scalars=1, limit=24, flops=4_000_000_000, moved=14_000_000,
    )
    mine = call(
        second_expert_kernel, sums,
        (place, act, pre_grad, expert_in, expert_out, back_select),
        scratch=(pltpu.VMEM((2, 320, D), BF16),),
        scalars=1, limit=12, flops=1_000_000_000, moved=4_000_000,
    )
    partial = (mine.astype(F32) + swap(theirs, "c").astype(F32)).astype(BF16)
    back = lax.all_to_all(
        jnp.concatenate([partial, partial], axis=0), pair_axis, 0, 0, tiled=True
    )
    rows_own = call(
        tokens_kernel, shape((SEQ, D), BF16), (low_back, high_back, back),
        limit=12, flops=2_000_000_000, moved=3_000_000,
    )
    rows_own, queries_late, middle_late = lax.optimization_barrier((rows_own, queries, middle))
    weights, stats = call(
        window_kernel, (shape((HEADS_HERE, 2, SEQ, 256), BF16), shape((SEQ, 128), F32)),
        (table, queries_late, keys, lse, tiles, layer_input, middle_late, probs, route),
        limit=14, flops=300_000_000, moved=6_000_000,
    )
    rows_other, stats = lax.optimization_barrier((swap(rows_own, "c"), stats))
    half = shape((256 + 16, D), BF16)
    layer_output, middle_grad, grads, norm_mine, norm_theirs = call(
        backward_kernel,
        (wide, shape((SEQ, D), F32), shape((D, GRADS), BF16), half, half),
        (place, layer_input, middle, mixed, probs, route, out_grad,
         rows_own, rows_other, router, gain_two, output_weight, context, queries, keys,
         values, normed, weights, stats, wq, wk, wv),
        scratch=(pltpu.VMEM((SEQ, D), BF16), pltpu.VMEM((SEQ, 128), BF16),
                 pltpu.VMEM((SEQ, D), BF16), pltpu.VMEM((SEQ, D), F32),
                 pltpu.VMEM((SEQ, D), BF16), pltpu.VMEM((SEQ, D), F32),
                 pltpu.VMEM((D, GRADS), BF16), pltpu.SemaphoreType.DMA((6,))),
        far_out=(0, 1, 2),
        scalars=1, limit=24, flops=4_000_000_000, moved=12_000_000,
    )
    halved = (norm_mine.astype(F32) + swap(norm_theirs, "c").astype(F32)).astype(BF16)
    scattered = lax.all_to_all(grads, experts_axis, 0, 0, tiled=True)
    halved_link = swap(halved, "l")
    reduced = (halved.astype(F32) + halved_link.astype(F32)).astype(BF16)
    reduced_other = swap(reduced, "c")
    spread = call(
        reduce_kernel, shape((D, GRADS), BF16),
        (scattered, halved, halved_link, grads),
        far=(3,), alias={3: 0}, limit=12, flops=10_000_000, moved=3_000_000,
    )
    spread, slots, slot_grads, act, pre_grad = lax.optimization_barrier(
        (spread, slots, slot_grads, act, pre_grad)
    )
    expert_in_grad, expert_out_grad = expert_grads(slots, slot_grads, act, pre_grad)
    gathered = lax.all_to_all(spread, experts_axis, 0, 0, tiled=True)
    input_grad = call(
        input_kernel, shape((SEQ, D), F32),
        (place, reduced, reduced_other, layer_input, gain_one, middle_grad),
        alias={5: 0}, scalars=1, limit=12, flops=10_000_000, moved=5_000_000,
    )
    out = shape((WIDTH, D), F32)
    line = shape((D,), F32)
    gain_one_grad, gain_two_grad, bias_grad, query_grad, key_grad, value_grad, output_grad, \
        router_grad = call(
            finish_kernel,
            (line, line, shape((HEADS_HERE, BUCKETS), F32), out, out, out, out,
             shape((EXPERTS, D), F32)),
            (gathered,),
            scratch=(pltpu.VMEM((4, WIDTH, D), F32), pltpu.SemaphoreType.DMA((4,))),
            far_out=(3, 4, 5, 6), limit=16, flops=10_000_000, moved=6_000_000,
        )
    return (
        layer_output,
        input_grad,
        gain_one_grad,
        jnp.transpose(query_grad),
        jnp.transpose(key_grad),
        jnp.transpose(value_grad),
        output_grad,
        jnp.transpose(bias_grad),
        gain_two_grad,
        jnp.transpose(router_grad),
        expert_in_grad,
        expert_out_grad,
    )


def solution(mesh):
    fine = Mesh(mesh.devices.reshape(4, 4, 2, 2, 2), ("z", "x", "h", "l", "c"))
    ex = ("z", "x", "h")
    te = ("l", "c")
    in_specs = (
        P(ex, None), P(), P(None, te), P(None, te), P(None, te), P(te, None), P(None, te), P(),
        P(), P(ex, None, te), P(ex, te, None), P(ex), P(ex), P(ex), P(ex, None),
    )
    out_specs = (
        P(ex, None), P(ex, None), P(), P(None, te), P(None, te), P(None, te), P(te, None),
        P(None, te), P(), P(), P(ex, None, te), P(ex, te, None),
    )
    return jax.shard_map(shards, mesh=fine, in_specs=in_specs, out_specs=out_specs, check_vma=False)
```
